32 devices in a mesh: blk: 8 (over z, y), head: 4 (over x, core).
Axes of the slice: x: 2, y: 2, z: 4, core: 2. Of those that a mesh axis runs over, the one named last changes fastest.
Arguments:
- encoder_input: bfloat16 [2, 16, 256, 768], P(None, 'blk', 'head'), may hold values from -6 to 6
- passage_lengths: int32 [2, 16], P(None, 'blk'), may hold values from 32 to 256, as said below
- decoder_input: bfloat16 [2, 20, 768], P(None, 'head'), may hold values from -6 to 6
- encoder_query: bfloat16 [768, 768], P('blk', 'head'), may hold values from -0.21875 to 0.21875
- encoder_key: bfloat16 [768, 768], P('blk', 'head'), may hold values from -0.21875 to 0.21875
- encoder_value: bfloat16 [768, 768], P('blk', 'head'), may hold values from -0.21875 to 0.21875
- encoder_output: bfloat16 [768, 768], P('head', 'blk'), may hold values from -1.75 to 1.75
- encoder_inner: bfloat16 [768, 3072], P('blk', 'head'), may hold values from -0.21875 to 0.21875
- encoder_outer: bfloat16 [3072, 768], P('head', 'blk'), may hold values from -0.109375 to 0.109375
- decoder_query: bfloat16 [768, 768], P('blk', 'head'), may hold values from -0.21875 to 0.21875
- decoder_key: bfloat16 [768, 768], P('blk', 'head'), may hold values from -0.21875 to 0.21875
- decoder_value: bfloat16 [768, 768], P('blk', 'head'), may hold values from -0.21875 to 0.21875
- decoder_output: bfloat16 [768, 768], P('head', 'blk'), may hold values from -0.625 to 0.625
- cross_query: bfloat16 [768, 768], P('blk', 'head'), may hold values from -0.21875 to 0.21875
- cross_key: bfloat16 [768, 768], P('blk', 'head'), may hold values from -0.21875 to 0.21875
- cross_value: bfloat16 [768, 768], P('blk', 'head'), may hold values from -0.21875 to 0.21875
- cross_output: bfloat16 [768, 768], P('head', 'blk'), may hold values from -4 to 4
- decoder_inner: bfloat16 [768, 3072], P('blk', 'head'), may hold values from -0.21875 to 0.21875
- decoder_outer: bfloat16 [3072, 768], P('head', 'blk'), may hold values from -0.109375 to 0.109375
- encoder_gains: float32 [2, 768], replicated, may hold values from 0.1 to 1.9
- decoder_gains: float32 [3, 768], replicated, may hold values from 0.1 to 1.9
- encoder_cotangent: bfloat16 [2, 16, 256, 768], P(None, 'blk', 'head'), may hold values from -6 to 6
- decoder_cotangent: bfloat16 [2, 20, 768], P(None, 'head'), may hold values from -6 to 6
Outputs:
- encoder_states: bfloat16 [2, 16, 256, 768], P(None, 'blk', 'head')
- decoder_states: bfloat16 [2, 20, 768], P(None, 'head')
- encoder_input_grad: float32 [2, 16, 256, 768], P(None, 'blk', 'head')
- decoder_input_grad: float32 [2, 20, 768], P(None, 'head')
- encoder_query_grad: float32 [768, 768], P('blk', 'head')
- encoder_key_grad: float32 [768, 768], P('blk', 'head')
- encoder_value_grad: float32 [768, 768], P('blk', 'head')
- encoder_output_grad: float32 [768, 768], P('head', 'blk')
- encoder_inner_grad: float32 [768, 3072], P('blk', 'head')
- encoder_outer_grad: float32 [3072, 768], P('head', 'blk')
- decoder_query_grad: float32 [768, 768], P('blk', 'head')
- decoder_key_grad: float32 [768, 768], P('blk', 'head')
- decoder_value_grad: float32 [768, 768], P('blk', 'head')
- decoder_output_grad: float32 [768, 768], P('head', 'blk')
- cross_query_grad: float32 [768, 768], P('blk', 'head')
- cross_key_grad: float32 [768, 768], P('blk', 'head')
- cross_value_grad: float32 [768, 768], P('blk', 'head')
- cross_output_grad: float32 [768, 768], P('head', 'blk')
- decoder_inner_grad: float32 [768, 3072], P('blk', 'head')
- decoder_outer_grad: float32 [3072, 768], P('head', 'blk')
- encoder_gains_grad: float32 [2, 768], replicated
- decoder_gains_grad: float32 [3, 768], replicated
The draws below stay inside these ranges and needn't reach their ends.
Inputs may be any that keep to these rules, and one draw needn't show every extreme that they name: `passage_lengths`: used token slots of each passage; the first passage of every question fills all 256 slots.
All inputs are finite; a program needn't handle non-finite values.
Results may differ from the reference program's by a relative error of at most 0.029.
The reference program's roundings to bfloat16 on the way count: a program that leaves them out, or rounds other values in their place, can miss the bound.
Values may be sent and summed in bfloat16 or wider, within the bound.
No kernel may reach another device: no remote copies, remote signals or barrier semaphores. Data moves between devices by JAX's collectives and lax.ppermute only.
A program may use at most 128 MiB of HBM per device.

```python
import jax
import jax.numpy as jnp
from jax import lax

D = 768
HEADS = 12
HDIM = 64
FF = 3072
SLOT = 256
PASS_DEV = 2
QUESTIONS = 2
DEC = 20
PASSAGES = 16
KEYS = 4096
N_BLK = 8


def draw_passage_lengths(key, part):
    key = jax.random.fold_in(key, 11)
    drawn = jax.random.randint(key, (QUESTIONS, PASSAGES), SLOT // 8, SLOT + 1)
    leading = jnp.arange(PASSAGES)[None, :] == 0
    return jnp.where(leading, SLOT, drawn).astype(jnp.int32)


def level_of(key, extent, pieces, smallest, largest):
    factor_of, own = 1.0, jax.random.fold_in(key, 6)
    for position, blocks in pieces:
        steps = jnp.exp(jax.random.uniform(jax.random.fold_in(own, position), (blocks,), jnp.float32, smallest / len(pieces), largest / len(pieces)))
        factor_of = factor_of * jnp.repeat(steps, extent[position] // blocks).reshape([-1 if axis == position else 1 for axis in range(len(extent))])
    return factor_of


def scatter_about(key, shape, scale, bound, shards=(), held_as=jnp.bfloat16):
    entries = jax.random.normal(key, shape, jnp.float32) * scale
    if len(shards) > 0:
        entries = level_of(key, shape, shards, -0.22, 0.18) * entries
    return jnp.clip(entries, min=-bound, max=bound).astype(held_as)


def setup_inputs(seed: int = 0) -> dict:
    key_list = jax.random.split(jax.random.key(seed), 24)
    encoder_input = scatter_about(key_list[0], (QUESTIONS, PASSAGES, SLOT, D), 1.0, 6.0, ((1, 8), (2, 4)))
    passage_lengths = draw_passage_lengths(jax.random.fold_in(key_list[23], 71), 0)
    decoder_input = scatter_about(key_list[2], (QUESTIONS, DEC, D), 1.0, 6.0, ((1, 4),))
    encoder_query = scatter_about(key_list[3], (D, D), D ** -0.5, 0.21875, ((0, 8), (1, 4)))
    encoder_key = scatter_about(key_list[4], (D, D), D ** -0.5, 0.21875, ((0, 8), (1, 4)))
    encoder_value = scatter_about(key_list[5], (D, D), D ** -0.5, 0.21875, ((0, 8), (1, 4)))
    encoder_output = scatter_about(key_list[6], (D, D), (max(1, D // 64)) ** -0.5, 1.75, ((0, 4), (1, 8)))
    encoder_inner = scatter_about(key_list[7], (D, FF), D ** -0.5, 0.21875, ((0, 8), (1, 4)))
    encoder_outer = scatter_about(key_list[8], (FF, D), FF ** -0.5, 0.109375, ((0, 4), (1, 8)))
    decoder_query = scatter_about(key_list[9], (D, D), D ** -0.5, 0.21875, ((0, 8), (1, 4)))
    decoder_key = scatter_about(key_list[10], (D, D), D ** -0.5, 0.21875, ((0, 8), (1, 4)))
    decoder_value = scatter_about(key_list[11], (D, D), D ** -0.5, 0.21875, ((0, 8), (1, 4)))
    decoder_output = scatter_about(key_list[12], (D, D), (max(1, D // 8)) ** -0.5, 0.625, ((0, 4), (1, 8)))
    cross_query = scatter_about(key_list[13], (D, D), D ** -0.5, 0.21875, ((0, 8), (1, 4)))
    cross_key = scatter_about(key_list[14], (D, D), D ** -0.5, 0.21875, ((0, 8), (1, 4)))
    cross_value = scatter_about(key_list[15], (D, D), D ** -0.5, 0.21875, ((0, 8), (1, 4)))
    cross_output = scatter_about(key_list[16], (D, D), (0.3 * (KEYS // D) ** 0.5), 4.0, ((0, 4), (1, 8)))
    decoder_inner = scatter_about(key_list[17], (D, FF), D ** -0.5, 0.21875, ((0, 8), (1, 4)))
    decoder_outer = scatter_about(key_list[18], (FF, D), FF ** -0.5, 0.109375, ((0, 4), (1, 8)))
    encoder_gains = jnp.clip(1.0 + 0.18 * jax.random.normal(key_list[19], (2, D), jnp.float32), 0.1, 1.9)
    decoder_gains = jnp.clip(1.0 + 0.18 * jax.random.normal(key_list[20], (3, D), jnp.float32), 0.1, 1.9)
    encoder_cotangent = scatter_about(key_list[21], (QUESTIONS, PASSAGES, SLOT, D), 1.0, 6.0, ((1, 8), (2, 4)))
    decoder_cotangent = scatter_about(key_list[22], (QUESTIONS, DEC, D), 1.0, 6.0, ((1, 4),))
    return {"encoder_input": encoder_input, "passage_lengths": passage_lengths, "decoder_input": decoder_input, "encoder_query": encoder_query, "encoder_key": encoder_key, "encoder_value": encoder_value, "encoder_output": encoder_output, "encoder_inner": encoder_inner, "encoder_outer": encoder_outer, "decoder_query": decoder_query, "decoder_key": decoder_key, "decoder_value": decoder_value, "decoder_output": decoder_output, "cross_query": cross_query, "cross_key": cross_key, "cross_value": cross_value, "cross_output": cross_output, "decoder_inner": decoder_inner, "decoder_outer": decoder_outer, "encoder_gains": encoder_gains, "decoder_gains": decoder_gains, "encoder_cotangent": encoder_cotangent, "decoder_cotangent": decoder_cotangent}


@jax.custom_vjp
def low(v):
    return lax.optimization_barrier(v.astype(jnp.bfloat16)).astype(jnp.float32)

@jax.custom_vjp
def low_back(v):
    return v

def low_keep(v):
    return (low(v), None)

def low_pass(kept, grad):
    return (grad,)

def back_keep(v):
    return (v, None)

def back_low(kept, grad):
    return (low(grad),)
low.defvjp(low_keep, low_pass)
low_back.defvjp(back_keep, back_low)
highest = lax.Precision.HIGHEST
masked_score = -1000000000.0

def rounded(v):
    return low_back(low(v))

def project(left, weight):
    return jnp.einsum('...k,kn->...n', left, weight, precision=highest)

def norm_rows(values, gain):
    return values * lax.rsqrt(lax.optimization_barrier(jnp.mean(values * values, axis=-1, keepdims=True)) + 1e-06) * gain

def attention(query, keys, vals, allowed, scale):
    scores = low_back(jnp.einsum('bqhc,bkhc->bhqk', query, keys, precision=highest) * scale)
    scores = jnp.where(allowed, scores, masked_score)
    probs = low(jax.nn.softmax(scores, axis=-1))
    return rounded(jnp.einsum('bhqk,bkhc->bqhc', probs, vals, precision=highest))

def encoder_block(params, inputs, lengths):
    weights, gains = params
    w_query, w_key, w_value, w_output, w_inner, w_outer = weights
    blocks, slot, width = inputs.shape
    scale = HDIM ** (-0.5)
    normed = low(norm_rows(inputs, gains[0]))
    query = rounded(project(normed, w_query)).reshape(blocks, slot, HEADS, HDIM)
    keys = rounded(project(normed, w_key)).reshape(blocks, slot, HEADS, HDIM)
    vals = rounded(project(normed, w_value)).reshape(blocks, slot, HEADS, HDIM)
    allowed = (jnp.arange(slot)[None, :] < lengths[:, None])[:, None, None, :]
    context = attention(query, keys, vals, allowed, scale).reshape(blocks, slot, width)
    hidden = inputs + low_back(project(context, w_output))
    second = low(norm_rows(hidden, gains[1]))
    inner = low_back(project(second, w_inner))
    active = low(jax.nn.gelu(inner, approximate=True))
    return low(hidden + low_back(project(active, w_outer)))

def forward(encoder_input, lengths, decoder_input, weights, enc_gains, dec_gains):
    gains = jnp.concatenate([enc_gains, dec_gains], axis=0)
    scale = HDIM ** (-0.5)
    blocks = QUESTIONS * N_BLK
    enc_blocks = encoder_input.reshape(blocks, PASS_DEV, SLOT, D)
    len_blocks = lengths.reshape(blocks, PASS_DEV)
    params = (weights[:6], gains)

    def one_block(pair):
        return encoder_block(params, pair[0], pair[1])
    states = lax.map(jax.checkpoint(one_block), (enc_blocks, len_blocks))
    states = states.reshape(QUESTIONS, KEYS, D)
    dq_w, dk_w, dv_w, do_w, cq_w, ck_w, cv_w, co_w, inner_w, outer_w = weights[6:]
    cross_keys = rounded(project(states, ck_w)).reshape(QUESTIONS, KEYS, HEADS, HDIM)
    cross_vals = rounded(project(states, cv_w)).reshape(QUESTIONS, KEYS, HEADS, HDIM)
    key_valid = (jnp.arange(SLOT)[None, None, :] < lengths[:, :, None]).reshape(QUESTIONS, KEYS)
    normed = low(norm_rows(decoder_input, gains[2]))
    query = rounded(project(normed, dq_w)).reshape(QUESTIONS, DEC, HEADS, HDIM)
    keys = rounded(project(normed, dk_w)).reshape(QUESTIONS, DEC, HEADS, HDIM)
    vals = rounded(project(normed, dv_w)).reshape(QUESTIONS, DEC, HEADS, HDIM)
    causal = (jnp.arange(DEC)[:, None] >= jnp.arange(DEC)[None, :])[None, None]
    context = attention(query, keys, vals, causal, scale).reshape(QUESTIONS, DEC, D)
    after_self = decoder_input + low_back(project(context, do_w))
    fourth = low(norm_rows(after_self, gains[3]))
    cross_query = rounded(project(fourth, cq_w)).reshape(QUESTIONS, DEC, HEADS, HDIM)
    cross_scores = jnp.einsum('qihc,qthc->qhit', cross_query, cross_keys, precision=highest) * scale
    cross_scores = jnp.where(key_valid[:, None, None, :], cross_scores, masked_score)
    cross_probs = jax.nn.softmax(cross_scores, axis=-1)
    cross_context = rounded(jnp.einsum('qhit,qthc->qihc', cross_probs, cross_vals, precision=highest))
    cross_context = cross_context.reshape(QUESTIONS, DEC, D)
    after_cross = after_self + low_back(project(cross_context, co_w))
    fifth = low(norm_rows(after_cross, gains[4]))
    inner = low_back(project(fifth, inner_w))
    active = low(jax.nn.gelu(inner, approximate=True))
    outputs = after_cross + low_back(project(active, outer_w))
    return (states, outputs)

def reference(encoder_input, passage_lengths, decoder_input, encoder_query, encoder_key, encoder_value, encoder_output, encoder_inner, encoder_outer, decoder_query, decoder_key, decoder_value, decoder_output, cross_query, cross_key, cross_value, cross_output, decoder_inner, decoder_outer, encoder_gains, decoder_gains, encoder_cotangent, decoder_cotangent):
    listed = (encoder_query, encoder_key, encoder_value, encoder_output, encoder_inner, encoder_outer, decoder_query, decoder_key, decoder_value, decoder_output, cross_query, cross_key, cross_value, cross_output, decoder_inner, decoder_outer)
    weights = tuple((weight.astype(jnp.float32) for weight in listed))

    def wrapped(enc_values, dec_values, weight_values, enc_gain_values, dec_gain_values):
        return forward(enc_values, passage_lengths, dec_values, weight_values, enc_gain_values, dec_gain_values)
    (states, outputs), pull = jax.vjp(wrapped, encoder_input.astype(jnp.float32), decoder_input.astype(jnp.float32), weights, encoder_gains.astype(jnp.float32), decoder_gains.astype(jnp.float32))
    enc_grad, dec_grad, grads, enc_gain_grad, dec_gain_grad = pull((encoder_cotangent.astype(jnp.float32).reshape(QUESTIONS, KEYS, D), decoder_cotangent.astype(jnp.float32)))
    return (states.reshape(encoder_input.shape).astype(jnp.bfloat16), outputs.astype(jnp.bfloat16), enc_grad, dec_grad, grads[0], grads[1], grads[2], grads[3], grads[4], grads[5], grads[6], grads[7], grads[8], grads[9], grads[10], grads[11], grads[12], grads[13], grads[14], grads[15], enc_gain_grad, dec_gain_grad)
```

```python
import math

import jax
import jax.numpy as jnp
import numpy as np
from jax import lax
from jax.experimental import pallas as pl
from jax.experimental.pallas import tpu as pltpu
from jax.sharding import PartitionSpec as P

HDIM = 64
SCALE = HDIM ** (-0.5)
LANES = 128
EPS = 1e-06
masked_score = -1000000000.0
f32 = jnp.float32
bf16 = jnp.bfloat16

PLACES, HEAD, BLK, LENGTHS = 0, 8, 9, 10


def swap(value, axis, bits):
    size = lax.axis_size(axis)
    return lax.ppermute(value, axis, [(i, i ^ bits) for i in range(size)])


def spread(rows):
    across = swap(rows, "head", 2)
    beside = swap(rows, "head", 1)
    return [rows, beside, across, swap(across, "head", 1)]


def collect(keep, send_beside, keep_across, send_corner):
    corner = swap(send_corner, "head", 1)
    beside = swap(send_beside, "head", 1)
    across = swap((keep_across + corner.astype(f32)).astype(bf16), "head", 2)
    return [keep, beside, across]


def share(value):
    return [swap(value, "head", k) for k in (1, 2, 3)]


def tree_sum(value, axes):
    for axis in axes:
        bits = 1
        while bits < lax.axis_size(axis):
            value = value + swap(value, axis, bits)
            bits *= 2
    return value


def ring_order(count):
    return [*range(0, count, 2), *range(count - 1, 0, -2)]


OFFSETS = (0, -1, 1, -2, 2, -3, 3, -4)


def ring_steps(count):
    order = ring_order(count)
    forth = [(order[i], order[(i + 1) % count]) for i in range(count)]
    return forth, [(b, a) for a, b in forth]


def place_table(count):
    order = ring_order(count)
    at = {b: i for i, b in enumerate(order)}
    return np.array(
        [[order[(at[b] + o) % count] for o in OFFSETS] for b in range(count)], np.int32
    )


def fetch(own):
    count = lax.axis_size("blk")
    if count != 8:
        everything = lax.all_gather(own, "blk", axis=0, tiled=True)
        return jnp.split(everything, 8, axis=0)
    forth, back = ring_steps(count)
    left = right = own
    pieces = [own]
    for _ in range(3):
        left = lax.ppermute(left, "blk", forth)
        right = lax.ppermute(right, "blk", back)
        pieces += [left, right]
    return [*pieces, lax.ppermute(left, "blk", forth)]


def reduce_pieces(pieces):
    count = lax.axis_size("blk")
    if count != 8:
        everything = jnp.concatenate([p.astype(f32) for p in pieces], axis=0)
        return lax.psum_scatter(everything, "blk", scatter_dimension=0, tiled=True)
    forth, back = ring_steps(count)
    by = dict(zip(OFFSETS, pieces, strict=True))
    ahead, behind = by[-4], by[-3]

    def add(a, b):
        return (a.astype(f32) + b.astype(f32)).astype(bf16)

    for k in (3, 2, 1):
        ahead = add(lax.ppermute(ahead, "blk", forth), by[k])
        if k > 1:
            behind = add(lax.ppermute(behind, "blk", back), by[1 - k])
    ahead = lax.ppermute(ahead, "blk", forth)
    behind = lax.ppermute(behind, "blk", back)
    return by[0] + ahead.astype(f32) + behind.astype(f32)


def dot(left, right, over=(1, 0)):
    return lax.dot_general(
        left, right, (((over[0],), (over[1],)), ((), ())), preferred_element_type=f32
    )


def dot_t(left, right):
    return dot(left, right, (1, 1))


def t_dot(left, right):
    return dot(left, right, (0, 0))


def norm_rows(values, gain):
    return values * lax.rsqrt(jnp.mean(values * values, axis=-1, keepdims=True) + EPS) * gain


def norm_back(values, gain, grad):
    inverse = lax.rsqrt(jnp.mean(values * values, axis=-1, keepdims=True) + EPS)
    unit = values * inverse
    weighted = grad * gain
    along = jnp.mean(weighted * unit, axis=-1, keepdims=True)
    return inverse * (weighted - unit * along), grad * unit


def gelu_both(values):
    root = math.sqrt(2.0 / math.pi)
    square = values * values
    bent = jnp.tanh(root * values * (1.0 + 0.044715 * square))
    half = 0.5 * (1.0 + bent)
    slope = half + 0.5 * values * (1.0 - bent * bent) * root * (1.0 + 3 * 0.044715 * square)
    return values * half, slope


def heads_in(width):
    return [slice(at, at + HDIM) for at in range(0, width, HDIM)]


def assemble(info, pieces, targets):
    rows = pieces[0].shape[0]
    for t, piece in enumerate(pieces):
        at = pl.ds(pl.multiple_of(info[PLACES + t] * rows, 16), rows)
        column = 0
        for target in targets:
            target[at, :] = piece[:, column : column + target.shape[1]]
            column += target.shape[1]


def hand_out(info, sources, pieces):
    rows = pieces[0].shape[0]
    for t, piece in enumerate(pieces):
        at = pl.ds(pl.multiple_of(info[PLACES + t] * rows, 16), rows)
        column = 0
        for source in sources:
            piece[:, column : column + source.shape[1]] = source[at, :].astype(piece.dtype)
            column += source.shape[1]


def token_rows(refs):
    return jnp.concatenate([r[0] for r in refs], axis=0)


def emit(partial, outs):
    part = outs[0].shape[1]
    for r, out in enumerate(outs):
        out[0] = partial[r * part : (r + 1) * part].astype(out.dtype)


def slots_used(info, b, part, slot):
    column = lax.broadcasted_iota(jnp.int32, (1, slot), 1)
    position = (lax.div(column, part) ^ info[HEAD]) * part + lax.rem(column, part)
    return position < info[LENGTHS + b]


def call(body, info, stepped, fixed, out_stepped, out_fixed, scratch=(), flops=0, steps=1):
    def by_step(shape):
        return pl.BlockSpec((1, *shape[1:]), lambda b: (b,) + (0,) * (len(shape) - 1))

    def whole(shape):
        return pl.BlockSpec(shape, lambda b: (0,) * len(shape))

    counts = [len(stepped), len(fixed), len(out_stepped), len(out_fixed), len(scratch)]
    stops = np.cumsum(counts)

    def split(info_ref, *refs):
        body(info_ref, *(refs[e - c : e] for c, e in zip(counts, stops, strict=True)))

    arrays = [*stepped, *fixed, *out_stepped, *out_fixed]
    moved = sum(math.prod(a.shape) * a.dtype.itemsize for a in arrays)
    return pl.pallas_call(
        split,
        grid=(steps,),
        in_specs=[
            pl.BlockSpec(memory_space=pltpu.SMEM),
            *(by_step(a.shape) for a in stepped),
            *(whole(a.shape) for a in fixed),
        ],
        out_specs=[
            *(by_step(a.shape) for a in out_stepped),
            *(whole(a.shape) for a in out_fixed),
        ],
        out_shape=[*out_stepped, *out_fixed],
        scratch_shapes=list(scratch),
        compiler_params=pltpu.CompilerParams(
            dimension_semantics=("arbitrary",), vmem_limit_bytes=48 * 1024 * 1024
        ),
        cost_estimate=pl.CostEstimate(
            flops=int(flops), bytes_accessed=int(moved), transcendentals=0
        ),
    )(info, *stepped, *fixed)


def like(shape, dtype):
    return jax.ShapeDtypeStruct(tuple(shape), dtype)


def by_rows(fn, info, stepped, fixed, dtypes, gain=False):
    steps, _, width = stepped[0].shape

    def body(info_ref, ins, whole, outs, sums, _):
        results = fn(*(r[0].astype(f32) for r in ins), *(r[...] for r in whole))
        for out, value in zip(outs, results, strict=False):
            out[0] = value.astype(out.dtype)
        for total in sums:

            @pl.when(pl.program_id(0) == 0)
            def _():
                total[...] = jnp.zeros_like(total)

            total[...] += jnp.sum(results[-1], axis=0, keepdims=True)

    return call(
        body,
        info,
        stepped,
        fixed,
        [like(stepped[0].shape, d) for d in dtypes],
        [like((1, width), f32)] * gain,
        flops=10 * math.prod(stepped[0].shape),
        steps=steps,
    )


def partial_rows(blocks, part, width):
    return [like((blocks, part, width), d) for d in (f32, bf16, f32, bf16)]


def piece_shapes(rows, columns):
    return [like((rows, columns), f32), *[like((rows, columns), bf16)] * 7]


def encoder_attention(info, normed, pieces):
    blocks, part, width = normed[0].shape
    slot = part * len(normed)
    size = pieces[0].shape[1] // 4
    count = size // HDIM

    def body(info, rows, pieces, outs, weights, _):
        qkv, probs, context = outs[:3]
        w_in, w_out = weights
        b = pl.program_id(0)

        @pl.when(b == 0)
        def _():
            assemble(info, pieces, weights)

        qkv[0] = dot(token_rows(rows), w_in[...]).astype(bf16)
        allowed = slots_used(info, b, part, slot)
        for k, at in enumerate(heads_in(size)):
            query, keys, vals = (qkv[0, :, j * size + at.start : j * size + at.stop] for j in range(3))
            scores = jnp.where(allowed, dot_t(query, keys) * SCALE, masked_score)
            spread_out = jnp.exp(scores - jnp.max(scores, axis=-1, keepdims=True))
            weight = (spread_out / jnp.sum(spread_out, axis=-1, keepdims=True)).astype(bf16)
            probs[0, k] = weight
            context[0, :, at] = dot(weight, vals).astype(bf16)
        emit(dot_t(context[0], w_out[...]), outs[3:])

    return call(
        body,
        info,
        normed,
        pieces,
        [
            like((blocks, slot, 3 * size), bf16),
            like((blocks, count, slot, slot), bf16),
            like((blocks, slot, size), bf16),
            *partial_rows(blocks, part, width),
        ],
        [like((width, 3 * size), bf16), like((width, size), bf16)],
        flops=2 * blocks * slot * (width * size * 4 + 8 * slot * size),
        steps=blocks,
    )


def encoder_attention_back(info, grads, normed, qkv, probs, context, w_in, w_out, gains):
    blocks, part, width = normed[0].shape
    slot = part * len(normed)
    size = w_out.shape[1]

    def body(info, stepped, fixed, outs, ends, scratch):
        grad_refs, normed_refs = stepped[:4], stepped[4:8]
        qkv, probs, context = stepped[8:]
        w_in, w_out, gains = fixed
        pieces, gain_out = ends[:-1], ends[-1]
        total_in, total_out, moved = scratch
        b = pl.program_id(0)

        @pl.when(b == 0)
        def _():
            total_in[...] = jnp.zeros_like(total_in)
            total_out[...] = jnp.zeros_like(total_out)
            gain_out[...] = jnp.zeros_like(gain_out)

        grad = token_rows(grad_refs)
        rows = token_rows(normed_refs)
        dcontext = dot(grad, w_out[...]).astype(bf16)
        for k, at in enumerate(heads_in(size)):
            query, keys, vals = (qkv[0, :, j * size + at.start : j * size + at.stop] for j in range(3))
            weight = probs[0, k]
            dprobs = dot_t(dcontext[:, at], vals)
            wide = weight.astype(f32)
            dscores = wide * (dprobs - jnp.sum(wide * dprobs, axis=-1, keepdims=True))
            dscores = dscores.astype(bf16)
            terms = (
                dot(dscores, keys) * SCALE,
                t_dot(dscores, query) * SCALE,
                t_dot(weight, dcontext[:, at]),
            )
            for j, term in enumerate(terms):
                moved[:, j * size + at.start : j * size + at.stop] = term.astype(bf16)
        partial = dot_t(moved[...], w_in[...])
        emit(partial, outs)
        gain_out[...] += jnp.sum(partial * rows.astype(f32), axis=0, keepdims=True) / gains[0:1, :]
        total_in[...] += t_dot(rows, moved[...])
        total_out[...] += t_dot(grad, context[0])

        @pl.when(b == blocks - 1)
        def _():
            hand_out(info, (total_in, total_out), pieces)

    results = call(
        body,
        info,
        [*grads, *normed, qkv, probs, context],
        [w_in, w_out, gains],
        partial_rows(blocks, part, width),
        [*piece_shapes(width // 8, 4 * size), like((1, width), f32)],
        [
            pltpu.VMEM((width, 3 * size), f32),
            pltpu.VMEM((width, size), f32),
            pltpu.VMEM((slot, 3 * size), bf16),
        ],
        flops=2 * blocks * slot * (width * size * 8 + 20 * slot * size),
        steps=blocks,
    )
    return results[:4], results[4:12], results[12]


def encoder_ffn(info, normed, inner_pieces, outer_pieces):
    blocks, part, width = normed[0].shape
    slot = part * len(normed)
    hidden = inner_pieces[0].shape[1]

    def body(info, rows, pieces, outs, weights, _):
        active, slope = outs[:2]
        w_inner, w_outer = weights

        @pl.when(pl.program_id(0) == 0)
        def _():
            assemble(info, pieces[:8], (w_inner,))
            assemble(info, pieces[8:], (w_outer,))

        value, bend = gelu_both(dot(token_rows(rows), w_inner[...]))
        active[0] = value.astype(bf16)
        slope[0] = bend.astype(bf16)
        emit(dot_t(active[0], w_outer[...]), outs[2:])

    return call(
        body,
        info,
        normed,
        [*inner_pieces, *outer_pieces],
        [*[like((blocks, slot, hidden), bf16)] * 2, *partial_rows(blocks, part, width)],
        [like((width, hidden), bf16)] * 2,
        flops=4 * blocks * slot * width * hidden,
        steps=blocks,
    )


def encoder_ffn_back(info, grads, slope, w_inner, w_outer):
    blocks, part, width = grads[0].shape
    slot = part * len(grads)
    hidden = w_inner.shape[1]

    def body(info, stepped, weights, outs, ends, _):
        dinner = outs[0]
        w_inner, w_outer = weights
        back = dot(token_rows(stepped[:4]), w_outer[...])
        dinner[0] = (back * stepped[4][0].astype(f32)).astype(bf16)
        emit(dot_t(dinner[0], w_inner[...]), outs[1:])

    return call(
        body,
        info,
        [*grads, slope],
        [w_inner, w_outer],
        [like((blocks, slot, hidden), bf16), *partial_rows(blocks, part, width)],
        [],
        flops=4 * blocks * slot * width * hidden,
        steps=blocks,
    )


def weight_grads(info, left, right):
    blocks, part, width = left[0].shape
    columns = right.shape[2]

    def body(info, stepped, _, outs, pieces, scratch):
        total = scratch[0]
        b = pl.program_id(0)

        @pl.when(b == 0)
        def _():
            total[...] = jnp.zeros_like(total)

        total[...] += t_dot(token_rows(stepped[:4]), stepped[4][0])

        @pl.when(b == blocks - 1)
        def _():
            hand_out(info, (total,), pieces)

    return call(
        body,
        info,
        [*left, right],
        [],
        [],
        piece_shapes(width // 8, columns),
        [pltpu.VMEM((width, columns), f32)],
        flops=2 * blocks * part * 4 * width * columns,
        steps=blocks,
    )


def cross_forward(info, states, pieces, queries, own_question, count_pass):
    blocks, part, width = states[0].shape
    slot = part * len(states)
    size = queries.shape[1]
    rows_dec = queries.shape[0]

    def body(info, rows, fixed, outs, ends, scratch):
        pieces, queries, question = fixed[:8], fixed[8], fixed[9]
        stats, weight = ends
        held = scratch[0]
        b = pl.program_id(0)

        @pl.when(b == 0)
        def _():
            assemble(info, pieces, (weight,))

        made = dot(token_rows(rows), weight[...]).astype(bf16)
        outs[0][0] = made
        held[pl.ds(pl.multiple_of(b * slot, slot), slot), :] = made

        @pl.when(b == blocks - 1)
        def _():
            allowed = jnp.concatenate(
                [
                    slots_used(info, k, part, slot) & (question[...] == k // count_pass)
                    for k in range(blocks)
                ],
                axis=1,
            )
            lane = lax.broadcasted_iota(jnp.int32, (rows_dec, HDIM), 1)
            for k, at in enumerate(heads_in(size)):
                scores = dot_t(queries[:, at], held[:, at]) * SCALE
                scores = jnp.where(allowed, scores, masked_score)
                top = jnp.max(scores, axis=-1, keepdims=True)
                spread_out = jnp.exp(scores - top)
                total = jnp.sum(spread_out, axis=-1, keepdims=True)
                vals = held[:, size + at.start : size + at.stop]
                stats[:, k * LANES : k * LANES + HDIM] = dot(spread_out.astype(bf16), vals)
                stats[:, k * LANES + HDIM : (k + 1) * LANES] = jnp.where(lane == 0, top, total)

    return call(
        body,
        info,
        states,
        [*pieces, queries, own_question],
        [like((blocks, slot, 2 * size), bf16)],
        [like((rows_dec, size // HDIM * LANES), f32), like((width, 2 * size), bf16)],
        [pltpu.VMEM((blocks * slot, 2 * size), bf16)],
        flops=4 * blocks * slot * width * size,
        steps=blocks,
    )


def merge(info, own, other, bits):
    def body(info, _, ins, __, outs, ___):
        mine, yours = ins[0][...], ins[1][...]
        later = (info[BLK] & bits) != 0
        first, second = jnp.where(later, yours, mine), jnp.where(later, mine, yours)
        lane = lax.broadcasted_iota(jnp.int32, (first.shape[0], HDIM), 1)
        for at in range(0, first.shape[1], LANES):
            pairs = [(v[:, at + HDIM : at + HDIM + 1], v[:, at + HDIM + 1 : at + HDIM + 2]) for v in (first, second)]
            top = jnp.maximum(pairs[0][0], pairs[1][0])
            by_first, by_second = jnp.exp(pairs[0][0] - top), jnp.exp(pairs[1][0] - top)
            total = pairs[0][1] * by_first + pairs[1][1] * by_second
            outs[0][:, at : at + HDIM] = (
                first[:, at : at + HDIM] * by_first + second[:, at : at + HDIM] * by_second
            )
            outs[0][:, at + HDIM : at + LANES] = jnp.where(lane == 0, top, total)

    return call(body, info, [], [own, other], [], [like(own.shape, f32)])[0]


def cross_out(info, stats, w_output):
    rows, columns = stats.shape
    size = columns // LANES * HDIM
    width = w_output.shape[0]

    def body(info, _, ins, __, outs, scratch):
        stats, w_output = ins
        out, log_total, context, own, sent = outs
        log_total[...] = jnp.zeros_like(log_total)
        for k, at in enumerate(heads_in(size)):
            base = k * LANES
            top = stats[:, base + HDIM : base + HDIM + 1]
            total = stats[:, base + HDIM + 1 : base + HDIM + 2]
            out[:, at] = stats[:, base : base + HDIM] / total
            log_total[:, k : k + 1] = top + jnp.log(total)
        context[...] = out[...].astype(bf16)
        own[...] = dot_t(context[...], w_output[...])
        sent[...] = own[...].astype(bf16)

    return call(
        body,
        info,
        [],
        [stats, w_output],
        [],
        [
            like((rows, size), f32),
            like((rows, LANES), f32),
            like((rows, size), bf16),
            like((rows, width), f32),
            like((rows, width), bf16),
        ],
        flops=2 * rows * size * width,
    )


def cross_back(info, key_vals, inputs, own_question, count_pass, slot, part):
    cotangent, after_cross, terms, gains, w_output, out, log_total, queries, weight = inputs
    blocks = key_vals.shape[0]
    rows_dec, width = after_cross.shape
    size = queries.shape[1]

    def body(info, stepped, fixed, outs, ends, scratch):
        cotangent, after_cross, own, r1, r2, r3, gains, w_output, out, log_total, queries, weight, question = fixed
        key_vals = stepped[0]
        dkey_vals = outs[0]
        dcross, dcross_low, gain_out, dqueries = ends
        dcontext, row_terms = scratch
        b = pl.program_id(0)

        @pl.when(b == 0)
        def _():
            total = own[...] + r1[...].astype(f32) + r2[...].astype(f32) + r3[...].astype(f32)
            back, gain_rows = norm_back(after_cross[...], gains[2:3, :], total)
            dcross[...] = cotangent[...].astype(f32) + back
            dcross_low[...] = dcross[...].astype(bf16)
            gain_out[...] = gain_rows
            dcontext[...] = dot(dcross_low[...], w_output[...]).astype(bf16)
            for k, at in enumerate(heads_in(size)):
                row_terms[:, k : k + 1] = jnp.sum(
                    dcontext[:, at].astype(f32) * out[:, at], axis=-1, keepdims=True
                )
            dqueries[...] = jnp.zeros_like(dqueries)

        allowed = slots_used(info, b, part, slot) & (question[...] == lax.div(b, count_pass))
        for k, at in enumerate(heads_in(size)):
            keys, vals = key_vals[0, :, at], key_vals[0, :, size + at.start : size + at.stop]
            scores = dot_t(queries[:, at], keys) * SCALE
            scores = jnp.where(allowed, scores, masked_score)
            probs = jnp.exp(scores - log_total[:, k : k + 1])
            dprobs = dot_t(dcontext[:, at], vals)
            dscores = (probs * (dprobs - row_terms[:, k : k + 1])).astype(bf16)
            dqueries[:, at] += dot(dscores, keys) * SCALE
            dkey_vals[0, :, at] = (t_dot(dscores, queries[:, at]) * SCALE).astype(bf16)
            dkey_vals[0, :, size + at.start : size + at.stop] = t_dot(
                probs.astype(bf16), dcontext[:, at]
            ).astype(bf16)
        emit(dot_t(dkey_vals[0], weight[...]), outs[1:])

    return call(
        body,
        info,
        [key_vals],
        [cotangent, after_cross, *terms, gains, w_output, out, log_total, queries, weight, own_question],
        [like(key_vals.shape, bf16), *partial_rows(blocks, part, width)],
        [
            like((rows_dec, width), f32),
            like((rows_dec, width), bf16),
            like((rows_dec, width), f32),
            like((rows_dec, size), f32),
        ],
        [pltpu.VMEM((rows_dec, size), bf16), pltpu.VMEM((rows_dec, LANES), f32)],
        flops=4 * blocks * slot * width * size,
        steps=blocks,
    )


def summed(refs):
    total = refs[0][...]
    for ref in refs[1:]:
        total = total + ref[...].astype(f32)
    return total


def decoder_self(info, rows, gains, pieces, order):
    count, width = rows.shape
    size = pieces[0].shape[1] // 4

    def body(info, _, ins, __, outs, scratch):
        rows, gains, order_q, order_k = ins[:4]
        normed, qkv, probs, context, own, sent, w_in, w_out = outs
        assemble(info, ins[4:], (w_in, w_out))
        normed[...] = norm_rows(rows[...].astype(f32), gains[0:1, :]).astype(bf16)
        qkv[...] = dot(normed[...], w_in[...]).astype(bf16)
        query_at, key_at = order_q[...], order_k[...]
        same = lax.div(query_at, 1000) == lax.div(key_at, 1000)
        allowed = same & (key_at <= query_at) & (key_at >= 0) & (query_at >= 0)
        for k, at in enumerate(heads_in(size)):
            query, keys, vals = (qkv[:, j * size + at.start : j * size + at.stop] for j in range(3))
            scores = jnp.where(allowed, dot_t(query, keys) * SCALE, masked_score)
            spread_out = jnp.exp(scores - jnp.max(scores, axis=-1, keepdims=True))
            weight = spread_out / jnp.sum(spread_out, axis=-1, keepdims=True)
            weight = jnp.where(allowed, weight, 0.0)
            probs[k] = weight
            context[:, at] = dot(weight.astype(bf16), vals).astype(bf16)
        own[...] = dot_t(context[...], w_out[...])
        sent[...] = own[...].astype(bf16)

    return call(
        body,
        info,
        [],
        [rows, gains, *order, *pieces],
        [],
        [
            like((count, width), bf16),
            like((count, 3 * size), bf16),
            like((size // HDIM, count, count), f32),
            like((count, size), bf16),
            like((count, width), f32),
            like((count, width), bf16),
            like((width, 3 * size), bf16),
            like((width, size), bf16),
        ],
        flops=2 * count * width * size * 4,
    )


def decoder_queries(info, rows, terms, cotangent, gains, cross_pieces, inner_pieces, outer_pieces):
    count, width = rows.shape
    size = cross_pieces[0].shape[1] // 2
    hidden = inner_pieces[0].shape[1]

    def body(info, _, ins, __, outs, scratch):
        rows, own, r1, r2, r3, cotangent, gains = ins[:7]
        after_self, normed, queries, back, w_query, w_output, w_inner, w_outer = outs
        assemble(info, ins[7:15], (w_query, w_output))
        assemble(info, ins[15:23], (w_inner,))
        assemble(info, ins[23:31], (w_outer,))
        after_self[...] = rows[...].astype(f32) + summed((own, r1, r2, r3))
        normed[...] = norm_rows(after_self[...], gains[1:2, :]).astype(bf16)
        queries[...] = dot(normed[...], w_query[...]).astype(bf16)
        back[...] = dot(cotangent[...], w_outer[...])

    return call(
        body,
        info,
        [],
        [rows, *terms, cotangent, gains, *cross_pieces, *inner_pieces, *outer_pieces],
        [],
        [
            like((count, width), f32),
            like((count, width), bf16),
            like((count, size), bf16),
            like((count, hidden), f32),
            like((width, size), bf16),
            like((width, size), bf16),
            like((width, hidden), bf16),
            like((width, hidden), bf16),
        ],
        flops=2 * count * width * (size + hidden),
    )


def decoder_ffn(info, after_self, terms, back, gains, w_inner):
    count, width = after_self.shape
    hidden = w_inner.shape[1]

    def body(info, _, ins, __, outs, scratch):
        after_self, own, r1, r2, r3, back, gains, w_inner = ins
        after_cross, normed, active, dinner, own_back, sent_back = outs
        after_cross[...] = after_self[...] + summed((own, r1, r2, r3))
        normed[...] = norm_rows(after_cross[...], gains[2:3, :]).astype(bf16)
        value, slope = gelu_both(dot(normed[...], w_inner[...]))
        active[...] = value.astype(bf16)
        dinner[...] = (slope * back[...]).astype(bf16)
        own_back[...] = dot_t(dinner[...], w_inner[...])
        sent_back[...] = own_back[...].astype(bf16)

    return call(
        body,
        info,
        [],
        [after_self, *terms, back, gains, w_inner],
        [],
        [
            like((count, width), f32),
            like((count, width), bf16),
            like((count, hidden), bf16),
            like((count, hidden), bf16),
            like((count, width), f32),
            like((count, width), bf16),
        ],
        flops=4 * count * width * hidden,
    )


def project_rows(info, rows, weight):
    count, width = rows.shape[0], weight.shape[0]

    def body(info, _, ins, __, outs, scratch):
        outs[0][...] = dot_t(ins[0][...].astype(bf16), ins[1][...])
        outs[1][...] = outs[0][...].astype(bf16)

    return call(
        body,
        info,
        [],
        [rows, weight],
        [],
        [like((count, width), f32), like((count, width), bf16)],
        flops=2 * count * width * weight.shape[1],
    )


def decoder_self_back(info, dcross, after_self, terms, gains, w_out, w_in, qkv, probs):
    count, width = after_self.shape
    size = w_out.shape[1]

    def body(info, _, ins, __, outs, scratch):
        dcross, after_self, own, r1, r2, r3, gains, w_out, w_in, qkv, probs = ins
        dself, dself_low, gain_rows, moved, own_back, sent_back = outs
        back, gain_rows[...] = norm_back(after_self[...], gains[1:2, :], summed((own, r1, r2, r3)))
        dself[...] = dcross[...] + back
        dself_low[...] = dself[...].astype(bf16)
        dcontext = dot(dself_low[...], w_out[...]).astype(bf16)
        for k, at in enumerate(heads_in(size)):
            query, keys, vals = (qkv[:, j * size + at.start : j * size + at.stop] for j in range(3))
            weight = probs[k]
            dprobs = dot_t(dcontext[:, at], vals)
            dscores = weight * (dprobs - jnp.sum(weight * dprobs, axis=-1, keepdims=True))
            dscores = dscores.astype(bf16)
            found = (
                dot(dscores, keys) * SCALE,
                t_dot(dscores, query) * SCALE,
                t_dot(weight.astype(bf16), dcontext[:, at]),
            )
            for j, term in enumerate(found):
                moved[:, j * size + at.start : j * size + at.stop] = term.astype(bf16)
        own_back[...] = dot_t(moved[...], w_in[...])
        sent_back[...] = own_back[...].astype(bf16)

    return call(
        body,
        info,
        [],
        [dcross, after_self, *terms, gains, w_out, w_in, qkv, probs],
        [],
        [
            like((count, width), f32),
            like((count, width), bf16),
            like((count, width), f32),
            like((count, 3 * size), bf16),
            like((count, width), f32),
            like((count, width), bf16),
        ],
        flops=2 * count * width * size * 4,
    )


def decoder_ends(info, rows, dself, terms, gains, after_cross, out_terms):
    count, width = dself.shape

    def body(info, _, ins, __, outs, scratch):
        rows, dself, after_cross, gains = ins[:4]
        grad, gain_rows, states = outs
        back, gain_rows[...] = norm_back(rows[...].astype(f32), gains[0:1, :], summed(ins[4:8]))
        grad[...] = dself[...] + back
        states[...] = (after_cross[...] + summed(ins[8:12])).astype(bf16)

    return call(
        body,
        info,
        [],
        [rows, dself, after_cross, gains, *terms, *out_terms],
        [],
        [like((count, width), f32), like((count, width), f32), like((count, width), bf16)],
    )


def decoder_weight_grads(info, own, pairs_in, pairs_out):
    count, width = pairs_in[0][0].shape

    def body(info, _, ins, __, outs, scratch):
        row = lax.broadcasted_iota(jnp.int32, (own, width), 0) + info[BLK] * own
        column = lax.broadcasted_iota(jnp.int32, (own, width), 1)
        pick = jnp.where(row == column, 1.0, 0.0).astype(bf16)
        n = 2 * len(pairs_in)
        for k, out in enumerate(outs):
            left, right = ins[2 * k][...], ins[2 * k + 1][...]
            if 2 * k < n:
                out[...] = t_dot(dot_t(left, pick).astype(bf16), right)
            else:
                out[...] = t_dot(left, dot_t(right, pick).astype(bf16))

    outs = [like((own, r.shape[1]), f32) for _, r in pairs_in]
    outs += [like((l.shape[1], own), f32) for l, _ in pairs_out]
    flat = [a for pair in (*pairs_in, *pairs_out) for a in pair]
    return call(body, info, [], flat, [], outs, flops=2 * count * own * width * 10)


def shards(
    encoder_input,
    passage_lengths,
    decoder_input,
    encoder_query,
    encoder_key,
    encoder_value,
    encoder_output,
    encoder_inner,
    encoder_outer,
    decoder_query,
    decoder_key,
    decoder_value,
    decoder_output,
    cross_query,
    cross_key,
    cross_value,
    cross_output,
    decoder_inner,
    decoder_outer,
    encoder_gains,
    decoder_gains,
    encoder_cotangent,
    decoder_cotangent,
):
    head, blk = lax.axis_index("head"), lax.axis_index("blk")
    blk_count, head_count = lax.axis_size("blk"), lax.axis_size("head")
    count_q, count_pass, part, width = encoder_input.shape
    blocks = count_q * count_pass
    slot = part * head_count
    own = width // blk_count
    if blk_count == 8:
        places = jnp.asarray(place_table(8))[blk]
    else:
        places = jnp.arange(8, dtype=jnp.int32)
    info = jnp.concatenate(
        [places, jnp.stack([head, blk]).astype(jnp.int32), passage_lengths.reshape(blocks)]
    )

    attention_pieces = fetch(
        jnp.concatenate([encoder_query, encoder_key, encoder_value, encoder_output.T], axis=1)
    )
    inner_pieces = fetch(encoder_inner)
    outer_pieces = fetch(encoder_outer.T)
    self_pieces = fetch(
        jnp.concatenate([decoder_query, decoder_key, decoder_value, decoder_output.T], axis=1)
    )
    cross_kv_pieces = fetch(jnp.concatenate([cross_key, cross_value], axis=1))
    cross_qo_pieces = fetch(jnp.concatenate([cross_query, cross_output.T], axis=1))
    dec_inner_pieces = fetch(decoder_inner)
    dec_outer_pieces = fetch(decoder_outer.T)

    inputs = encoder_input.reshape(blocks, part, width)
    first = by_rows(
        lambda x, g: (norm_rows(x, g[0:1]),), info, [inputs], [encoder_gains], [bf16]
    )[0]
    first_all = spread(first)
    qkv, probs, context, *partial, w_in, w_out = encoder_attention(
        info, first_all, attention_pieces
    )

    def enter_ffn(x, a, b, c, g):
        hidden = x + a + b + c
        return hidden, norm_rows(hidden, g[1:2])

    hidden, second = by_rows(
        enter_ffn, info, [inputs, *collect(*partial)], [encoder_gains], [f32, bf16]
    )
    second_all = spread(second)
    active, slope, *partial, w_inner, w_outer = encoder_ffn(
        info, second_all, inner_pieces, outer_pieces
    )
    states = by_rows(
        lambda h, a, b, c: (h + a + b + c,), info, [hidden, *collect(*partial)], [], [bf16]
    )[0]
    states_all = spread(states)

    dec_part = decoder_input.shape[1]
    dec_own = count_q * dec_part
    dec_rows = dec_own * head_count
    filled = -(-dec_rows // 16) * 16
    pair = jnp.stack([decoder_input, decoder_cotangent]).reshape(2, dec_own, width)
    parts = jnp.stack([pair, *share(pair)])
    parts = jnp.where(head & 1, parts[jnp.array([1, 0, 3, 2])], parts)
    parts = jnp.where(head & 2, parts[jnp.array([2, 3, 0, 1])], parts)
    both = parts.transpose(1, 0, 2, 3).reshape(2, dec_rows, width)
    both = jnp.pad(both, ((0, 0), (0, filled - dec_rows), (0, 0)))
    dec_in, cotangent = both[0], both[1]
    index = np.arange(filled)
    question = (index % dec_own) // dec_part
    position = index // dec_own * dec_part + index % dec_part
    order = np.where(index < dec_rows, question * 1000 + position, -1).astype(np.int32)
    order = (jnp.asarray(order[:, None]), jnp.asarray(order[None, :]))
    question = jnp.asarray(question[:, None].astype(np.int32))

    third, dec_qkv, dec_probs, dec_context, mine, sent, dec_w_in, dec_w_out = decoder_self(
        info, dec_in, decoder_gains, self_pieces, order
    )
    (
        after_self,
        fourth,
        queries,
        outer_back,
        w_cross_query,
        w_cross_output,
        w_dec_inner,
        w_dec_outer,
    ) = decoder_queries(
        info,
        dec_in,
        [mine, *share(sent)],
        cotangent,
        decoder_gains,
        cross_qo_pieces,
        dec_inner_pieces,
        dec_outer_pieces,
    )

    key_vals, stats, w_cross = cross_forward(
        info, states_all, cross_kv_pieces, queries, question, count_pass
    )
    bits = 1
    while bits < blk_count:
        stats = merge(info, stats, swap(stats, "blk", bits), bits)
        bits *= 2
    out, log_total, cross_context, mine, sent = cross_out(info, stats, w_cross_output)
    after_cross, fifth, dec_active, dec_dinner, mine, sent = decoder_ffn(
        info, after_self, [mine, *share(sent)], outer_back, decoder_gains, w_dec_inner
    )
    dkey_vals, *rest = cross_back(
        info,
        key_vals,
        (
            cotangent,
            after_cross,
            [mine, *share(sent)],
            decoder_gains,
            w_cross_output,
            out,
            log_total,
            queries,
            w_cross,
        ),
        question,
        count_pass,
        slot,
        part,
    )
    partial, (dcross, dcross_low, gain_four, dqueries) = rest[:4], rest[4:]

    def enter_back(cot, a, b, c):
        grad = cot + a + b + c
        return grad, grad

    dstates, dstates_low = by_rows(
        enter_back,
        info,
        [encoder_cotangent.reshape(blocks, part, width), *collect(*partial)],
        [],
        [f32, bf16],
    )
    dstates_all = spread(dstates_low)
    grad_cross = reduce_pieces(weight_grads(info, states_all, dkey_vals))
    dinner, *partial = encoder_ffn_back(info, dstates_all, slope, w_inner, w_outer)

    def middle_back(dy, h, a, b, c, g):
        back, gain_rows = norm_back(h, g[1:2], a + b + c)
        grad = dy + back
        return grad, grad, gain_rows

    dhidden, dhidden_low, gain_one = by_rows(
        middle_back,
        info,
        [dstates, hidden, *collect(*partial)],
        [encoder_gains],
        [f32, bf16],
        gain=True,
    )
    dhidden_all = spread(dhidden_low)
    grad_outer = reduce_pieces(weight_grads(info, dstates_all, active))
    grad_inner = reduce_pieces(weight_grads(info, second_all, dinner))

    partial, pieces, gain_zero = encoder_attention_back(
        info, dhidden_all, first_all, qkv, probs, context, w_in, w_out, encoder_gains
    )

    def last_back(dh, x, a, b, c, g):
        return (dh + norm_back(x, g[0:1], a + b + c)[0],)

    input_grad = by_rows(
        last_back, info, [dhidden, inputs, *collect(*partial)], [encoder_gains], [f32]
    )[0]
    grad_attention = reduce_pieces(pieces)

    dqueries = tree_sum(dqueries, ("blk",)).astype(bf16)
    mine, sent = project_rows(info, dqueries, w_cross_query)
    dself, dself_low, gain_three, dself_qkv, own_back, sent_back = decoder_self_back(
        info,
        dcross,
        after_self,
        [mine, *share(sent)],
        decoder_gains,
        dec_w_out,
        dec_w_in,
        dec_qkv,
        dec_probs,
    )
    out_mine, out_sent = project_rows(info, dec_active, w_dec_outer)
    dec_grad, gain_two, dec_states = decoder_ends(
        info,
        dec_in,
        dself,
        [own_back, *share(sent_back)],
        decoder_gains,
        after_cross,
        [out_mine, *share(out_sent)],
    )
    (
        grad_dec_qkv,
        grad_cross_query,
        grad_dec_inner,
        grad_dec_output,
        grad_cross_output,
        grad_dec_outer,
    ) = decoder_weight_grads(
        info,
        own,
        [(third, dself_qkv), (fourth, dqueries), (fifth, dec_dinner)],
        [(dec_context, dself_low), (cross_context, dcross_low), (dec_active, cotangent)],
    )

    def own_rows(values):
        return lax.dynamic_slice_in_dim(values, head * dec_own, dec_own, 0)

    leading = (blk == 0).astype(f32)
    dec_gains = [
        jnp.sum(own_rows(g), axis=0, keepdims=True) * leading
        for g in (gain_two, gain_three, gain_four)
    ]
    gains = tree_sum(
        jnp.concatenate([gain_zero, gain_one, *dec_gains], axis=0), ("head", "blk")
    )

    def dec_shape(values):
        return own_rows(values).reshape(count_q, dec_part, width)

    size = encoder_query.shape[1]
    return (
        states.reshape(encoder_input.shape),
        dec_shape(dec_states),
        input_grad.reshape(encoder_input.shape),
        dec_shape(dec_grad),
        grad_attention[:, :size],
        grad_attention[:, size : 2 * size],
        grad_attention[:, 2 * size : 3 * size],
        grad_attention[:, 3 * size :].T,
        grad_inner,
        grad_outer.T,
        grad_dec_qkv[:, :size],
        grad_dec_qkv[:, size : 2 * size],
        grad_dec_qkv[:, 2 * size :],
        grad_dec_output,
        grad_cross_query,
        grad_cross[:, :size],
        grad_cross[:, size:],
        grad_cross_output,
        grad_dec_inner,
        grad_dec_outer,
        gains[:2],
        gains[2:],
    )


def solution(mesh):
    placed = (
        P(None, "blk", "head", None),
        P(None, "blk"),
        P(None, "head", None),
        P("blk", "head"),
        P("blk", "head"),
        P("blk", "head"),
        P("head", "blk"),
        P("blk", "head"),
        P("head", "blk"),
        P("blk", "head"),
        P("blk", "head"),
        P("blk", "head"),
        P("head", "blk"),
        P("blk", "head"),
        P("blk", "head"),
        P("blk", "head"),
        P("head", "blk"),
        P("blk", "head"),
        P("head", "blk"),
        P(),
        P(),
        P(None, "blk", "head", None),
        P(None, "head", None),
    )
    return jax.shard_map(
        shards,
        mesh=mesh,
        in_specs=placed,
        out_specs=(placed[0], placed[2], placed[0], placed[2], *placed[3:19], P(), P()),
        check_vma=False,
    )
```

```python
import math

import jax
import jax.numpy as jnp
import numpy as np
from jax import lax
from jax.experimental import pallas as pl
from jax.experimental.pallas import tpu as pltpu
from jax.sharding import PartitionSpec as P

HDIM = 64
SCALE = HDIM ** (-0.5)
LANES = 128
EPS = 1e-06
VMEM_LIMIT = 40 * 1024 * 1024
LARGE = 1 << 18
masked_score = -1000000000.0
f32 = jnp.float32
bf16 = jnp.bfloat16

PLACES, HEAD, BLK, LENGTHS = 0, 8, 9, 10


def swap(value, axis, bits):
    size = lax.axis_size(axis)
    return lax.ppermute(value, axis, [(i, i ^ bits) for i in range(size)])


def sync(*values):
    return lax.optimization_barrier(values)


def share(value):
    return [swap(value, "head", k) for k in (1, 2, 3)]


def ring_order(count):
    return [*range(0, count, 2), *range(count - 1, 0, -2)]


OFFSETS = (0, -1, 1, -2, 2, -3, 3, -4)


def ring_steps(count):
    order = ring_order(count)
    forth = [(order[i], order[(i + 1) % count]) for i in range(count)]
    return forth, [(b, a) for a, b in forth]


def place_table(count):
    order = ring_order(count)
    at = {b: i for i, b in enumerate(order)}
    return np.array(
        [[order[(at[b] + o) % count] for o in OFFSETS] for b in range(count)], np.int32
    )


def gather_rows(own):
    return lax.all_gather(own, "blk", axis=0, tiled=True)


def fetch_start(own):
    if lax.axis_size("blk") == 8:
        return {0: own}
    return dict(zip(OFFSETS, jnp.split(gather_rows(own), 8, axis=0), strict=True))


def fetch_step(pieces, *offsets):
    count = lax.axis_size("blk")
    if count != 8:
        return pieces
    forth, back = ring_steps(count)
    more = {
        k: lax.ppermute(pieces[k + 1 if k < 0 else k - 1], "blk", forth if k < 0 else back)
        for k in offsets
    }
    return {**pieces, **more}


def in_turn(pieces):
    return [pieces[k] if k in pieces else pieces[-k] for k in OFFSETS]


def add_low(a, b):
    return (a.astype(f32) + b.astype(f32)).astype(bf16)


def reduce_step(pieces, moving, step):
    count = lax.axis_size("blk")
    if count != 8:
        return []
    forth, back = ring_steps(count)
    by = dict(zip(OFFSETS, pieces, strict=True))
    if step == 1:
        ahead, behind = by[-4], by[-3]
    else:
        ahead = add_low(moving[0], by[5 - step])
        behind = add_low(moving[1], by[step - 4]) if step < 4 else None
    ahead = lax.ppermute(ahead, "blk", forth)
    return [ahead, moving[1] if behind is None else lax.ppermute(behind, "blk", back)]


def reduce_terms(pieces, moving):
    if lax.axis_size("blk") != 8:
        everything = jnp.concatenate([p.astype(f32) for p in pieces], axis=0)
        return [lax.psum_scatter(everything, "blk", scatter_dimension=0, tiled=True)]
    return [pieces[0], *moving]


def dot(left, right, over=(1, 0)):
    return lax.dot_general(
        left, right, (((over[0],), (over[1],)), ((), ())), preferred_element_type=f32
    )


def dot_t(left, right):
    return dot(left, right, (1, 1))


def t_dot(left, right):
    return dot(left, right, (0, 0))


def norm_rows(values, gain):
    return values * lax.rsqrt(jnp.mean(values * values, axis=-1, keepdims=True) + EPS) * gain


def norm_back(values, gain, grad):
    inverse = lax.rsqrt(jnp.mean(values * values, axis=-1, keepdims=True) + EPS)
    unit = values * inverse
    weighted = grad * gain
    along = jnp.mean(weighted * unit, axis=-1, keepdims=True)
    return inverse * (weighted - unit * along), grad * unit


def gelu_both(values):
    root = math.sqrt(2.0 / math.pi)
    square = values * values
    bent = jnp.tanh(root * values * (1.0 + 0.044715 * square))
    half = 0.5 * (1.0 + bent)
    slope = half + 0.5 * values * (1.0 - bent * bent) * root * (1.0 + 3 * 0.044715 * square)
    return values * half, slope


def heads_in(width):
    return [slice(at, at + HDIM) for at in range(0, width, HDIM)]


def assemble(info, pieces, targets, signals):
    rows = pieces[0].shape[0]
    copies = []
    for t, piece in enumerate(pieces):
        at = pl.ds(pl.multiple_of(info[PLACES + t] * rows, 16), rows)
        column = 0
        for k, target in enumerate(targets):
            wide = target.shape[1]
            copies.append(
                pltpu.make_async_copy(
                    piece.at[:, column : column + wide], target.at[at, :], signals.at[k, t]
                )
            )
            column += wide
    for copy in copies:
        copy.start()
    for copy in copies:
        copy.wait()


def hand_out(info, sources, pieces):
    rows = pieces[0].shape[0]
    for t, piece in enumerate(pieces):
        at = pl.ds(pl.multiple_of(info[PLACES + t] * rows, 16), rows)
        column = 0
        for source in sources:
            piece[:, column : column + source.shape[1]] = source[at, :].astype(piece.dtype)
            column += source.shape[1]


def token_rows(refs):
    return jnp.concatenate([r[0] for r in refs], axis=0)


def emit(partial, outs):
    part = outs[0].shape[1]
    for r, out in enumerate(outs):
        out[0] = partial[r * part : (r + 1) * part].astype(out.dtype)


def slots_used(info, b, part, slot):
    column = lax.broadcasted_iota(jnp.int32, (1, slot), 1)
    position = (lax.div(column, part) ^ info[HEAD]) * part + lax.rem(column, part)
    return position < info[LENGTHS + b]


def call(
    body, info, stepped, fixed, out_stepped, out_fixed, scratch=(), flops=0, steps=1, near=False
):
    def by_step(shape):
        return pl.BlockSpec((1, *shape[1:]), lambda b: (b,) + (0,) * (len(shape) - 1))

    def whole(a):
        if isinstance(a, Far):
            return pl.BlockSpec(memory_space=pltpu.HBM)
        index = (0, a.index) if type(a) is Columns else (0,) * len(a.shape)
        return pl.BlockSpec(a.shape, lambda b: index)

    counts = [len(stepped), len(fixed), len(out_stepped), len(out_fixed), len(scratch)]
    stops = np.cumsum(counts)

    def split(info_ref, *refs):
        body(info_ref, *(refs[e - c : e] for c, e in zip(counts, stops, strict=True)))

    def large(a):
        return not near and math.prod(a.shape) * a.dtype.itemsize >= LARGE

    def given(a):
        array = a.array if isinstance(a, (Columns, Far)) else a
        return pltpu.with_memory_space_constraint(array, pltpu.HBM) if large(a) else array

    def made(a):
        return a.array if isinstance(a, Near) else pltpu.HBM(a.shape, a.dtype) if large(a) else a

    arrays = [*stepped, *fixed, *out_stepped, *out_fixed]
    moved = sum(math.prod(a.shape) * a.dtype.itemsize for a in arrays)
    return pl.pallas_call(
        split,
        grid=(steps,),
        in_specs=[
            pl.BlockSpec(memory_space=pltpu.SMEM),
            *(by_step(a.shape) for a in stepped),
            *(whole(a) for a in fixed),
        ],
        out_specs=[
            *(by_step(a.shape) for a in out_stepped),
            *(whole(a) for a in out_fixed),
        ],
        out_shape=[made(a) for a in (*out_stepped, *out_fixed)],
        scratch_shapes=list(scratch),
        compiler_params=pltpu.CompilerParams(
            dimension_semantics=("arbitrary",), vmem_limit_bytes=VMEM_LIMIT
        ),
        cost_estimate=pl.CostEstimate(
            flops=int(flops), bytes_accessed=int(moved), transcendentals=0
        ),
    )(info, *(given(a) for a in (*stepped, *fixed)))


class Columns:
    def __init__(self, array, width, index):
        self.array, self.index, self.dtype = array, index, array.dtype
        self.shape = (array.shape[0], width)


class Near(Columns):
    def __init__(self, array):
        self.array, self.shape, self.dtype = array, array.shape, array.dtype


class Far:
    def __init__(self, array):
        self.array, self.shape, self.dtype = array, array.shape, array.dtype


def like(shape, dtype):
    return jax.ShapeDtypeStruct(tuple(shape), dtype)


def by_rows(fn, info, stepped, fixed, dtypes, gain=False):
    steps, _, width = stepped[0].shape

    def body(info_ref, ins, whole, outs, sums, _):
        results = fn(*(r[0].astype(f32) for r in ins), *(r[...] for r in whole))
        for out, value in zip(outs, results, strict=False):
            out[0] = value.astype(out.dtype)
        for total in sums:

            @pl.when(pl.program_id(0) == 0)
            def _():
                total[...] = jnp.zeros_like(total)

            total[...] += jnp.sum(results[-1], axis=0, keepdims=True)

    return call(
        body,
        info,
        stepped,
        fixed,
        [like(stepped[0].shape, d) for d in dtypes],
        [like((1, width), f32)] * gain,
        flops=10 * math.prod(stepped[0].shape),
        steps=steps,
        near=True,
    )


def partial_rows(blocks, part, width):
    return [Near(like((blocks, part, width), d)) for d in (f32, bf16, f32, bf16)]


def piece_shapes(rows, columns):
    return [like((rows, columns), f32), *[Near(like((rows, columns), bf16))] * 7]


def encoder_attention(info, normed, pieces):
    blocks, part, width = normed[0].shape
    slot = part * len(normed)
    size = pieces[0].shape[1] // 4
    count = size // HDIM

    def body(info, rows, pieces, outs, weights, scratch):
        qkv, probs, context = outs[:3]
        w_in, w_out = weights
        together, signals = scratch
        b = pl.program_id(0)

        @pl.when(b == 0)
        def _():
            assemble(info, pieces, (together,), signals)
            w_in[...] = together[:, : 3 * size]
            w_out[...] = together[:, 3 * size :]

        qkv[0] = dot(token_rows(rows), w_in[...]).astype(bf16)
        allowed = slots_used(info, b, part, slot)
        for k, at in enumerate(heads_in(size)):
            query, keys, vals = (qkv[0, :, j * size + at.start : j * size + at.stop] for j in range(3))
            scores = jnp.where(allowed, dot_t(query, keys) * SCALE, masked_score)
            spread_out = jnp.exp(scores - jnp.max(scores, axis=-1, keepdims=True))
            weight = (spread_out / jnp.sum(spread_out, axis=-1, keepdims=True)).astype(bf16)
            probs[0, k] = weight
            context[0, :, at] = dot(weight, vals).astype(bf16)
        emit(dot_t(context[0], w_out[...]), outs[3:])

    return call(
        body,
        info,
        normed,
        [Far(p) for p in pieces],
        [
            like((blocks, slot, 3 * size), bf16),
            like((blocks, count, slot, slot), bf16),
            like((blocks, slot, size), bf16),
            *partial_rows(blocks, part, width),
        ],
        [like((width, 3 * size), bf16), like((width, size), bf16)],
        [pltpu.VMEM((width, 4 * size), bf16), pltpu.SemaphoreType.DMA((1, len(pieces)))],
        flops=2 * blocks * slot * (width * size * 4 + 8 * slot * size),
        steps=blocks,
    )


def encoder_attention_back(info, grads, normed, qkv, probs, context, w_in, w_out, gains):
    blocks, part, width = normed[0].shape
    slot = part * len(normed)
    size = w_out.shape[1]

    def body(info, stepped, fixed, outs, ends, scratch):
        grad_refs, normed_refs = stepped[:4], stepped[4:8]
        qkv, probs, context = stepped[8:]
        w_in, w_out, gains = fixed
        pieces, gain_out = ends[:-1], ends[-1]
        total_in, total_out, moved = scratch
        b = pl.program_id(0)

        @pl.when(b == 0)
        def _():
            total_in[...] = jnp.zeros_like(total_in)
            total_out[...] = jnp.zeros_like(total_out)
            gain_out[...] = jnp.zeros_like(gain_out)

        grad = token_rows(grad_refs)
        rows = token_rows(normed_refs)
        dcontext = dot(grad, w_out[...]).astype(bf16)
        for k, at in enumerate(heads_in(size)):
            query, keys, vals = (qkv[0, :, j * size + at.start : j * size + at.stop] for j in range(3))
            weight = probs[0, k]
            dprobs = dot_t(dcontext[:, at], vals)
            wide = weight.astype(f32)
            dscores = wide * (dprobs - jnp.sum(wide * dprobs, axis=-1, keepdims=True))
            dscores = dscores.astype(bf16)
            terms = (
                dot(dscores, keys) * SCALE,
                t_dot(dscores, query) * SCALE,
                t_dot(weight, dcontext[:, at]),
            )
            for j, term in enumerate(terms):
                moved[:, j * size + at.start : j * size + at.stop] = term.astype(bf16)
        partial = dot_t(moved[...], w_in[...])
        emit(partial, outs)
        gain_out[...] += jnp.sum(partial * rows.astype(f32), axis=0, keepdims=True) / gains[0:1, :]
        total_in[...] += t_dot(rows, moved[...])
        total_out[...] += t_dot(grad, context[0])

        @pl.when(b == blocks - 1)
        def _():
            hand_out(info, (total_in, total_out), pieces)

    results = call(
        body,
        info,
        [*grads, *normed, qkv, probs, context],
        [w_in, w_out, gains],
        partial_rows(blocks, part, width),
        [*piece_shapes(width // 8, 4 * size), like((1, width), f32)],
        [
            pltpu.VMEM((width, 3 * size), f32),
            pltpu.VMEM((width, size), f32),
            pltpu.VMEM((slot, 3 * size), bf16),
        ],
        flops=2 * blocks * slot * (width * size * 8 + 20 * slot * size),
        steps=blocks,
    )
    return results[:4], results[4:12], results[12]


def encoder_ffn(info, normed, pieces):
    blocks, part, width = normed[0].shape
    slot = part * len(normed)
    hidden = pieces[0].shape[1] // 2

    def body(info, rows, pieces, outs, weights, scratch):
        active, slope = outs[:2]
        w_inner, w_outer = weights

        @pl.when(pl.program_id(0) == 0)
        def _():
            assemble(info, pieces, weights, scratch[0])

        value, bend = gelu_both(dot(token_rows(rows), w_inner[...]))
        active[0] = value.astype(bf16)
        slope[0] = bend.astype(bf16)
        emit(dot_t(active[0], w_outer[...]), outs[2:])

    return call(
        body,
        info,
        normed,
        [Far(p) for p in pieces],
        [*[like((blocks, slot, hidden), bf16)] * 2, *partial_rows(blocks, part, width)],
        [like((width, hidden), bf16)] * 2,
        [pltpu.SemaphoreType.DMA((2, len(pieces)))],
        flops=4 * blocks * slot * width * hidden,
        steps=blocks,
    )


def encoder_ffn_back(info, grads, slope, w_inner, w_outer):
    blocks, part, width = grads[0].shape
    slot = part * len(grads)
    hidden = w_inner.shape[1]

    def body(info, stepped, weights, outs, ends, _):
        dinner = outs[0]
        w_inner, w_outer = weights
        back = dot(token_rows(stepped[:4]), w_outer[...])
        dinner[0] = (back * stepped[4][0].astype(f32)).astype(bf16)
        emit(dot_t(dinner[0], w_inner[...]), outs[1:])

    return call(
        body,
        info,
        [*grads, slope],
        [w_inner, w_outer],
        [like((blocks, slot, hidden), bf16), *partial_rows(blocks, part, width)],
        [],
        flops=4 * blocks * slot * width * hidden,
        steps=blocks,
    )


def weight_grads(info, pairs, more=()):
    blocks, part, width = pairs[0][0][0].shape
    widths = [right.shape[2] for _, right in pairs]
    total_width = sum(widths) + sum(m.shape[1] for m in more)

    def body(info, stepped, more, _, ends, totals):
        b = pl.program_id(0)
        totals = totals if more else ends
        for k, total in enumerate(totals):
            left, right = stepped[5 * k : 5 * k + 4], stepped[5 * k + 4]
            found = t_dot(token_rows(left), right[0])

            @pl.when(b == 0)
            def _():
                total[...] = found

            @pl.when(b > 0)
            def _():
                total[...] += found

        if more:

            @pl.when(b == blocks - 1)
            def _():
                hand_out(info, (*more, *totals), ends)

    return call(
        body,
        info,
        [a for left, right in pairs for a in (*left, right)],
        more,
        [],
        piece_shapes(width // 8, total_width)
        if more
        else [like((width, w), f32) for w in widths],
        [pltpu.VMEM((width, w), f32) for w in widths] if more else [],
        flops=2 * blocks * part * 4 * width * total_width,
        steps=blocks,
    )


def finish(info, terms, widths, turned):
    rows = terms[0].shape[0]
    shapes = [(w, rows) if t else (rows, w) for w, t in zip(widths, turned, strict=True)]

    def body(info, _, ins, __, outs, ___):
        total = summed(ins)
        column = 0
        for out, wide, turn in zip(outs, widths, turned, strict=True):
            found = total[:, column : column + wide]
            out[...] = found.T if turn else found
            column += wide

    return call(body, info, [], terms, [], [like(s, f32) for s in shapes])


def cross_forward(info, states, weight, queries, own_question, count_pass):
    blocks, part, width = states[0].shape
    slot = part * len(states)
    size = queries.shape[1]
    rows_dec = queries.shape[0]

    def body(info, rows, fixed, outs, ends, scratch):
        weight, queries, question = fixed
        stats = ends[0]
        held = scratch[0]
        b = pl.program_id(0)
        made = dot(token_rows(rows), weight[...]).astype(bf16)
        outs[0][0] = made
        held[pl.ds(pl.multiple_of(b * slot, slot), slot), :] = made

        @pl.when(b == blocks - 1)
        def _():
            allowed = jnp.concatenate(
                [
                    slots_used(info, k, part, slot) & (question[...] == k // count_pass)
                    for k in range(blocks)
                ],
                axis=1,
            )
            lane = lax.broadcasted_iota(jnp.int32, (rows_dec, HDIM), 1)
            for k, at in enumerate(heads_in(size)):
                scores = dot_t(queries[:, at], held[:, at]) * SCALE
                scores = jnp.where(allowed, scores, masked_score)
                top = jnp.max(scores, axis=-1, keepdims=True)
                spread_out = jnp.exp(scores - top)
                total = jnp.sum(spread_out, axis=-1, keepdims=True)
                vals = held[:, size + at.start : size + at.stop]
                stats[:, k * LANES : k * LANES + HDIM] = dot(spread_out.astype(bf16), vals)
                stats[:, k * LANES + HDIM : (k + 1) * LANES] = jnp.where(lane == 0, top, total)

    return call(
        body,
        info,
        states,
        [weight, queries, own_question],
        [like((blocks, slot, 2 * size), bf16)],
        [like((rows_dec, size // HDIM * LANES), f32)],
        [pltpu.VMEM((blocks * slot, 2 * size), bf16)],
        flops=4 * blocks * slot * width * size,
        steps=blocks,
    )


def merge(info, own, other, bits):
    def body(info, _, ins, __, outs, ___):
        mine, yours = ins[0][...], ins[1][...]
        later = (info[BLK] & bits) != 0
        first, second = jnp.where(later, yours, mine), jnp.where(later, mine, yours)
        lane = lax.broadcasted_iota(jnp.int32, (first.shape[0], HDIM), 1)
        for at in range(0, first.shape[1], LANES):
            pairs = [(v[:, at + HDIM : at + HDIM + 1], v[:, at + HDIM + 1 : at + HDIM + 2]) for v in (first, second)]
            top = jnp.maximum(pairs[0][0], pairs[1][0])
            by_first, by_second = jnp.exp(pairs[0][0] - top), jnp.exp(pairs[1][0] - top)
            total = pairs[0][1] * by_first + pairs[1][1] * by_second
            outs[0][:, at : at + HDIM] = (
                first[:, at : at + HDIM] * by_first + second[:, at : at + HDIM] * by_second
            )
            outs[0][:, at + HDIM : at + LANES] = jnp.where(lane == 0, top, total)

    return call(body, info, [], [own, other], [], [like(own.shape, f32)])[0]


def cross_out(info, stats, w_output):
    rows, columns = stats.shape
    size = columns // LANES * HDIM
    width = w_output.shape[0]

    def body(info, _, ins, __, outs, scratch):
        stats, w_output = ins
        out, log_total, context, own, sent = outs
        log_total[...] = jnp.zeros_like(log_total)
        for k, at in enumerate(heads_in(size)):
            base = k * LANES
            top = stats[:, base + HDIM : base + HDIM + 1]
            total = stats[:, base + HDIM + 1 : base + HDIM + 2]
            out[:, at] = stats[:, base : base + HDIM] / total
            log_total[:, k : k + 1] = top + jnp.log(total)
        context[...] = out[...].astype(bf16)
        own[...] = dot_t(context[...], w_output[...])
        sent[...] = own[...].astype(bf16)

    return call(
        body,
        info,
        [],
        [stats, w_output],
        [],
        [
            like((rows, size), f32),
            like((rows, LANES), f32),
            like((rows, size), bf16),
            like((rows, width), f32),
            like((rows, width), bf16),
        ],
        flops=2 * rows * size * width,
    )


def cross_back(info, key_vals, inputs, own_question, count_pass, slot, part):
    cotangent, after_cross, terms, gains, w_output, out, log_total, queries, weight = inputs
    blocks = key_vals.shape[0]
    rows_dec, width = after_cross.shape
    size = queries.shape[1]

    def body(info, stepped, fixed, outs, ends, scratch):
        cotangent, after_cross, own, r1, r2, r3, gains, w_output, out, log_total, queries, weight, question = fixed
        key_vals = stepped[0]
        dkey_vals = outs[0]
        dcross, dcross_low, gain_out, dqueries = ends
        dcontext, row_terms = scratch
        b = pl.program_id(0)

        @pl.when(b == 0)
        def _():
            total = own[...] + r1[...].astype(f32) + r2[...].astype(f32) + r3[...].astype(f32)
            back, gain_rows = norm_back(after_cross[...], gains[2:3, :], total)
            dcross[...] = cotangent[...].astype(f32) + back
            dcross_low[...] = dcross[...].astype(bf16)
            gain_out[...] = gain_rows
            dcontext[...] = dot(dcross_low[...], w_output[...]).astype(bf16)
            for k, at in enumerate(heads_in(size)):
                row_terms[:, k : k + 1] = jnp.sum(
                    dcontext[:, at].astype(f32) * out[:, at], axis=-1, keepdims=True
                )
            dqueries[...] = jnp.zeros_like(dqueries)

        allowed = slots_used(info, b, part, slot) & (question[...] == lax.div(b, count_pass))
        for k, at in enumerate(heads_in(size)):
            keys, vals = key_vals[0, :, at], key_vals[0, :, size + at.start : size + at.stop]
            scores = dot_t(queries[:, at], keys) * SCALE
            scores = jnp.where(allowed, scores, masked_score)
            probs = jnp.exp(scores - log_total[:, k : k + 1])
            dprobs = dot_t(dcontext[:, at], vals)
            dscores = (probs * (dprobs - row_terms[:, k : k + 1])).astype(bf16)
            dqueries[:, at] += dot(dscores, keys) * SCALE
            dkey_vals[0, :, at] = (t_dot(dscores, queries[:, at]) * SCALE).astype(bf16)
            dkey_vals[0, :, size + at.start : size + at.stop] = t_dot(
                probs.astype(bf16), dcontext[:, at]
            ).astype(bf16)
        emit(dot_t(dkey_vals[0], weight[...]), outs[1:])

    return call(
        body,
        info,
        [key_vals],
        [cotangent, after_cross, *terms, gains, w_output, out, log_total, queries, weight, own_question],
        [like(key_vals.shape, bf16), *partial_rows(blocks, part, width)],
        [
            like((rows_dec, width), f32),
            like((rows_dec, width), bf16),
            like((rows_dec, width), f32),
            like((rows_dec, size), f32),
        ],
        [pltpu.VMEM((rows_dec, size), bf16), pltpu.VMEM((rows_dec, LANES), f32)],
        flops=4 * blocks * slot * width * size,
        steps=blocks,
    )


def summed(refs):
    total = refs[0][...]
    for ref in refs[1:]:
        total = total + ref[...].astype(f32)
    return total


def decoder_self(info, rows, gains, weight, order):
    count, width = rows.shape
    size = weight.shape[1] // 4

    def body(info, _, ins, __, outs, scratch):
        rows, gains, order_q, order_k, weight = ins
        normed, qkv, probs, context, own, sent = outs
        normed[...] = norm_rows(rows[...].astype(f32), gains[0:1, :]).astype(bf16)
        qkv[...] = dot(normed[...], weight[:, : 3 * size]).astype(bf16)
        query_at, key_at = order_q[...], order_k[...]
        same = lax.div(query_at, 1000) == lax.div(key_at, 1000)
        allowed = same & (key_at <= query_at) & (key_at >= 0) & (query_at >= 0)
        for k, at in enumerate(heads_in(size)):
            query, keys, vals = (qkv[:, j * size + at.start : j * size + at.stop] for j in range(3))
            scores = jnp.where(allowed, dot_t(query, keys) * SCALE, masked_score)
            spread_out = jnp.exp(scores - jnp.max(scores, axis=-1, keepdims=True))
            share_out = spread_out / jnp.sum(spread_out, axis=-1, keepdims=True)
            share_out = jnp.where(allowed, share_out, 0.0)
            probs[k] = share_out
            context[:, at] = dot(share_out.astype(bf16), vals).astype(bf16)
        own[...] = dot_t(context[...], weight[:, 3 * size :])
        sent[...] = own[...].astype(bf16)

    return call(
        body,
        info,
        [],
        [rows, gains, *order, weight],
        [],
        [
            like((count, width), bf16),
            like((count, 3 * size), bf16),
            like((size // HDIM, count, count), f32),
            like((count, size), bf16),
            like((count, width), f32),
            like((count, width), bf16),
        ],
        flops=2 * count * width * size * 4,
    )


def decoder_queries(info, rows, terms, gains, weight):
    count, width = rows.shape
    size = weight.shape[1] // 2

    def body(info, _, ins, __, outs, scratch):
        rows, own, r1, r2, r3, gains, weight = ins
        after_self, normed, queries, w_query, w_output = outs
        w_query[...] = weight[:, :size]
        w_output[...] = weight[:, size:]
        after_self[...] = rows[...].astype(f32) + summed((own, r1, r2, r3))
        normed[...] = norm_rows(after_self[...], gains[1:2, :]).astype(bf16)
        queries[...] = dot(normed[...], w_query[...]).astype(bf16)

    return call(
        body,
        info,
        [],
        [rows, *terms, gains, weight],
        [],
        [
            like((count, width), f32),
            like((count, width), bf16),
            like((count, size), bf16),
            like((width, size), bf16),
            like((width, size), bf16),
        ],
        flops=2 * count * width * size,
    )


def decoder_back(info, cotangent, pieces):
    count, width = cotangent.shape
    hidden = pieces[0].shape[1] // 2

    def body(info, _, ins, __, outs, scratch):
        w_inner, w_outer, back = outs
        assemble(info, ins[1:], (w_inner, w_outer), scratch[0])
        back[...] = dot(ins[0][...], w_outer[...])

    return call(
        body,
        info,
        [],
        [cotangent, *(Far(p) for p in pieces)],
        [],
        [*[like((width, hidden), bf16)] * 2, like((count, hidden), f32)],
        [pltpu.SemaphoreType.DMA((2, len(pieces)))],
        flops=2 * count * width * hidden,
    )


def decoder_ffn(info, after_self, terms, back, gains, w_inner):
    count, width = after_self.shape
    hidden = w_inner.shape[1]

    def body(info, _, ins, __, outs, scratch):
        after_self, own, r1, r2, r3, back, gains, w_inner = ins
        after_cross, normed, active, dinner, own_back, sent_back = outs
        after_cross[...] = after_self[...] + summed((own, r1, r2, r3))
        normed[...] = norm_rows(after_cross[...], gains[2:3, :]).astype(bf16)
        value, slope = gelu_both(dot(normed[...], w_inner[...]))
        active[...] = value.astype(bf16)
        dinner[...] = (slope * back[...]).astype(bf16)
        own_back[...] = dot_t(dinner[...], w_inner[...])
        sent_back[...] = own_back[...].astype(bf16)

    return call(
        body,
        info,
        [],
        [after_self, *terms, back, gains, w_inner],
        [],
        [
            like((count, width), f32),
            like((count, width), bf16),
            like((count, hidden), bf16),
            like((count, hidden), bf16),
            like((count, width), f32),
            like((count, width), bf16),
        ],
        flops=4 * count * width * hidden,
    )


def project_rows(info, rows, weight):
    count, width = rows.shape[0], weight.shape[0]

    def body(info, _, ins, __, outs, scratch):
        outs[0][...] = dot_t(ins[0][...].astype(bf16), ins[1][...])
        outs[1][...] = outs[0][...].astype(bf16)

    return call(
        body,
        info,
        [],
        [rows, weight],
        [],
        [like((count, width), f32), like((count, width), bf16)],
        flops=2 * count * width * weight.shape[1],
    )


def decoder_self_back(
    info, dcross, after_self, terms, gains, weight, qkv, probs, active, w_outer
):
    count, width = after_self.shape
    size = weight.shape[1] // 4

    def body(info, _, ins, __, outs, scratch):
        dcross, after_self, own, r1, r2, r3, gains, weight, qkv, probs, active, w_outer = ins
        dself, dself_low, gain_rows, moved, own_back, sent_back = outs
        back, gain_rows[...] = norm_back(after_self[...], gains[1:2, :], summed((own, r1, r2, r3)))
        dself[...] = dcross[...] + back
        dself_low[...] = dself[...].astype(bf16)
        dcontext = dot(dself_low[...], weight[:, 3 * size :]).astype(bf16)
        for k, at in enumerate(heads_in(size)):
            query, keys, vals = (qkv[:, j * size + at.start : j * size + at.stop] for j in range(3))
            share_out = probs[k]
            dprobs = dot_t(dcontext[:, at], vals)
            dscores = share_out * (dprobs - jnp.sum(share_out * dprobs, axis=-1, keepdims=True))
            dscores = dscores.astype(bf16)
            found = (
                dot(dscores, keys) * SCALE,
                t_dot(dscores, query) * SCALE,
                t_dot(share_out.astype(bf16), dcontext[:, at]),
            )
            for j, term in enumerate(found):
                moved[:, j * size + at.start : j * size + at.stop] = term.astype(bf16)
        own_back[:count, :] = dot_t(moved[...], weight[:, : 3 * size])
        own_back[count:, :] = dot_t(active[...], w_outer[...])
        sent_back[...] = own_back[...].astype(bf16)

    return call(
        body,
        info,
        [],
        [dcross, after_self, *terms, gains, weight, qkv, probs, active, w_outer],
        [],
        [
            like((count, width), f32),
            like((count, width), bf16),
            like((count, width), f32),
            like((count, 3 * size), bf16),
            like((2 * count, width), f32),
            like((2 * count, width), bf16),
        ],
        flops=2 * count * width * size * 8,
    )


def decoder_ends(info, rows, dself, terms, gains, after_cross):
    count, width = dself.shape

    def body(info, _, ins, __, outs, scratch):
        rows, dself, after_cross, gains = ins[:4]
        grad, gain_rows, states = outs
        total = summed(ins[4:8])
        back, gain_rows[...] = norm_back(rows[...].astype(f32), gains[0:1, :], total[:count])
        grad[...] = dself[...] + back
        states[...] = (after_cross[...] + total[count:]).astype(bf16)

    return call(
        body,
        info,
        [],
        [rows, dself, after_cross, gains, *terms],
        [],
        [like((count, width), f32), like((count, width), f32), like((count, width), bf16)],
    )


def decoder_weight_grads(info, own, pairs_in, pairs_out):
    count, width = pairs_in[0][0].shape

    def body(info, _, ins, __, outs, scratch):
        row = lax.broadcasted_iota(jnp.int32, (own, width), 0) + info[BLK] * own
        column = lax.broadcasted_iota(jnp.int32, (own, width), 1)
        pick = jnp.where(row == column, 1.0, 0.0).astype(bf16)
        n = 2 * len(pairs_in)
        for k, out in enumerate(outs):
            left, right = ins[2 * k][...], ins[2 * k + 1][...]
            if 2 * k < n:
                out[...] = t_dot(dot_t(left, pick).astype(bf16), right)
            else:
                out[...] = t_dot(left, dot_t(right, pick).astype(bf16))

    outs = [like((own, r.shape[1]), f32) for _, r in pairs_in]
    outs += [like((l.shape[1], own), f32) for l, _ in pairs_out]
    flat = [a for pair in (*pairs_in, *pairs_out) for a in pair]
    return call(body, info, [], flat, [], outs, flops=2 * count * own * width * 10)


def shards(
    encoder_input,
    passage_lengths,
    decoder_input,
    encoder_query,
    encoder_key,
    encoder_value,
    encoder_output,
    encoder_inner,
    encoder_outer,
    decoder_query,
    decoder_key,
    decoder_value,
    decoder_output,
    cross_query,
    cross_key,
    cross_value,
    cross_output,
    decoder_inner,
    decoder_outer,
    encoder_gains,
    decoder_gains,
    encoder_cotangent,
    decoder_cotangent,
):
    head, blk = lax.axis_index("head"), lax.axis_index("blk")
    blk_count, head_count = lax.axis_size("blk"), lax.axis_size("head")
    count_q, count_pass, part, width = encoder_input.shape
    blocks = count_q * count_pass
    slot = part * head_count
    own = width // blk_count
    if blk_count == 8:
        places = jnp.asarray(place_table(8))[blk]
    else:
        places = jnp.arange(8, dtype=jnp.int32)
    info = jnp.concatenate(
        [places, jnp.stack([head, blk]).astype(jnp.int32), passage_lengths.reshape(blocks)]
    )

    size, units = encoder_query.shape[1], encoder_inner.shape[1]
    inputs = encoder_input.reshape(blocks, part, width)
    dec_part = decoder_input.shape[1]
    dec_own = count_q * dec_part
    dec_rows = dec_own * head_count
    filled = -(-dec_rows // 16) * 16

    attention = jnp.concatenate(
        [encoder_query, encoder_key, encoder_value, encoder_output.T], axis=1
    )
    attention, inputs = sync(attention, inputs)
    attention = fetch_step(fetch_start(attention), -1, 1)
    first = by_rows(
        lambda x, g: (norm_rows(x, g[0:1]),), info, [inputs], [encoder_gains], [bf16]
    )[0]
    cross_self = jnp.concatenate(
        [
            cross_key,
            cross_value,
            cross_query,
            cross_output.T,
            decoder_query,
            decoder_key,
            decoder_value,
            decoder_output.T,
        ],
        axis=1,
    )
    attention, first, cross_self = sync(attention, first, cross_self)

    cross_self = gather_rows(cross_self)
    attention = fetch_step(attention, -2, 2)
    first_all = [first, swap(first, "head", 1), swap(first, "head", 2)]
    ffn = jnp.concatenate([encoder_inner, encoder_outer.T], axis=1)
    attention, first_all, ffn = sync(attention, first_all, ffn)

    attention = fetch_step(attention, -3, 3)
    first_all.append(swap(first_all[2], "head", 1))
    pair = jnp.stack([decoder_input, decoder_cotangent]).reshape(2, dec_own, width)
    both = lax.all_gather(pair, "head", axis=1, tiled=True)
    both = jnp.pad(both, ((0, 0), (0, filled - dec_rows), (0, 0)))
    attention, first_all, ffn, both = sync(attention, first_all, ffn, both)

    attention, ffn = fetch_step(attention, -4), fetch_step(fetch_start(ffn), 1)
    dec_ffn = jnp.concatenate([decoder_inner, decoder_outer.T], axis=1)
    attention, ffn, first_all, dec_ffn = sync(attention, ffn, first_all, dec_ffn)

    qkv, probs, context, *partial, w_in, w_out = encoder_attention(
        info, first_all, in_turn(attention)
    )
    ffn = fetch_step(ffn, -1, 2)
    partial, ffn = sync(partial, ffn)

    def to_core(partial):
        return [swap(partial[1], "head", 1), swap(partial[3], "head", 1)]

    def to_chip(partial, beside):
        return swap((partial[2] + beside[1].astype(f32)).astype(bf16), "head", 2)

    beside = to_core(partial)
    partial, beside, ffn = sync(partial, beside, ffn)
    across = to_chip(partial, beside)
    ffn = fetch_step(ffn, -2, 3)
    partial, beside, across, ffn = sync(partial, beside, across, ffn)

    def enter_ffn(x, a, b, c, g):
        hidden = x + a + b + c
        return hidden, norm_rows(hidden, g[1:2])

    hidden, second = by_rows(
        enter_ffn, info, [inputs, partial[0], beside[0], across], [encoder_gains], [f32, bf16]
    )
    second, ffn = sync(second, ffn)
    ffn = fetch_step(ffn, -3, 4)
    second_all = [second, swap(second, "head", 1), swap(second, "head", 2)]
    second_all, ffn, dec_ffn = sync(second_all, ffn, dec_ffn)
    second_all.append(swap(second_all[2], "head", 1))
    second_all, dec_ffn = sync(second_all, dec_ffn)

    dec_ffn = fetch_step(fetch_start(dec_ffn), -1, 1)
    active, slope, *partial, w_inner, w_outer = encoder_ffn(info, second_all, in_turn(ffn))
    partial, dec_ffn = sync(partial, dec_ffn)
    beside = to_core(partial)
    partial, beside, cross_self, both, dec_ffn = sync(partial, beside, cross_self, both, dec_ffn)
    dec_in, cotangent = both[0], both[1]
    w_cross, w_cross_qo = (Columns(cross_self, 2 * size, k) for k in (0, 1))
    w_self = Columns(cross_self, 4 * size, 1)

    index = np.arange(filled)
    question = (index % dec_own) // dec_part
    position = index // dec_own * dec_part + index % dec_part
    order = np.where(index < dec_rows, question * 1000 + position, -1).astype(np.int32)
    order = (jnp.asarray(order[:, None]), jnp.asarray(order[None, :]))
    question = jnp.asarray(question[:, None].astype(np.int32))

    across = to_chip(partial, beside)
    third, dec_qkv, dec_probs, dec_context, mine, sent = decoder_self(
        info, dec_in, decoder_gains, w_self, order
    )
    dec_ffn = fetch_step(dec_ffn, -2, 2)
    partial, beside, across, mine, sent, dec_ffn = sync(
        partial, beside, across, mine, sent, dec_ffn
    )
    states = by_rows(
        lambda h, a, b, c: (h + a + b + c,),
        info,
        [hidden, partial[0], beside[0], across],
        [],
        [bf16],
    )[0]
    states, sent, dec_ffn = sync(states, sent, dec_ffn)
    states_all = [states, swap(states, "head", 1), swap(states, "head", 2)]
    terms = [mine, *share(sent)]
    dec_ffn = fetch_step(dec_ffn, -3, 3)
    states_all, terms, dec_ffn = sync(states_all, terms, dec_ffn)
    states_all.append(swap(states_all[2], "head", 1))
    after_self, fourth, queries, w_cross_query, w_cross_output = decoder_queries(
        info, dec_in, terms, decoder_gains, w_cross_qo
    )
    states_all, queries, dec_ffn = sync(states_all, queries, dec_ffn)

    key_vals, stats = cross_forward(info, states_all, w_cross, queries, question, count_pass)
    dec_ffn = fetch_step(dec_ffn, -4)
    bits = [1 << k for k in range((blk_count - 1).bit_length())]
    stats, dec_ffn = sync(stats, dec_ffn)
    w_dec_inner, w_dec_outer, outer_back = decoder_back(info, cotangent, in_turn(dec_ffn))
    for k in bits:
        stats = merge(info, stats, swap(stats, "blk", k), k)
        if k == bits[0]:
            stats, outer_back = sync(stats, outer_back)
    out, log_total, cross_context, mine, sent = cross_out(info, stats, w_cross_output)
    after_cross, fifth, dec_active, dec_dinner, mine, sent = decoder_ffn(
        info, after_self, [mine, *share(sent)], outer_back, decoder_gains, w_dec_inner
    )
    dkey_vals, *rest = cross_back(
        info,
        key_vals,
        (
            cotangent,
            after_cross,
            [mine, *share(sent)],
            decoder_gains,
            w_cross_output,
            out,
            log_total,
            queries,
            w_cross,
        ),
        question,
        count_pass,
        slot,
        part,
    )
    partial, (dcross, dcross_low, gain_four, dqueries) = rest[:4], rest[4:]

    def some(value, which):
        for k in which:
            value = value + swap(value, "blk", k)
        return value

    partial, dqueries, dkey_vals = sync(partial, dqueries, dkey_vals)
    beside = to_core(partial)
    partial, beside, dkey_vals, dqueries = sync(partial, beside, dkey_vals, dqueries)
    across = to_chip(partial, beside)
    dqueries = some(dqueries, bits[:1])
    cross_sum = weight_grads(info, [(states_all, dkey_vals)])[0]
    partial, beside, across, cross_sum, dqueries = sync(
        partial, beside, across, cross_sum, dqueries
    )

    def enter_back(cot, a, b, c):
        grad = cot + a + b + c
        return grad, grad

    dstates, dstates_low = by_rows(
        enter_back,
        info,
        [encoder_cotangent.reshape(blocks, part, width), partial[0], beside[0], across],
        [],
        [f32, bf16],
    )
    dstates_low, dqueries = sync(dstates_low, dqueries)
    dstates_all = [dstates_low, swap(dstates_low, "head", 1), swap(dstates_low, "head", 2)]
    dqueries = some(dqueries, bits[1:]).astype(bf16)
    dstates_all, dqueries = sync(dstates_all, dqueries)
    dstates_all.append(swap(dstates_all[2], "head", 1))
    mine, sent = project_rows(info, dqueries, w_cross_query)
    dstates_all, sent = sync(dstates_all, sent)
    dinner, *partial = encoder_ffn_back(info, dstates_all, slope, w_inner, w_outer)
    terms = [mine, *share(sent)]
    partial, dinner, terms = sync(partial, dinner, terms)
    beside = to_core(partial)
    partial, beside, dinner = sync(partial, beside, dinner)
    across = to_chip(partial, beside)
    ffn_sums = weight_grads(
        info, [(second_all, dinner), (dstates_all, active)], [cross_sum]
    )
    partial, beside, across, ffn_sums, terms = sync(partial, beside, across, ffn_sums, terms)

    def middle_back(dy, h, a, b, c, g):
        back, gain_rows = norm_back(h, g[1:2], a + b + c)
        grad = dy + back
        return grad, grad, gain_rows

    dhidden, dhidden_low, gain_one = by_rows(
        middle_back,
        info,
        [dstates, hidden, partial[0], beside[0], across],
        [encoder_gains],
        [f32, bf16],
        gain=True,
    )
    dhidden_low, ffn_sums, terms = sync(dhidden_low, ffn_sums, terms)
    dhidden_all = [dhidden_low, swap(dhidden_low, "head", 1), swap(dhidden_low, "head", 2)]
    ffn_moving = reduce_step(ffn_sums, None, 1)
    dself, dself_low, gain_three, dself_qkv, own_back, sent_back = decoder_self_back(
        info,
        dcross,
        after_self,
        terms,
        decoder_gains,
        w_self,
        dec_qkv,
        dec_probs,
        dec_active,
        w_dec_outer,
    )
    dhidden_all, ffn_moving, sent_back = sync(dhidden_all, ffn_moving, sent_back)
    dhidden_all.append(swap(dhidden_all[2], "head", 1))
    dhidden_all, ffn_moving, sent_back = sync(dhidden_all, ffn_moving, sent_back)

    partial, sums, gain_zero = encoder_attention_back(
        info, dhidden_all, first_all, qkv, probs, context, w_in, w_out, encoder_gains
    )
    ffn_moving = reduce_step(ffn_sums, ffn_moving, 2)
    terms = [own_back, *share(sent_back)]
    partial, sums, ffn_moving, gain_zero, terms = sync(
        partial, sums, ffn_moving, gain_zero, terms
    )
    moving = reduce_step(sums, None, 1)
    beside = to_core(partial)
    dec_grad, gain_two, dec_states = decoder_ends(
        info, dec_in, dself, terms, decoder_gains, after_cross
    )

    def own_rows(values):
        return lax.dynamic_slice_in_dim(values, head * dec_own, dec_own, 0)

    leading = (blk == 0).astype(f32)
    dec_gains = [
        jnp.sum(own_rows(g), axis=0, keepdims=True) * leading
        for g in (gain_two, gain_three, gain_four)
    ]
    gains = jnp.concatenate([gain_zero, gain_one, *dec_gains], axis=0)
    gains = gains + swap(gains, "head", 1)
    partial, beside, moving, gains, ffn_moving = sync(partial, beside, moving, gains, ffn_moving)
    across = to_chip(partial, beside)
    moving = reduce_step(sums, moving, 2)
    ffn_moving = reduce_step(ffn_sums, ffn_moving, 3)
    gains = gains + swap(gains, "head", 2)
    (
        grad_dec_qkv,
        grad_cross_query,
        grad_dec_inner,
        grad_dec_output,
        grad_cross_output,
        grad_dec_outer,
    ) = decoder_weight_grads(
        info,
        own,
        [(third, dself_qkv), (fourth, dqueries), (fifth, dec_dinner)],
        [(dec_context, dself_low), (cross_context, dcross_low), (dec_active, cotangent)],
    )
    partial, beside, across, moving, gains, ffn_moving = sync(
        partial, beside, across, moving, gains, ffn_moving
    )

    def last_back(dh, x, a, b, c, g):
        return (dh + norm_back(x, g[0:1], a + b + c)[0],)

    moving = reduce_step(sums, moving, 3)
    ffn_moving = reduce_step(ffn_sums, ffn_moving, 4)
    gains = some(gains, bits[:1])
    input_grad = by_rows(
        last_back,
        info,
        [dhidden, inputs, partial[0], beside[0], across],
        [encoder_gains],
        [f32],
    )[0]
    moving, ffn_moving, gains = sync(moving, ffn_moving, gains)
    moving = reduce_step(sums, moving, 4)
    gains = some(gains, bits[1:])
    grad_cross_key, grad_cross_value, grad_inner, grad_outer = finish(
        info,
        reduce_terms(ffn_sums, ffn_moving),
        (size, size, units, units),
        (False, False, False, True),
    )
    grad_query, grad_key, grad_value, grad_output = finish(
        info, reduce_terms(sums, moving), (size,) * 4, (False, False, False, True)
    )

    def dec_shape(values):
        return own_rows(values).reshape(count_q, dec_part, width)

    return (
        states.reshape(encoder_input.shape),
        dec_shape(dec_states),
        input_grad.reshape(encoder_input.shape),
        dec_shape(dec_grad),
        grad_query,
        grad_key,
        grad_value,
        grad_output,
        grad_inner,
        grad_outer,
        grad_dec_qkv[:, :size],
        grad_dec_qkv[:, size : 2 * size],
        grad_dec_qkv[:, 2 * size :],
        grad_dec_output,
        grad_cross_query,
        grad_cross_key,
        grad_cross_value,
        grad_cross_output,
        grad_dec_inner,
        grad_dec_outer,
        gains[:2],
        gains[2:],
    )


def solution(mesh):
    placed = (
        P(None, "blk", "head", None),
        P(None, "blk"),
        P(None, "head", None),
        P("blk", "head"),
        P("blk", "head"),
        P("blk", "head"),
        P("head", "blk"),
        P("blk", "head"),
        P("head", "blk"),
        P("blk", "head"),
        P("blk", "head"),
        P("blk", "head"),
        P("head", "blk"),
        P("blk", "head"),
        P("blk", "head"),
        P("blk", "head"),
        P("head", "blk"),
        P("blk", "head"),
        P("head", "blk"),
        P(),
        P(),
        P(None, "blk", "head", None),
        P(None, "head", None),
    )
    return jax.shard_map(
        shards,
        mesh=mesh,
        in_specs=placed,
        out_specs=(placed[0], placed[2], placed[0], placed[2], *placed[3:19], P(), P()),
        check_vma=False,
    )
```

```python
import math

import jax
import jax.numpy as jnp
import numpy as np
from jax import lax
from jax.experimental import pallas as pl
from jax.experimental.pallas import tpu as pltpu
from jax.sharding import PartitionSpec as P

HDIM = 64
SCALE = HDIM ** (-0.5)
LANES = 128
EPS = 1e-06
VMEM_LIMIT = 24 * 1024 * 1024
LARGE = 1 << 18
RIDERS = 48
masked_score = -1000000000.0
f32 = jnp.float32
bf16 = jnp.bfloat16

PLACES, HEAD, BLK, LENGTHS = 0, 8, 9, 10


def swap(value, axis, bits):
    size = lax.axis_size(axis)
    return lax.ppermute(value, axis, [(i, i ^ bits) for i in range(size)])


def sync(*values):
    return lax.optimization_barrier(values)


def share(value):
    return [swap(value, "head", k) for k in (1, 2, 3)]


def ring_order(count):
    return [*range(0, count, 2), *range(count - 1, 0, -2)]


OFFSETS = (0, -1, 1, -2, 2, -3, 3, -4)


def ring_steps(count):
    order = ring_order(count)
    forth = [(order[i], order[(i + 1) % count]) for i in range(count)]
    return forth, [(b, a) for a, b in forth]


def place_table(count):
    order = ring_order(count)
    at = {b: i for i, b in enumerate(order)}
    return np.array(
        [[order[(at[b] + o) % count] for o in OFFSETS] for b in range(count)], np.int32
    )


def gather_rows(own):
    return lax.all_gather(own, "blk", axis=0, tiled=True)


def fetch_start(own):
    if lax.axis_size("blk") == 8:
        return {0: own}
    return dict(zip(OFFSETS, jnp.split(gather_rows(own), 8, axis=0), strict=True))


def fetch_step(pieces, *offsets):
    count = lax.axis_size("blk")
    if count != 8:
        return pieces
    forth, back = ring_steps(count)
    more = {
        k: lax.ppermute(pieces[k + 1 if k < 0 else k - 1], "blk", forth if k < 0 else back)
        for k in offsets
    }
    return {**pieces, **more}


def in_turn(pieces):
    return [pieces[k] if k in pieces else pieces[-k] for k in OFFSETS]


@jax.tree_util.register_pytree_node_class
class Part:
    def __init__(self, array, start, width):
        self.array, self.start, self.width = array, start, width

    def tree_flatten(self):
        return (self.array,), (self.start, self.width)

    @classmethod
    def tree_unflatten(cls, places, arrays):
        return cls(*arrays, *places)

    def read(self, ref):
        return ref[:, self.start : self.start + self.width]


def part(value):
    return value if isinstance(value, Part) else Part(value, 0, value.shape[1])


def reduce_step(info, *rings):
    count = lax.axis_size("blk")
    if count != 8:
        return [[] for _ in rings]
    forth, back = ring_steps(count)
    plan = [[], []]
    for pieces, moving, step in rings:
        by = dict(zip(OFFSETS, pieces, strict=True))
        plan[0].append([*([] if step == 1 else [moving[0]]), by[(-4, 3, 2, 1)[step - 1]]])
        if step < 4:
            plan[1].append([*([] if step == 1 else [moving[1]]), by[(-3, -2, -1)[step - 1]]])
    plan = [p for p in plan if p]
    if len(rings) == 1 and rings[0][2] == 1:
        sent = [p[0][0] for p in plan]
    else:
        parts = [part(v) for p in plan for terms in p for v in terms]

        def body(info, _, ins, __, outs, ___):
            found = iter(zip(parts, ins, strict=True))
            for out, p in zip(outs, plan, strict=True):
                column = 0
                for terms in p:
                    values = [piece.read(ref) for piece, ref in (next(found) for _ in terms)]
                    total = values[0]
                    if len(values) == 2:
                        total = (total.astype(f32) + values[1].astype(f32)).astype(bf16)
                    out[:, column : column + total.shape[1]] = total
                    column += total.shape[1]

        rows = rings[0][0][0].shape[0]
        wide = [sum(part(terms[0]).width for terms in p) for p in plan]
        shapes = [like((rows, w), bf16) for w in wide]
        sent = call(body, info, [], [p.array for p in parts], [], shapes, near=True)
    came = [lax.ppermute(v, "blk", way) for v, way in zip(sent, (forth, back), strict=False)]
    results, column = [], 0
    for k, (pieces, moving, step) in enumerate(rings):
        wide = pieces[0].shape[1]
        found = [Part(came[0], column, wide)]
        if step == 4:
            found.append(moving[1])
        else:
            before = sum(r[0][0].shape[1] for r in rings[:k] if r[2] < 4)
            found.append(Part(came[1], before, wide))
        results.append(found)
        column += wide
    return results


def reduce_terms(pieces, moving):
    if lax.axis_size("blk") != 8:
        everything = jnp.concatenate([p.astype(f32) for p in pieces], axis=0)
        return [lax.psum_scatter(everything, "blk", scatter_dimension=0, tiled=True)]
    return [pieces[0], *moving]


def dot(left, right, over=(1, 0)):
    return lax.dot_general(
        left, right, (((over[0],), (over[1],)), ((), ())), preferred_element_type=f32
    )


def dot_t(left, right):
    return dot(left, right, (1, 1))


def t_dot(left, right):
    return dot(left, right, (0, 0))


def norm_rows(values, gain):
    return values * lax.rsqrt(jnp.mean(values * values, axis=-1, keepdims=True) + EPS) * gain


def norm_back(values, gain, grad):
    inverse = lax.rsqrt(jnp.mean(values * values, axis=-1, keepdims=True) + EPS)
    unit = values * inverse
    weighted = grad * gain
    along = jnp.mean(weighted * unit, axis=-1, keepdims=True)
    return inverse * (weighted - unit * along), grad * unit


def gelu_both(values):
    root = math.sqrt(2.0 / math.pi)
    square = values * values
    bent = jnp.tanh(root * values * (1.0 + 0.044715 * square))
    half = 0.5 * (1.0 + bent)
    slope = half + 0.5 * values * (1.0 - bent * bent) * root * (1.0 + 3 * 0.044715 * square)
    return values * half, slope


def heads_in(width):
    return [slice(at, at + HDIM) for at in range(0, width, HDIM)]


def assemble(info, pieces, targets, signals, column_from=0):
    rows = pieces[0].shape[0]
    copies = []
    for t, piece in enumerate(pieces):
        at = pl.ds(pl.multiple_of(info[PLACES + t] * rows, 16), rows)
        column = column_from
        for k, target in enumerate(targets):
            wide = target.shape[1]
            copies.append(
                pltpu.make_async_copy(
                    piece.at[:, column : column + wide], target.at[at, :], signals.at[k, t]
                )
            )
            column += wide
    for copy in copies:
        copy.start()
    for copy in copies:
        copy.wait()


def hand_out(info, sources, pieces):
    rows = pieces[0].shape[0]
    for t, piece in enumerate(pieces):
        at = pl.ds(pl.multiple_of(info[PLACES + t] * rows, 16), rows)
        column = 0
        for source in sources:
            piece[:, column : column + source.shape[1]] = source[at, :].astype(piece.dtype)
            column += source.shape[1]


def token_rows(refs):
    return jnp.concatenate([r[0] for r in refs], axis=0)


def emit(partial, outs):
    part = outs[0].shape[1]
    for r, out in enumerate(outs):
        out[0] = partial[r * part : (r + 1) * part].astype(out.dtype)


def slots_used(info, b, part, slot):
    column = lax.broadcasted_iota(jnp.int32, (1, slot), 1)
    position = (lax.div(column, part) ^ info[HEAD]) * part + lax.rem(column, part)
    return position < info[LENGTHS + b]


def call(
    body, info, stepped, fixed, out_stepped, out_fixed, scratch=(), flops=0, steps=1, near=False, least=LARGE
):
    def by_step(shape):
        last = shape[0] - 1
        return pl.BlockSpec((1, *shape[1:]), lambda b: (jnp.minimum(b, last),) + (0,) * (len(shape) - 1))

    def whole(a):
        if isinstance(a, Far):
            return pl.BlockSpec(memory_space=pltpu.HBM)
        if isinstance(a, Rider):
            return pl.BlockSpec(a.shape, lambda b: (a.index, 0, 0))
        index = (0, a.index) if type(a) is Columns else (0,) * len(a.shape)
        return pl.BlockSpec(a.shape, lambda b: index)

    counts = [len(stepped), len(fixed), len(out_stepped), len(out_fixed), len(scratch)]
    stops = np.cumsum(counts)

    def split(info_ref, *refs):
        body(info_ref, *(refs[e - c : e] for c, e in zip(counts, stops, strict=True)))

    def large(a):
        return not near and math.prod(a.shape) * a.dtype.itemsize >= least

    def given(a):
        array = a.array if isinstance(a, (Columns, Far, Rider)) else a
        return pltpu.with_memory_space_constraint(array, pltpu.HBM) if large(a) else array

    def made(a):
        if isinstance(a, Later) or (large(a) and not isinstance(a, Near)):
            return pltpu.HBM(a.shape, a.dtype)
        return a.array if isinstance(a, Near) else a

    arrays = [*stepped, *fixed, *out_stepped, *out_fixed]
    moved = sum(math.prod(a.shape) * a.dtype.itemsize for a in arrays)
    return pl.pallas_call(
        split,
        grid=(steps,),
        in_specs=[
            pl.BlockSpec(memory_space=pltpu.SMEM),
            *(by_step(a.shape) for a in stepped),
            *(whole(a) for a in fixed),
        ],
        out_specs=[
            *(by_step(a.shape) for a in out_stepped),
            *(whole(a) for a in out_fixed),
        ],
        out_shape=[made(a) for a in (*out_stepped, *out_fixed)],
        scratch_shapes=list(scratch),
        compiler_params=pltpu.CompilerParams(
            dimension_semantics=("arbitrary",), vmem_limit_bytes=VMEM_LIMIT
        ),
        cost_estimate=pl.CostEstimate(
            flops=int(flops), bytes_accessed=int(moved), transcendentals=0
        ),
    )(info, *(given(a) for a in (*stepped, *fixed)))


class Columns:
    def __init__(self, array, width, index):
        self.array, self.index, self.dtype = array, index, array.dtype
        self.shape = (array.shape[0], width)


class Near(Columns):
    def __init__(self, array):
        self.array, self.shape, self.dtype = array, array.shape, array.dtype


class Later(Near):
    pass


class Rider:
    def __init__(self, array, index):
        self.array, self.index, self.dtype = array, index, array.dtype
        self.shape = (1, *array.shape[1:])


class Far:
    def __init__(self, array):
        self.array, self.shape, self.dtype = array, array.shape, array.dtype


def like(shape, dtype):
    return jax.ShapeDtypeStruct(tuple(shape), dtype)


def by_rows(fn, info, stepped, fixed, dtypes, gain=False, riders=None, kept=True):
    steps, _, width = stepped[0].shape
    count = 0 if riders is None else riders.shape[0] // RIDERS
    alone = [like(stepped[0].shape, d) for d in dtypes]
    outs = alone if riders is None or kept else alone[:-1]
    more = 0 if riders is None else riders.shape[0] // count
    together = [like((steps + count, *stepped[0].shape[1:]), dtypes[-1])] if more else []

    def body(info_ref, ins, whole, outs, sums, _):
        b = pl.program_id(0)
        if more:
            whole, rows = whole[:-1], whole[-1]

        @pl.when(b < steps)
        def _():
            results = fn(*(r[0].astype(f32) for r in ins), *(r[...] for r in whole))
            for out, value in zip(outs, results, strict=False):
                out[0] = value.astype(out.dtype)
            if more:
                outs[-1][0] = results[len(dtypes) - 1].astype(outs[-1].dtype)
            for total in sums:
                found = jnp.sum(results[-1], axis=0, keepdims=True)

                @pl.when(b == 0)
                def _():
                    total[...] = found

                @pl.when(b > 0)
                def _():
                    total[...] += found

        for k in range(count):

            @pl.when(b == steps + k)
            def _():
                outs[-1][0, :more, :] = rows[k * more : (k + 1) * more, :]

    return call(
        body,
        info,
        stepped,
        [*fixed, riders] if more else fixed,
        [*outs, *together],
        [like((1, width), f32)] * gain,
        flops=10 * math.prod(stepped[0].shape),
        steps=steps + count,
        near=True,
    )


def partial_rows(blocks, part, width):
    return [Near(like((blocks, part, width), d)) for d in (f32, bf16, f32, bf16)]


def piece_shapes(rows, columns):
    return [Later(like((rows, columns), d)) for d in (f32, *[bf16] * 7)]


def encoder_attention(info, normed, pieces):
    blocks, part, width = normed[0].shape
    slot = part * len(normed)
    size = pieces[0].shape[1] // 4
    count = size // HDIM

    def body(info, rows, pieces, outs, weights, scratch):
        qkv, probs, context = outs[:3]
        w_in, w_out = weights
        together, signals = scratch
        b = pl.program_id(0)

        @pl.when(b == 0)
        def _():
            assemble(info, pieces, (together,), signals)
            w_in[...] = together[:, : 3 * size]
            w_out[...] = together[:, 3 * size :]

        qkv[0] = dot(token_rows(rows), w_in[...]).astype(bf16)
        allowed = slots_used(info, b, part, slot)
        for k, at in enumerate(heads_in(size)):
            query, keys, vals = (qkv[0, :, j * size + at.start : j * size + at.stop] for j in range(3))
            scores = jnp.where(allowed, dot_t(query * SCALE, keys), masked_score)
            spread_out = jnp.exp(scores - jnp.max(scores, axis=-1, keepdims=True))
            inverse = 1.0 / jnp.sum(spread_out, axis=-1, keepdims=True)
            weight = (spread_out * inverse).astype(bf16)
            probs[0, k] = weight
            context[0, :, at] = dot(weight, vals).astype(bf16)
        emit(dot_t(context[0], w_out[...]), outs[3:])

    return call(
        body,
        info,
        normed,
        [Far(p) for p in pieces],
        [
            like((blocks, slot, 3 * size), bf16),
            like((blocks, count, slot, slot), bf16),
            like((blocks, slot, size), bf16),
            *partial_rows(blocks, part, width),
        ],
        [like((width, 3 * size), bf16), like((width, size), bf16)],
        [pltpu.VMEM((width, 4 * size), bf16), pltpu.SemaphoreType.DMA((1, len(pieces)))],
        flops=2 * blocks * slot * (width * size * 4 + 8 * slot * size),
        steps=blocks,
    )


def encoder_attention_back(info, grads, normed, qkv, probs, context, w_in, w_out, gains):
    blocks, part, width = normed[0].shape
    slot = part * len(normed)
    size = w_out.shape[1]

    def body(info, stepped, fixed, outs, ends, scratch):
        grad_refs, normed_refs = stepped[:4], stepped[4:8]
        qkv, probs, context = stepped[8:]
        w_in, w_out, gains = fixed
        pieces, gain_out = ends[:-1], ends[-1]
        total_in, total_out, moved = scratch
        b = pl.program_id(0)

        @pl.when(b == 0)
        def _():
            total_in[...] = jnp.zeros_like(total_in)
            total_out[...] = jnp.zeros_like(total_out)
            gain_out[...] = jnp.zeros_like(gain_out)

        grad = token_rows(grad_refs)
        rows = token_rows(normed_refs)
        dcontext = dot(grad, w_out[...]).astype(bf16)
        for k, at in enumerate(heads_in(size)):
            query, keys, vals = (qkv[0, :, j * size + at.start : j * size + at.stop] for j in range(3))
            weight = probs[0, k]
            dprobs = dot_t(dcontext[:, at], vals)
            wide = weight.astype(f32)
            dscores = wide * (dprobs - jnp.sum(wide * dprobs, axis=-1, keepdims=True))
            dscores = dscores.astype(bf16)
            terms = (
                dot(dscores, keys) * SCALE,
                t_dot(dscores, query) * SCALE,
                t_dot(weight, dcontext[:, at]),
            )
            for j, term in enumerate(terms):
                moved[:, j * size + at.start : j * size + at.stop] = term.astype(bf16)
        partial = dot_t(moved[...], w_in[...])
        emit(partial, outs)
        gain_out[...] += jnp.sum(partial * rows.astype(f32), axis=0, keepdims=True) / gains[0:1, :]
        total_in[...] += t_dot(rows, moved[...])
        total_out[...] += t_dot(grad, context[0])

        @pl.when(b == blocks - 1)
        def _():
            hand_out(info, (total_in, total_out), pieces)

    results = call(
        body,
        info,
        [*grads, *normed, qkv, probs, context],
        [w_in, w_out, gains],
        partial_rows(blocks, part, width),
        [*piece_shapes(width // 8, 4 * size), like((1, width), f32)],
        [
            pltpu.VMEM((width, 3 * size), f32),
            pltpu.VMEM((width, size), f32),
            pltpu.VMEM((slot, 3 * size), bf16),
        ],
        flops=2 * blocks * slot * (width * size * 8 + 20 * slot * size),
        steps=blocks,
    )
    return results[:4], results[4:12], results[12]


def encoder_ffn(info, normed, pieces, hidden):
    blocks, part, width = normed[0].shape
    slot = part * len(normed)

    def body(info, rows, pieces, outs, weights, scratch):
        active, slope = outs[:2]
        w_inner, w_outer = weights

        @pl.when(pl.program_id(0) == 0)
        def _():
            assemble(info, pieces, weights, scratch[0])

        value, bend = gelu_both(dot(token_rows(rows), w_inner[...]))
        active[0] = value.astype(bf16)
        slope[0] = bend.astype(bf16)
        emit(dot_t(active[0], w_outer[...]), outs[2:])

    return call(
        body,
        info,
        normed,
        [Far(p) for p in pieces],
        [*[like((blocks, slot, hidden), bf16)] * 2, *partial_rows(blocks, part, width)],
        [like((width, hidden), bf16)] * 2,
        [pltpu.SemaphoreType.DMA((2, len(pieces)))],
        flops=4 * blocks * slot * width * hidden,
        steps=blocks,
    )


def encoder_ffn_back(info, grads, slope, w_inner, w_outer):
    blocks, (_, part, width) = slope.shape[0], grads[0].shape
    slot = part * len(grads)
    hidden = w_inner.shape[1]

    def body(info, stepped, weights, outs, ends, _):
        dinner = outs[0]
        w_inner, w_outer = weights
        back = dot(token_rows(stepped[:4]), w_outer[...])
        dinner[0] = (back * stepped[4][0].astype(f32)).astype(bf16)
        emit(dot_t(dinner[0], w_inner[...]), outs[1:])

    return call(
        body,
        info,
        [*grads, slope],
        [w_inner, w_outer],
        [like((blocks, slot, hidden), bf16), *partial_rows(blocks, part, width)],
        [],
        flops=4 * blocks * slot * width * hidden,
        steps=blocks,
    )


def weight_grads(info, pairs, more=(), cut=True):
    blocks, (_, part, width) = pairs[0][1].shape[0], pairs[0][0][0].shape
    widths = [right.shape[2] for _, right in pairs]

    def body(info, stepped, more, __, ends, totals):
        b = pl.program_id(0)
        totals = totals if cut else ends
        for k, total in enumerate(totals):
            left, right = stepped[5 * k : 5 * k + 4], stepped[5 * k + 4]
            found = t_dot(token_rows(left), right[0])

            @pl.when(b == 0)
            def _():
                total[...] = found

            @pl.when(b > 0)
            def _():
                total[...] += found

        if cut:

            @pl.when(b == blocks - 1)
            def _():
                hand_out(info, (*totals, *more), ends)

    return call(
        body,
        info,
        [a for left, right in pairs for a in (*left, right)],
        more,
        [],
        piece_shapes(width // 8, sum(widths) + sum(m.shape[1] for m in more))
        if cut
        else [like((width, w), f32) for w in widths],
        [pltpu.VMEM((width, w), f32) for w in widths] if cut else [],
        flops=2 * blocks * part * 4 * width * sum(widths),
        steps=blocks,
    )


def finish(info, terms, widths, turned):
    terms = [part(t) for t in terms]
    rows = terms[0].array.shape[0]
    shapes = [(w, rows) if t else (rows, w) for w, t in zip(widths, turned, strict=True)]

    def body(info, _, ins, __, outs, ___):
        total = terms[0].read(ins[0])
        for term, ref in zip(terms[1:], ins[1:], strict=True):
            total = total + term.read(ref).astype(f32)
        column = 0
        for out, wide, turn in zip(outs, widths, turned, strict=True):
            found = total[:, column : column + wide]
            out[...] = found.T if turn else found
            column += wide

    return call(body, info, [], [t.array for t in terms], [], [like(s, f32) for s in shapes])


def cross_forward(info, states, pieces, column_from, queries, own_question, count_q, count_pass):
    blocks = count_q * count_pass
    _, part, width = states[0].shape
    slot = part * len(states)
    size = queries.shape[1]
    rows_dec = queries.shape[0]

    def body(info, rows, fixed, outs, ends, scratch):
        pieces, queries, question = fixed[:-2], fixed[-2], fixed[-1]
        stats, weight = ends
        held, signals = scratch
        b = pl.program_id(0)

        @pl.when(b == 0)
        def _():
            assemble(info, pieces, (weight,), signals, column_from)

        made = dot(token_rows(rows), weight[...]).astype(bf16)
        outs[0][0] = made
        held[pl.ds(pl.multiple_of(b * slot, slot), slot), :] = made

        @pl.when(b == blocks - 1)
        def _():
            allowed = jnp.concatenate(
                [
                    slots_used(info, k, part, slot) & (question[...] == k // count_pass)
                    for k in range(blocks)
                ],
                axis=1,
            )
            lane = lax.broadcasted_iota(jnp.int32, (rows_dec, HDIM), 1)
            for k, at in enumerate(heads_in(size)):
                scores = dot_t(queries[:, at], held[:, at]) * SCALE
                scores = jnp.where(allowed, scores, masked_score)
                top = jnp.max(scores, axis=-1, keepdims=True)
                spread_out = jnp.exp(scores - top)
                total = jnp.sum(spread_out, axis=-1, keepdims=True)
                vals = held[:, size + at.start : size + at.stop]
                stats[:, k * LANES : k * LANES + HDIM] = dot(spread_out.astype(bf16), vals)
                stats[:, k * LANES + HDIM : (k + 1) * LANES] = jnp.where(lane == 0, top, total)

    return call(
        body,
        info,
        states,
        [*(Far(p) for p in pieces), queries, own_question],
        [like((blocks, slot, 2 * size), bf16)],
        [like((rows_dec, size // HDIM * LANES), f32), like((width, 2 * size), bf16)],
        [
            pltpu.VMEM((blocks * slot, 2 * size), bf16),
            pltpu.SemaphoreType.DMA((1, len(pieces))),
        ],
        flops=4 * blocks * slot * width * size,
        steps=blocks,
    )


def merged(first, second):
    lane = lax.broadcasted_iota(jnp.int32, (first.shape[0], HDIM), 1)
    found = []
    for at in range(0, first.shape[1], LANES):
        tops = [v[:, at + HDIM : at + HDIM + 1] for v in (first, second)]
        totals = [v[:, at + HDIM + 1 : at + HDIM + 2] for v in (first, second)]
        top = jnp.maximum(*tops)
        scales = [jnp.exp(t - top) for t in tops]
        total = totals[0] * scales[0] + totals[1] * scales[1]
        found.append(first[:, at : at + HDIM] * scales[0] + second[:, at : at + HDIM] * scales[1])
        found.append(jnp.where(lane == 0, top, total))
    return jnp.concatenate(found, axis=1)


def in_order(info, bits, own, other):
    later = (info[BLK] & bits) != 0
    return jnp.where(later, other, own), jnp.where(later, own, other)


def merge(info, own, other, bits):
    def body(info, _, ins, __, outs, ___):
        outs[0][...] = merged(*in_order(info, bits, ins[0][...], ins[1][...]))

    return call(body, info, [], [own, other], [], [like(own.shape, f32)])[0]


def cross_out(info, stats, bits, w_output):
    rows, columns = stats[0].shape
    size = columns // LANES * HDIM
    width = w_output.shape[0]

    def body(info, _, ins, __, outs, scratch):
        w_output = ins[-1]
        out, log_total, context, own, sent = outs
        values = [r[...] for r in ins[:-1]]
        near = merged(*in_order(info, bits[0], *values[:2]))
        far = merged(*in_order(info, bits[0], *values[2:]))
        stats = merged(*in_order(info, bits[1], near, far))
        log_total[...] = jnp.zeros_like(log_total)
        for k, at in enumerate(heads_in(size)):
            base = k * LANES
            top = stats[:, base + HDIM : base + HDIM + 1]
            total = stats[:, base + HDIM + 1 : base + HDIM + 2]
            out[:, at] = stats[:, base : base + HDIM] / total
            log_total[:, k : k + 1] = top + jnp.log(total)
        context[...] = out[...].astype(bf16)
        own[...] = dot_t(context[...], w_output[...])
        sent[...] = own[...].astype(bf16)

    return call(
        body,
        info,
        [],
        [*stats, w_output],
        [],
        [
            like((rows, size), f32),
            like((rows, LANES), f32),
            Later(like((rows, size), bf16)),
            like((rows, width), f32),
            like((rows, width), bf16),
        ],
        flops=2 * rows * size * width,
    )


def cross_back(info, key_vals, inputs, own_question, count_pass, slot, part):
    cotangent, after_cross, terms, gains, w_output, out, log_total, queries, weight = inputs
    blocks = key_vals.shape[0]
    rows_dec, width = after_cross.shape
    size = queries.shape[1]

    def body(info, stepped, fixed, outs, ends, scratch):
        cotangent, after_cross, own, r1, r2, r3, gains, w_output, out, log_total, queries, weight, question = fixed
        key_vals = stepped[0]
        dkey_vals = outs[0]
        dcross, dcross_low, gain_out, dqueries = ends
        dcontext, row_terms = scratch
        b = pl.program_id(0)

        @pl.when(b == 0)
        def _():
            total = own[...] + r1[...].astype(f32) + r2[...].astype(f32) + r3[...].astype(f32)
            back, gain_rows = norm_back(after_cross[...], gains[2:3, :], total)
            dcross[...] = cotangent[...].astype(f32) + back
            dcross_low[...] = dcross[...].astype(bf16)
            gain_out[...] = gain_rows
            dcontext[...] = dot(dcross_low[...], w_output[...]).astype(bf16)
            for k, at in enumerate(heads_in(size)):
                row_terms[:, k : k + 1] = jnp.sum(
                    dcontext[:, at].astype(f32) * out[:, at], axis=-1, keepdims=True
                )
            dqueries[...] = jnp.zeros_like(dqueries)

        allowed = slots_used(info, b, part, slot) & (question[...] == lax.div(b, count_pass))
        for k, at in enumerate(heads_in(size)):
            keys, vals = key_vals[0, :, at], key_vals[0, :, size + at.start : size + at.stop]
            scores = dot_t(queries[:, at], keys) * SCALE
            scores = jnp.where(allowed, scores, masked_score)
            probs = jnp.exp(scores - log_total[:, k : k + 1])
            dprobs = dot_t(dcontext[:, at], vals)
            dscores = (probs * (dprobs - row_terms[:, k : k + 1])).astype(bf16)
            dqueries[:, at] += dot(dscores, keys) * SCALE
            dkey_vals[0, :, at] = (t_dot(dscores, queries[:, at]) * SCALE).astype(bf16)
            dkey_vals[0, :, size + at.start : size + at.stop] = t_dot(
                probs.astype(bf16), dcontext[:, at]
            ).astype(bf16)
        emit(dot_t(dkey_vals[0], weight[...]), outs[1:])

    return call(
        body,
        info,
        [key_vals],
        [cotangent, after_cross, *terms, gains, w_output, out, log_total, queries, weight, own_question],
        [like(key_vals.shape, bf16), *partial_rows(blocks, part, width)],
        [
            Later(like((rows_dec, width), f32)),
            Later(like((rows_dec, width), bf16)),
            Later(like((rows_dec, width), f32)),
            like((rows_dec, size), f32),
        ],
        [pltpu.VMEM((rows_dec, size), bf16), pltpu.VMEM((rows_dec, LANES), f32)],
        flops=4 * blocks * slot * width * size,
        steps=blocks,
    )


def summed(refs):
    count = refs[0].shape[0]

    def rows(ref):
        return ref[...] if len(ref.shape) == 2 else ref[0, : min(count, RIDERS), :]

    terms = [rows(ref).astype(f32) for ref in refs[1:]]
    each = len(terms) // 3
    if each == 2:
        terms = [jnp.concatenate(terms[k : k + 2], axis=0) for k in (0, 2, 4)]
    total = refs[0][...]
    for term in terms:
        total = total + term
    return total


def decoder_self(info, rows, gains, pieces, column_from, size, order):
    count, width = rows.shape

    def body(info, _, ins, __, outs, scratch):
        rows, gains, order_q, order_k = ins[:4]
        normed, qkv, probs, context, own, sent, weight = outs
        assemble(info, ins[4:], (weight,), scratch[0], column_from)
        normed[...] = norm_rows(rows[...].astype(f32), gains[0:1, :]).astype(bf16)
        qkv[...] = dot(normed[...], weight[:, : 3 * size]).astype(bf16)
        query_at, key_at = order_q[...], order_k[...]
        same = lax.div(query_at, 1000) == lax.div(key_at, 1000)
        allowed = same & (key_at <= query_at) & (key_at >= 0) & (query_at >= 0)
        for k, at in enumerate(heads_in(size)):
            query, keys, vals = (qkv[:, j * size + at.start : j * size + at.stop] for j in range(3))
            scores = jnp.where(allowed, dot_t(query, keys) * SCALE, masked_score)
            spread_out = jnp.exp(scores - jnp.max(scores, axis=-1, keepdims=True))
            share_out = spread_out / jnp.sum(spread_out, axis=-1, keepdims=True)
            share_out = jnp.where(allowed, share_out, 0.0)
            probs[k] = share_out
            context[:, at] = dot(share_out.astype(bf16), vals).astype(bf16)
        own[...] = dot_t(context[...], weight[:, 3 * size :])
        sent[...] = own[...].astype(bf16)

    return call(
        body,
        info,
        [],
        [rows, gains, *order, *(Far(p) for p in pieces)],
        [],
        [
            Later(like((count, width), bf16)),
            Later(like((count, 3 * size), bf16)),
            Later(like((size // HDIM, count, count), f32)),
            Later(like((count, size), bf16)),
            like((count, width), f32),
            like((count, width), bf16),
            Later(like((width, 4 * size), bf16)),
        ],
        [pltpu.SemaphoreType.DMA((1, len(pieces)))],
        flops=2 * count * width * size * 4,
    )


def decoder_queries(info, rows, terms, gains, pieces, column_from, size):
    count, width = rows.shape

    def body(info, _, ins, __, outs, scratch):
        rows, own, r1, r2, r3, gains = ins[:6]
        after_self, normed, queries, w_query, w_output = outs
        weight, signals = scratch
        assemble(info, ins[6:], (weight,), signals, column_from)
        w_query[...] = weight[:, :size]
        w_output[...] = weight[:, size:]
        after_self[...] = rows[...].astype(f32) + summed((own, r1, r2, r3))
        normed[...] = norm_rows(after_self[...], gains[1:2, :]).astype(bf16)
        queries[...] = dot(normed[...], w_query[...]).astype(bf16)

    return call(
        body,
        info,
        [],
        [rows, *terms, gains, *(Far(p) for p in pieces)],
        [],
        [
            like((count, width), f32),
            Later(like((count, width), bf16)),
            like((count, size), bf16),
            Later(like((width, size), bf16)),
            like((width, size), bf16),
        ],
        [pltpu.VMEM((width, 2 * size), bf16), pltpu.SemaphoreType.DMA((1, len(pieces)))],
        flops=2 * count * width * size,
    )


def decoder_back(info, cotangent, pieces):
    count, width = cotangent.shape
    hidden = pieces[0].shape[1] // 2

    def body(info, _, ins, __, outs, scratch):
        w_inner, w_outer, back = outs
        assemble(info, ins[1:], (w_inner, w_outer), scratch[0])
        back[...] = dot(ins[0][...], w_outer[...])

    return call(
        body,
        info,
        [],
        [cotangent, *(Far(p) for p in pieces)],
        [],
        [*[like((width, hidden), bf16)] * 2, like((count, hidden), f32)],
        [pltpu.SemaphoreType.DMA((2, len(pieces)))],
        flops=2 * count * width * hidden,
    )


def decoder_ffn(info, after_self, terms, back, gains, w_inner):
    count, width = after_self.shape
    hidden = w_inner.shape[1]

    def body(info, _, ins, __, outs, scratch):
        after_self, own, r1, r2, r3, back, gains, w_inner = ins
        after_cross, normed, active, dinner, own_back, sent_back = outs
        after_cross[...] = after_self[...] + summed((own, r1, r2, r3))
        normed[...] = norm_rows(after_cross[...], gains[2:3, :]).astype(bf16)
        value, slope = gelu_both(dot(normed[...], w_inner[...]))
        active[...] = value.astype(bf16)
        dinner[...] = (slope * back[...]).astype(bf16)
        own_back[...] = dot_t(dinner[...], w_inner[...])
        sent_back[...] = own_back[...].astype(bf16)

    return call(
        body,
        info,
        [],
        [after_self, *terms, back, gains, w_inner],
        [],
        [
            like((count, width), f32),
            Later(like((count, width), bf16)),
            Later(like((count, hidden), bf16)),
            Later(like((count, hidden), bf16)),
            like((count, width), f32),
            like((count, width), bf16),
        ],
        flops=4 * count * width * hidden,
    )


def query_back(info, terms, weight):
    (count, size), width = terms[0].shape, weight.shape[0]

    def body(info, _, ins, __, outs, scratch):
        low, own, sent = outs
        low[...] = ((ins[0][...] + ins[1][...]) + (ins[2][...] + ins[3][...])).astype(bf16)
        own[...] = dot_t(low[...], ins[4][...])
        sent[...] = own[...].astype(bf16)

    return call(
        body,
        info,
        [],
        [*terms, weight],
        [],
        [
            Later(like((count, size), bf16)),
            like((count, width), f32),
            like((count, width), bf16),
        ],
        flops=2 * count * width * size,
    )


def decoder_self_back(
    info, dcross, after_self, terms, gains, weight, qkv, probs, active, w_outer
):
    count, width = after_self.shape
    size = weight.shape[1] // 4

    def body(info, _, ins, __, outs, scratch):
        dcross, after_self, *terms, gains, weight, qkv, probs, active, w_outer = ins
        dself, dself_low, gain_rows, moved, own_back, sent_back = outs
        back, gain_rows[...] = norm_back(after_self[...], gains[1:2, :], summed(terms))
        dself[...] = dcross[...] + back
        dself_low[...] = dself[...].astype(bf16)
        dcontext = dot(dself_low[...], weight[:, 3 * size :]).astype(bf16)
        for k, at in enumerate(heads_in(size)):
            query, keys, vals = (qkv[:, j * size + at.start : j * size + at.stop] for j in range(3))
            share_out = probs[k]
            dprobs = dot_t(dcontext[:, at], vals)
            dscores = share_out * (dprobs - jnp.sum(share_out * dprobs, axis=-1, keepdims=True))
            dscores = dscores.astype(bf16)
            found = (
                dot(dscores, keys) * SCALE,
                t_dot(dscores, query) * SCALE,
                t_dot(share_out.astype(bf16), dcontext[:, at]),
            )
            for j, term in enumerate(found):
                moved[:, j * size + at.start : j * size + at.stop] = term.astype(bf16)
        own_back[:count, :] = dot_t(moved[...], weight[:, : 3 * size])
        own_back[count:, :] = dot_t(active[...], w_outer[...])
        sent_back[...] = own_back[...].astype(bf16)

    return call(
        body,
        info,
        [],
        [dcross, after_self, *terms, gains, weight, qkv, probs, active, w_outer],
        [],
        [
            like((count, width), f32),
            Later(like((count, width), bf16)),
            like((count, width), f32),
            Later(like((count, 3 * size), bf16)),
            like((2 * count, width), f32),
            like((2 * count, width), bf16),
        ],
        flops=2 * count * width * size * 8,
    )


def decoder_ends(info, rows, dself, terms, gains, after_cross, gain_rows, gain_sums, dec_own):
    count, width = dself.shape

    def body(info, _, ins, __, outs, scratch):
        rows, dself, after_cross, gains = ins[:4]
        three, four, zero, one = ins[-4:]
        grad, states, found = outs
        total = summed(ins[4:-4])
        back, two = norm_back(rows[...].astype(f32), gains[0:1, :], total[:count])
        grad[...] = dself[...] + back
        states[...] = (after_cross[...] + total[count:]).astype(bf16)
        row = lax.div(lax.broadcasted_iota(jnp.int32, (count, 1), 0), dec_own)
        mine = (row == info[HEAD]) & (info[BLK] == 0)
        found[0:1, :] = zero[...]
        found[1:2, :] = one[...]
        for k, values in enumerate((two, three[...], four[...])):
            found[2 + k : 3 + k, :] = jnp.sum(jnp.where(mine, values, 0.0), axis=0, keepdims=True)

    return call(
        body,
        info,
        [],
        [rows, dself, after_cross, gains, *terms, *gain_rows, *gain_sums],
        [],
        [like((count, width), f32), like((count, width), bf16), like((5, width), f32)],
    )


def decoder_weight_grads(info, own, pairs_in, pairs_out):
    count, width = pairs_in[0][0].shape

    def body(info, _, ins, __, outs, scratch):
        row = lax.broadcasted_iota(jnp.int32, (own, width), 0) + info[BLK] * own
        column = lax.broadcasted_iota(jnp.int32, (own, width), 1)
        pick = jnp.where(row == column, 1.0, 0.0).astype(bf16)
        outs, ins = iter(outs), iter(ins)
        for _, _, arrays in pairs_in:
            left, right = next(ins)[...], next(ins)[...]
            found = t_dot(dot_t(left, pick).astype(bf16), right)
            wide = found.shape[1] // arrays
            for k in range(arrays):
                next(outs)[...] = found[:, k * wide : (k + 1) * wide]
        for _ in pairs_out:
            left, right = next(ins)[...], next(ins)[...]
            next(outs)[...] = t_dot(left, dot_t(right, pick).astype(bf16))

    outs = [like((own, r.shape[1] // n), f32) for _, r, n in pairs_in for _ in range(n)]
    outs += [like((l.shape[1], own), f32) for l, _ in pairs_out]
    flat = [a for pair in pairs_in for a in pair[:2]] + [a for pair in pairs_out for a in pair]
    return call(body, info, [], flat, [], outs, flops=2 * count * own * width * 10, least=0)


def shards(
    encoder_input,
    passage_lengths,
    decoder_input,
    encoder_query,
    encoder_key,
    encoder_value,
    encoder_output,
    encoder_inner,
    encoder_outer,
    decoder_query,
    decoder_key,
    decoder_value,
    decoder_output,
    cross_query,
    cross_key,
    cross_value,
    cross_output,
    decoder_inner,
    decoder_outer,
    encoder_gains,
    decoder_gains,
    encoder_cotangent,
    decoder_cotangent,
):
    head, blk = lax.axis_index("head"), lax.axis_index("blk")
    blk_count, head_count = lax.axis_size("blk"), lax.axis_size("head")
    count_q, count_pass, part, width = encoder_input.shape
    blocks = count_q * count_pass
    slot = part * head_count
    own = width // blk_count
    if blk_count == 8:
        places = jnp.asarray(place_table(8))[blk]
    else:
        places = jnp.arange(8, dtype=jnp.int32)
    info = jnp.concatenate(
        [places, jnp.stack([head, blk]).astype(jnp.int32), passage_lengths.reshape(blocks)]
    )

    size, units = encoder_query.shape[1], encoder_inner.shape[1]
    inputs = encoder_input.reshape(blocks, part, width)
    dec_part = decoder_input.shape[1]
    dec_own = count_q * dec_part
    dec_rows = dec_own * head_count
    filled = -(-dec_rows // 16) * 16

    attention = jnp.concatenate(
        [encoder_query, encoder_key, encoder_value, encoder_output.T], axis=1
    )
    attention, inputs = sync(attention, inputs)
    attention = fetch_step(fetch_start(attention), -1, 1)
    first = by_rows(
        lambda x, g: (norm_rows(x, g[0:1]),), info, [inputs], [encoder_gains], [bf16]
    )[0]
    attention, first = sync(attention, first)

    attention = fetch_step(attention, -2, 2)
    first_all = [first, swap(first, "head", 1), swap(first, "head", 2)]
    ffn = jnp.concatenate(
        [
            encoder_inner,
            encoder_outer.T,
            decoder_query,
            decoder_key,
            decoder_value,
            decoder_output.T,
            cross_key,
            cross_value,
            cross_query,
            cross_output.T,
        ],
        axis=1,
    )
    at_self, at_cross = 2 * units, 2 * units + 4 * size
    attention, first_all, ffn = sync(attention, first_all, ffn)

    attention = fetch_step(attention, -3, 3)
    first_all.append(swap(first_all[2], "head", 1))
    pair = jnp.stack([decoder_input, decoder_cotangent]).reshape(2, dec_own, width)
    both = lax.all_gather(pair, "head", axis=1, tiled=True)
    both = jnp.pad(both, ((0, 0), (0, filled - dec_rows), (0, 0)))
    attention, first_all, ffn, both = sync(attention, first_all, ffn, both)

    attention, ffn = fetch_step(attention, -4), fetch_step(fetch_start(ffn), 1)
    dec_ffn = jnp.concatenate([decoder_inner, decoder_outer.T], axis=1)
    attention, ffn, first_all, dec_ffn = sync(attention, ffn, first_all, dec_ffn)

    ffn = fetch_step(ffn, -1, 2)
    qkv, probs, context, *partial, w_in, w_out = encoder_attention(
        info, first_all, in_turn(attention)
    )
    partial, ffn = sync(partial, ffn)

    def to_core(partial):
        return [swap(partial[1], "head", 1), swap(partial[3], "head", 1)]

    def to_chip(partial, beside):
        return swap((partial[2] + beside[1].astype(f32)).astype(bf16), "head", 2)

    beside = to_core(partial)
    partial, beside, ffn = sync(partial, beside, ffn)
    across = to_chip(partial, beside)
    ffn = fetch_step(ffn, -2, 3)
    partial, beside, across, ffn = sync(partial, beside, across, ffn)

    def enter_ffn(x, a, b, c, g):
        hidden = x + a + b + c
        return hidden, norm_rows(hidden, g[1:2])

    hidden, second = by_rows(
        enter_ffn, info, [inputs, partial[0], beside[0], across], [encoder_gains], [f32, bf16]
    )
    def spread(rows):
        return [rows, swap(rows, "head", 1), swap(rows, "head", 2)]

    def riders(all_rows, count=1):
        return [Rider(rows, blocks + k) for rows in all_rows[1:] for k in range(count)]

    second, ffn, dec_ffn = sync(second, ffn, dec_ffn)
    second_all = spread(second)
    ffn = fetch_step(ffn, -3, 4)
    second_all, ffn = sync(second_all, ffn)
    second_all.append(swap(second_all[2], "head", 1))
    second_all, ffn, dec_ffn = sync(second_all, ffn, dec_ffn)
    ffn = in_turn(ffn)

    dec_ffn = fetch_step(fetch_start(dec_ffn), -1, 1)
    active, slope, *partial, w_inner, w_outer = encoder_ffn(info, second_all, ffn, units)
    partial, dec_ffn = sync(partial, dec_ffn)
    beside = to_core(partial)
    partial, beside, both, dec_ffn = sync(partial, beside, both, dec_ffn)
    dec_in, cotangent = both[0], both[1]

    index = np.arange(filled)
    question = (index % dec_own) // dec_part
    position = index // dec_own * dec_part + index % dec_part
    order = np.where(index < dec_rows, question * 1000 + position, -1).astype(np.int32)
    order = (jnp.asarray(order[:, None]), jnp.asarray(order[None, :]))
    question = jnp.asarray(question[:, None].astype(np.int32))

    across = to_chip(partial, beside)
    dec_ffn = fetch_step(dec_ffn, -2, 2)
    third, dec_qkv, dec_probs, dec_context, mine, sent, w_self = decoder_self(
        info, dec_in, decoder_gains, ffn, at_self, size, order
    )
    partial, beside, across, mine, sent, dec_ffn = sync(
        partial, beside, across, mine, sent, dec_ffn
    )
    states, states_sent = by_rows(
        lambda h, a, b, c: (h + a + b + c,),
        info,
        [hidden, partial[0], beside[0], across],
        [],
        [bf16],
        riders=sent,
    )
    states_sent, dec_ffn = sync(states_sent, dec_ffn)
    states_all = spread(states_sent)
    dec_ffn = fetch_step(dec_ffn, -3, 3)
    states_all, dec_ffn = sync(states_all, dec_ffn)
    states_all.append(swap(states_all[2], "head", 1))
    states_all, dec_ffn = sync(states_all, dec_ffn)
    after_self, fourth, queries, w_cross_query, w_cross_output = decoder_queries(
        info,
        dec_in,
        [mine, *riders(states_all)],
        decoder_gains,
        ffn,
        at_cross + 2 * size,
        size,
    )

    dec_ffn = fetch_step(dec_ffn, -4)
    key_vals, stats, w_cross = cross_forward(
        info, states_all, ffn, at_cross, queries, question, count_q, count_pass
    )
    bits = [1 << k for k in range((blk_count - 1).bit_length())]
    last_two = (bits[-2], bits[-1], bits[-2] + bits[-1])
    for k in bits[:-2]:
        stats = merge(info, stats, swap(stats, "blk", k), k)
    stats, dec_ffn = sync(stats, dec_ffn)
    stats_all = [stats, *(swap(stats, "blk", k) for k in last_two)]
    w_dec_inner, w_dec_outer, outer_back = decoder_back(info, cotangent, in_turn(dec_ffn))
    stats_all, outer_back = sync(stats_all, outer_back)
    out, log_total, cross_context, mine, sent = cross_out(
        info, stats_all, bits[-2:], w_cross_output
    )
    after_cross, fifth, dec_active, dec_dinner, mine, sent = decoder_ffn(
        info, after_self, [mine, *share(sent)], outer_back, decoder_gains, w_dec_inner
    )
    dkey_vals, *rest = cross_back(
        info,
        key_vals,
        (
            cotangent,
            after_cross,
            [mine, *share(sent)],
            decoder_gains,
            w_cross_output,
            out,
            log_total,
            queries,
            w_cross,
        ),
        question,
        count_pass,
        slot,
        part,
    )
    partial, (dcross, dcross_low, gain_four, dqueries) = rest[:4], rest[4:]

    def some(value, which):
        for k in which:
            value = value + swap(value, "blk", k)
        return value

    partial, dqueries, dkey_vals = sync(partial, dqueries, dkey_vals)
    beside = to_core(partial)
    dqueries = some(dqueries, bits[:-2])
    partial, beside, dkey_vals, dqueries = sync(partial, beside, dkey_vals, dqueries)
    across = to_chip(partial, beside)
    terms = [dqueries, *(swap(dqueries, "blk", k) for k in last_two)]
    cross_sum = weight_grads(info, [(states_all, dkey_vals)], cut=False)[0]
    partial, beside, across, cross_sum, terms = sync(partial, beside, across, cross_sum, terms)

    def enter_back(cot, a, b, c):
        grad = cot + a + b + c
        return grad, grad

    dqueries, mine, sent = query_back(info, terms, w_cross_query)
    dstates, dstates_low = by_rows(
        enter_back,
        info,
        [encoder_cotangent.reshape(blocks, part, width), partial[0], beside[0], across],
        [],
        [f32, bf16],
        riders=sent,
        kept=False,
    )
    dstates_low, cross_sum = sync(dstates_low, cross_sum)
    dstates_all = spread(dstates_low)
    dstates_all = sync(*dstates_all)
    dstates_all = sync(*dstates_all, swap(dstates_all[2], "head", 1))
    dinner, *partial = encoder_ffn_back(info, dstates_all, slope, w_inner, w_outer)
    partial, dinner = sync(partial, dinner)
    beside = to_core(partial)
    partial, beside, dinner, dstates_all = sync(partial, beside, dinner, dstates_all)
    across = to_chip(partial, beside)
    dself, dself_low, gain_three, dself_qkv, own_back, sent_back = decoder_self_back(
        info,
        dcross,
        after_self,
        [mine, *riders(dstates_all)],
        decoder_gains,
        w_self,
        dec_qkv,
        dec_probs,
        dec_active,
        w_dec_outer,
    )
    ffn_sums = weight_grads(
        info, [(second_all, dinner), (dstates_all, active)], [cross_sum]
    )
    partial, beside, across, ffn_sums, sent_back = sync(
        partial, beside, across, ffn_sums, sent_back
    )

    def middle_back(dy, h, a, b, c, g):
        back, gain_rows = norm_back(h, g[1:2], a + b + c)
        grad = dy + back
        return grad, grad, gain_rows

    dhidden, dhidden_low, gain_one = by_rows(
        middle_back,
        info,
        [dstates, hidden, partial[0], beside[0], across],
        [encoder_gains],
        [f32, bf16],
        gain=True,
        riders=sent_back,
        kept=False,
    )
    dhidden_low, ffn_sums = sync(dhidden_low, ffn_sums)
    dhidden_all = spread(dhidden_low)
    ffn_moving = reduce_step(info, (ffn_sums, None, 1))[0]
    dhidden_all, ffn_moving = sync(dhidden_all, ffn_moving)
    dhidden_all.append(swap(dhidden_all[2], "head", 1))
    dhidden_all, ffn_moving = sync(dhidden_all, ffn_moving)
    terms = [own_back, *riders(dhidden_all, 2)]

    ffn_moving = reduce_step(info, (ffn_sums, ffn_moving, 2))[0]
    partial, sums, gain_zero = encoder_attention_back(
        info, dhidden_all, first_all, qkv, probs, context, w_in, w_out, encoder_gains
    )
    partial, sums, ffn_moving, gain_zero = sync(partial, sums, ffn_moving, gain_zero)
    ffn_moving, moving = reduce_step(info, (ffn_sums, ffn_moving, 3), (sums, None, 1))
    beside = to_core(partial)
    dec_grad, dec_states, gains = decoder_ends(
        info,
        dec_in,
        dself,
        terms,
        decoder_gains,
        after_cross,
        [gain_three, gain_four],
        [gain_zero, gain_one],
        dec_own,
    )
    gains = gains + swap(gains, "head", 1)
    (
        grad_dec_query,
        grad_dec_key,
        grad_dec_value,
        grad_cross_query,
        grad_dec_inner,
        grad_dec_outer,
        grad_dec_output,
        grad_cross_output,
    ) = decoder_weight_grads(
        info,
        own,
        [
            (third, dself_qkv, 3),
            (fourth, dqueries, 1),
            (fifth, dec_dinner, 1),
            (cotangent, dec_active, 1),
        ],
        [(dec_context, dself_low), (cross_context, dcross_low)],
    )
    partial, beside, moving, gains, ffn_moving, grad_dec_query = sync(
        partial, beside, moving, gains, ffn_moving, grad_dec_query
    )

    def own_rows(values):
        return lax.dynamic_slice_in_dim(values, head * dec_own, dec_own, 0)

    ffn_moving, moving = reduce_step(info, (ffn_sums, ffn_moving, 4), (sums, moving, 2))
    across = to_chip(partial, beside)
    gains = gains + swap(gains, "head", 2)
    gains = some(gains, bits[:1])
    dec_states, dec_grad = own_rows(dec_states), own_rows(dec_grad)
    partial, beside, across, moving, gains, ffn_moving, dec_states, dec_grad = sync(
        partial, beside, across, moving, gains, ffn_moving, dec_states, dec_grad
    )

    def last_back(dh, x, a, b, c, g):
        return (dh + norm_back(x, g[0:1], a + b + c)[0],)

    moving = reduce_step(info, (sums, moving, 3))[0]
    gains = some(gains, bits[1:-1])
    input_grad = by_rows(
        last_back,
        info,
        [dhidden, inputs, partial[0], beside[0], across],
        [encoder_gains],
        [f32],
    )[0]
    grad_inner, grad_outer, grad_cross_key, grad_cross_value = finish(
        info,
        reduce_terms(ffn_sums, ffn_moving),
        (units, units, size, size),
        (False,) * 4,
    )
    moving, gains, input_grad, grad_inner = sync(moving, gains, input_grad, grad_inner)
    moving = reduce_step(info, (sums, moving, 4))[0]
    last = swap(gains, "blk", bits[-1])
    enc_gain_grads, dec_gain_grads = gains[:2] + last[:2], gains[2:] + last[2:]
    grad_query, grad_key, grad_value, grad_output = finish(
        info, reduce_terms(sums, moving), (size,) * 4, (False, False, False, True)
    )

    def dec_shape(values):
        return values.reshape(count_q, dec_part, width)

    return (
        states.reshape(encoder_input.shape),
        dec_shape(dec_states),
        input_grad.reshape(encoder_input.shape),
        dec_shape(dec_grad),
        grad_query,
        grad_key,
        grad_value,
        grad_output,
        grad_inner,
        grad_outer.T,
        grad_dec_query,
        grad_dec_key,
        grad_dec_value,
        grad_dec_output,
        grad_cross_query,
        grad_cross_key,
        grad_cross_value,
        grad_cross_output,
        grad_dec_inner,
        grad_dec_outer.T,
        enc_gain_grads,
        dec_gain_grads,
    )


def solution(mesh):
    placed = (
        P(None, "blk", "head", None),
        P(None, "blk"),
        P(None, "head", None),
        P("blk", "head"),
        P("blk", "head"),
        P("blk", "head"),
        P("head", "blk"),
        P("blk", "head"),
        P("head", "blk"),
        P("blk", "head"),
        P("blk", "head"),
        P("blk", "head"),
        P("head", "blk"),
        P("blk", "head"),
        P("blk", "head"),
        P("blk", "head"),
        P("head", "blk"),
        P("blk", "head"),
        P("head", "blk"),
        P(),
        P(),
        P(None, "blk", "head", None),
        P(None, "head", None),
    )
    return jax.shard_map(
        shards,
        mesh=mesh,
        in_specs=placed,
        out_specs=(placed[0], placed[2], placed[0], placed[2], *placed[3:19], P(), P()),
        check_vma=False,
    )
```

```python
import math

import jax
import jax.numpy as jnp
import numpy as np
from jax import lax
from jax.experimental import pallas as pl
from jax.experimental.pallas import tpu as pltpu
from jax.sharding import PartitionSpec as P

HDIM = 64
SCALE = HDIM ** (-0.5)
LANES = 128
EPS = 1e-06
VMEM_LIMIT = 24 * 1024 * 1024
LARGE = 1 << 18
masked_score = -1000000000.0
f32 = jnp.float32
bf16 = jnp.bfloat16

PLACES, HEAD, BLK, LENGTHS = 0, 8, 9, 10


def swap(value, axis, bits):
    size = lax.axis_size(axis)
    return lax.ppermute(value, axis, [(i, i ^ bits) for i in range(size)])


def sync(*values):
    return lax.optimization_barrier(values)


def share(value):
    return [swap(value, "head", k) for k in (1, 2, 3)]


def ring_order(count):
    return [*range(0, count, 2), *range(count - 1, 0, -2)]


OFFSETS = (0, -1, 1, -2, 2, -3, 3, -4)


def ring_steps(count):
    order = ring_order(count)
    forth = [(order[i], order[(i + 1) % count]) for i in range(count)]
    return forth, [(b, a) for a, b in forth]


def place_table(count):
    order = ring_order(count)
    at = {b: i for i, b in enumerate(order)}
    return np.array(
        [[order[(at[b] + o) % count] for o in OFFSETS] for b in range(count)], np.int32
    )


def gather_rows(own):
    return lax.all_gather(own, "blk", axis=0, tiled=True)


def fetch_start(own):
    if lax.axis_size("blk") == 8:
        return {0: own}
    return dict(zip(OFFSETS, jnp.split(gather_rows(own), 8, axis=0), strict=True))


def fetch_step(pieces, *offsets):
    count = lax.axis_size("blk")
    if count != 8:
        return pieces
    forth, back = ring_steps(count)
    more = {
        k: lax.ppermute(pieces[k + 1 if k < 0 else k - 1], "blk", forth if k < 0 else back)
        for k in offsets
    }
    return {**pieces, **more}


def in_turn(pieces):
    return [pieces[k] if k in pieces else pieces[-k] for k in OFFSETS]


@jax.tree_util.register_pytree_node_class
class Part:
    def __init__(self, array, start, width):
        self.array, self.start, self.width = array, start, width

    def tree_flatten(self):
        return (self.array,), (self.start, self.width)

    @classmethod
    def tree_unflatten(cls, places, arrays):
        return cls(*arrays, *places)

    def read(self, ref):
        return ref[:, self.start : self.start + self.width]


def part(value):
    return value if isinstance(value, Part) else Part(value, 0, value.shape[1])


def reduce_step(info, *rings):
    count = lax.axis_size("blk")
    if count != 8:
        return [[] for _ in rings]
    forth, back = ring_steps(count)
    plan = [[], []]
    for pieces, moving, step in rings:
        by = dict(zip(OFFSETS, pieces, strict=True))
        plan[0].append([*([] if step == 1 else [moving[0]]), by[(-4, 3, 2, 1)[step - 1]]])
        if step < 4:
            plan[1].append([*([] if step == 1 else [moving[1]]), by[(-3, -2, -1)[step - 1]]])
    plan = [p for p in plan if p]
    if len(rings) == 1 and rings[0][2] == 1:
        sent = [p[0][0] for p in plan]
    else:
        parts = [part(v) for p in plan for terms in p for v in terms]

        def body(info, _, ins, __, outs, ___):
            found = iter(zip(parts, ins, strict=True))
            for out, p in zip(outs, plan, strict=True):
                column = 0
                for terms in p:
                    values = [piece.read(ref) for piece, ref in (next(found) for _ in terms)]
                    total = values[0]
                    if len(values) == 2:
                        total = (total.astype(f32) + values[1].astype(f32)).astype(bf16)
                    out[:, column : column + total.shape[1]] = total
                    column += total.shape[1]

        rows = rings[0][0][0].shape[0]
        wide = [sum(part(terms[0]).width for terms in p) for p in plan]
        shapes = [like((rows, w), bf16) for w in wide]
        sent = call(body, info, [], [p.array for p in parts], [], shapes, near=True)
    came = [lax.ppermute(v, "blk", way) for v, way in zip(sent, (forth, back), strict=False)]
    results, column = [], 0
    for k, (pieces, moving, step) in enumerate(rings):
        wide = pieces[0].shape[1]
        found = [Part(came[0], column, wide)]
        if step == 4:
            found.append(moving[1])
        else:
            before = sum(r[0][0].shape[1] for r in rings[:k] if r[2] < 4)
            found.append(Part(came[1], before, wide))
        results.append(found)
        column += wide
    return results


def reduce_terms(pieces, moving):
    if lax.axis_size("blk") != 8:
        everything = jnp.concatenate([p.astype(f32) for p in pieces], axis=0)
        return [lax.psum_scatter(everything, "blk", scatter_dimension=0, tiled=True)]
    return [pieces[0], *moving]


def dot(left, right, over=(1, 0)):
    return lax.dot_general(
        left, right, (((over[0],), (over[1],)), ((), ())), preferred_element_type=f32
    )


def dot_t(left, right):
    return dot(left, right, (1, 1))


def t_dot(left, right):
    return dot(left, right, (0, 0))


def norm_rows(values, gain):
    return values * lax.rsqrt(jnp.mean(values * values, axis=-1, keepdims=True) + EPS) * gain


def norm_back(values, gain, grad):
    inverse = lax.rsqrt(jnp.mean(values * values, axis=-1, keepdims=True) + EPS)
    unit = values * inverse
    weighted = grad * gain
    along = jnp.mean(weighted * unit, axis=-1, keepdims=True)
    return inverse * (weighted - unit * along), grad * unit


def gelu_both(values):
    root = math.sqrt(2.0 / math.pi)
    square = values * values
    bent = jnp.tanh(root * values * (1.0 + 0.044715 * square))
    half = 0.5 * (1.0 + bent)
    slope = half + 0.5 * values * (1.0 - bent * bent) * root * (1.0 + 3 * 0.044715 * square)
    return values * half, slope


def heads_in(width):
    return [slice(at, at + HDIM) for at in range(0, width, HDIM)]


def head_parts(values, count):
    size = values.shape[1] // count
    return [[values[:, j * size :][:, at] for at in heads_in(size)] for j in range(count)]


def assemble(info, pieces, targets, signals, column_from=0):
    rows = pieces[0].shape[0]
    copies = []
    for t, piece in enumerate(pieces):
        at = pl.ds(pl.multiple_of(info[PLACES + t] * rows, 16), rows)
        column = column_from
        for k, target in enumerate(targets):
            wide = target.shape[1]
            copies.append(
                pltpu.make_async_copy(
                    piece.at[:, column : column + wide], target.at[at, :], signals.at[k, t]
                )
            )
            column += wide
    for copy in copies:
        copy.start()
    for copy in copies:
        copy.wait()


def hand_out(info, sources, pieces):
    rows = pieces[0].shape[0]
    for t, piece in enumerate(pieces):
        at = pl.ds(pl.multiple_of(info[PLACES + t] * rows, 16), rows)
        column = 0
        for source in sources:
            piece[:, column : column + source.shape[1]] = source[at, :].astype(piece.dtype)
            column += source.shape[1]


def token_rows(refs):
    return jnp.concatenate([r[k] for k in range(refs[0].shape[0]) for r in refs], axis=0)


def emit(partial, outs):
    each, part, _ = outs[0].shape
    for k in range(each):
        for r, out in enumerate(outs):
            at = (k * len(outs) + r) * part
            out[k] = partial[at : at + part].astype(out.dtype)


def slots_used(info, b, part, slot):
    column = lax.broadcasted_iota(jnp.int32, (1, slot), 1)
    position = (lax.div(column, part) ^ info[HEAD]) * part + lax.rem(column, part)
    return position < info[LENGTHS + b]


def keys_used(info, question, passages, part, slot, count_pass):
    return jnp.concatenate(
        [
            slots_used(info, k, part, slot) & (question[...] == k // count_pass)
            for k in passages
        ],
        axis=1,
    )


def call(
    body, info, stepped, fixed, out_stepped, out_fixed, scratch=(), flops=0, steps=1, near=False, least=LARGE, each=1
):
    def by_step(shape):
        last = shape[0] // each - 1
        return pl.BlockSpec((each, *shape[1:]), lambda b: (jnp.minimum(b, last),) + (0,) * (len(shape) - 1))

    def whole(a):
        if isinstance(a, Far):
            return pl.BlockSpec(memory_space=pltpu.HBM)
        if isinstance(a, Rider):
            return pl.BlockSpec(a.shape, lambda b: (a.index, 0, 0))
        index = (0, a.index) if type(a) is Columns else (0,) * len(a.shape)
        return pl.BlockSpec(a.shape, lambda b: index)

    counts = [len(stepped), len(fixed), len(out_stepped), len(out_fixed), len(scratch)]
    stops = np.cumsum(counts)

    def split(info_ref, *refs):
        body(info_ref, *(refs[e - c : e] for c, e in zip(counts, stops, strict=True)))

    def large(a):
        return not near and math.prod(a.shape) * a.dtype.itemsize >= least

    def given(a):
        array = a.array if isinstance(a, (Columns, Far, Rider)) else a
        return pltpu.with_memory_space_constraint(array, pltpu.HBM) if large(a) else array

    def made(a):
        if isinstance(a, Later) or (large(a) and not isinstance(a, Near)):
            return pltpu.HBM(a.shape, a.dtype)
        return a.array if isinstance(a, Near) else a

    arrays = [*stepped, *fixed, *out_stepped, *out_fixed]
    moved = sum(math.prod(a.shape) * a.dtype.itemsize for a in arrays)
    return pl.pallas_call(
        split,
        grid=(steps,),
        in_specs=[
            pl.BlockSpec(memory_space=pltpu.SMEM),
            *(by_step(a.shape) for a in stepped),
            *(whole(a) for a in fixed),
        ],
        out_specs=[
            *(by_step(a.shape) for a in out_stepped),
            *(whole(a) for a in out_fixed),
        ],
        out_shape=[made(a) for a in (*out_stepped, *out_fixed)],
        scratch_shapes=list(scratch),
        compiler_params=pltpu.CompilerParams(
            dimension_semantics=("arbitrary",), vmem_limit_bytes=VMEM_LIMIT
        ),
        cost_estimate=pl.CostEstimate(
            flops=int(flops), bytes_accessed=int(moved), transcendentals=0
        ),
    )(info, *(given(a) for a in (*stepped, *fixed)))


class Columns:
    def __init__(self, array, width, index):
        self.array, self.index, self.dtype = array, index, array.dtype
        self.shape = (array.shape[0], width)


class Near(Columns):
    def __init__(self, array):
        self.array, self.shape, self.dtype = array, array.shape, array.dtype


class Later(Near):
    pass


class Rider:
    def __init__(self, array, index):
        self.array, self.index, self.dtype = array, index, array.dtype
        self.shape = (1, *array.shape[1:])


class Far:
    def __init__(self, array):
        self.array, self.shape, self.dtype = array, array.shape, array.dtype


def like(shape, dtype):
    return jax.ShapeDtypeStruct(tuple(shape), dtype)


def by_rows(fn, info, stepped, fixed, dtypes, gain=False, riders=None, kept=True):
    steps, _, width = stepped[0].shape
    count = 0 if riders is None else 1
    alone = [like(stepped[0].shape, d) for d in dtypes]
    outs = alone if riders is None or kept else alone[:-1]
    more = 0 if riders is None else riders.shape[0]
    together = [like((steps + count, *stepped[0].shape[1:]), dtypes[-1])] if more else []

    def body(info_ref, ins, whole, outs, sums, _):
        b = pl.program_id(0)
        if more:
            whole, rows = whole[:-1], whole[-1]

        @pl.when(b < steps)
        def _():
            results = fn(*(r[0].astype(f32) for r in ins), *(r[...] for r in whole))
            for out, value in zip(outs, results, strict=False):
                out[0] = value.astype(out.dtype)
            if more:
                outs[-1][0] = results[len(dtypes) - 1].astype(outs[-1].dtype)
            for total in sums:
                found = jnp.sum(results[-1], axis=0, keepdims=True)

                @pl.when(b == 0)
                def _():
                    total[...] = found

                @pl.when(b > 0)
                def _():
                    total[...] += found

        if more:

            @pl.when(b == steps)
            def _():
                outs[-1][0, :more, :] = rows[...]

    return call(
        body,
        info,
        stepped,
        [*fixed, riders] if more else fixed,
        [*outs, *together],
        [like((1, width), f32)] * gain,
        flops=10 * math.prod(stepped[0].shape),
        steps=steps + count,
        near=True,
    )


def partial_rows(blocks, part, width):
    return [Near(like((blocks, part, width), d)) for d in (f32, bf16, f32, bf16)]


def piece_shapes(rows, columns):
    return [Later(like((rows, columns), d)) for d in (f32, *[bf16] * 7)]


def attention_scratch(width, size, pieces):
    return [
        *(pltpu.VMEM((width, k * size), bf16) for k in (3, 1, 4)),
        pltpu.SemaphoreType.DMA((1, len(pieces))),
    ]


def encoder_attention(info, normed, pieces):
    blocks, part, width = normed[0].shape
    slot = part * len(normed)
    size = pieces[0].shape[1] // 4
    count = size // HDIM

    def body(info, rows, pieces, outs, _, scratch):
        qkv, probs, context = outs[:3]
        w_in, w_out, together, signals = scratch
        b = pl.program_id(0)

        @pl.when(b == 0)
        def _():
            assemble(info, pieces, (together,), signals)
            w_in[...] = together[:, : 3 * size]
            w_out[...] = together[:, 3 * size :]

        qkv[0] = dot(token_rows(rows), w_in[...]).astype(bf16)
        allowed = slots_used(info, b, part, slot)
        query, keys, vals = head_parts(qkv[0], 3)
        found = []
        for k, scores in enumerate([dot_t(q * SCALE, t) for q, t in zip(query, keys, strict=True)]):
            scores = jnp.where(allowed, scores, masked_score)
            spread_out = jnp.exp(scores - jnp.max(scores, axis=-1, keepdims=True))
            inverse = 1.0 / jnp.sum(spread_out, axis=-1, keepdims=True)
            found.append((spread_out * inverse).astype(bf16))
            probs[0, k] = found[-1]
        found = [dot(w, v) for w, v in zip(found, vals, strict=True)]
        context[0] = jnp.concatenate(found, axis=1).astype(bf16)
        emit(dot_t(context[0], w_out[...]), outs[3:])

    return call(
        body,
        info,
        normed,
        [Far(p) for p in pieces],
        [
            like((blocks, slot, 3 * size), bf16),
            like((blocks, count, slot, slot), bf16),
            like((blocks, slot, size), bf16),
            *partial_rows(blocks, part, width),
        ],
        [],
        attention_scratch(width, size, pieces),
        flops=2 * blocks * slot * (width * size * 4 + 8 * slot * size),
        steps=blocks,
    )


def encoder_attention_back(info, grads, normed, qkv, probs, context, pieces, gains):
    blocks, part, width = normed[0].shape
    slot = part * len(normed)
    size = context.shape[2]

    def body(info, stepped, fixed, outs, ends, scratch):
        grad_refs, normed_refs = stepped[:4], stepped[4:8]
        qkv, probs, context = stepped[8:]
        weight_pieces, gains = fixed[:-1], fixed[-1]
        pieces, gain_out = ends[:-1], ends[-1]
        w_in, w_out, together, signals, total_in, total_out, moved = scratch
        b = pl.program_id(0)

        @pl.when(b == 0)
        def _():
            assemble(info, weight_pieces, (together,), signals)
            w_in[...] = together[:, : 3 * size]
            w_out[...] = together[:, 3 * size :]
            total_in[...] = jnp.zeros_like(total_in)
            total_out[...] = jnp.zeros_like(total_out)
            gain_out[...] = jnp.zeros_like(gain_out)

        grad = token_rows(grad_refs)
        rows = token_rows(normed_refs)
        dcontext = dot(grad, w_out[...]).astype(bf16)
        query, keys, vals = head_parts(qkv[0], 3)
        cuts = head_parts(dcontext, 1)[0]
        backs = [dot_t(c, v) for c, v in zip(cuts, vals, strict=True)]
        dvals = [t_dot(probs[0, k], c) for k, c in enumerate(cuts)]
        lows = []
        for k, back in enumerate(backs):
            wide = probs[0, k].astype(f32)
            low = wide * (back - jnp.sum(wide * back, axis=-1, keepdims=True))
            lows.append(low.astype(bf16))
        dquery = [dot(d, t) * SCALE for d, t in zip(lows, keys, strict=True)]
        dkeys = [t_dot(d, q) * SCALE for d, q in zip(lows, query, strict=True)]
        moved[...] = jnp.concatenate([*dquery, *dkeys, *dvals], axis=1).astype(bf16)
        partial = dot_t(moved[...], w_in[...])
        emit(partial, outs)
        gain_out[...] += jnp.sum(partial * rows.astype(f32), axis=0, keepdims=True) / gains[0:1, :]
        total_in[...] += t_dot(rows, moved[...])
        total_out[...] += t_dot(grad, context[0])

        @pl.when(b == blocks - 1)
        def _():
            hand_out(info, (total_in, total_out), pieces)

    results = call(
        body,
        info,
        [*grads, *normed, qkv, probs, context],
        [*(Far(p) for p in pieces), gains],
        partial_rows(blocks, part, width),
        [*piece_shapes(width // 8, 4 * size), like((1, width), f32)],
        [
            *attention_scratch(width, size, pieces),
            pltpu.VMEM((width, 3 * size), f32),
            pltpu.VMEM((width, size), f32),
            pltpu.VMEM((slot, 3 * size), bf16),
        ],
        flops=2 * blocks * slot * (width * size * 8 + 20 * slot * size),
        steps=blocks,
    )
    return results[:4], results[4:12], results[12]


def ffn_scratch(width, hidden, pieces):
    return [
        *[pltpu.VMEM((width, hidden), bf16)] * 2,
        pltpu.SemaphoreType.DMA((2, len(pieces))),
    ]


def encoder_ffn(info, normed, pieces, hidden):
    blocks, part, width = normed[0].shape
    slot = part * len(normed)

    def body(info, rows, pieces, outs, _, scratch):
        active, slope = outs[:2]
        w_inner, w_outer, signals = scratch

        @pl.when(pl.program_id(0) == 0)
        def _():
            assemble(info, pieces, (w_inner, w_outer), signals)

        value, bend = gelu_both(dot(token_rows(rows), w_inner[...]))
        low = value.astype(bf16)
        active[...] = low.reshape(active.shape)
        slope[...] = bend.astype(bf16).reshape(slope.shape)
        emit(dot_t(low, w_outer[...]), outs[2:])

    return call(
        body,
        info,
        normed,
        [Far(p) for p in pieces],
        [*[like((blocks, slot, hidden), bf16)] * 2, *partial_rows(blocks, part, width)],
        [],
        ffn_scratch(width, hidden, pieces),
        flops=4 * blocks * slot * width * hidden,
        steps=blocks // 2,
        each=2,
    )


def encoder_ffn_back(info, grads, slope, pieces):
    blocks, (_, part, width) = slope.shape[0], grads[0].shape
    slot = part * len(grads)
    hidden = slope.shape[2]

    def body(info, stepped, pieces, outs, ends, scratch):
        dinner = outs[0]
        w_inner, w_outer, signals = scratch

        @pl.when(pl.program_id(0) == 0)
        def _():
            assemble(info, pieces, (w_inner, w_outer), signals)

        back = dot(token_rows(stepped[:4]), w_outer[...])
        low = (back * stepped[4][...].reshape(back.shape).astype(f32)).astype(bf16)
        dinner[...] = low.reshape(dinner.shape)
        emit(dot_t(low, w_inner[...]), outs[1:])

    return call(
        body,
        info,
        [*grads, slope],
        [Far(p) for p in pieces],
        [like((blocks, slot, hidden), bf16), *partial_rows(blocks, part, width)],
        [],
        ffn_scratch(width, hidden, pieces),
        flops=4 * blocks * slot * width * hidden,
        steps=blocks // 2,
        each=2,
    )


def weight_grads(info, pairs, more=(), cut=True):
    blocks, (_, part, width) = pairs[0][1].shape[0], pairs[0][0][0].shape
    widths = [right.shape[2] for _, right in pairs]

    def body(info, stepped, more, __, ends, totals):
        totals = totals if cut else ends
        for k, total in enumerate(totals):
            left, right = token_rows(stepped[5 * k : 5 * k + 4]), stepped[5 * k + 4]
            total[...] = t_dot(left, right[...].reshape(left.shape[0], total.shape[1]))
        if cut:
            hand_out(info, (*totals, *more), ends)

    return call(
        body,
        info,
        [a for left, right in pairs for a in (*left, right)],
        more,
        [],
        piece_shapes(width // 8, sum(widths) + sum(m.shape[1] for m in more))
        if cut
        else [like((width, w), f32) for w in widths],
        [pltpu.VMEM((width, w), f32) for w in widths] if cut else [],
        flops=2 * blocks * part * 4 * width * sum(widths),
        each=blocks,
    )


def finish(info, terms, widths, turned):
    terms = [part(t) for t in terms]
    rows = terms[0].array.shape[0]
    shapes = [(w, rows) if t else (rows, w) for w, t in zip(widths, turned, strict=True)]

    def body(info, _, ins, __, outs, ___):
        total = terms[0].read(ins[0])
        for term, ref in zip(terms[1:], ins[1:], strict=True):
            total = total + term.read(ref).astype(f32)
        column = 0
        for out, wide, turn in zip(outs, widths, turned, strict=True):
            found = total[:, column : column + wide]
            out[...] = found.T if turn else found
            column += wide

    return call(body, info, [], [t.array for t in terms], [], [like(s, f32) for s in shapes])


def cross_forward(info, states, pieces, column_from, decoder, own_question, count_q, count_pass):
    rows_in, terms, gains = decoder
    blocks = count_q * count_pass
    _, part, width = states[0].shape
    slot = part * len(states)
    rows_dec = rows_in.shape[0]
    size = (pieces[0].shape[1] - column_from) // 4
    steps = 2

    def body(info, rows, fixed, outs, ends, scratch):
        pieces, question = fixed[: len(pieces_given)], fixed[-1]
        rows_in, *terms, gains = fixed[len(pieces_given) : -1]
        after_self, normed, queries, w_query, w_output, stats, weight = ends
        held, asked, signals = scratch
        b = pl.program_id(0)

        @pl.when(b == 0)
        def _():
            assemble(info, pieces, (weight, asked), signals, column_from)
            w_query[...] = asked[:, :size]
            w_output[...] = asked[:, size:]
            after_self[...] = rows_in[...].astype(f32) + summed(terms)
            normed[...] = norm_rows(after_self[...], gains[1:2, :]).astype(bf16)
            queries[...] = dot(normed[...], w_query[...]).astype(bf16)

        made = dot(token_rows(rows), weight[...]).astype(bf16)
        outs[0][...] = made.reshape(outs[0].shape)
        each = made.shape[0]
        held[pl.ds(pl.multiple_of(b * each, each), each), :] = made

        @pl.when(b == steps - 1)
        def _():
            allowed = keys_used(info, question, range(blocks), part, slot, count_pass)
            lane = lax.broadcasted_iota(jnp.int32, (rows_dec, HDIM), 1)
            keys, vals = head_parts(held[...], 2)
            asking = head_parts(queries[...], 1)[0]
            scores = [dot_t(q * SCALE, t) for q, t in zip(asking, keys, strict=True)]
            for k, score in enumerate(scores):
                score = jnp.where(allowed, score, masked_score)
                top = jnp.max(score, axis=-1, keepdims=True)
                spread_out = jnp.exp(score - top)
                total = jnp.sum(spread_out, axis=-1, keepdims=True)
                at = k * LANES
                stats[:, at : at + HDIM] = dot(spread_out.astype(bf16), vals[k])
                stats[:, at + HDIM : at + LANES] = jnp.where(lane == 0, top, total)

    pieces_given = pieces
    return call(
        body,
        info,
        states,
        [*(Far(p) for p in pieces), rows_in, *terms, gains, own_question],
        [like((blocks, slot, 2 * size), bf16)],
        [
            Later(like((rows_dec, width), f32)),
            Later(like((rows_dec, width), bf16)),
            like((rows_dec, size), bf16),
            Later(like((width, size), bf16)),
            like((width, size), bf16),
            like((rows_dec, size // HDIM * LANES), f32),
            like((width, 2 * size), bf16),
        ],
        [
            pltpu.VMEM((blocks * slot, 2 * size), bf16),
            pltpu.VMEM((width, 2 * size), bf16),
            pltpu.SemaphoreType.DMA((2, len(pieces))),
        ],
        flops=4 * blocks * slot * width * size,
        steps=steps,
        each=blocks // steps,
    )


def merged(first, second):
    lane = lax.broadcasted_iota(jnp.int32, (first.shape[0], HDIM), 1)
    found = []
    for at in range(0, first.shape[1], LANES):
        tops = [v[:, at + HDIM : at + HDIM + 1] for v in (first, second)]
        totals = [v[:, at + HDIM + 1 : at + HDIM + 2] for v in (first, second)]
        top = jnp.maximum(*tops)
        scales = [jnp.exp(t - top) for t in tops]
        total = totals[0] * scales[0] + totals[1] * scales[1]
        found.append(first[:, at : at + HDIM] * scales[0] + second[:, at : at + HDIM] * scales[1])
        found.append(jnp.where(lane == 0, top, total))
    return jnp.concatenate(found, axis=1)


def in_order(info, bits, own, other):
    later = (info[BLK] & bits) != 0
    return jnp.where(later, other, own), jnp.where(later, own, other)


def merge(info, own, other, bits):
    def body(info, _, ins, __, outs, ___):
        outs[0][...] = merged(*in_order(info, bits, ins[0][...], ins[1][...]))

    return call(body, info, [], [own, other], [], [like(own.shape, f32)])[0]


def cross_out(info, stats, bits, w_output):
    rows, columns = stats[0].shape
    size = columns // LANES * HDIM
    width = w_output.shape[0]

    def body(info, _, ins, __, outs, scratch):
        w_output = ins[-1]
        out, log_total, context, own, sent = outs
        values = [r[...] for r in ins[:-1]]
        near = merged(*in_order(info, bits[0], *values[:2]))
        far = merged(*in_order(info, bits[0], *values[2:]))
        stats = merged(*in_order(info, bits[1], near, far))
        log_total[...] = jnp.zeros_like(log_total)
        for k, at in enumerate(heads_in(size)):
            base = k * LANES
            top = stats[:, base + HDIM : base + HDIM + 1]
            total = stats[:, base + HDIM + 1 : base + HDIM + 2]
            out[:, at] = stats[:, base : base + HDIM] / total
            log_total[:, k : k + 1] = top + jnp.log(total)
        context[...] = out[...].astype(bf16)
        own[...] = dot_t(context[...], w_output[...])
        sent[...] = own[...].astype(bf16)

    return call(
        body,
        info,
        [],
        [*stats, w_output],
        [],
        [
            like((rows, size), f32),
            like((rows, LANES), f32),
            Later(like((rows, size), bf16)),
            like((rows, width), f32),
            like((rows, width), bf16),
        ],
        flops=2 * rows * size * width,
    )


def cross_back(info, key_vals, inputs, own_question, count_pass, slot, part):
    cotangent, after_cross, terms, gains, w_output, out, log_total, queries, weight = inputs
    blocks = key_vals.shape[0]
    rows_dec, width = after_cross.shape
    size = queries.shape[1]

    def body(info, stepped, fixed, outs, ends, scratch):
        cotangent, after_cross, own, r1, r2, r3, gains, w_output, out, log_total, queries, weight, question = fixed
        key_vals = stepped[0]
        dkey_vals = outs[0]
        dcross, dcross_low, gain_out, dqueries = ends
        total = summed((own, r1, r2, r3))
        back, gain_out[...] = norm_back(after_cross[...], gains[2:3, :], total)
        dcross[...] = cotangent[...].astype(f32) + back
        dcross_low[...] = dcross[...].astype(bf16)
        dcontext = dot(dcross_low[...], w_output[...]).astype(bf16)
        allowed = keys_used(info, question, range(blocks), part, slot, count_pass)
        keys, vals = head_parts(key_vals[...].reshape(blocks * slot, 2 * size), 2)
        asking = head_parts(queries[...], 1)[0]
        cuts = head_parts(dcontext, 1)[0]
        outs_of = head_parts(out[...], 1)[0]
        scores = [dot_t(q * SCALE, t) for q, t in zip(asking, keys, strict=True)]
        backs = [dot_t(c, v) for c, v in zip(cuts, vals, strict=True)]
        probs, lows = [], []
        for k, score in enumerate(scores):
            row_term = jnp.sum(cuts[k].astype(f32) * outs_of[k], axis=-1, keepdims=True)
            score = jnp.where(allowed, score, masked_score)
            probs.append(jnp.exp(score - log_total[:, k : k + 1]))
            lows.append((probs[k] * (backs[k] - row_term)).astype(bf16))
        dvals = [t_dot(p.astype(bf16), c) for p, c in zip(probs, cuts, strict=True)]
        dkeys = [t_dot(d, q) * SCALE for d, q in zip(lows, asking, strict=True)]
        found = [dot(d, t) * SCALE for d, t in zip(lows, keys, strict=True)]
        dqueries[...] = jnp.concatenate(found, axis=1)
        made = jnp.concatenate([*dkeys, *dvals], axis=1).astype(bf16)
        dkey_vals[...] = made.reshape(dkey_vals.shape)
        emit(dot_t(made, weight[...]), outs[1:])

    return call(
        body,
        info,
        [key_vals],
        [cotangent, after_cross, *terms, gains, w_output, out, log_total, queries, weight, own_question],
        [like(key_vals.shape, bf16), *partial_rows(blocks, part, width)],
        [
            Later(like((rows_dec, width), f32)),
            Later(like((rows_dec, width), bf16)),
            Later(like((rows_dec, width), f32)),
            like((rows_dec, size), f32),
        ],
        flops=4 * blocks * slot * width * size,
        each=blocks,
    )


def summed(refs):
    count = refs[0].shape[0]

    def rows(ref):
        return ref[...] if len(ref.shape) == 2 else ref[0, :count, :]

    terms = [rows(ref).astype(f32) for ref in refs[1:]]
    total = refs[0][...]
    for term in terms:
        total = total + term
    return total


def decoder_self(info, rows, gains, pieces, column_from, size, order):
    count, width = rows.shape

    def body(info, _, ins, __, outs, scratch):
        rows, gains, order_q, order_k = ins[:4]
        normed, qkv, probs, context, own, sent, weight = outs
        assemble(info, ins[4:], (weight,), scratch[0], column_from)
        normed[...] = norm_rows(rows[...].astype(f32), gains[0:1, :]).astype(bf16)
        qkv[...] = dot(normed[...], weight[:, : 3 * size]).astype(bf16)
        query_at, key_at = order_q[...], order_k[...]
        same = lax.div(query_at, 1000) == lax.div(key_at, 1000)
        allowed = same & (key_at <= query_at) & (key_at >= 0) & (query_at >= 0)
        for k, at in enumerate(heads_in(size)):
            query, keys, vals = (qkv[:, j * size + at.start : j * size + at.stop] for j in range(3))
            scores = jnp.where(allowed, dot_t(query, keys) * SCALE, masked_score)
            spread_out = jnp.exp(scores - jnp.max(scores, axis=-1, keepdims=True))
            share_out = spread_out / jnp.sum(spread_out, axis=-1, keepdims=True)
            share_out = jnp.where(allowed, share_out, 0.0)
            probs[k] = share_out
            context[:, at] = dot(share_out.astype(bf16), vals).astype(bf16)
        own[...] = dot_t(context[...], weight[:, 3 * size :])
        sent[...] = own[...].astype(bf16)

    return call(
        body,
        info,
        [],
        [rows, gains, *order, *(Far(p) for p in pieces)],
        [],
        [
            Later(like((count, width), bf16)),
            Later(like((count, 3 * size), bf16)),
            Later(like((size // HDIM, count, count), f32)),
            Later(like((count, size), bf16)),
            like((count, width), f32),
            like((count, width), bf16),
            Later(like((width, 4 * size), bf16)),
        ],
        [pltpu.SemaphoreType.DMA((1, len(pieces)))],
        flops=2 * count * width * size * 4,
    )


def decoder_back(info, cotangent, pieces):
    count, width = cotangent.shape
    hidden = pieces[0].shape[1] // 2

    def body(info, _, ins, __, outs, scratch):
        w_inner, w_outer, back = outs
        assemble(info, ins[1:], (w_inner, w_outer), scratch[0])
        back[...] = dot(ins[0][...], w_outer[...])

    return call(
        body,
        info,
        [],
        [cotangent, *(Far(p) for p in pieces)],
        [],
        [*[like((width, hidden), bf16)] * 2, like((count, hidden), f32)],
        [pltpu.SemaphoreType.DMA((2, len(pieces)))],
        flops=2 * count * width * hidden,
    )


def decoder_ffn(info, after_self, terms, back, gains, w_inner):
    count, width = after_self.shape
    hidden = w_inner.shape[1]

    def body(info, _, ins, __, outs, scratch):
        after_self, own, r1, r2, r3, back, gains, w_inner = ins
        after_cross, normed, active, dinner, own_back, sent_back = outs
        after_cross[...] = after_self[...] + summed((own, r1, r2, r3))
        normed[...] = norm_rows(after_cross[...], gains[2:3, :]).astype(bf16)
        value, slope = gelu_both(dot(normed[...], w_inner[...]))
        active[...] = value.astype(bf16)
        dinner[...] = (slope * back[...]).astype(bf16)
        own_back[...] = dot_t(dinner[...], w_inner[...])
        sent_back[...] = own_back[...].astype(bf16)

    return call(
        body,
        info,
        [],
        [after_self, *terms, back, gains, w_inner],
        [],
        [
            like((count, width), f32),
            Later(like((count, width), bf16)),
            Later(like((count, hidden), bf16)),
            Later(like((count, hidden), bf16)),
            like((count, width), f32),
            like((count, width), bf16),
        ],
        flops=4 * count * width * hidden,
    )


def rows_back(info, terms, weight):
    (count, size), width = terms[0].shape, weight.shape[0]

    def body(info, _, ins, __, outs, scratch):
        low, own, sent = outs
        total = ins[0][...]
        for term in ins[1:-1]:
            total = total + term[...]
        low[...] = total.astype(bf16)
        own[...] = dot_t(low[...], ins[-1][...])
        sent[...] = own[...].astype(bf16)

    return call(
        body,
        info,
        [],
        [*terms, weight],
        [],
        [
            Later(like((count, size), bf16)),
            like((count, width), f32),
            like((count, width), bf16),
        ],
        flops=2 * count * width * size,
    )


def decoder_self_back(
    info, dcross, after_self, terms, gains, weight, qkv, probs
):
    count, width = after_self.shape
    size = weight.shape[1] // 4

    def body(info, _, ins, __, outs, scratch):
        dcross, after_self, *terms, gains, weight, qkv, probs = ins
        dself, dself_low, gain_rows, moved, own_back, sent_back = outs
        back, gain_rows[...] = norm_back(after_self[...], gains[1:2, :], summed(terms))
        dself[...] = dcross[...] + back
        dself_low[...] = dself[...].astype(bf16)
        dcontext = dot(dself_low[...], weight[:, 3 * size :]).astype(bf16)
        for k, at in enumerate(heads_in(size)):
            query, keys, vals = (qkv[:, j * size + at.start : j * size + at.stop] for j in range(3))
            share_out = probs[k]
            dprobs = dot_t(dcontext[:, at], vals)
            dscores = share_out * (dprobs - jnp.sum(share_out * dprobs, axis=-1, keepdims=True))
            dscores = dscores.astype(bf16)
            found = (
                dot(dscores, keys) * SCALE,
                t_dot(dscores, query) * SCALE,
                t_dot(share_out.astype(bf16), dcontext[:, at]),
            )
            for j, term in enumerate(found):
                moved[:, j * size + at.start : j * size + at.stop] = term.astype(bf16)
        own_back[...] = dot_t(moved[...], weight[:, : 3 * size])
        sent_back[...] = own_back[...].astype(bf16)

    return call(
        body,
        info,
        [],
        [dcross, after_self, *terms, gains, weight, qkv, probs],
        [],
        [
            like((count, width), f32),
            Later(like((count, width), bf16)),
            like((count, width), f32),
            Later(like((count, 3 * size), bf16)),
            like((count, width), f32),
            like((count, width), bf16),
        ],
        flops=2 * count * width * size * 8,
    )


def decoder_ends(
    info, rows, dself, terms, gains, after_cross, out_terms, gain_rows, gain_sums, dec_own
):
    count, width = dself.shape

    def body(info, _, ins, __, outs, scratch):
        rows, dself, after_cross, gains = ins[:4]
        three, four, zero, one = ins[-4:]
        grad, states, found = outs
        total, out_total = summed(ins[4:8]), summed(ins[8:12])
        back, two = norm_back(rows[...].astype(f32), gains[0:1, :], total)
        grad[...] = dself[...] + back
        states[...] = (after_cross[...] + out_total).astype(bf16)
        row = lax.div(lax.broadcasted_iota(jnp.int32, (count, 1), 0), dec_own)
        mine = (row == info[HEAD]) & (info[BLK] == 0)
        found[0:1, :] = zero[...]
        found[1:2, :] = one[...]
        for k, values in enumerate((two, three[...], four[...])):
            found[2 + k : 3 + k, :] = jnp.sum(jnp.where(mine, values, 0.0), axis=0, keepdims=True)

    return call(
        body,
        info,
        [],
        [rows, dself, after_cross, gains, *terms, *out_terms, *gain_rows, *gain_sums],
        [],
        [like((count, width), f32), like((count, width), bf16), like((5, width), f32)],
    )


def decoder_weight_grads(info, own, pairs_in, pairs_out):
    count, width = pairs_in[0][0].shape

    def body(info, _, ins, __, outs, scratch):
        row = lax.broadcasted_iota(jnp.int32, (own, width), 0) + info[BLK] * own
        column = lax.broadcasted_iota(jnp.int32, (own, width), 1)
        pick = jnp.where(row == column, 1.0, 0.0).astype(bf16)
        outs, ins = iter(outs), iter(ins)
        for _, _, arrays in pairs_in:
            left, right = next(ins)[...], next(ins)[...]
            found = t_dot(dot_t(left, pick).astype(bf16), right)
            wide = found.shape[1] // arrays
            for k in range(arrays):
                next(outs)[...] = found[:, k * wide : (k + 1) * wide]
        for _ in pairs_out:
            left, right = next(ins)[...], next(ins)[...]
            next(outs)[...] = t_dot(left, dot_t(right, pick).astype(bf16))

    outs = [like((own, r.shape[1] // n), f32) for _, r, n in pairs_in for _ in range(n)]
    outs += [like((l.shape[1], own), f32) for l, _ in pairs_out]
    flat = [a for pair in pairs_in for a in pair[:2]] + [a for pair in pairs_out for a in pair]
    return call(body, info, [], flat, [], outs, flops=2 * count * own * width * 10, least=0)


def shards(
    encoder_input,
    passage_lengths,
    decoder_input,
    encoder_query,
    encoder_key,
    encoder_value,
    encoder_output,
    encoder_inner,
    encoder_outer,
    decoder_query,
    decoder_key,
    decoder_value,
    decoder_output,
    cross_query,
    cross_key,
    cross_value,
    cross_output,
    decoder_inner,
    decoder_outer,
    encoder_gains,
    decoder_gains,
    encoder_cotangent,
    decoder_cotangent,
):
    head, blk = lax.axis_index("head"), lax.axis_index("blk")
    blk_count, head_count = lax.axis_size("blk"), lax.axis_size("head")
    count_q, count_pass, part, width = encoder_input.shape
    blocks = count_q * count_pass
    slot = part * head_count
    own = width // blk_count
    if blk_count == 8:
        places = jnp.asarray(place_table(8))[blk]
    else:
        places = jnp.arange(8, dtype=jnp.int32)
    info = jnp.concatenate(
        [places, jnp.stack([head, blk]).astype(jnp.int32), passage_lengths.reshape(blocks)]
    )

    size, units = encoder_query.shape[1], encoder_inner.shape[1]
    inputs = encoder_input.reshape(blocks, part, width)
    dec_part = decoder_input.shape[1]
    dec_own = count_q * dec_part
    dec_rows = dec_own * head_count
    filled = -(-dec_rows // 16) * 16

    attention = jnp.concatenate(
        [encoder_query, encoder_key, encoder_value, encoder_output.T], axis=1
    )
    attention, inputs = sync(attention, inputs)
    attention = fetch_step(fetch_start(attention), -1, 1)
    first = by_rows(
        lambda x, g: (norm_rows(x, g[0:1]),), info, [inputs], [encoder_gains], [bf16]
    )[0]
    attention, first = sync(attention, first)

    attention = fetch_step(attention, -2, 2)
    first_all = [first, swap(first, "head", 1), swap(first, "head", 2)]
    ffn = jnp.concatenate(
        [
            encoder_inner,
            encoder_outer.T,
            decoder_query,
            decoder_key,
            decoder_value,
            decoder_output.T,
            cross_key,
            cross_value,
            cross_query,
            cross_output.T,
        ],
        axis=1,
    )
    at_self, at_cross = 2 * units, 2 * units + 4 * size
    attention, first_all, ffn = sync(attention, first_all, ffn)

    attention = fetch_step(attention, -3, 3)
    first_all.append(swap(first_all[2], "head", 1))
    pair = jnp.stack([decoder_input, decoder_cotangent]).reshape(2, dec_own, width)
    both = lax.all_gather(pair, "head", axis=1, tiled=True)
    both = jnp.pad(both, ((0, 0), (0, filled - dec_rows), (0, 0)))
    attention, first_all, ffn, both = sync(attention, first_all, ffn, both)

    attention, ffn = fetch_step(attention, -4), fetch_step(fetch_start(ffn), 1)
    dec_ffn = jnp.concatenate([decoder_inner, decoder_outer.T], axis=1)
    attention, ffn, first_all, dec_ffn = sync(attention, ffn, first_all, dec_ffn)

    ffn = fetch_step(ffn, -1, 2)
    qkv, probs, context, *partial = encoder_attention(
        info, first_all, in_turn(attention)
    )
    partial, ffn = sync(partial, ffn)

    def to_core(partial):
        return [swap(partial[1], "head", 1), swap(partial[3], "head", 1)]

    def to_chip(partial, beside):
        return swap((partial[2] + beside[1].astype(f32)).astype(bf16), "head", 2)

    beside = to_core(partial)
    partial, beside, ffn = sync(partial, beside, ffn)
    across = to_chip(partial, beside)
    ffn = fetch_step(ffn, -2, 3)
    partial, beside, across, ffn = sync(partial, beside, across, ffn)

    def enter_ffn(x, a, b, c, g):
        hidden = x + a + b + c
        return hidden, norm_rows(hidden, g[1:2])

    hidden, second = by_rows(
        enter_ffn, info, [inputs, partial[0], beside[0], across], [encoder_gains], [f32, bf16]
    )
    def spread(rows):
        return [rows, swap(rows, "head", 1), swap(rows, "head", 2)]

    def riders(all_rows):
        return [Rider(rows, blocks) for rows in all_rows[1:]]

    second, ffn, dec_ffn = sync(second, ffn, dec_ffn)
    second_all = spread(second)
    ffn = fetch_step(ffn, -3, 4)
    second_all, ffn = sync(second_all, ffn)
    second_all.append(swap(second_all[2], "head", 1))
    second_all, ffn, dec_ffn = sync(second_all, ffn, dec_ffn)
    ffn = in_turn(ffn)

    dec_ffn = fetch_step(fetch_start(dec_ffn), -1, 1)
    active, slope, *partial = encoder_ffn(info, second_all, ffn, units)
    partial, dec_ffn = sync(partial, dec_ffn)
    beside = to_core(partial)
    partial, beside, both, dec_ffn = sync(partial, beside, both, dec_ffn)
    dec_in, cotangent = both[0], both[1]

    index = np.arange(filled)
    question = (index % dec_own) // dec_part
    position = index // dec_own * dec_part + index % dec_part
    order = np.where(index < dec_rows, question * 1000 + position, -1).astype(np.int32)
    order = (jnp.asarray(order[:, None]), jnp.asarray(order[None, :]))
    question = jnp.asarray(question[:, None].astype(np.int32))

    across = to_chip(partial, beside)
    dec_ffn = fetch_step(dec_ffn, -2, 2)
    third, dec_qkv, dec_probs, dec_context, mine, sent, w_self = decoder_self(
        info, dec_in, decoder_gains, ffn, at_self, size, order
    )
    partial, beside, across, mine, sent, dec_ffn = sync(
        partial, beside, across, mine, sent, dec_ffn
    )
    states, states_sent = by_rows(
        lambda h, a, b, c: (h + a + b + c,),
        info,
        [hidden, partial[0], beside[0], across],
        [],
        [bf16],
        riders=sent,
    )
    states_sent, dec_ffn = sync(states_sent, dec_ffn)
    states_all = spread(states_sent)
    dec_ffn = fetch_step(dec_ffn, -3, 3)
    states_all, dec_ffn = sync(states_all, dec_ffn)
    states_all.append(swap(states_all[2], "head", 1))
    states_all, dec_ffn = sync(states_all, dec_ffn)

    dec_ffn = fetch_step(dec_ffn, -4)
    (
        key_vals,
        after_self,
        fourth,
        queries,
        w_cross_query,
        w_cross_output,
        stats,
        w_cross,
    ) = cross_forward(
        info,
        states_all,
        ffn,
        at_cross,
        (dec_in, [mine, *riders(states_all)], decoder_gains),
        question,
        count_q,
        count_pass,
    )
    bits = [1 << k for k in range((blk_count - 1).bit_length())]
    last_two = (bits[-2], bits[-1], bits[-2] + bits[-1])
    for k in bits[:-2]:
        stats = merge(info, stats, swap(stats, "blk", k), k)
    stats, dec_ffn = sync(stats, dec_ffn)
    stats_all = [stats, *(swap(stats, "blk", k) for k in last_two)]
    w_dec_inner, w_dec_outer, outer_back = decoder_back(info, cotangent, in_turn(dec_ffn))
    stats_all, outer_back = sync(stats_all, outer_back)
    out, log_total, cross_context, mine, sent = cross_out(
        info, stats_all, bits[-2:], w_cross_output
    )
    after_cross, fifth, dec_active, dec_dinner, mine, sent = decoder_ffn(
        info, after_self, [mine, *share(sent)], outer_back, decoder_gains, w_dec_inner
    )
    dkey_vals, *rest = cross_back(
        info,
        key_vals,
        (
            cotangent,
            after_cross,
            [mine, *share(sent)],
            decoder_gains,
            w_cross_output,
            out,
            log_total,
            queries,
            w_cross,
        ),
        question,
        count_pass,
        slot,
        part,
    )
    partial, (dcross, dcross_low, gain_four, dqueries) = rest[:4], rest[4:]

    def some(value, which):
        for k in which:
            value = value + swap(value, "blk", k)
        return value

    partial, dqueries, dkey_vals = sync(partial, dqueries, dkey_vals)
    beside = to_core(partial)
    partial, beside, dkey_vals, dqueries = sync(partial, beside, dkey_vals, dqueries)
    across = to_chip(partial, beside)
    dqueries = some(dqueries, bits[:-1])
    cross_sum = weight_grads(info, [(states_all, dkey_vals)], cut=False)[0]
    _, out_mine, out_sent = rows_back(info, [dec_active], w_dec_outer)
    partial, beside, across, cross_sum, dqueries, out_sent = sync(
        partial, beside, across, cross_sum, dqueries, out_sent
    )

    def enter_back(cot, a, b, c):
        grad = cot + a + b + c
        return grad, grad

    dstates, dstates_low = by_rows(
        enter_back,
        info,
        [encoder_cotangent.reshape(blocks, part, width), partial[0], beside[0], across],
        [],
        [f32, bf16],
        riders=out_sent,
        kept=False,
    )
    dstates_low, cross_sum, dqueries = sync(dstates_low, cross_sum, dqueries)
    dstates_all = spread(dstates_low)
    terms = [dqueries, swap(dqueries, "blk", bits[-1])]
    dqueries, mine, sent = rows_back(info, terms, w_cross_query)
    dstates_all, sent = sync(dstates_all, sent)
    dstates_all.append(swap(dstates_all[2], "head", 1))
    dstates_all, sent = sync(dstates_all, sent)
    out_terms = [out_mine, *riders(dstates_all)]
    dinner, *partial = encoder_ffn_back(info, dstates_all, slope, ffn)
    terms = [mine, *share(sent)]
    partial, dinner, terms = sync(partial, dinner, terms)
    beside = to_core(partial)
    partial, beside, dinner, dstates_all = sync(partial, beside, dinner, dstates_all)
    across = to_chip(partial, beside)
    dself, dself_low, gain_three, dself_qkv, own_back, sent_back = decoder_self_back(
        info,
        dcross,
        after_self,
        terms,
        decoder_gains,
        w_self,
        dec_qkv,
        dec_probs,
    )
    ffn_sums = weight_grads(
        info, [(second_all, dinner), (dstates_all, active)], [cross_sum]
    )
    partial, beside, across, ffn_sums, sent_back = sync(
        partial, beside, across, ffn_sums, sent_back
    )

    def middle_back(dy, h, a, b, c, g):
        back, gain_rows = norm_back(h, g[1:2], a + b + c)
        grad = dy + back
        return grad, grad, gain_rows

    dhidden, dhidden_low, gain_one = by_rows(
        middle_back,
        info,
        [dstates, hidden, partial[0], beside[0], across],
        [encoder_gains],
        [f32, bf16],
        gain=True,
        riders=sent_back,
        kept=False,
    )
    dhidden_low, ffn_sums = sync(dhidden_low, ffn_sums)
    dhidden_all = spread(dhidden_low)
    ffn_moving = reduce_step(info, (ffn_sums, None, 1))[0]
    dhidden_all, ffn_moving = sync(dhidden_all, ffn_moving)
    dhidden_all.append(swap(dhidden_all[2], "head", 1))
    dhidden_all, ffn_moving = sync(dhidden_all, ffn_moving)
    terms = [own_back, *riders(dhidden_all)]

    ffn_moving = reduce_step(info, (ffn_sums, ffn_moving, 2))[0]
    partial, sums, gain_zero = encoder_attention_back(
        info, dhidden_all, first_all, qkv, probs, context, in_turn(attention), encoder_gains
    )
    partial, sums, ffn_moving, gain_zero = sync(partial, sums, ffn_moving, gain_zero)
    ffn_moving, moving = reduce_step(info, (ffn_sums, ffn_moving, 3), (sums, None, 1))
    beside = to_core(partial)
    dec_grad, dec_states, gains = decoder_ends(
        info,
        dec_in,
        dself,
        terms,
        decoder_gains,
        after_cross,
        out_terms,
        [gain_three, gain_four],
        [gain_zero, gain_one],
        dec_own,
    )
    gains = gains + swap(gains, "head", 1)
    (
        grad_dec_query,
        grad_dec_key,
        grad_dec_value,
        grad_cross_query,
        grad_dec_inner,
        grad_dec_outer,
        grad_dec_output,
        grad_cross_output,
    ) = decoder_weight_grads(
        info,
        own,
        [
            (third, dself_qkv, 3),
            (fourth, dqueries, 1),
            (fifth, dec_dinner, 1),
            (cotangent, dec_active, 1),
        ],
        [(dec_context, dself_low), (cross_context, dcross_low)],
    )
    partial, beside, moving, gains, ffn_moving, grad_dec_query = sync(
        partial, beside, moving, gains, ffn_moving, grad_dec_query
    )

    def own_rows(values):
        return lax.dynamic_slice_in_dim(values, head * dec_own, dec_own, 0)

    ffn_moving, moving = reduce_step(info, (ffn_sums, ffn_moving, 4), (sums, moving, 2))
    across = to_chip(partial, beside)
    gains = gains + swap(gains, "head", 2)
    gains = some(gains, bits[:1])
    dec_states, dec_grad = own_rows(dec_states), own_rows(dec_grad)
    partial, beside, across, moving, gains, ffn_moving, dec_states, dec_grad = sync(
        partial, beside, across, moving, gains, ffn_moving, dec_states, dec_grad
    )

    def last_back(dh, x, a, b, c, g):
        return (dh + norm_back(x, g[0:1], a + b + c)[0],)

    moving = reduce_step(info, (sums, moving, 3))[0]
    gains = some(gains, bits[1:-1])
    input_grad = by_rows(
        last_back,
        info,
        [dhidden, inputs, partial[0], beside[0], across],
        [encoder_gains],
        [f32],
    )[0]
    grad_inner, grad_outer, grad_cross_key, grad_cross_value = finish(
        info,
        reduce_terms(ffn_sums, ffn_moving),
        (units, units, size, size),
        (False,) * 4,
    )
    moving, gains, input_grad, grad_inner = sync(moving, gains, input_grad, grad_inner)
    moving = reduce_step(info, (sums, moving, 4))[0]
    last = swap(gains, "blk", bits[-1])
    enc_gain_grads, dec_gain_grads = gains[:2] + last[:2], gains[2:] + last[2:]
    grad_query, grad_key, grad_value, grad_output = finish(
        info, reduce_terms(sums, moving), (size,) * 4, (False, False, False, True)
    )

    def dec_shape(values):
        return values.reshape(count_q, dec_part, width)

    return (
        states.reshape(encoder_input.shape),
        dec_shape(dec_states),
        input_grad.reshape(encoder_input.shape),
        dec_shape(dec_grad),
        grad_query,
        grad_key,
        grad_value,
        grad_output,
        grad_inner,
        grad_outer.T,
        grad_dec_query,
        grad_dec_key,
        grad_dec_value,
        grad_dec_output,
        grad_cross_query,
        grad_cross_key,
        grad_cross_value,
        grad_cross_output,
        grad_dec_inner,
        grad_dec_outer.T,
        enc_gain_grads,
        dec_gain_grads,
    )


def solution(mesh):
    placed = (
        P(None, "blk", "head", None),
        P(None, "blk"),
        P(None, "head", None),
        P("blk", "head"),
        P("blk", "head"),
        P("blk", "head"),
        P("head", "blk"),
        P("blk", "head"),
        P("head", "blk"),
        P("blk", "head"),
        P("blk", "head"),
        P("blk", "head"),
        P("head", "blk"),
        P("blk", "head"),
        P("blk", "head"),
        P("blk", "head"),
        P("head", "blk"),
        P("blk", "head"),
        P("head", "blk"),
        P(),
        P(),
        P(None, "blk", "head", None),
        P(None, "head", None),
    )
    return jax.shard_map(
        shards,
        mesh=mesh,
        in_specs=placed,
        out_specs=(placed[0], placed[2], placed[0], placed[2], *placed[3:19], P(), P()),
        check_vma=False,
    )
```

```python
import math

import jax
import jax.numpy as jnp
import numpy as np
from jax import lax
from jax.experimental import pallas as pl
from jax.experimental.pallas import tpu as pltpu
from jax.sharding import PartitionSpec as P

HDIM = 64
SCALE = HDIM ** (-0.5)
LANES = 128
EPS = 1e-06
VMEM_LIMIT = 24 * 1024 * 1024
LARGE = 1 << 18
masked_score = -1000000000.0
f32 = jnp.float32
bf16 = jnp.bfloat16

PLACES, HEAD, BLK, LENGTHS = 0, 8, 9, 10


def swap(value, axis, bits):
    size = lax.axis_size(axis)
    return lax.ppermute(value, axis, [(i, i ^ bits) for i in range(size)])


def sync(*values):
    return lax.optimization_barrier(values)


def share(value):
    return [swap(value, "head", k) for k in (1, 2, 3)]


def ring_order(count):
    return [*range(0, count, 2), *range(count - 1, 0, -2)]


OFFSETS = (0, -1, 1, -2, 2, -3, 3, -4)


def ring_steps(count):
    order = ring_order(count)
    forth = [(order[i], order[(i + 1) % count]) for i in range(count)]
    return forth, [(b, a) for a, b in forth]


def place_table(count):
    order = ring_order(count)
    at = {b: i for i, b in enumerate(order)}
    return np.array(
        [[order[(at[b] + o) % count] for o in OFFSETS] for b in range(count)], np.int32
    )


def gather_rows(own):
    return lax.all_gather(own, "blk", axis=0, tiled=True)


def fetch_start(own):
    if lax.axis_size("blk") == 8:
        return {0: own}
    return dict(zip(OFFSETS, jnp.split(gather_rows(own), 8, axis=0), strict=True))


def fetch_step(pieces, *offsets):
    count = lax.axis_size("blk")
    if count != 8:
        return pieces
    forth, back = ring_steps(count)
    more = {
        k: lax.ppermute(pieces[k + 1 if k < 0 else k - 1], "blk", forth if k < 0 else back)
        for k in offsets
    }
    return {**pieces, **more}


def in_turn(pieces):
    return [pieces[k] if k in pieces else pieces[-k] for k in OFFSETS]


@jax.tree_util.register_pytree_node_class
class Part:
    def __init__(self, array, start, width):
        self.array, self.start, self.width = array, start, width

    def tree_flatten(self):
        return (self.array,), (self.start, self.width)

    @classmethod
    def tree_unflatten(cls, places, arrays):
        return cls(*arrays, *places)

    def read(self, ref):
        return ref[:, self.start : self.start + self.width]


def part(value):
    return value if isinstance(value, Part) else Part(value, 0, value.shape[1])


def reduce_step(info, *rings):
    count = lax.axis_size("blk")
    if count != 8:
        return [[] for _ in rings]
    forth, back = ring_steps(count)
    plan = [[], []]
    for pieces, moving, step in rings:
        by = dict(zip(OFFSETS, pieces, strict=True))
        plan[0].append([*([] if step == 1 else [moving[0]]), by[(-4, 3, 2, 1)[step - 1]]])
        if step < 4:
            plan[1].append([*([] if step == 1 else [moving[1]]), by[(-3, -2, -1)[step - 1]]])
    plan = [p for p in plan if p]
    if len(rings) == 1 and rings[0][2] == 1:
        sent = [p[0][0] for p in plan]
    else:
        parts = [part(v) for p in plan for terms in p for v in terms]

        def body(info, _, ins, __, outs, ___):
            found = iter(zip(parts, ins, strict=True))
            for out, p in zip(outs, plan, strict=True):
                column = 0
                for terms in p:
                    values = [piece.read(ref) for piece, ref in (next(found) for _ in terms)]
                    total = values[0]
                    if len(values) == 2:
                        total = (total.astype(f32) + values[1].astype(f32)).astype(bf16)
                    out[:, column : column + total.shape[1]] = total
                    column += total.shape[1]

        rows = rings[0][0][0].shape[0]
        wide = [sum(part(terms[0]).width for terms in p) for p in plan]
        shapes = [like((rows, w), bf16) for w in wide]
        sent = call(body, info, [], [p.array for p in parts], [], [Near(v) for v in shapes], least=0)
    came = [lax.ppermute(v, "blk", way) for v, way in zip(sent, (forth, back), strict=False)]
    results, column = [], 0
    for k, (pieces, moving, step) in enumerate(rings):
        wide = pieces[0].shape[1]
        found = [Part(came[0], column, wide)]
        if step == 4:
            found.append(moving[1])
        else:
            before = sum(r[0][0].shape[1] for r in rings[:k] if r[2] < 4)
            found.append(Part(came[1], before, wide))
        results.append(found)
        column += wide
    return results


def reduce_terms(pieces, moving):
    if lax.axis_size("blk") != 8:
        everything = jnp.concatenate([p.astype(f32) for p in pieces], axis=0)
        return [lax.psum_scatter(everything, "blk", scatter_dimension=0, tiled=True)]
    return [pieces[0], *moving]


def dot(left, right, over=(1, 0)):
    return lax.dot_general(
        left, right, (((over[0],), (over[1],)), ((), ())), preferred_element_type=f32
    )


def dot_t(left, right):
    return dot(left, right, (1, 1))


def t_dot(left, right):
    return dot(left, right, (0, 0))


def norm_rows(values, gain):
    return values * lax.rsqrt(jnp.mean(values * values, axis=-1, keepdims=True) + EPS) * gain


def norm_back(values, gain, grad):
    inverse = lax.rsqrt(jnp.mean(values * values, axis=-1, keepdims=True) + EPS)
    unit = values * inverse
    weighted = grad * gain
    along = jnp.mean(weighted * unit, axis=-1, keepdims=True)
    return inverse * (weighted - unit * along), grad * unit


def gelu_both(values):
    root = math.sqrt(2.0 / math.pi)
    square = values * values
    bent = jnp.tanh(root * values * (1.0 + 0.044715 * square))
    half = 0.5 * (1.0 + bent)
    slope = half + 0.5 * values * (1.0 - bent * bent) * root * (1.0 + 3 * 0.044715 * square)
    return values * half, slope


def heads_in(width):
    return [slice(at, at + HDIM) for at in range(0, width, HDIM)]


def head_parts(values, count):
    size = values.shape[1] // count
    return [[values[:, j * size :][:, at] for at in heads_in(size)] for j in range(count)]


def assemble(info, pieces, targets, signals, column_from=0):
    rows = pieces[0].shape[0]
    copies = []
    for t, piece in enumerate(pieces):
        at = pl.ds(pl.multiple_of(info[PLACES + t] * rows, 16), rows)
        column = column_from
        for k, target in enumerate(targets):
            wide = target.shape[1]
            copies.append(
                pltpu.make_async_copy(
                    piece.at[:, column : column + wide], target.at[at, :], signals.at[k, t]
                )
            )
            column += wide
    for copy in copies:
        copy.start()
    for copy in copies:
        copy.wait()


def hand_out(info, sources, pieces):
    rows = pieces[0].shape[0]
    for t, piece in enumerate(pieces):
        at = pl.ds(pl.multiple_of(info[PLACES + t] * rows, 16), rows)
        column = 0
        for source in sources:
            piece[:, column : column + source.shape[1]] = source[at, :].astype(piece.dtype)
            column += source.shape[1]


def token_rows(refs):
    return jnp.concatenate([r[k] for k in range(refs[0].shape[0]) for r in refs], axis=0)


def emit(partial, outs):
    each, part, _ = outs[0].shape
    for k in range(each):
        for r, out in enumerate(outs):
            at = (k * len(outs) + r) * part
            out[k] = partial[at : at + part].astype(out.dtype)


def slots_used(info, b, part, slot):
    column = lax.broadcasted_iota(jnp.int32, (1, slot), 1)
    position = (lax.div(column, part) ^ info[HEAD]) * part + lax.rem(column, part)
    return position < info[LENGTHS + b]


def keys_used(info, question, passages, part, slot, count_pass):
    return jnp.concatenate(
        [
            slots_used(info, k, part, slot) & (question[...] == k // count_pass)
            for k in passages
        ],
        axis=1,
    )


def call(
    body, info, stepped, fixed, out_stepped, out_fixed, scratch=(), flops=0, steps=1, near=False, least=LARGE, each=1
):
    def by_step(shape):
        last = shape[0] // each - 1
        return pl.BlockSpec((each, *shape[1:]), lambda b: (jnp.minimum(b, last),) + (0,) * (len(shape) - 1))

    def whole(a):
        if isinstance(a, Far):
            return pl.BlockSpec(memory_space=pltpu.HBM)
        if isinstance(a, Rider):
            return pl.BlockSpec(a.shape, lambda b: (a.index, 0, 0))
        index = (0, a.index) if type(a) is Columns else (0,) * len(a.shape)
        return pl.BlockSpec(a.shape, lambda b: index)

    counts = [len(stepped), len(fixed), len(out_stepped), len(out_fixed), len(scratch)]
    stops = np.cumsum(counts)

    def split(info_ref, *refs):
        body(info_ref, *(refs[e - c : e] for c, e in zip(counts, stops, strict=True)))

    def large(a):
        return not near and math.prod(a.shape) * a.dtype.itemsize >= least

    def given(a):
        array = a.array if isinstance(a, (Columns, Far, Rider)) else a
        far = large(a) or isinstance(a, Rider)
        return pltpu.with_memory_space_constraint(array, pltpu.HBM) if far else array

    def made(a):
        if isinstance(a, Later) or (large(a) and not isinstance(a, Near)):
            return pltpu.HBM(a.shape, a.dtype)
        return a.array if isinstance(a, Near) else a

    arrays = [*stepped, *fixed, *out_stepped, *out_fixed]
    moved = sum(math.prod(a.shape) * a.dtype.itemsize for a in arrays)
    return pl.pallas_call(
        split,
        grid=(steps,),
        in_specs=[
            pl.BlockSpec(memory_space=pltpu.SMEM),
            *(by_step(a.shape) for a in stepped),
            *(whole(a) for a in fixed),
        ],
        out_specs=[
            *(by_step(a.shape) for a in out_stepped),
            *(whole(a) for a in out_fixed),
        ],
        out_shape=[made(a) for a in (*out_stepped, *out_fixed)],
        scratch_shapes=list(scratch),
        compiler_params=pltpu.CompilerParams(
            dimension_semantics=("arbitrary",), vmem_limit_bytes=VMEM_LIMIT
        ),
        cost_estimate=pl.CostEstimate(
            flops=int(flops), bytes_accessed=int(moved), transcendentals=0
        ),
    )(info, *(given(a) for a in (*stepped, *fixed)))


class Columns:
    def __init__(self, array, width, index):
        self.array, self.index, self.dtype = array, index, array.dtype
        self.shape = (array.shape[0], width)


class Near(Columns):
    def __init__(self, array):
        self.array, self.shape, self.dtype = array, array.shape, array.dtype


class Later(Near):
    pass


class Rider:
    def __init__(self, array, index):
        self.array, self.index, self.dtype = array, index, array.dtype
        self.shape = (1, *array.shape[1:])


class Far:
    def __init__(self, array):
        self.array, self.shape, self.dtype = array, array.shape, array.dtype


def like(shape, dtype):
    return jax.ShapeDtypeStruct(tuple(shape), dtype)


def by_rows(fn, info, stepped, fixed, dtypes, gain=False, riders=None, kept=True):
    steps, _, width = stepped[0].shape
    count = 0 if riders is None else 1
    alone = [like(stepped[0].shape, d) for d in dtypes]
    outs = alone if riders is None or kept else alone[:-1]
    more = 0 if riders is None else riders.shape[0]
    together = [like((steps + count, *stepped[0].shape[1:]), dtypes[-1])] if more else []

    def body(info_ref, ins, whole, outs, sums, _):
        b = pl.program_id(0)
        if more:
            whole, rows = whole[:-1], whole[-1]

        @pl.when(b < steps)
        def _():
            results = fn(*(r[0].astype(f32) for r in ins), *(r[...] for r in whole))
            for out, value in zip(outs, results, strict=False):
                out[0] = value.astype(out.dtype)
            if more:
                outs[-1][0] = results[len(dtypes) - 1].astype(outs[-1].dtype)
            for total in sums:
                found = jnp.sum(results[-1], axis=0, keepdims=True)

                @pl.when(b == 0)
                def _():
                    total[...] = found

                @pl.when(b > 0)
                def _():
                    total[...] += found

        if more:

            @pl.when(b == steps)
            def _():
                outs[-1][0, :more, :] = rows[...]

    return call(
        body,
        info,
        stepped,
        [*fixed, riders] if more else fixed,
        [*outs, *together],
        [like((1, width), f32)] * gain,
        flops=10 * math.prod(stepped[0].shape),
        steps=steps + count,
        near=True,
    )


def partial_rows(blocks, part, width):
    return [Near(like((blocks, part, width), d)) for d in (f32, bf16, f32, bf16)]


def piece_shapes(rows, columns):
    return [Later(like((rows, columns), d)) for d in (f32, *[bf16] * 7)]


def attention_scratch(width, size, pieces):
    return [
        *(pltpu.VMEM((width, k * size), bf16) for k in (3, 1, 4)),
        pltpu.SemaphoreType.DMA((1, len(pieces))),
    ]


def encoder_attention(info, normed, pieces):
    blocks, part, width = normed[0].shape
    slot = part * len(normed)
    size = pieces[0].shape[1] // 4
    count = size // HDIM

    def body(info, rows, pieces, outs, _, scratch):
        qkv, probs, context = outs[:3]
        w_in, w_out, together, signals = scratch
        b = pl.program_id(0)

        @pl.when(b == 0)
        def _():
            assemble(info, pieces, (together,), signals)
            w_in[...] = together[:, : 3 * size]
            w_out[...] = together[:, 3 * size :]

        qkv[0] = dot(token_rows(rows), w_in[...]).astype(bf16)
        allowed = slots_used(info, b, part, slot)
        query, keys, vals = head_parts(qkv[0], 3)
        found = []
        for k, scores in enumerate([dot_t(q * SCALE, t) for q, t in zip(query, keys, strict=True)]):
            scores = jnp.where(allowed, scores, masked_score)
            spread_out = jnp.exp(scores - jnp.max(scores, axis=-1, keepdims=True))
            inverse = 1.0 / jnp.sum(spread_out, axis=-1, keepdims=True)
            found.append((spread_out * inverse).astype(bf16))
            probs[0, k] = found[-1]
        found = [dot(w, v) for w, v in zip(found, vals, strict=True)]
        context[0] = jnp.concatenate(found, axis=1).astype(bf16)
        emit(dot_t(context[0], w_out[...]), outs[3:])

    return call(
        body,
        info,
        normed,
        [Far(p) for p in pieces],
        [
            like((blocks, slot, 3 * size), bf16),
            like((blocks, count, slot, slot), bf16),
            like((blocks, slot, size), bf16),
            *partial_rows(blocks, part, width),
        ],
        [],
        attention_scratch(width, size, pieces),
        flops=2 * blocks * slot * (width * size * 4 + 8 * slot * size),
        steps=blocks,
    )


def encoder_attention_back(info, grads, normed, qkv, probs, context, pieces, gains):
    blocks, part, width = normed[0].shape
    slot = part * len(normed)
    size = context.shape[2]

    def body(info, stepped, fixed, outs, ends, scratch):
        grad_refs, normed_refs = stepped[:4], stepped[4:8]
        qkv, probs, context = stepped[8:]
        weight_pieces, gains = fixed[:-1], fixed[-1]
        pieces, gain_out = ends[:-1], ends[-1]
        w_in, w_out, together, signals, total_in, total_out, moved = scratch
        b = pl.program_id(0)

        @pl.when(b == 0)
        def _():
            assemble(info, weight_pieces, (together,), signals)
            w_in[...] = together[:, : 3 * size]
            w_out[...] = together[:, 3 * size :]
            total_in[...] = jnp.zeros_like(total_in)
            total_out[...] = jnp.zeros_like(total_out)
            gain_out[...] = jnp.zeros_like(gain_out)

        grad = token_rows(grad_refs)
        rows = token_rows(normed_refs)
        dcontext = dot(grad, w_out[...]).astype(bf16)
        query, keys, vals = head_parts(qkv[0], 3)
        cuts = head_parts(dcontext, 1)[0]
        backs = [dot_t(c, v) for c, v in zip(cuts, vals, strict=True)]
        dvals = [t_dot(probs[0, k], c) for k, c in enumerate(cuts)]
        lows = []
        for k, back in enumerate(backs):
            wide = probs[0, k].astype(f32)
            low = wide * (back - jnp.sum(wide * back, axis=-1, keepdims=True))
            lows.append(low.astype(bf16))
        dquery = [dot(d, t) * SCALE for d, t in zip(lows, keys, strict=True)]
        dkeys = [t_dot(d, q) * SCALE for d, q in zip(lows, query, strict=True)]
        moved[...] = jnp.concatenate([*dquery, *dkeys, *dvals], axis=1).astype(bf16)
        partial = dot_t(moved[...], w_in[...])
        emit(partial, outs)
        gain_out[...] += jnp.sum(partial * rows.astype(f32), axis=0, keepdims=True) / gains[0:1, :]
        total_in[...] += t_dot(rows, moved[...])
        total_out[...] += t_dot(grad, context[0])

        @pl.when(b == blocks - 1)
        def _():
            hand_out(info, (total_in, total_out), pieces)

    results = call(
        body,
        info,
        [*grads, *normed, qkv, probs, context],
        [*(Far(p) for p in pieces), gains],
        partial_rows(blocks, part, width),
        [*piece_shapes(width // 8, 4 * size), like((1, width), f32)],
        [
            *attention_scratch(width, size, pieces),
            pltpu.VMEM((width, 3 * size), f32),
            pltpu.VMEM((width, size), f32),
            pltpu.VMEM((slot, 3 * size), bf16),
        ],
        flops=2 * blocks * slot * (width * size * 8 + 20 * slot * size),
        steps=blocks,
    )
    return results[:4], results[4:12], results[12]


def ffn_scratch(width, hidden, pieces):
    return [
        *[pltpu.VMEM((width, hidden), bf16)] * 2,
        pltpu.SemaphoreType.DMA((2, len(pieces))),
    ]


def encoder_ffn(info, normed, pieces, hidden):
    blocks, part, width = normed[0].shape
    slot = part * len(normed)

    def body(info, rows, pieces, outs, _, scratch):
        active, slope = outs[:2]
        w_inner, w_outer, signals = scratch

        @pl.when(pl.program_id(0) == 0)
        def _():
            assemble(info, pieces, (w_inner, w_outer), signals)

        value, bend = gelu_both(dot(token_rows(rows), w_inner[...]))
        low = value.astype(bf16)
        active[...] = low.reshape(active.shape)
        slope[...] = bend.astype(bf16).reshape(slope.shape)
        emit(dot_t(low, w_outer[...]), outs[2:])

    return call(
        body,
        info,
        normed,
        [Far(p) for p in pieces],
        [*[like((blocks, slot, hidden), bf16)] * 2, *partial_rows(blocks, part, width)],
        [],
        ffn_scratch(width, hidden, pieces),
        flops=4 * blocks * slot * width * hidden,
        steps=blocks // 2,
        each=2,
    )


def encoder_ffn_back(info, grads, slope, pieces):
    blocks, (_, part, width) = slope.shape[0], grads[0].shape
    slot = part * len(grads)
    hidden = slope.shape[2]

    def body(info, stepped, pieces, outs, ends, scratch):
        dinner = outs[0]
        w_inner, w_outer, signals = scratch

        @pl.when(pl.program_id(0) == 0)
        def _():
            assemble(info, pieces, (w_inner, w_outer), signals)

        back = dot(token_rows(stepped[:4]), w_outer[...])
        low = (back * stepped[4][...].reshape(back.shape).astype(f32)).astype(bf16)
        dinner[...] = low.reshape(dinner.shape)
        emit(dot_t(low, w_inner[...]), outs[1:])

    return call(
        body,
        info,
        [*grads, slope],
        [Far(p) for p in pieces],
        [like((blocks, slot, hidden), bf16), *partial_rows(blocks, part, width)],
        [],
        ffn_scratch(width, hidden, pieces),
        flops=4 * blocks * slot * width * hidden,
        steps=blocks // 2,
        each=2,
    )


def weight_grads(info, pairs, more=(), cut=True):
    blocks, (_, part, width) = pairs[0][1].shape[0], pairs[0][0][0].shape
    widths = [right.shape[2] for _, right in pairs]

    def body(info, stepped, more, __, ends, totals):
        totals = totals if cut else ends
        for k, total in enumerate(totals):
            left, right = token_rows(stepped[5 * k : 5 * k + 4]), stepped[5 * k + 4]
            total[...] = t_dot(left, right[...].reshape(left.shape[0], total.shape[1]))
        if cut:
            hand_out(info, (*totals, *more), ends)

    return call(
        body,
        info,
        [a for left, right in pairs for a in (*left, right)],
        more,
        [],
        piece_shapes(width // 8, sum(widths) + sum(m.shape[1] for m in more))
        if cut
        else [like((width, w), f32) for w in widths],
        [pltpu.VMEM((width, w), f32) for w in widths] if cut else [],
        flops=2 * blocks * part * 4 * width * sum(widths),
        each=blocks,
    )


def finish(info, terms, widths, turned):
    terms = [part(t) for t in terms]
    rows = terms[0].array.shape[0]
    shapes = [(w, rows) if t else (rows, w) for w, t in zip(widths, turned, strict=True)]

    def body(info, _, ins, __, outs, ___):
        total = terms[0].read(ins[0])
        for term, ref in zip(terms[1:], ins[1:], strict=True):
            total = total + term.read(ref).astype(f32)
        column = 0
        for out, wide, turn in zip(outs, widths, turned, strict=True):
            found = total[:, column : column + wide]
            out[...] = found.T if turn else found
            column += wide

    return call(body, info, [], [t.array for t in terms], [], [like(s, f32) for s in shapes])


def cross_forward(info, states, pieces, column_from, decoder, own_question, count_q, count_pass):
    rows_in, terms, gains = decoder
    blocks = count_q * count_pass
    _, part, width = states[0].shape
    slot = part * len(states)
    rows_dec = rows_in.shape[0]
    size = (pieces[0].shape[1] - column_from) // 4
    steps = 2

    def body(info, rows, fixed, outs, ends, scratch):
        pieces, question = fixed[: len(pieces_given)], fixed[-1]
        rows_in, *terms, gains = fixed[len(pieces_given) : -1]
        after_self, normed, queries, w_query, w_output, stats, weight = ends
        held, asked, signals = scratch
        b = pl.program_id(0)

        @pl.when(b == 0)
        def _():
            assemble(info, pieces, (weight, asked), signals, column_from)
            w_query[...] = asked[:, :size]
            w_output[...] = asked[:, size:]
            after_self[...] = rows_in[...].astype(f32) + summed(terms)
            normed[...] = norm_rows(after_self[...], gains[1:2, :]).astype(bf16)
            queries[...] = dot(normed[...], w_query[...]).astype(bf16)

        made = dot(token_rows(rows), weight[...]).astype(bf16)
        outs[0][...] = made.reshape(outs[0].shape)
        each = made.shape[0]
        held[pl.ds(pl.multiple_of(b * each, each), each), :] = made

        @pl.when(b == steps - 1)
        def _():
            allowed = keys_used(info, question, range(blocks), part, slot, count_pass)
            lane = lax.broadcasted_iota(jnp.int32, (rows_dec, HDIM), 1)
            keys, vals = head_parts(held[...], 2)
            asking = head_parts(queries[...], 1)[0]
            scores = [dot_t(q * SCALE, t) for q, t in zip(asking, keys, strict=True)]
            for k, score in enumerate(scores):
                score = jnp.where(allowed, score, masked_score)
                top = jnp.max(score, axis=-1, keepdims=True)
                spread_out = jnp.exp(score - top)
                total = jnp.sum(spread_out, axis=-1, keepdims=True)
                at = k * LANES
                stats[:, at : at + HDIM] = dot(spread_out.astype(bf16), vals[k])
                stats[:, at + HDIM : at + LANES] = jnp.where(lane == 0, top, total)

    pieces_given = pieces
    return call(
        body,
        info,
        states,
        [*(Far(p) for p in pieces), rows_in, *terms, gains, own_question],
        [like((blocks, slot, 2 * size), bf16)],
        [
            Later(like((rows_dec, width), f32)),
            Later(like((rows_dec, width), bf16)),
            like((rows_dec, size), bf16),
            Later(like((width, size), bf16)),
            like((width, size), bf16),
            like((rows_dec, size // HDIM * LANES), f32),
            like((width, 2 * size), bf16),
        ],
        [
            pltpu.VMEM((blocks * slot, 2 * size), bf16),
            pltpu.VMEM((width, 2 * size), bf16),
            pltpu.SemaphoreType.DMA((2, len(pieces))),
        ],
        flops=4 * blocks * slot * width * size,
        steps=steps,
        each=blocks // steps,
    )


def merged(first, second):
    lane = lax.broadcasted_iota(jnp.int32, (first.shape[0], HDIM), 1)
    found = []
    for at in range(0, first.shape[1], LANES):
        tops = [v[:, at + HDIM : at + HDIM + 1] for v in (first, second)]
        totals = [v[:, at + HDIM + 1 : at + HDIM + 2] for v in (first, second)]
        top = jnp.maximum(*tops)
        scales = [jnp.exp(t - top) for t in tops]
        total = totals[0] * scales[0] + totals[1] * scales[1]
        found.append(first[:, at : at + HDIM] * scales[0] + second[:, at : at + HDIM] * scales[1])
        found.append(jnp.where(lane == 0, top, total))
    return jnp.concatenate(found, axis=1)


def in_order(info, bits, own, other):
    later = (info[BLK] & bits) != 0
    return jnp.where(later, other, own), jnp.where(later, own, other)


def merge(info, own, other, bits):
    def body(info, _, ins, __, outs, ___):
        outs[0][...] = merged(*in_order(info, bits, ins[0][...], ins[1][...]))

    return call(body, info, [], [own, other], [], [like(own.shape, f32)])[0]


def cross_out(info, stats, bits, w_output):
    rows, columns = stats[0].shape
    size = columns // LANES * HDIM
    width = w_output.shape[0]

    def body(info, _, ins, __, outs, scratch):
        w_output = ins[-1]
        out, log_total, context, own, sent = outs
        values = [r[...] for r in ins[:-1]]
        near = merged(*in_order(info, bits[0], *values[:2]))
        far = merged(*in_order(info, bits[0], *values[2:]))
        stats = merged(*in_order(info, bits[1], near, far))
        log_total[...] = jnp.zeros_like(log_total)
        for k, at in enumerate(heads_in(size)):
            base = k * LANES
            top = stats[:, base + HDIM : base + HDIM + 1]
            total = stats[:, base + HDIM + 1 : base + HDIM + 2]
            out[:, at] = stats[:, base : base + HDIM] / total
            log_total[:, k : k + 1] = top + jnp.log(total)
        context[...] = out[...].astype(bf16)
        own[...] = dot_t(context[...], w_output[...])
        sent[...] = own[...].astype(bf16)

    return call(
        body,
        info,
        [],
        [*stats, w_output],
        [],
        [
            like((rows, size), f32),
            like((rows, LANES), f32),
            Later(like((rows, size), bf16)),
            like((rows, width), f32),
            like((rows, width), bf16),
        ],
        flops=2 * rows * size * width,
    )


def cross_back(info, key_vals, inputs, own_question, count_pass, slot, part):
    cotangent, after_cross, terms, gains, w_output, out, log_total, queries, weight = inputs
    blocks = key_vals.shape[0]
    rows_dec, width = after_cross.shape
    size = queries.shape[1]

    def body(info, stepped, fixed, outs, ends, scratch):
        cotangent, after_cross, own, r1, r2, r3, gains, w_output, out, log_total, queries, weight, question = fixed
        key_vals = stepped[0]
        dkey_vals = outs[0]
        dcross, dcross_low, gain_out, dqueries = ends
        total = summed((own, r1, r2, r3))
        back, gain_out[...] = norm_back(after_cross[...], gains[2:3, :], total)
        dcross[...] = cotangent[...].astype(f32) + back
        dcross_low[...] = dcross[...].astype(bf16)
        dcontext = dot(dcross_low[...], w_output[...]).astype(bf16)
        allowed = keys_used(info, question, range(blocks), part, slot, count_pass)
        keys, vals = head_parts(key_vals[...].reshape(blocks * slot, 2 * size), 2)
        asking = head_parts(queries[...], 1)[0]
        cuts = head_parts(dcontext, 1)[0]
        outs_of = head_parts(out[...], 1)[0]
        scores = [dot_t(q * SCALE, t) for q, t in zip(asking, keys, strict=True)]
        backs = [dot_t(c, v) for c, v in zip(cuts, vals, strict=True)]
        probs, lows = [], []
        for k, score in enumerate(scores):
            row_term = jnp.sum(cuts[k].astype(f32) * outs_of[k], axis=-1, keepdims=True)
            score = jnp.where(allowed, score, masked_score)
            probs.append(jnp.exp(score - log_total[:, k : k + 1]))
            lows.append((probs[k] * (backs[k] - row_term)).astype(bf16))
        dvals = [t_dot(p.astype(bf16), c) for p, c in zip(probs, cuts, strict=True)]
        dkeys = [t_dot(d, q) * SCALE for d, q in zip(lows, asking, strict=True)]
        found = [dot(d, t) * SCALE for d, t in zip(lows, keys, strict=True)]
        dqueries[...] = jnp.concatenate(found, axis=1)
        made = jnp.concatenate([*dkeys, *dvals], axis=1).astype(bf16)
        dkey_vals[...] = made.reshape(dkey_vals.shape)
        emit(dot_t(made, weight[...]), outs[1:])

    return call(
        body,
        info,
        [key_vals],
        [cotangent, after_cross, *terms, gains, w_output, out, log_total, queries, weight, own_question],
        [like(key_vals.shape, bf16), *partial_rows(blocks, part, width)],
        [
            Later(like((rows_dec, width), f32)),
            Later(like((rows_dec, width), bf16)),
            Later(like((rows_dec, width), f32)),
            like((rows_dec, size), f32),
        ],
        flops=4 * blocks * slot * width * size,
        each=blocks,
    )


def summed(refs):
    count = refs[0].shape[0]

    def rows(ref):
        return ref[...] if len(ref.shape) == 2 else ref[0, :count, :]

    terms = [rows(ref).astype(f32) for ref in refs[1:]]
    total = refs[0][...]
    for term in terms:
        total = total + term
    return total


def decoder_self(info, rows, gains, pieces, column_from, size, order):
    count, width = rows.shape

    def body(info, _, ins, __, outs, scratch):
        rows, gains, order_q, order_k = ins[:4]
        normed, qkv, probs, context, own, sent, weight = outs
        assemble(info, ins[4:], (weight,), scratch[0], column_from)
        normed[...] = norm_rows(rows[...].astype(f32), gains[0:1, :]).astype(bf16)
        qkv[...] = dot(normed[...], weight[:, : 3 * size]).astype(bf16)
        query_at, key_at = order_q[...], order_k[...]
        same = lax.div(query_at, 1000) == lax.div(key_at, 1000)
        allowed = same & (key_at <= query_at) & (key_at >= 0) & (query_at >= 0)
        for k, at in enumerate(heads_in(size)):
            query, keys, vals = (qkv[:, j * size + at.start : j * size + at.stop] for j in range(3))
            scores = jnp.where(allowed, dot_t(query, keys) * SCALE, masked_score)
            spread_out = jnp.exp(scores - jnp.max(scores, axis=-1, keepdims=True))
            share_out = spread_out / jnp.sum(spread_out, axis=-1, keepdims=True)
            share_out = jnp.where(allowed, share_out, 0.0)
            probs[k] = share_out
            context[:, at] = dot(share_out.astype(bf16), vals).astype(bf16)
        own[...] = dot_t(context[...], weight[:, 3 * size :])
        sent[...] = own[...].astype(bf16)

    return call(
        body,
        info,
        [],
        [rows, gains, *order, *(Far(p) for p in pieces)],
        [],
        [
            Later(like((count, width), bf16)),
            Later(like((count, 3 * size), bf16)),
            Later(like((size // HDIM, count, count), f32)),
            Later(like((count, size), bf16)),
            like((count, width), f32),
            like((count, width), bf16),
            Later(like((width, 4 * size), bf16)),
        ],
        [pltpu.SemaphoreType.DMA((1, len(pieces)))],
        flops=2 * count * width * size * 4,
    )


def decoder_back(info, cotangent, pieces):
    count, width = cotangent.shape
    hidden = pieces[0].shape[1] // 2

    def body(info, _, ins, __, outs, scratch):
        w_inner, w_outer, back = outs
        assemble(info, ins[1:], (w_inner, w_outer), scratch[0])
        back[...] = dot(ins[0][...], w_outer[...])

    return call(
        body,
        info,
        [],
        [cotangent, *(Far(p) for p in pieces)],
        [],
        [*[like((width, hidden), bf16)] * 2, like((count, hidden), f32)],
        [pltpu.SemaphoreType.DMA((2, len(pieces)))],
        flops=2 * count * width * hidden,
    )


def decoder_ffn(info, after_self, terms, back, gains, w_inner):
    count, width = after_self.shape
    hidden = w_inner.shape[1]

    def body(info, _, ins, __, outs, scratch):
        after_self, own, r1, r2, r3, back, gains, w_inner = ins
        after_cross, normed, active, dinner, own_back, sent_back = outs
        after_cross[...] = after_self[...] + summed((own, r1, r2, r3))
        normed[...] = norm_rows(after_cross[...], gains[2:3, :]).astype(bf16)
        value, slope = gelu_both(dot(normed[...], w_inner[...]))
        active[...] = value.astype(bf16)
        dinner[...] = (slope * back[...]).astype(bf16)
        own_back[...] = dot_t(dinner[...], w_inner[...])
        sent_back[...] = own_back[...].astype(bf16)

    return call(
        body,
        info,
        [],
        [after_self, *terms, back, gains, w_inner],
        [],
        [
            like((count, width), f32),
            Later(like((count, width), bf16)),
            Later(like((count, hidden), bf16)),
            Later(like((count, hidden), bf16)),
            like((count, width), f32),
            like((count, width), bf16),
        ],
        flops=4 * count * width * hidden,
    )


def rows_back(info, terms, weight):
    (count, size), width = terms[0].shape, weight.shape[0]

    def body(info, _, ins, __, outs, scratch):
        low, own, sent = outs
        total = ins[0][...]
        for term in ins[1:-1]:
            total = total + term[...]
        low[...] = total.astype(bf16)
        own[...] = dot_t(low[...], ins[-1][...])
        sent[...] = own[...].astype(bf16)

    return call(
        body,
        info,
        [],
        [*terms, weight],
        [],
        [
            Later(like((count, size), bf16)),
            like((count, width), f32),
            like((count, width), bf16),
        ],
        flops=2 * count * width * size,
    )


def decoder_self_back(
    info, dcross, after_self, terms, gains, weight, qkv, probs
):
    count, width = after_self.shape
    size = weight.shape[1] // 4

    def body(info, _, ins, __, outs, scratch):
        dcross, after_self, *terms, gains, weight, qkv, probs = ins
        dself, dself_low, gain_rows, moved, own_back, sent_back = outs
        back, gain_rows[...] = norm_back(after_self[...], gains[1:2, :], summed(terms))
        dself[...] = dcross[...] + back
        dself_low[...] = dself[...].astype(bf16)
        dcontext = dot(dself_low[...], weight[:, 3 * size :]).astype(bf16)
        for k, at in enumerate(heads_in(size)):
            query, keys, vals = (qkv[:, j * size + at.start : j * size + at.stop] for j in range(3))
            share_out = probs[k]
            dprobs = dot_t(dcontext[:, at], vals)
            dscores = share_out * (dprobs - jnp.sum(share_out * dprobs, axis=-1, keepdims=True))
            dscores = dscores.astype(bf16)
            found = (
                dot(dscores, keys) * SCALE,
                t_dot(dscores, query) * SCALE,
                t_dot(share_out.astype(bf16), dcontext[:, at]),
            )
            for j, term in enumerate(found):
                moved[:, j * size + at.start : j * size + at.stop] = term.astype(bf16)
        own_back[...] = dot_t(moved[...], weight[:, : 3 * size])
        sent_back[...] = own_back[...].astype(bf16)

    return call(
        body,
        info,
        [],
        [dcross, after_self, *terms, gains, weight, qkv, probs],
        [],
        [
            like((count, width), f32),
            Later(like((count, width), bf16)),
            like((count, width), f32),
            Later(like((count, 3 * size), bf16)),
            like((count, width), f32),
            like((count, width), bf16),
        ],
        flops=2 * count * width * size * 8,
    )


def decoder_ends(
    info, rows, dself, terms, gains, after_cross, out_terms, gain_rows, gain_sums, dec_own
):
    count, width = dself.shape

    def body(info, _, ins, __, outs, scratch):
        rows, dself, after_cross, gains = ins[:4]
        three, four, zero, one = ins[-4:]
        grad, states, found = outs
        total, out_total = summed(ins[4:8]), summed(ins[8:12])
        back, two = norm_back(rows[...].astype(f32), gains[0:1, :], total)
        grad[...] = dself[...] + back
        states[...] = (after_cross[...] + out_total).astype(bf16)
        row = lax.div(lax.broadcasted_iota(jnp.int32, (count, 1), 0), dec_own)
        mine = (row == info[HEAD]) & (info[BLK] == 0)
        found[0:1, :] = zero[...]
        found[1:2, :] = one[...]
        for k, values in enumerate((two, three[...], four[...])):
            found[2 + k : 3 + k, :] = jnp.sum(jnp.where(mine, values, 0.0), axis=0, keepdims=True)

    return call(
        body,
        info,
        [],
        [rows, dself, after_cross, gains, *terms, *out_terms, *gain_rows, *gain_sums],
        [],
        [like((count, width), f32), like((count, width), bf16), like((5, width), f32)],
    )


def decoder_weight_grads(info, own, pairs_in, pairs_out):
    count, width = pairs_in[0][0].shape

    def body(info, _, ins, __, outs, scratch):
        row = lax.broadcasted_iota(jnp.int32, (own, width), 0) + info[BLK] * own
        column = lax.broadcasted_iota(jnp.int32, (own, width), 1)
        pick = jnp.where(row == column, 1.0, 0.0).astype(bf16)
        outs, ins = iter(outs), iter(ins)
        for _, _, arrays in pairs_in:
            left, right = next(ins)[...], next(ins)[...]
            found = t_dot(dot_t(left, pick).astype(bf16), right)
            wide = found.shape[1] // arrays
            for k in range(arrays):
                next(outs)[...] = found[:, k * wide : (k + 1) * wide]
        for _ in pairs_out:
            left, right = next(ins)[...], next(ins)[...]
            next(outs)[...] = t_dot(left, dot_t(right, pick).astype(bf16))

    outs = [like((own, r.shape[1] // n), f32) for _, r, n in pairs_in for _ in range(n)]
    outs += [like((l.shape[1], own), f32) for l, _ in pairs_out]
    flat = [a for pair in pairs_in for a in pair[:2]] + [a for pair in pairs_out for a in pair]
    return call(body, info, [], flat, [], outs, flops=2 * count * own * width * 10, least=0)


def shards(
    encoder_input,
    passage_lengths,
    decoder_input,
    encoder_query,
    encoder_key,
    encoder_value,
    encoder_output,
    encoder_inner,
    encoder_outer,
    decoder_query,
    decoder_key,
    decoder_value,
    decoder_output,
    cross_query,
    cross_key,
    cross_value,
    cross_output,
    decoder_inner,
    decoder_outer,
    encoder_gains,
    decoder_gains,
    encoder_cotangent,
    decoder_cotangent,
):
    head, blk = lax.axis_index("head"), lax.axis_index("blk")
    blk_count, head_count = lax.axis_size("blk"), lax.axis_size("head")
    count_q, count_pass, part, width = encoder_input.shape
    blocks = count_q * count_pass
    slot = part * head_count
    own = width // blk_count
    if blk_count == 8:
        places = jnp.asarray(place_table(8))[blk]
    else:
        places = jnp.arange(8, dtype=jnp.int32)
    info = jnp.concatenate(
        [places, jnp.stack([head, blk]).astype(jnp.int32), passage_lengths.reshape(blocks)]
    )

    size, units = encoder_query.shape[1], encoder_inner.shape[1]
    inputs = encoder_input.reshape(blocks, part, width)
    dec_part = decoder_input.shape[1]
    dec_own = count_q * dec_part
    dec_rows = dec_own * head_count
    filled = -(-dec_rows // 16) * 16

    attention = jnp.concatenate(
        [encoder_query, encoder_key, encoder_value, encoder_output.T], axis=1
    )
    attention, inputs = sync(attention, inputs)
    attention = fetch_step(fetch_start(attention), -1, 1)
    first = by_rows(
        lambda x, g: (norm_rows(x, g[0:1]),), info, [inputs], [encoder_gains], [bf16]
    )[0]
    attention, first = sync(attention, first)

    attention = fetch_step(attention, -2, 2)
    first_all = [first, swap(first, "head", 1), swap(first, "head", 2)]
    ffn = jnp.concatenate(
        [
            encoder_inner,
            encoder_outer.T,
            decoder_query,
            decoder_key,
            decoder_value,
            decoder_output.T,
            cross_key,
            cross_value,
            cross_query,
            cross_output.T,
        ],
        axis=1,
    )
    at_self, at_cross = 2 * units, 2 * units + 4 * size
    attention, ffn = sync(attention, ffn)

    attention = fetch_step(attention, -3, 3)
    pair = jnp.stack([decoder_input, decoder_cotangent]).reshape(2, dec_own, width)
    both = lax.all_gather(pair, "head", axis=1, tiled=True)
    both = jnp.pad(both, ((0, 0), (0, filled - dec_rows), (0, 0)))
    attention, first_all, ffn, both = sync(attention, first_all, ffn, both)

    attention, ffn = fetch_step(attention, -4), fetch_step(fetch_start(ffn), 1)
    first_all.append(swap(first_all[2], "head", 1))
    dec_ffn = jnp.concatenate([decoder_inner, decoder_outer.T], axis=1)
    attention, ffn, first_all, dec_ffn = sync(attention, ffn, first_all, dec_ffn)

    ffn = fetch_step(ffn, -1, 2)
    qkv, probs, context, *partial = encoder_attention(
        info, first_all, in_turn(attention)
    )
    partial, ffn = sync(partial, ffn)

    def to_core(partial):
        return [swap(partial[1], "head", 1), swap(partial[3], "head", 1)]

    def to_chip(partial, beside):
        return swap((partial[2] + beside[1].astype(f32)).astype(bf16), "head", 2)

    beside = to_core(partial)
    partial, beside, ffn = sync(partial, beside, ffn)
    across = to_chip(partial, beside)
    ffn = fetch_step(ffn, -2, 3)
    partial, beside, across, ffn = sync(partial, beside, across, ffn)

    def enter_ffn(x, a, b, c, g):
        hidden = x + a + b + c
        return hidden, norm_rows(hidden, g[1:2])

    hidden, second = by_rows(
        enter_ffn, info, [inputs, partial[0], beside[0], across], [encoder_gains], [f32, bf16]
    )
    def spread(rows):
        return [rows, swap(rows, "head", 1), swap(rows, "head", 2)]

    def riders(all_rows):
        return [Rider(rows, blocks) for rows in all_rows[1:]]

    second, ffn, dec_ffn = sync(second, ffn, dec_ffn)
    second_all = spread(second)
    ffn = fetch_step(ffn, -3, 4)
    second_all, ffn, dec_ffn = sync(second_all, ffn, dec_ffn)
    dec_ffn = fetch_step(fetch_start(dec_ffn), -1, 1)
    second_all.append(swap(second_all[2], "head", 1))
    second_all, ffn = sync(second_all, ffn)
    ffn = in_turn(ffn)

    active, slope, *partial = encoder_ffn(info, second_all, ffn, units)
    partial, dec_ffn = sync(partial, dec_ffn)
    beside = to_core(partial)
    partial, beside, both, dec_ffn = sync(partial, beside, both, dec_ffn)
    dec_in, cotangent = both[0], both[1]

    index = np.arange(filled)
    question = (index % dec_own) // dec_part
    position = index // dec_own * dec_part + index % dec_part
    order = np.where(index < dec_rows, question * 1000 + position, -1).astype(np.int32)
    order = (jnp.asarray(order[:, None]), jnp.asarray(order[None, :]))
    question = jnp.asarray(question[:, None].astype(np.int32))

    across = to_chip(partial, beside)
    dec_ffn = fetch_step(dec_ffn, -2, 2)
    third, dec_qkv, dec_probs, dec_context, mine, sent, w_self = decoder_self(
        info, dec_in, decoder_gains, ffn, at_self, size, order
    )
    partial, beside, across, mine, sent, dec_ffn = sync(
        partial, beside, across, mine, sent, dec_ffn
    )
    states, states_sent = by_rows(
        lambda h, a, b, c: (h + a + b + c,),
        info,
        [hidden, partial[0], beside[0], across],
        [],
        [bf16],
        riders=sent,
    )
    states_sent, dec_ffn = sync(states_sent, dec_ffn)
    states_all = spread(states_sent)
    dec_ffn = fetch_step(dec_ffn, -3, 3)
    states_all, dec_ffn = sync(states_all, dec_ffn)
    dec_ffn = fetch_step(dec_ffn, -4)
    states_all = sync(*states_all, swap(states_all[2], "head", 1))

    (
        key_vals,
        after_self,
        fourth,
        queries,
        w_cross_query,
        w_cross_output,
        stats,
        w_cross,
    ) = cross_forward(
        info,
        states_all,
        ffn,
        at_cross,
        (dec_in, [mine, *riders(states_all)], decoder_gains),
        question,
        count_q,
        count_pass,
    )
    bits = [1 << k for k in range((blk_count - 1).bit_length())]
    last_two = (bits[-2], bits[-1], bits[-2] + bits[-1])
    for k in bits[:-2]:
        stats = merge(info, stats, swap(stats, "blk", k), k)
    stats, dec_ffn = sync(stats, dec_ffn)
    stats_all = [stats, *(swap(stats, "blk", k) for k in last_two)]
    w_dec_inner, w_dec_outer, outer_back = decoder_back(info, cotangent, in_turn(dec_ffn))
    stats_all, outer_back = sync(stats_all, outer_back)
    out, log_total, cross_context, mine, sent = cross_out(
        info, stats_all, bits[-2:], w_cross_output
    )
    after_cross, fifth, dec_active, dec_dinner, mine, sent = decoder_ffn(
        info, after_self, [mine, *share(sent)], outer_back, decoder_gains, w_dec_inner
    )
    dkey_vals, *rest = cross_back(
        info,
        key_vals,
        (
            cotangent,
            after_cross,
            [mine, *share(sent)],
            decoder_gains,
            w_cross_output,
            out,
            log_total,
            queries,
            w_cross,
        ),
        question,
        count_pass,
        slot,
        part,
    )
    partial, (dcross, dcross_low, gain_four, dqueries) = rest[:4], rest[4:]

    def some(value, which):
        for k in which:
            value = value + swap(value, "blk", k)
        return value

    partial, dqueries, dkey_vals = sync(partial, dqueries, dkey_vals)
    beside = to_core(partial)
    partial, beside, dkey_vals, dqueries = sync(partial, beside, dkey_vals, dqueries)
    across = to_chip(partial, beside)
    dqueries = some(dqueries, bits[:-1])
    cross_sum = weight_grads(info, [(states_all, dkey_vals)], cut=False)[0]
    _, out_mine, out_sent = rows_back(info, [dec_active], w_dec_outer)
    partial, beside, across, cross_sum, dqueries, out_sent = sync(
        partial, beside, across, cross_sum, dqueries, out_sent
    )

    def enter_back(cot, a, b, c):
        grad = cot + a + b + c
        return grad, grad

    dstates, dstates_low = by_rows(
        enter_back,
        info,
        [encoder_cotangent.reshape(blocks, part, width), partial[0], beside[0], across],
        [],
        [f32, bf16],
        riders=out_sent,
        kept=False,
    )
    dstates_low, cross_sum, dqueries = sync(dstates_low, cross_sum, dqueries)
    dstates_all = spread(dstates_low)
    terms = [dqueries, swap(dqueries, "blk", bits[-1])]
    dqueries, mine, sent = rows_back(info, terms, w_cross_query)
    dstates_all, sent = sync(dstates_all, sent)
    dstates_all.append(swap(dstates_all[2], "head", 1))
    dstates_all, sent = sync(dstates_all, sent)
    out_terms = [out_mine, *riders(dstates_all)]
    dinner, *partial = encoder_ffn_back(info, dstates_all, slope, ffn)
    terms = [mine, *share(sent)]
    partial, dinner, terms = sync(partial, dinner, terms)
    beside = to_core(partial)
    partial, beside, dinner, dstates_all = sync(partial, beside, dinner, dstates_all)
    across = to_chip(partial, beside)
    dself, dself_low, gain_three, dself_qkv, own_back, sent_back = decoder_self_back(
        info,
        dcross,
        after_self,
        terms,
        decoder_gains,
        w_self,
        dec_qkv,
        dec_probs,
    )
    ffn_sums = weight_grads(
        info, [(second_all, dinner), (dstates_all, active)], [cross_sum]
    )
    partial, beside, across, ffn_sums, sent_back = sync(
        partial, beside, across, ffn_sums, sent_back
    )

    def middle_back(dy, h, a, b, c, g):
        back, gain_rows = norm_back(h, g[1:2], a + b + c)
        grad = dy + back
        return grad, grad, gain_rows

    dhidden, dhidden_low, gain_one = by_rows(
        middle_back,
        info,
        [dstates, hidden, partial[0], beside[0], across],
        [encoder_gains],
        [f32, bf16],
        gain=True,
        riders=sent_back,
        kept=False,
    )
    dhidden_low, ffn_sums = sync(dhidden_low, ffn_sums)
    dhidden_all = spread(dhidden_low)
    ffn_moving = reduce_step(info, (ffn_sums, None, 1))[0]
    dhidden_all, ffn_moving = sync(dhidden_all, ffn_moving)
    ffn_moving = reduce_step(info, (ffn_sums, ffn_moving, 2))[0]
    dhidden_all = sync(*dhidden_all, swap(dhidden_all[2], "head", 1))
    terms = [own_back, *riders(dhidden_all)]

    partial, sums, gain_zero = encoder_attention_back(
        info, dhidden_all, first_all, qkv, probs, context, in_turn(attention), encoder_gains
    )
    partial, sums, ffn_moving, gain_zero = sync(partial, sums, ffn_moving, gain_zero)
    ffn_moving, moving = reduce_step(info, (ffn_sums, ffn_moving, 3), (sums, None, 1))
    beside = to_core(partial)
    dec_grad, dec_states, gains = decoder_ends(
        info,
        dec_in,
        dself,
        terms,
        decoder_gains,
        after_cross,
        out_terms,
        [gain_three, gain_four],
        [gain_zero, gain_one],
        dec_own,
    )
    gains = gains + swap(gains, "head", 1)
    (
        grad_dec_query,
        grad_dec_key,
        grad_dec_value,
        grad_cross_query,
        grad_dec_inner,
        grad_dec_outer,
        grad_dec_output,
        grad_cross_output,
    ) = decoder_weight_grads(
        info,
        own,
        [
            (third, dself_qkv, 3),
            (fourth, dqueries, 1),
            (fifth, dec_dinner, 1),
            (cotangent, dec_active, 1),
        ],
        [(dec_context, dself_low), (cross_context, dcross_low)],
    )
    partial, beside, moving, gains, ffn_moving, grad_dec_query = sync(
        partial, beside, moving, gains, ffn_moving, grad_dec_query
    )

    def own_rows(values):
        return lax.dynamic_slice_in_dim(values, head * dec_own, dec_own, 0)

    ffn_moving, moving = reduce_step(info, (ffn_sums, ffn_moving, 4), (sums, moving, 2))
    across = to_chip(partial, beside)
    gains = gains + swap(gains, "head", 2)
    gains = some(gains, bits[:1])
    dec_states, dec_grad = own_rows(dec_states), own_rows(dec_grad)
    partial, beside, across, moving, gains, ffn_moving = sync(
        partial, beside, across, moving, gains, ffn_moving
    )

    def last_back(dh, x, a, b, c, g):
        return (dh + norm_back(x, g[0:1], a + b + c)[0],)

    moving = reduce_step(info, (sums, moving, 3))[0]
    gains = some(gains, bits[1:-1])
    input_grad = by_rows(
        last_back,
        info,
        [dhidden, inputs, partial[0], beside[0], across],
        [encoder_gains],
        [f32],
    )[0]
    moving, gains, input_grad, ffn_moving = sync(moving, gains, input_grad, ffn_moving)
    moving = reduce_step(info, (sums, moving, 4))[0]
    last = swap(gains, "blk", bits[-1])
    grad_inner, grad_outer, grad_cross_key, grad_cross_value = finish(
        info,
        reduce_terms(ffn_sums, ffn_moving),
        (units, units, size, size),
        (False,) * 4,
    )
    enc_gain_grads, dec_gain_grads = gains[:2] + last[:2], gains[2:] + last[2:]
    grad_query, grad_key, grad_value, grad_output = finish(
        info, reduce_terms(sums, moving), (size,) * 4, (False, False, False, True)
    )

    def dec_shape(values):
        return values.reshape(count_q, dec_part, width)

    return (
        states.reshape(encoder_input.shape),
        dec_shape(dec_states),
        input_grad.reshape(encoder_input.shape),
        dec_shape(dec_grad),
        grad_query,
        grad_key,
        grad_value,
        grad_output,
        grad_inner,
        grad_outer.T,
        grad_dec_query,
        grad_dec_key,
        grad_dec_value,
        grad_dec_output,
        grad_cross_query,
        grad_cross_key,
        grad_cross_value,
        grad_cross_output,
        grad_dec_inner,
        grad_dec_outer.T,
        enc_gain_grads,
        dec_gain_grads,
    )


def solution(mesh):
    placed = (
        P(None, "blk", "head", None),
        P(None, "blk"),
        P(None, "head", None),
        P("blk", "head"),
        P("blk", "head"),
        P("blk", "head"),
        P("head", "blk"),
        P("blk", "head"),
        P("head", "blk"),
        P("blk", "head"),
        P("blk", "head"),
        P("blk", "head"),
        P("head", "blk"),
        P("blk", "head"),
        P("blk", "head"),
        P("blk", "head"),
        P("head", "blk"),
        P("blk", "head"),
        P("head", "blk"),
        P(),
        P(),
        P(None, "blk", "head", None),
        P(None, "head", None),
    )
    return jax.shard_map(
        shards,
        mesh=mesh,
        in_specs=placed,
        out_specs=(placed[0], placed[2], placed[0], placed[2], *placed[3:19], P(), P()),
        check_vma=False,
    )
```

```python
import math

import jax
import jax.numpy as jnp
import numpy as np
from jax import lax
from jax.experimental import pallas as pl
from jax.experimental.pallas import tpu as pltpu
from jax.sharding import PartitionSpec as P

HDIM = 64
SCALE = HDIM ** (-0.5)
LANES = 128
EPS = 1e-06
VMEM_LIMIT = 24 * 1024 * 1024
LARGE = 1 << 19
masked_score = -1000000000.0
f32 = jnp.float32
bf16 = jnp.bfloat16

PLACES, HEAD, BLK, LENGTHS = 0, 8, 9, 10


def swap(value, axis, bits):
    size = lax.axis_size(axis)
    return lax.ppermute(value, axis, [(i, i ^ bits) for i in range(size)])


def sync(*values):
    return lax.optimization_barrier(values)


def share(value):
    return [swap(value, "head", k) for k in (1, 2, 3)]


def ring_order(count):
    return [*range(0, count, 2), *range(count - 1, 0, -2)]


OFFSETS = (0, -1, 1, -2, 2, -3, 3, -4)


def ring_steps(count):
    order = ring_order(count)
    forth = [(order[i], order[(i + 1) % count]) for i in range(count)]
    return forth, [(b, a) for a, b in forth]


def place_table(count):
    order = ring_order(count)
    at = {b: i for i, b in enumerate(order)}
    return np.array(
        [[order[(at[b] + o) % count] for o in OFFSETS] for b in range(count)], np.int32
    )


def gather_rows(own):
    return lax.all_gather(own, "blk", axis=0, tiled=True)


def fetch_start(own):
    if lax.axis_size("blk") == 8:
        return {0: own}
    return dict(zip(OFFSETS, jnp.split(gather_rows(own), 8, axis=0), strict=True))


def fetch_step(pieces, *offsets):
    count = lax.axis_size("blk")
    if count != 8:
        return pieces
    forth, back = ring_steps(count)
    more = {
        k: lax.ppermute(pieces[k + 1 if k < 0 else k - 1], "blk", forth if k < 0 else back)
        for k in offsets
    }
    return {**pieces, **more}


def in_turn(pieces):
    return [pieces[k] if k in pieces else pieces[-k] for k in OFFSETS]


@jax.tree_util.register_pytree_node_class
class Part:
    def __init__(self, array, start, width):
        self.array, self.start, self.width = array, start, width

    def tree_flatten(self):
        return (self.array,), (self.start, self.width)

    @classmethod
    def tree_unflatten(cls, places, arrays):
        return cls(*arrays, *places)

    def read(self, ref):
        return ref[:, self.start : self.start + self.width]


def part(value):
    return value if isinstance(value, Part) else Part(value, 0, value.shape[1])


def reduce_step(info, *rings, hold=None):
    count = lax.axis_size("blk")
    if count != 8:
        return [[] for _ in rings] + [hold]
    forth, back = ring_steps(count)
    plan = [[], []]
    for pieces, moving, step in rings:
        by = dict(zip(OFFSETS, pieces, strict=True))
        plan[0].append([*([] if step == 1 else [moving[0]]), by[(-4, 3, 2, 1)[step - 1]]])
        if step < 4:
            plan[1].append([*([] if step == 1 else [moving[1]]), by[(-3, -2, -1)[step - 1]]])
    plan = [p for p in plan if p]
    if len(rings) == 1 and rings[0][2] == 1:
        sent = [p[0][0] for p in plan]
    else:
        parts = [part(v) for p in plan for terms in p for v in terms]

        def body(info, _, ins, __, outs, ___):
            found = iter(zip(parts, ins, strict=True))
            for out, p in zip(outs, plan, strict=True):
                column = 0
                for terms in p:
                    values = [piece.read(ref) for piece, ref in (next(found) for _ in terms)]
                    total = values[0]
                    if len(values) == 2:
                        total = (total.astype(f32) + values[1].astype(f32)).astype(bf16)
                    out[:, column : column + total.shape[1]] = total
                    column += total.shape[1]

        rows = rings[0][0][0].shape[0]
        wide = [sum(part(terms[0]).width for terms in p) for p in plan]
        shapes = [like((rows, w), bf16) for w in wide]
        sent = call(body, info, [], [p.array for p in parts], [], [Near(v) for v in shapes], least=0)
    if hold is not None:
        sent, hold = sync(sent, hold)
    came = [lax.ppermute(v, "blk", way) for v, way in zip(sent, (forth, back), strict=False)]
    results, column = [], 0
    for k, (pieces, moving, step) in enumerate(rings):
        wide = pieces[0].shape[1]
        found = [Part(came[0], column, wide)]
        if step == 4:
            found.append(moving[1])
        else:
            before = sum(r[0][0].shape[1] for r in rings[:k] if r[2] < 4)
            found.append(Part(came[1], before, wide))
        results.append(found)
        column += wide
    return [*results, hold]


def reduce_terms(pieces, moving):
    if lax.axis_size("blk") != 8:
        everything = jnp.concatenate([p.astype(f32) for p in pieces], axis=0)
        return [lax.psum_scatter(everything, "blk", scatter_dimension=0, tiled=True)]
    return [pieces[0], *moving]


def dot(left, right, over=(1, 0)):
    return lax.dot_general(
        left, right, (((over[0],), (over[1],)), ((), ())), preferred_element_type=f32
    )


def dot_t(left, right):
    return dot(left, right, (1, 1))


def t_dot(left, right):
    return dot(left, right, (0, 0))


def norm_rows(values, gain):
    return values * lax.rsqrt(jnp.mean(values * values, axis=-1, keepdims=True) + EPS) * gain


def norm_back(values, gain, grad):
    inverse = lax.rsqrt(jnp.mean(values * values, axis=-1, keepdims=True) + EPS)
    unit = values * inverse
    weighted = grad * gain
    along = jnp.mean(weighted * unit, axis=-1, keepdims=True)
    return inverse * (weighted - unit * along), grad * unit


def gelu_both(values):
    root = math.sqrt(2.0 / math.pi)
    square = values * values
    bent = jnp.tanh(root * values * (1.0 + 0.044715 * square))
    half = 0.5 * (1.0 + bent)
    slope = half + 0.5 * values * (1.0 - bent * bent) * root * (1.0 + 3 * 0.044715 * square)
    return values * half, slope


def heads_in(width):
    return [slice(at, at + HDIM) for at in range(0, width, HDIM)]


def head_parts(values, count):
    size = values.shape[1] // count
    return [[values[:, j * size :][:, at] for at in heads_in(size)] for j in range(count)]


def assemble(info, pieces, targets, signals, column_from=0):
    rows = pieces[0].shape[0]
    copies = []
    for t, piece in enumerate(pieces):
        at = pl.ds(pl.multiple_of(info[PLACES + t] * rows, 16), rows)
        column = column_from
        for k, target in enumerate(targets):
            wide = target.shape[1]
            copies.append(
                pltpu.make_async_copy(
                    piece.at[:, column : column + wide], target.at[at, :], signals.at[k, t]
                )
            )
            column += wide
    for copy in copies:
        copy.start()
    for copy in copies:
        copy.wait()


def hand_out(info, sources, pieces):
    rows = pieces[0].shape[0]
    for t, piece in enumerate(pieces):
        at = pl.ds(pl.multiple_of(info[PLACES + t] * rows, 16), rows)
        column = 0
        for source in sources:
            piece[:, column : column + source.shape[1]] = source[at, :].astype(piece.dtype)
            column += source.shape[1]


def token_rows(refs):
    return jnp.concatenate([r[k] for k in range(refs[0].shape[0]) for r in refs], axis=0)


def emit(partial, outs):
    each, part, _ = outs[0].shape
    for k in range(each):
        for r, out in enumerate(outs):
            at = (k * len(outs) + r) * part
            out[k] = partial[at : at + part].astype(out.dtype)


def slots_used(info, b, part, slot):
    column = lax.broadcasted_iota(jnp.int32, (1, slot), 1)
    position = (lax.div(column, part) ^ info[HEAD]) * part + lax.rem(column, part)
    return position < info[LENGTHS + b]


def keys_used(info, question, passages, part, slot, count_pass):
    return jnp.concatenate(
        [
            slots_used(info, k, part, slot) & (question[...] == k // count_pass)
            for k in passages
        ],
        axis=1,
    )


def call(
    body, info, stepped, fixed, out_stepped, out_fixed, scratch=(), flops=0, steps=1, near=False, least=LARGE, each=1
):
    def by_step(shape):
        last = shape[0] // each - 1
        return pl.BlockSpec((each, *shape[1:]), lambda b: (jnp.minimum(b, last),) + (0,) * (len(shape) - 1))

    def whole(a):
        if type(a) is Far:
            return pl.BlockSpec(memory_space=pltpu.HBM)
        if isinstance(a, Rider):
            return pl.BlockSpec(a.shape, lambda b: (a.index, 0, 0))
        index = (0, a.index) if type(a) is Columns else (0,) * len(a.shape)
        return pl.BlockSpec(a.shape, lambda b: index)

    counts = [len(stepped), len(fixed), len(out_stepped), len(out_fixed), len(scratch)]
    stops = np.cumsum(counts)

    def split(info_ref, *refs):
        body(info_ref, *(refs[e - c : e] for c, e in zip(counts, stops, strict=True)))

    def large(a):
        return not near and math.prod(a.shape) * a.dtype.itemsize >= least

    def given(a):
        array = a.array if isinstance(a, (Columns, Far, Rider)) else a
        far = (large(a) and not isinstance(a, Close)) or isinstance(a, Rider)
        return pltpu.with_memory_space_constraint(array, pltpu.HBM) if far else array

    def made(a):
        if isinstance(a, Later) or (large(a) and not isinstance(a, Near)):
            return pltpu.HBM(a.shape, a.dtype)
        return a.array if isinstance(a, Near) else a

    arrays = [*stepped, *fixed, *out_stepped, *out_fixed]
    moved = sum(math.prod(a.shape) * a.dtype.itemsize for a in arrays)
    return pl.pallas_call(
        split,
        grid=(steps,),
        in_specs=[
            pl.BlockSpec(memory_space=pltpu.SMEM),
            *(by_step(a.shape) for a in stepped),
            *(whole(a) for a in fixed),
        ],
        out_specs=[
            *(by_step(a.shape) for a in out_stepped),
            *(whole(a) for a in out_fixed),
        ],
        out_shape=[made(a) for a in (*out_stepped, *out_fixed)],
        scratch_shapes=list(scratch),
        compiler_params=pltpu.CompilerParams(
            dimension_semantics=("arbitrary",), vmem_limit_bytes=VMEM_LIMIT
        ),
        cost_estimate=pl.CostEstimate(
            flops=int(flops), bytes_accessed=int(moved), transcendentals=0
        ),
    )(info, *(given(a) for a in (*stepped, *fixed)))


class Columns:
    def __init__(self, array, width, index):
        self.array, self.index, self.dtype = array, index, array.dtype
        self.shape = (array.shape[0], width)


class Near(Columns):
    def __init__(self, array):
        self.array, self.shape, self.dtype = array, array.shape, array.dtype


class Later(Near):
    pass


class Rider:
    def __init__(self, array, index):
        self.array, self.index, self.dtype = array, index, array.dtype
        self.shape = (1, *array.shape[1:])


class Far:
    def __init__(self, array):
        self.array, self.shape, self.dtype = array, array.shape, array.dtype


class Close(Far):
    pass


def like(shape, dtype):
    return jax.ShapeDtypeStruct(tuple(shape), dtype)


def by_rows(fn, info, stepped, fixed, dtypes, gain=False, riders=None, kept=True):
    steps, _, width = stepped[0].shape
    count = 0 if riders is None else 1
    alone = [like(stepped[0].shape, d) for d in dtypes]
    outs = alone if riders is None or kept else alone[:-1]
    more = 0 if riders is None else riders.shape[0]
    together = [like((steps + count, *stepped[0].shape[1:]), dtypes[-1])] if more else []

    def body(info_ref, ins, whole, outs, sums, _):
        b = pl.program_id(0)
        if more:
            whole, rows = whole[:-1], whole[-1]

        @pl.when(b < steps)
        def _():
            results = fn(*(r[0].astype(f32) for r in ins), *(r[...] for r in whole))
            for out, value in zip(outs, results, strict=False):
                out[0] = value.astype(out.dtype)
            if more:
                outs[-1][0] = results[len(dtypes) - 1].astype(outs[-1].dtype)
            for total in sums:
                found = jnp.sum(results[-1], axis=0, keepdims=True)

                @pl.when(b == 0)
                def _():
                    total[...] = found

                @pl.when(b > 0)
                def _():
                    total[...] += found

        if more:

            @pl.when(b == steps)
            def _():
                outs[-1][0, :more, :] = rows[...]

    return call(
        body,
        info,
        stepped,
        [*fixed, riders] if more else fixed,
        [*outs, *together],
        [like((1, width), f32)] * gain,
        flops=10 * math.prod(stepped[0].shape),
        steps=steps + count,
        near=True,
    )


def partial_rows(blocks, part, width):
    return [Near(like((blocks, part, width), d)) for d in (f32, bf16, f32, bf16)]


def piece_shapes(rows, columns):
    return [Later(like((rows, columns), d)) for d in (f32, *[bf16] * 7)]


def gathered(info, pieces, widths, column_from=0):
    rows, wide = pieces[0].shape[0] * len(pieces), sum(widths)

    def body(info, _, ins, __, outs, scratch):
        together, signals = scratch
        assemble(info, ins, (together,), signals, column_from)
        column = 0
        for out in outs:
            out[...] = together[:, column : column + out.shape[1]]
            column += out.shape[1]

    return call(
        body,
        info,
        [],
        [Far(p) for p in pieces],
        [],
        [Near(like((rows, w), bf16)) for w in widths],
        [pltpu.VMEM((rows, wide), bf16), pltpu.SemaphoreType.DMA((1, len(pieces)))],
    )


def attention_scratch(width, size, pieces):
    return [
        *(pltpu.VMEM((width, k * size), bf16) for k in (3, 1, 4)),
        pltpu.SemaphoreType.DMA((1, len(pieces))),
    ]


def encoder_attention(info, normed, pieces):
    blocks, part, width = normed[0].shape
    slot = part * len(normed)
    size = pieces[0].shape[1] // 4
    count = size // HDIM

    def body(info, rows, pieces, outs, _, scratch):
        qkv, probs, context = outs[:3]
        w_in, w_out, together, signals = scratch
        b = pl.program_id(0)

        @pl.when(b == 0)
        def _():
            assemble(info, pieces, (together,), signals)
            w_in[...] = together[:, : 3 * size]
            w_out[...] = together[:, 3 * size :]

        qkv[0] = dot(token_rows(rows), w_in[...]).astype(bf16)
        allowed = slots_used(info, b, part, slot)
        query, keys, vals = head_parts(qkv[0], 3)
        found = []
        for k, scores in enumerate([dot_t(q * SCALE, t) for q, t in zip(query, keys, strict=True)]):
            scores = jnp.where(allowed, scores, masked_score)
            spread_out = jnp.exp(scores - jnp.max(scores, axis=-1, keepdims=True))
            inverse = 1.0 / jnp.sum(spread_out, axis=-1, keepdims=True)
            found.append((spread_out * inverse).astype(bf16))
            probs[0, k] = found[-1]
        found = [dot(w, v) for w, v in zip(found, vals, strict=True)]
        context[0] = jnp.concatenate(found, axis=1).astype(bf16)
        emit(dot_t(context[0], w_out[...]), outs[3:])

    return call(
        body,
        info,
        normed,
        [Far(p) for p in pieces],
        [
            like((blocks, slot, 3 * size), bf16),
            like((blocks, count, slot, slot), bf16),
            like((blocks, slot, size), bf16),
            *partial_rows(blocks, part, width),
        ],
        [],
        attention_scratch(width, size, pieces),
        flops=2 * blocks * slot * (width * size * 4 + 8 * slot * size),
        steps=blocks,
    )


def encoder_attention_back(info, grads, normed, qkv, probs, context, weights, gains):
    blocks, part, width = normed[0].shape
    slot = part * len(normed)
    size = context.shape[2]

    def body(info, stepped, fixed, outs, ends, scratch):
        grad_refs, normed_refs = stepped[:4], stepped[4:8]
        qkv, probs, context = stepped[8:]
        w_in, w_out, gains = fixed
        pieces, gain_out = ends[:-1], ends[-1]
        total_in, total_out, moved = scratch
        b = pl.program_id(0)

        @pl.when(b == 0)
        def _():
            total_in[...] = jnp.zeros_like(total_in)
            total_out[...] = jnp.zeros_like(total_out)
            gain_out[...] = jnp.zeros_like(gain_out)

        grad = token_rows(grad_refs)
        rows = token_rows(normed_refs)
        dcontext = dot(grad, w_out[...]).astype(bf16)
        query, keys, vals = head_parts(qkv[0], 3)
        cuts = head_parts(dcontext, 1)[0]
        backs = [dot_t(c, v) for c, v in zip(cuts, vals, strict=True)]
        dvals = [t_dot(probs[0, k], c) for k, c in enumerate(cuts)]
        lows = []
        for k, back in enumerate(backs):
            wide = probs[0, k].astype(f32)
            low = wide * (back - jnp.sum(wide * back, axis=-1, keepdims=True))
            lows.append(low.astype(bf16))
        dquery = [dot(d, t) * SCALE for d, t in zip(lows, keys, strict=True)]
        dkeys = [t_dot(d, q) * SCALE for d, q in zip(lows, query, strict=True)]
        moved[...] = jnp.concatenate([*dquery, *dkeys, *dvals], axis=1).astype(bf16)
        partial = dot_t(moved[...], w_in[...])
        emit(partial, outs)
        gain_out[...] += jnp.sum(partial * rows.astype(f32), axis=0, keepdims=True) / gains[0:1, :]
        total_in[...] += t_dot(rows, moved[...])
        total_out[...] += t_dot(grad, context[0])

        @pl.when(b == blocks - 1)
        def _():
            hand_out(info, (total_in, total_out), pieces)

    results = call(
        body,
        info,
        [*grads, *normed, qkv, probs, context],
        [*(Close(w) for w in weights), gains],
        partial_rows(blocks, part, width),
        [*piece_shapes(width // 8, 4 * size), like((1, width), f32)],
        [
            pltpu.VMEM((width, 3 * size), f32),
            pltpu.VMEM((width, size), f32),
            pltpu.VMEM((slot, 3 * size), bf16),
        ],
        flops=2 * blocks * slot * (width * size * 8 + 20 * slot * size),
        steps=blocks,
    )
    return results[:4], results[4:12], results[12]


def ffn_scratch(width, hidden, pieces):
    return [
        *[pltpu.VMEM((width, hidden), bf16)] * 2,
        pltpu.SemaphoreType.DMA((2, len(pieces))),
    ]


def encoder_ffn(info, normed, pieces, hidden):
    blocks, part, width = normed[0].shape
    slot = part * len(normed)

    def body(info, rows, pieces, outs, _, scratch):
        active, slope = outs[:2]
        w_inner, w_outer, signals = scratch

        @pl.when(pl.program_id(0) == 0)
        def _():
            assemble(info, pieces, (w_inner, w_outer), signals)

        value, bend = gelu_both(dot(token_rows(rows), w_inner[...]))
        low = value.astype(bf16)
        active[...] = low.reshape(active.shape)
        slope[...] = bend.astype(bf16).reshape(slope.shape)
        emit(dot_t(low, w_outer[...]), outs[2:])

    return call(
        body,
        info,
        normed,
        [Far(p) for p in pieces],
        [*[like((blocks, slot, hidden), bf16)] * 2, *partial_rows(blocks, part, width)],
        [],
        ffn_scratch(width, hidden, pieces),
        flops=4 * blocks * slot * width * hidden,
        steps=blocks // 2,
        each=2,
    )


def encoder_ffn_back(info, grads, slope, weights):
    blocks, (_, part, width) = slope.shape[0], grads[0].shape
    slot = part * len(grads)
    hidden = slope.shape[2]

    def body(info, stepped, weights, outs, ends, scratch):
        dinner = outs[0]
        w_inner, w_outer = weights
        back = dot(token_rows(stepped[:4]), w_outer[...])
        low = (back * stepped[4][...].reshape(back.shape).astype(f32)).astype(bf16)
        dinner[...] = low.reshape(dinner.shape)
        emit(dot_t(low, w_inner[...]), outs[1:])

    return call(
        body,
        info,
        [*grads, slope],
        [Close(w) for w in weights],
        [like((blocks, slot, hidden), bf16), *partial_rows(blocks, part, width)],
        [],
        flops=4 * blocks * slot * width * hidden,
        steps=blocks // 2,
        each=2,
    )


def weight_grads(info, pairs, more=(), cut=True):
    blocks, (_, part, width) = pairs[0][1].shape[0], pairs[0][0][0].shape
    widths = [right.shape[2] for _, right in pairs]

    def body(info, stepped, more, __, ends, totals):
        totals = totals if cut else ends
        for k, total in enumerate(totals):
            left, right = token_rows(stepped[5 * k : 5 * k + 4]), stepped[5 * k + 4]
            total[...] = t_dot(left, right[...].reshape(left.shape[0], total.shape[1]))
        if cut:
            hand_out(info, (*totals, *more), ends)

    return call(
        body,
        info,
        [a for left, right in pairs for a in (*left, right)],
        more,
        [],
        piece_shapes(width // 8, sum(widths) + sum(m.shape[1] for m in more))
        if cut
        else [like((width, w), f32) for w in widths],
        [pltpu.VMEM((width, w), f32) for w in widths] if cut else [],
        flops=2 * blocks * part * 4 * width * sum(widths),
        each=blocks,
    )


def finish(info, terms, widths, turned):
    terms = [part(t) for t in terms]
    rows = terms[0].array.shape[0]
    shapes = [(w, rows) if t else (rows, w) for w, t in zip(widths, turned, strict=True)]

    def body(info, _, ins, __, outs, ___):
        total = terms[0].read(ins[0])
        for term, ref in zip(terms[1:], ins[1:], strict=True):
            total = total + term.read(ref).astype(f32)
        column = 0
        for out, wide, turn in zip(outs, widths, turned, strict=True):
            found = total[:, column : column + wide]
            out[...] = found.T if turn else found
            column += wide

    return call(body, info, [], [t.array for t in terms], [], [like(s, f32) for s in shapes])


def cross_forward(info, states, weights, decoder, own_question, count_q, count_pass):
    rows_in, terms, gains = decoder
    blocks = count_q * count_pass
    _, part, width = states[0].shape
    slot = part * len(states)
    rows_dec = rows_in.shape[0]
    size = weights[1].shape[1]
    steps = 2

    def body(info, rows, fixed, outs, ends, scratch):
        weight, w_query, rows_in, *terms, gains, question = fixed
        after_self, normed, queries, stats = ends
        held = scratch[0]
        b = pl.program_id(0)

        @pl.when(b == 0)
        def _():
            after_self[...] = rows_in[...].astype(f32) + summed(terms)
            normed[...] = norm_rows(after_self[...], gains[1:2, :]).astype(bf16)
            queries[...] = dot(normed[...], w_query[...]).astype(bf16)

        made = dot(token_rows(rows), weight[...]).astype(bf16)
        outs[0][...] = made.reshape(outs[0].shape)
        each = made.shape[0]
        held[pl.ds(pl.multiple_of(b * each, each), each), :] = made

        @pl.when(b == steps - 1)
        def _():
            allowed = keys_used(info, question, range(blocks), part, slot, count_pass)
            lane = lax.broadcasted_iota(jnp.int32, (rows_dec, HDIM), 1)
            keys, vals = head_parts(held[...], 2)
            asking = head_parts(queries[...], 1)[0]
            scores = [dot_t(q * SCALE, t) for q, t in zip(asking, keys, strict=True)]
            for k, score in enumerate(scores):
                score = jnp.where(allowed, score, masked_score)
                top = jnp.max(score, axis=-1, keepdims=True)
                spread_out = jnp.exp(score - top)
                total = jnp.sum(spread_out, axis=-1, keepdims=True)
                at = k * LANES
                stats[:, at : at + HDIM] = dot(spread_out.astype(bf16), vals[k])
                stats[:, at + HDIM : at + LANES] = jnp.where(lane == 0, top, total)

    return call(
        body,
        info,
        states,
        [*(Close(w) for w in weights), rows_in, *terms, gains, own_question],
        [like((blocks, slot, 2 * size), bf16)],
        [
            Later(like((rows_dec, width), f32)),
            Later(like((rows_dec, width), bf16)),
            like((rows_dec, size), bf16),
            like((rows_dec, size // HDIM * LANES), f32),
        ],
        [pltpu.VMEM((blocks * slot, 2 * size), bf16)],
        flops=4 * blocks * slot * width * size,
        steps=steps,
        each=blocks // steps,
    )


def merged(first, second):
    lane = lax.broadcasted_iota(jnp.int32, (first.shape[0], HDIM), 1)
    found = []
    for at in range(0, first.shape[1], LANES):
        tops = [v[:, at + HDIM : at + HDIM + 1] for v in (first, second)]
        totals = [v[:, at + HDIM + 1 : at + HDIM + 2] for v in (first, second)]
        top = jnp.maximum(*tops)
        scales = [jnp.exp(t - top) for t in tops]
        total = totals[0] * scales[0] + totals[1] * scales[1]
        found.append(first[:, at : at + HDIM] * scales[0] + second[:, at : at + HDIM] * scales[1])
        found.append(jnp.where(lane == 0, top, total))
    return jnp.concatenate(found, axis=1)


def in_order(info, bits, own, other):
    later = (info[BLK] & bits) != 0
    return jnp.where(later, other, own), jnp.where(later, own, other)


def merge(info, own, other, bits):
    def body(info, _, ins, __, outs, ___):
        outs[0][...] = merged(*in_order(info, bits, ins[0][...], ins[1][...]))

    return call(body, info, [], [own, other], [], [like(own.shape, f32)])[0]


def cross_out(info, stats, bits, w_output):
    rows, columns = stats[0].shape
    size = columns // LANES * HDIM
    width = w_output.shape[0]

    def body(info, _, ins, __, outs, scratch):
        w_output = ins[-1]
        out, log_total, context, own, sent = outs
        values = [r[...] for r in ins[:-1]]
        near = merged(*in_order(info, bits[0], *values[:2]))
        far = merged(*in_order(info, bits[0], *values[2:]))
        stats = merged(*in_order(info, bits[1], near, far))
        log_total[...] = jnp.zeros_like(log_total)
        for k, at in enumerate(heads_in(size)):
            base = k * LANES
            top = stats[:, base + HDIM : base + HDIM + 1]
            total = stats[:, base + HDIM + 1 : base + HDIM + 2]
            out[:, at] = stats[:, base : base + HDIM] / total
            log_total[:, k : k + 1] = top + jnp.log(total)
        context[...] = out[...].astype(bf16)
        own[...] = dot_t(context[...], w_output[...])
        sent[...] = own[...].astype(bf16)

    return call(
        body,
        info,
        [],
        [*stats, w_output],
        [],
        [
            like((rows, size), f32),
            like((rows, LANES), f32),
            Later(like((rows, size), bf16)),
            like((rows, width), f32),
            like((rows, width), bf16),
        ],
        flops=2 * rows * size * width,
    )


def cross_back(info, key_vals, inputs, own_question, count_pass, slot, part):
    cotangent, after_cross, terms, gains, w_output, out, log_total, queries, weight = inputs
    blocks = key_vals.shape[0]
    rows_dec, width = after_cross.shape
    size = queries.shape[1]

    def body(info, stepped, fixed, outs, ends, scratch):
        cotangent, after_cross, own, r1, r2, r3, gains, w_output, out, log_total, queries, weight, question = fixed
        key_vals = stepped[0]
        dkey_vals = outs[0]
        dcross, dcross_low, gain_out, dqueries = ends
        total = summed((own, r1, r2, r3))
        back, gain_out[...] = norm_back(after_cross[...], gains[2:3, :], total)
        dcross[...] = cotangent[...].astype(f32) + back
        dcross_low[...] = dcross[...].astype(bf16)
        dcontext = dot(dcross_low[...], w_output[...]).astype(bf16)
        allowed = keys_used(info, question, range(blocks), part, slot, count_pass)
        keys, vals = head_parts(key_vals[...].reshape(blocks * slot, 2 * size), 2)
        asking = head_parts(queries[...], 1)[0]
        cuts = head_parts(dcontext, 1)[0]
        outs_of = head_parts(out[...], 1)[0]
        scores = [dot_t(q * SCALE, t) for q, t in zip(asking, keys, strict=True)]
        backs = [dot_t(c, v) for c, v in zip(cuts, vals, strict=True)]
        probs, lows = [], []
        for k, score in enumerate(scores):
            row_term = jnp.sum(cuts[k].astype(f32) * outs_of[k], axis=-1, keepdims=True)
            score = jnp.where(allowed, score, masked_score)
            probs.append(jnp.exp(score - log_total[:, k : k + 1]))
            lows.append((probs[k] * (backs[k] - row_term)).astype(bf16))
        dvals = [t_dot(p.astype(bf16), c) for p, c in zip(probs, cuts, strict=True)]
        dkeys = [t_dot(d, q) * SCALE for d, q in zip(lows, asking, strict=True)]
        found = [dot(d, t) * SCALE for d, t in zip(lows, keys, strict=True)]
        dqueries[...] = jnp.concatenate(found, axis=1)
        made = jnp.concatenate([*dkeys, *dvals], axis=1).astype(bf16)
        dkey_vals[...] = made.reshape(dkey_vals.shape)
        emit(dot_t(made, weight[...]), outs[1:])

    return call(
        body,
        info,
        [key_vals],
        [
            cotangent,
            after_cross,
            *terms,
            gains,
            w_output,
            out,
            log_total,
            queries,
            Close(weight),
            own_question,
        ],
        [like(key_vals.shape, bf16), *partial_rows(blocks, part, width)],
        [
            Later(like((rows_dec, width), f32)),
            Later(like((rows_dec, width), bf16)),
            Later(like((rows_dec, width), f32)),
            like((rows_dec, size), f32),
        ],
        flops=4 * blocks * slot * width * size,
        each=blocks,
    )


def summed(refs):
    count = refs[0].shape[0]

    def rows(ref):
        return ref[...] if len(ref.shape) == 2 else ref[0, :count, :]

    terms = [rows(ref).astype(f32) for ref in refs[1:]]
    total = refs[0][...]
    for term in terms:
        total = total + term
    return total


def decoder_self(info, rows, gains, pieces, column_from, size, order):
    count, width = rows.shape

    def body(info, _, ins, __, outs, scratch):
        rows, gains, order_q, order_k = ins[:4]
        normed, qkv, probs, context, own, sent, weight = outs
        assemble(info, ins[4:], (weight,), scratch[0], column_from)
        normed[...] = norm_rows(rows[...].astype(f32), gains[0:1, :]).astype(bf16)
        qkv[...] = dot(normed[...], weight[:, : 3 * size]).astype(bf16)
        query_at, key_at = order_q[...], order_k[...]
        same = lax.div(query_at, 1000) == lax.div(key_at, 1000)
        allowed = same & (key_at <= query_at) & (key_at >= 0) & (query_at >= 0)
        for k, at in enumerate(heads_in(size)):
            query, keys, vals = (qkv[:, j * size + at.start : j * size + at.stop] for j in range(3))
            scores = jnp.where(allowed, dot_t(query, keys) * SCALE, masked_score)
            spread_out = jnp.exp(scores - jnp.max(scores, axis=-1, keepdims=True))
            share_out = spread_out / jnp.sum(spread_out, axis=-1, keepdims=True)
            share_out = jnp.where(allowed, share_out, 0.0)
            probs[k] = share_out
            context[:, at] = dot(share_out.astype(bf16), vals).astype(bf16)
        own[...] = dot_t(context[...], weight[:, 3 * size :])
        sent[...] = own[...].astype(bf16)

    return call(
        body,
        info,
        [],
        [rows, gains, *order, *(Far(p) for p in pieces)],
        [],
        [
            Later(like((count, width), bf16)),
            Later(like((count, 3 * size), bf16)),
            Later(like((size // HDIM, count, count), f32)),
            Later(like((count, size), bf16)),
            like((count, width), f32),
            like((count, width), bf16),
            Later(like((width, 4 * size), bf16)),
        ],
        [pltpu.SemaphoreType.DMA((1, len(pieces)))],
        flops=2 * count * width * size * 4,
    )


def decoder_back(info, cotangent, pieces):
    count, width = cotangent.shape
    hidden = pieces[0].shape[1] // 2

    def body(info, _, ins, __, outs, scratch):
        w_inner, w_outer, back = outs
        assemble(info, ins[1:], (w_inner, w_outer), scratch[0])
        back[...] = dot(ins[0][...], w_outer[...])

    return call(
        body,
        info,
        [],
        [cotangent, *(Far(p) for p in pieces)],
        [],
        [Near(like((width, hidden), bf16)), like((width, hidden), bf16), like((count, hidden), f32)],
        [pltpu.SemaphoreType.DMA((2, len(pieces)))],
        flops=2 * count * width * hidden,
    )


def decoder_ffn(info, after_self, terms, back, gains, w_inner):
    count, width = after_self.shape
    hidden = w_inner.shape[1]

    def body(info, _, ins, __, outs, scratch):
        after_self, own, r1, r2, r3, back, gains, w_inner = ins
        after_cross, normed, active, dinner, own_back, sent_back = outs
        after_cross[...] = after_self[...] + summed((own, r1, r2, r3))
        normed[...] = norm_rows(after_cross[...], gains[2:3, :]).astype(bf16)
        value, slope = gelu_both(dot(normed[...], w_inner[...]))
        active[...] = value.astype(bf16)
        dinner[...] = (slope * back[...]).astype(bf16)
        own_back[...] = dot_t(dinner[...], w_inner[...])
        sent_back[...] = own_back[...].astype(bf16)

    return call(
        body,
        info,
        [],
        [after_self, *terms, back, gains, Close(w_inner)],
        [],
        [
            like((count, width), f32),
            Later(like((count, width), bf16)),
            Later(like((count, hidden), bf16)),
            Later(like((count, hidden), bf16)),
            like((count, width), f32),
            like((count, width), bf16),
        ],
        flops=4 * count * width * hidden,
    )


def rows_back(info, terms, weight):
    (count, size), width = terms[0].shape, weight.shape[0]

    def body(info, _, ins, __, outs, scratch):
        low, own, sent = outs
        total = ins[0][...]
        for term in ins[1:-1]:
            total = total + term[...]
        low[...] = total.astype(bf16)
        own[...] = dot_t(low[...], ins[-1][...])
        sent[...] = own[...].astype(bf16)

    return call(
        body,
        info,
        [],
        [*terms, weight],
        [],
        [
            Later(like((count, size), bf16)),
            like((count, width), f32),
            like((count, width), bf16),
        ],
        flops=2 * count * width * size,
    )


def decoder_self_back(
    info, dcross, after_self, terms, gains, weight, qkv, probs
):
    count, width = after_self.shape
    size = weight.shape[1] // 4

    def body(info, _, ins, __, outs, scratch):
        dcross, after_self, *terms, gains, weight, qkv, probs = ins
        dself, dself_low, gain_rows, moved, own_back, sent_back = outs
        back, gain_rows[...] = norm_back(after_self[...], gains[1:2, :], summed(terms))
        dself[...] = dcross[...] + back
        dself_low[...] = dself[...].astype(bf16)
        dcontext = dot(dself_low[...], weight[:, 3 * size :]).astype(bf16)
        for k, at in enumerate(heads_in(size)):
            query, keys, vals = (qkv[:, j * size + at.start : j * size + at.stop] for j in range(3))
            share_out = probs[k]
            dprobs = dot_t(dcontext[:, at], vals)
            dscores = share_out * (dprobs - jnp.sum(share_out * dprobs, axis=-1, keepdims=True))
            dscores = dscores.astype(bf16)
            found = (
                dot(dscores, keys) * SCALE,
                t_dot(dscores, query) * SCALE,
                t_dot(share_out.astype(bf16), dcontext[:, at]),
            )
            for j, term in enumerate(found):
                moved[:, j * size + at.start : j * size + at.stop] = term.astype(bf16)
        own_back[...] = dot_t(moved[...], weight[:, : 3 * size])
        sent_back[...] = own_back[...].astype(bf16)

    return call(
        body,
        info,
        [],
        [dcross, after_self, *terms, gains, weight, qkv, probs],
        [],
        [
            like((count, width), f32),
            Later(like((count, width), bf16)),
            like((count, width), f32),
            Later(like((count, 3 * size), bf16)),
            like((count, width), f32),
            like((count, width), bf16),
        ],
        flops=2 * count * width * size * 8,
    )


def decoder_ends(
    info, rows, dself, terms, gains, after_cross, out_terms, gain_rows, gain_sums, dec_own
):
    count, width = dself.shape

    def body(info, _, ins, __, outs, scratch):
        rows, dself, after_cross, gains = ins[:4]
        three, four, zero, one = ins[-4:]
        grad, states, found = outs
        total, out_total = summed(ins[4:8]), summed(ins[8:12])
        back, two = norm_back(rows[...].astype(f32), gains[0:1, :], total)
        grad[...] = dself[...] + back
        states[...] = (after_cross[...] + out_total).astype(bf16)
        row = lax.div(lax.broadcasted_iota(jnp.int32, (count, 1), 0), dec_own)
        mine = (row == info[HEAD]) & (info[BLK] == 0)
        found[0:1, :] = zero[...]
        found[1:2, :] = one[...]
        for k, values in enumerate((two, three[...], four[...])):
            found[2 + k : 3 + k, :] = jnp.sum(jnp.where(mine, values, 0.0), axis=0, keepdims=True)

    return call(
        body,
        info,
        [],
        [rows, dself, after_cross, gains, *terms, *out_terms, *gain_rows, *gain_sums],
        [],
        [like((count, width), f32), like((count, width), bf16), like((5, width), f32)],
    )


def decoder_weight_grads(info, own, pairs_in, pairs_out):
    count, width = pairs_in[0][0].shape

    def body(info, _, ins, __, outs, scratch):
        row = lax.broadcasted_iota(jnp.int32, (own, width), 0) + info[BLK] * own
        column = lax.broadcasted_iota(jnp.int32, (own, width), 1)
        pick = jnp.where(row == column, 1.0, 0.0).astype(bf16)
        outs, ins = iter(outs), iter(ins)
        for _, _, arrays in pairs_in:
            left, right = next(ins)[...], next(ins)[...]
            found = t_dot(dot_t(left, pick).astype(bf16), right)
            wide = found.shape[1] // arrays
            for k in range(arrays):
                next(outs)[...] = found[:, k * wide : (k + 1) * wide]
        for _ in pairs_out:
            left, right = next(ins)[...], next(ins)[...]
            next(outs)[...] = t_dot(left, dot_t(right, pick).astype(bf16))

    outs = [like((own, r.shape[1] // n), f32) for _, r, n in pairs_in for _ in range(n)]
    outs += [like((l.shape[1], own), f32) for l, _ in pairs_out]
    flat = [a for pair in pairs_in for a in pair[:2]] + [a for pair in pairs_out for a in pair]
    return call(body, info, [], flat, [], outs, flops=2 * count * own * width * 10, least=0)


def shards(
    encoder_input,
    passage_lengths,
    decoder_input,
    encoder_query,
    encoder_key,
    encoder_value,
    encoder_output,
    encoder_inner,
    encoder_outer,
    decoder_query,
    decoder_key,
    decoder_value,
    decoder_output,
    cross_query,
    cross_key,
    cross_value,
    cross_output,
    decoder_inner,
    decoder_outer,
    encoder_gains,
    decoder_gains,
    encoder_cotangent,
    decoder_cotangent,
):
    head, blk = lax.axis_index("head"), lax.axis_index("blk")
    blk_count, head_count = lax.axis_size("blk"), lax.axis_size("head")
    count_q, count_pass, part, width = encoder_input.shape
    blocks = count_q * count_pass
    slot = part * head_count
    own = width // blk_count
    if blk_count == 8:
        places = jnp.asarray(place_table(8))[blk]
    else:
        places = jnp.arange(8, dtype=jnp.int32)
    info = jnp.concatenate(
        [places, jnp.stack([head, blk]).astype(jnp.int32), passage_lengths.reshape(blocks)]
    )

    size, units = encoder_query.shape[1], encoder_inner.shape[1]
    inputs = encoder_input.reshape(blocks, part, width)
    dec_part = decoder_input.shape[1]
    dec_own = count_q * dec_part
    dec_rows = dec_own * head_count
    filled = -(-dec_rows // 16) * 16

    attention = jnp.concatenate(
        [encoder_query, encoder_key, encoder_value, encoder_output.T], axis=1
    )
    attention, inputs = sync(attention, inputs)
    attention = fetch_step(fetch_start(attention), -1, 1)
    first = by_rows(
        lambda x, g: (norm_rows(x, g[0:1]),), info, [inputs], [encoder_gains], [bf16]
    )[0]
    attention, first = sync(attention, first)

    attention = fetch_step(attention, -2, 2)
    first_all = [first, swap(first, "head", 1), swap(first, "head", 2)]
    ffn = jnp.concatenate(
        [
            encoder_inner,
            encoder_outer.T,
            decoder_query,
            decoder_key,
            decoder_value,
            decoder_output.T,
            cross_key,
            cross_value,
            cross_query,
            cross_output.T,
        ],
        axis=1,
    )
    at_self, at_cross = 2 * units, 2 * units + 4 * size
    attention, ffn = sync(attention, ffn)

    attention = fetch_step(attention, -3, 3)
    pair = jnp.stack([decoder_input, decoder_cotangent]).reshape(2, dec_own, width)
    both = lax.all_gather(pair, "head", axis=1, tiled=True)
    both = jnp.pad(both, ((0, 0), (0, filled - dec_rows), (0, 0)))
    attention, first_all, ffn, both = sync(attention, first_all, ffn, both)

    attention, ffn = fetch_step(attention, -4), fetch_step(fetch_start(ffn), 1)
    first_all.append(swap(first_all[2], "head", 1))
    dec_ffn = jnp.concatenate([decoder_inner, decoder_outer.T], axis=1)
    attention, ffn, first_all, dec_ffn = sync(attention, ffn, first_all, dec_ffn)

    ffn = fetch_step(ffn, -1, 2)
    qkv, probs, context, *partial = encoder_attention(
        info, first_all, in_turn(attention)
    )
    partial, ffn = sync(partial, ffn)

    def to_core(partial):
        return swap(partial[3], "head", 1)

    def to_chip(partial, corner):
        far = (partial[2] + corner.astype(f32)).astype(bf16)
        return [swap(far, "head", 2), swap(partial[1], "head", 1)]

    ffn = fetch_step(ffn, -2, 3)
    partial, corner = sync(partial, to_core(partial))
    partial, arrived, ffn = sync(partial, to_chip(partial, corner), ffn)

    def enter_ffn(x, a, b, c, g):
        hidden = x + a + b + c
        return hidden, norm_rows(hidden, g[1:2])

    hidden, second = by_rows(
        enter_ffn, info, [inputs, partial[0], *arrived], [encoder_gains], [f32, bf16]
    )
    ffn = fetch_step(ffn, -3, 4)
    def spread(rows):
        return [rows, swap(rows, "head", 1), swap(rows, "head", 2)]

    def riders(all_rows):
        return [Rider(rows, blocks) for rows in all_rows[1:]]

    second, dec_ffn = sync(second, dec_ffn)
    second_all = spread(second)
    second_all, ffn, dec_ffn = sync(second_all, ffn, dec_ffn)
    dec_ffn = fetch_step(fetch_start(dec_ffn), -1, 1)
    second_all.append(swap(second_all[2], "head", 1))
    second_all, ffn = sync(second_all, ffn)
    ffn = in_turn(ffn)

    active, slope, *partial = encoder_ffn(info, second_all, ffn, units)
    partial, dec_ffn = sync(partial, dec_ffn)
    partial, corner, both, dec_ffn = sync(partial, to_core(partial), both, dec_ffn)
    dec_in, cotangent = both[0], both[1]

    index = np.arange(filled)
    question = (index % dec_own) // dec_part
    position = index // dec_own * dec_part + index % dec_part
    order = np.where(index < dec_rows, question * 1000 + position, -1).astype(np.int32)
    order = (jnp.asarray(order[:, None]), jnp.asarray(order[None, :]))
    question = jnp.asarray(question[:, None].astype(np.int32))

    arrived = to_chip(partial, corner)
    dec_ffn = fetch_step(dec_ffn, -2, 2)
    third, dec_qkv, dec_probs, dec_context, mine, sent, w_self = decoder_self(
        info, dec_in, decoder_gains, ffn, at_self, size, order
    )
    partial, arrived, mine, sent, dec_ffn = sync(partial, arrived, mine, sent, dec_ffn)
    states, states_sent = by_rows(
        lambda h, a, b, c: (h + a + b + c,),
        info,
        [hidden, partial[0], *arrived],
        [],
        [bf16],
        riders=sent,
    )
    states_sent, dec_ffn = sync(states_sent, dec_ffn)
    states_all = spread(states_sent)
    dec_ffn = fetch_step(dec_ffn, -3, 3)
    w_cross, w_cross_query, w_cross_output = gathered(
        info, ffn, (2 * size, size, size), at_cross
    )
    states_all, dec_ffn, w_cross = sync(states_all, dec_ffn, w_cross)
    dec_ffn = fetch_step(dec_ffn, -4)
    states_all = sync(*states_all, swap(states_all[2], "head", 1))

    key_vals, after_self, fourth, queries, stats = cross_forward(
        info,
        states_all,
        (w_cross, w_cross_query),
        (dec_in, [mine, *riders(states_all)], decoder_gains),
        question,
        count_q,
        count_pass,
    )
    bits = [1 << k for k in range((blk_count - 1).bit_length())]
    last_two = (bits[-2], bits[-1], bits[-2] + bits[-1])
    for k in bits[:-2]:
        stats = merge(info, stats, swap(stats, "blk", k), k)
    stats, dec_ffn = sync(stats, dec_ffn)
    stats_all = [stats, *(swap(stats, "blk", k) for k in last_two)]
    w_dec_inner, w_dec_outer, outer_back = decoder_back(info, cotangent, in_turn(dec_ffn))
    stats_all, outer_back = sync(stats_all, outer_back)
    out, log_total, cross_context, mine, sent = cross_out(
        info, stats_all, bits[-2:], w_cross_output
    )
    after_cross, fifth, dec_active, dec_dinner, mine, sent = decoder_ffn(
        info, after_self, [mine, *share(sent)], outer_back, decoder_gains, w_dec_inner
    )
    dkey_vals, *rest = cross_back(
        info,
        key_vals,
        (
            cotangent,
            after_cross,
            [mine, *share(sent)],
            decoder_gains,
            w_cross_output,
            out,
            log_total,
            queries,
            w_cross,
        ),
        question,
        count_pass,
        slot,
        part,
    )
    partial, (dcross, dcross_low, gain_four, dqueries) = rest[:4], rest[4:]

    def some(value, which):
        for k in which:
            value = value + swap(value, "blk", k)
        return value

    partial, dqueries, dkey_vals = sync(partial, dqueries, dkey_vals)
    partial, corner, dkey_vals, dqueries = sync(partial, to_core(partial), dkey_vals, dqueries)
    arrived = to_chip(partial, corner)
    dqueries = some(dqueries, bits[:-1])
    cross_sum = weight_grads(info, [(states_all, dkey_vals)], cut=False)[0]
    _, out_mine, out_sent = rows_back(info, [dec_active], w_dec_outer)
    partial, arrived, cross_sum, dqueries, out_sent = sync(
        partial, arrived, cross_sum, dqueries, out_sent
    )

    def enter_back(cot, a, b, c):
        grad = cot + a + b + c
        return grad, grad

    dstates, dstates_low = by_rows(
        enter_back,
        info,
        [encoder_cotangent.reshape(blocks, part, width), partial[0], *arrived],
        [],
        [f32, bf16],
        riders=out_sent,
        kept=False,
    )
    dstates_low, cross_sum, dqueries = sync(dstates_low, cross_sum, dqueries)
    dstates_all = spread(dstates_low)
    terms = [dqueries, swap(dqueries, "blk", bits[-1])]
    dqueries, mine, sent = rows_back(info, terms, w_cross_query)
    w_ffn = gathered(info, ffn, (units, units))
    dstates_all, sent, w_ffn = sync(dstates_all, sent, w_ffn)
    dstates_all.append(swap(dstates_all[2], "head", 1))
    dstates_all, sent = sync(dstates_all, sent)
    out_terms = [out_mine, *riders(dstates_all)]
    dinner, *partial = encoder_ffn_back(info, dstates_all, slope, w_ffn)
    terms = [mine, *share(sent)]
    partial, dinner, terms = sync(partial, dinner, terms)
    partial, corner, dinner, dstates_all = sync(partial, to_core(partial), dinner, dstates_all)
    arrived = to_chip(partial, corner)
    dself, dself_low, gain_three, dself_qkv, own_back, sent_back = decoder_self_back(
        info,
        dcross,
        after_self,
        terms,
        decoder_gains,
        w_self,
        dec_qkv,
        dec_probs,
    )
    ffn_sums = weight_grads(
        info, [(second_all, dinner), (dstates_all, active)], [cross_sum]
    )
    partial, arrived, ffn_sums, sent_back = sync(partial, arrived, ffn_sums, sent_back)

    def middle_back(dy, h, a, b, c, g):
        back, gain_rows = norm_back(h, g[1:2], a + b + c)
        grad = dy + back
        return grad, grad, gain_rows

    dhidden, dhidden_low, gain_one = by_rows(
        middle_back,
        info,
        [dstates, hidden, partial[0], *arrived],
        [encoder_gains],
        [f32, bf16],
        gain=True,
        riders=sent_back,
        kept=False,
    )
    dhidden_low, ffn_sums = sync(dhidden_low, ffn_sums)
    dhidden_all = spread(dhidden_low)
    ffn_moving = reduce_step(info, (ffn_sums, None, 1))[0]
    w_attention = gathered(info, in_turn(attention), (3 * size, size))
    dhidden_all, ffn_moving, w_attention = sync(dhidden_all, ffn_moving, w_attention)
    ffn_moving = reduce_step(info, (ffn_sums, ffn_moving, 2))[0]
    dhidden_all = sync(*dhidden_all, swap(dhidden_all[2], "head", 1))
    terms = [own_back, *riders(dhidden_all)]

    partial, sums, gain_zero = encoder_attention_back(
        info, dhidden_all, first_all, qkv, probs, context, w_attention, encoder_gains
    )
    partial, sums, ffn_moving, gain_zero = sync(partial, sums, ffn_moving, gain_zero)
    ffn_moving, moving = reduce_step(info, (ffn_sums, ffn_moving, 3), (sums, None, 1))[:2]
    corner = to_core(partial)
    dec_grad, dec_states, gains = decoder_ends(
        info,
        dec_in,
        dself,
        terms,
        decoder_gains,
        after_cross,
        out_terms,
        [gain_three, gain_four],
        [gain_zero, gain_one],
        dec_own,
    )
    for k in (1, 2):
        gains = gains + swap(gains, "head", k)
    (
        grad_dec_query,
        grad_dec_key,
        grad_dec_value,
        grad_cross_query,
        grad_dec_inner,
        grad_dec_outer,
        grad_dec_output,
        grad_cross_output,
    ) = decoder_weight_grads(
        info,
        own,
        [
            (third, dself_qkv, 3),
            (fourth, dqueries, 1),
            (fifth, dec_dinner, 1),
            (cotangent, dec_active, 1),
        ],
        [(dec_context, dself_low), (cross_context, dcross_low)],
    )
    partial, corner, moving, gains, ffn_moving, grad_dec_query = sync(
        partial, corner, moving, gains, ffn_moving, grad_dec_query
    )

    def dec_shape(values):
        return values.reshape(count_q, dec_part, width)

    def own_rows(values):
        return lax.dynamic_slice_in_dim(values, head * dec_own, dec_own, 0)

    ffn_moving, moving = reduce_step(info, (ffn_sums, ffn_moving, 4), (sums, moving, 2))[:2]
    arrived = to_chip(partial, corner)
    gains = some(gains, bits[:1])
    dec_states, dec_grad = dec_shape(own_rows(dec_states)), dec_shape(own_rows(dec_grad))
    partial, arrived, moving, gains, ffn_moving = sync(
        partial, arrived, moving, gains, ffn_moving
    )

    def last_back(dh, x, a, b, c, g):
        return (dh + norm_back(x, g[0:1], a + b + c)[0],)

    moving = reduce_step(info, (sums, moving, 3))[0]
    gains = some(gains, bits[1:-1])
    input_grad = by_rows(
        last_back,
        info,
        [dhidden, inputs, partial[0], *arrived],
        [encoder_gains],
        [f32],
    )[0]
    moving, gains, input_grad, ffn_moving = sync(moving, gains, input_grad, ffn_moving)
    moving, (gains, ffn_moving, dec_states, dec_grad) = reduce_step(
        info, (sums, moving, 4), hold=(gains, ffn_moving, dec_states, dec_grad)
    )
    last = swap(gains, "blk", bits[-1])
    grad_inner, grad_outer, grad_cross_key, grad_cross_value = finish(
        info,
        reduce_terms(ffn_sums, ffn_moving),
        (units, units, size, size),
        (False,) * 4,
    )
    enc_gain_grads, dec_gain_grads = gains[:2] + last[:2], gains[2:] + last[2:]
    grad_query, grad_key, grad_value, grad_output = finish(
        info, reduce_terms(sums, moving), (size,) * 4, (False, False, False, True)
    )

    return (
        states.reshape(encoder_input.shape),
        dec_states,
        input_grad.reshape(encoder_input.shape),
        dec_grad,
        grad_query,
        grad_key,
        grad_value,
        grad_output,
        grad_inner,
        grad_outer.T,
        grad_dec_query,
        grad_dec_key,
        grad_dec_value,
        grad_dec_output,
        grad_cross_query,
        grad_cross_key,
        grad_cross_value,
        grad_cross_output,
        grad_dec_inner,
        grad_dec_outer.T,
        enc_gain_grads,
        dec_gain_grads,
    )


def solution(mesh):
    placed = (
        P(None, "blk", "head", None),
        P(None, "blk"),
        P(None, "head", None),
        P("blk", "head"),
        P("blk", "head"),
        P("blk", "head"),
        P("head", "blk"),
        P("blk", "head"),
        P("head", "blk"),
        P("blk", "head"),
        P("blk", "head"),
        P("blk", "head"),
        P("head", "blk"),
        P("blk", "head"),
        P("blk", "head"),
        P("blk", "head"),
        P("head", "blk"),
        P("blk", "head"),
        P("head", "blk"),
        P(),
        P(),
        P(None, "blk", "head", None),
        P(None, "head", None),
    )
    return jax.shard_map(
        shards,
        mesh=mesh,
        in_specs=placed,
        out_specs=(placed[0], placed[2], placed[0], placed[2], *placed[3:19], P(), P()),
        check_vma=False,
    )
```

```python
import math

import jax
import jax.numpy as jnp
import numpy as np
from jax import lax
from jax.experimental import pallas as pl
from jax.experimental.pallas import tpu as pltpu
from jax.sharding import PartitionSpec as P

HDIM = 64
SCALE = HDIM ** (-0.5)
LANES = 128
EPS = 1e-06
VMEM_LIMIT = 24 * 1024 * 1024
LARGE = 1 << 19
masked_score = -1000000000.0
f32 = jnp.float32
bf16 = jnp.bfloat16

PLACES, HEAD, BLK, LENGTHS = 0, 8, 9, 10


def swap(value, axis, bits):
    size = lax.axis_size(axis)
    return lax.ppermute(value, axis, [(i, i ^ bits) for i in range(size)])


def sync(*values):
    return lax.optimization_barrier(values)


def share(value):
    return [swap(value, "head", k) for k in (1, 2, 3)]


def ring_order(count):
    return [*range(0, count, 2), *range(count - 1, 0, -2)]


OFFSETS = (0, -1, 1, -2, 2, -3, 3, -4)


def ring_steps(count):
    order = ring_order(count)
    forth = [(order[i], order[(i + 1) % count]) for i in range(count)]
    return forth, [(b, a) for a, b in forth]


def place_table(count):
    order = ring_order(count)
    at = {b: i for i, b in enumerate(order)}
    return np.array(
        [[order[(at[b] + o) % count] for o in OFFSETS] for b in range(count)], np.int32
    )


def gather_rows(own):
    return lax.all_gather(own, "blk", axis=0, tiled=True)


def fetch_start(own):
    if lax.axis_size("blk") == 8:
        return {0: own}
    return dict(zip(OFFSETS, jnp.split(gather_rows(own), 8, axis=0), strict=True))


def fetch_step(pieces, *offsets):
    count = lax.axis_size("blk")
    if count != 8:
        return pieces
    forth, back = ring_steps(count)
    more = {
        k: lax.ppermute(pieces[k + 1 if k < 0 else k - 1], "blk", forth if k < 0 else back)
        for k in offsets
    }
    return {**pieces, **more}


def in_turn(pieces):
    return [pieces[k] if k in pieces else pieces[-k] for k in OFFSETS]


@jax.tree_util.register_pytree_node_class
class Part:
    def __init__(self, array, start, width):
        self.array, self.start, self.width = array, start, width

    def tree_flatten(self):
        return (self.array,), (self.start, self.width)

    @classmethod
    def tree_unflatten(cls, places, arrays):
        return cls(*arrays, *places)

    def read(self, ref):
        return ref[:, self.start : self.start + self.width]


def part(value):
    return value if isinstance(value, Part) else Part(value, 0, value.shape[1])


def reduce_step(info, *rings, hold=None):
    count = lax.axis_size("blk")
    if count != 8:
        return [[] for _ in rings] + [hold]
    forth, back = ring_steps(count)
    plan = [[], []]
    for pieces, moving, step in rings:
        by = dict(zip(OFFSETS, pieces, strict=True))
        plan[0].append([*([] if step == 1 else [moving[0]]), by[(-4, 3, 2, 1)[step - 1]]])
        if step < 4:
            plan[1].append([*([] if step == 1 else [moving[1]]), by[(-3, -2, -1)[step - 1]]])
    plan = [p for p in plan if p]
    if len(rings) == 1 and rings[0][2] == 1:
        sent = [p[0][0] for p in plan]
    else:
        parts = [part(v) for p in plan for terms in p for v in terms]

        def body(info, _, ins, __, outs, ___):
            found = iter(zip(parts, ins, strict=True))
            for out, p in zip(outs, plan, strict=True):
                column = 0
                for terms in p:
                    values = [piece.read(ref) for piece, ref in (next(found) for _ in terms)]
                    total = values[0]
                    if len(values) == 2:
                        total = (total.astype(f32) + values[1].astype(f32)).astype(bf16)
                    out[:, column : column + total.shape[1]] = total
                    column += total.shape[1]

        rows = rings[0][0][0].shape[0]
        wide = [sum(part(terms[0]).width for terms in p) for p in plan]
        shapes = [like((rows, w), bf16) for w in wide]
        came_in = {id(m.array) for _, moving, _ in rings for m in moving or ()}
        given = [Close(p.array) if id(p.array) in came_in else p.array for p in parts]
        sent = call(body, info, [], given, [], [Near(v) for v in shapes], least=0)
    if hold is not None:
        sent, hold = sync(sent, hold)
    came = [lax.ppermute(v, "blk", way) for v, way in zip(sent, (forth, back), strict=False)]
    results, column = [], 0
    for k, (pieces, moving, step) in enumerate(rings):
        wide = pieces[0].shape[1]
        found = [Part(came[0], column, wide)]
        if step == 4:
            found.append(moving[1])
        else:
            before = sum(r[0][0].shape[1] for r in rings[:k] if r[2] < 4)
            found.append(Part(came[1], before, wide))
        results.append(found)
        column += wide
    return [*results, hold]


def reduce_terms(pieces, moving):
    if lax.axis_size("blk") != 8:
        everything = jnp.concatenate([p.astype(f32) for p in pieces], axis=0)
        return [lax.psum_scatter(everything, "blk", scatter_dimension=0, tiled=True)]
    return [pieces[0], *moving]


def dot(left, right, over=(1, 0)):
    return lax.dot_general(
        left, right, (((over[0],), (over[1],)), ((), ())), preferred_element_type=f32
    )


def dot_t(left, right):
    return dot(left, right, (1, 1))


def t_dot(left, right):
    return dot(left, right, (0, 0))


def norm_rows(values, gain):
    return values * lax.rsqrt(jnp.mean(values * values, axis=-1, keepdims=True) + EPS) * gain


def norm_back(values, gain, grad):
    inverse = lax.rsqrt(jnp.mean(values * values, axis=-1, keepdims=True) + EPS)
    unit = values * inverse
    weighted = grad * gain
    along = jnp.mean(weighted * unit, axis=-1, keepdims=True)
    return inverse * (weighted - unit * along), grad * unit


def gelu_both(values):
    root = math.sqrt(2.0 / math.pi)
    square = values * values
    bent = jnp.tanh(root * values * (1.0 + 0.044715 * square))
    half = 0.5 * (1.0 + bent)
    slope = half + 0.5 * values * (1.0 - bent * bent) * root * (1.0 + 3 * 0.044715 * square)
    return values * half, slope


def heads_in(width):
    return [slice(at, at + HDIM) for at in range(0, width, HDIM)]


def head_parts(values, count):
    size = values.shape[1] // count
    return [[values[:, j * size :][:, at] for at in heads_in(size)] for j in range(count)]


def assemble(info, pieces, targets, signals, column_from=0):
    rows = pieces[0].shape[0]
    copies = []
    for t, piece in enumerate(pieces):
        at = pl.ds(pl.multiple_of(info[PLACES + t] * rows, 16), rows)
        column = column_from
        for k, target in enumerate(targets):
            wide = target.shape[1]
            copies.append(
                pltpu.make_async_copy(
                    piece.at[:, column : column + wide], target.at[at, :], signals.at[k, t]
                )
            )
            column += wide
    for copy in copies:
        copy.start()
    for copy in copies:
        copy.wait()


def hand_out(info, sources, pieces):
    rows = pieces[0].shape[0]
    for t, piece in enumerate(pieces):
        at = pl.ds(pl.multiple_of(info[PLACES + t] * rows, 16), rows)
        column = 0
        for source in sources:
            piece[:, column : column + source.shape[1]] = source[at, :].astype(piece.dtype)
            column += source.shape[1]


def token_rows(refs):
    return jnp.concatenate([r[k] for k in range(refs[0].shape[0]) for r in refs], axis=0)


def emit(partial, outs):
    each, part, _ = outs[0].shape
    for k in range(each):
        for r, out in enumerate(outs):
            at = (k * len(outs) + r) * part
            out[k] = partial[at : at + part].astype(out.dtype)


def slots_used(info, b, part, slot):
    column = lax.broadcasted_iota(jnp.int32, (1, slot), 1)
    position = (lax.div(column, part) ^ info[HEAD]) * part + lax.rem(column, part)
    return position < info[LENGTHS + b]


def keys_used(info, question, passages, part, slot, count_pass):
    return jnp.concatenate(
        [
            slots_used(info, k, part, slot) & (question[...] == k // count_pass)
            for k in passages
        ],
        axis=1,
    )


def call(
    body, info, stepped, fixed, out_stepped, out_fixed, scratch=(), flops=0, steps=1, near=False, least=LARGE, each=1
):
    def by_step(shape):
        last = shape[0] // each - 1
        return pl.BlockSpec((each, *shape[1:]), lambda b: (jnp.minimum(b, last),) + (0,) * (len(shape) - 1))

    def whole(a):
        if type(a) is Far:
            return pl.BlockSpec(memory_space=pltpu.HBM)
        if isinstance(a, Rider):
            return pl.BlockSpec(a.shape, lambda b: (a.index, 0, 0))
        index = (0, a.index) if type(a) is Columns else (0,) * len(a.shape)
        return pl.BlockSpec(a.shape, lambda b: index)

    counts = [len(stepped), len(fixed), len(out_stepped), len(out_fixed), len(scratch)]
    stops = np.cumsum(counts)

    def split(info_ref, *refs):
        body(info_ref, *(refs[e - c : e] for c, e in zip(counts, stops, strict=True)))

    def large(a):
        return not near and math.prod(a.shape) * a.dtype.itemsize >= least

    def given(a):
        array = a.array if isinstance(a, (Columns, Far, Rider)) else a
        far = (large(a) and not isinstance(a, Close)) or isinstance(a, Rider)
        return pltpu.with_memory_space_constraint(array, pltpu.HBM) if far else array

    def made(a):
        if isinstance(a, Later) or (large(a) and not isinstance(a, Near)):
            return pltpu.HBM(a.shape, a.dtype)
        return a.array if isinstance(a, Near) else a

    arrays = [*stepped, *fixed, *out_stepped, *out_fixed]
    moved = sum(math.prod(a.shape) * a.dtype.itemsize for a in arrays)
    return pl.pallas_call(
        split,
        grid=(steps,),
        in_specs=[
            pl.BlockSpec(memory_space=pltpu.SMEM),
            *(by_step(a.shape) for a in stepped),
            *(whole(a) for a in fixed),
        ],
        out_specs=[
            *(by_step(a.shape) for a in out_stepped),
            *(whole(a) for a in out_fixed),
        ],
        out_shape=[made(a) for a in (*out_stepped, *out_fixed)],
        scratch_shapes=list(scratch),
        compiler_params=pltpu.CompilerParams(
            dimension_semantics=("arbitrary",), vmem_limit_bytes=VMEM_LIMIT
        ),
        cost_estimate=pl.CostEstimate(
            flops=int(flops), bytes_accessed=int(moved), transcendentals=0
        ),
    )(info, *(given(a) for a in (*stepped, *fixed)))


class Columns:
    def __init__(self, array, width, index):
        self.array, self.index, self.dtype = array, index, array.dtype
        self.shape = (array.shape[0], width)


class Near(Columns):
    def __init__(self, array):
        self.array, self.shape, self.dtype = array, array.shape, array.dtype


class Later(Near):
    pass


class Rider:
    def __init__(self, array, index):
        self.array, self.index, self.dtype = array, index, array.dtype
        self.shape = (1, *array.shape[1:])


class Far:
    def __init__(self, array):
        self.array, self.shape, self.dtype = array, array.shape, array.dtype


class Close(Far):
    pass


def like(shape, dtype):
    return jax.ShapeDtypeStruct(tuple(shape), dtype)


def by_rows(fn, info, stepped, fixed, dtypes, gain=False, riders=None, kept=True):
    steps, _, width = stepped[0].shape
    count = 0 if riders is None else 1
    alone = [like(stepped[0].shape, d) for d in dtypes]
    outs = alone if riders is None or kept else alone[:-1]
    more = 0 if riders is None else riders.shape[0]
    together = [like((steps + count, *stepped[0].shape[1:]), dtypes[-1])] if more else []

    def body(info_ref, ins, whole, outs, sums, _):
        b = pl.program_id(0)
        if more:
            whole, rows = whole[:-1], whole[-1]

        @pl.when(b < steps)
        def _():
            results = fn(*(r[0].astype(f32) for r in ins), *(r[...] for r in whole))
            for out, value in zip(outs, results, strict=False):
                out[0] = value.astype(out.dtype)
            if more:
                outs[-1][0] = results[len(dtypes) - 1].astype(outs[-1].dtype)
            for total in sums:
                found = jnp.sum(results[-1], axis=0, keepdims=True)

                @pl.when(b == 0)
                def _():
                    total[...] = found

                @pl.when(b > 0)
                def _():
                    total[...] += found

        if more:

            @pl.when(b == steps)
            def _():
                outs[-1][0, :more, :] = rows[...]

    return call(
        body,
        info,
        stepped,
        [*fixed, riders] if more else fixed,
        [*outs, *together],
        [like((1, width), f32)] * gain,
        flops=10 * math.prod(stepped[0].shape),
        steps=steps + count,
        near=True,
    )


def partial_rows(blocks, part, width):
    return [Near(like((blocks, part, width), d)) for d in (f32, bf16, f32, bf16)]


def piece_shapes(rows, columns):
    return [Later(like((rows, columns), d)) for d in (f32, *[bf16] * 7)]


def gathered(info, pieces, widths, column_from=0):
    rows, wide = pieces[0].shape[0] * len(pieces), sum(widths)

    def body(info, _, ins, __, outs, scratch):
        together, signals = scratch
        assemble(info, ins, (together,), signals, column_from)
        column = 0
        for out in outs:
            out[...] = together[:, column : column + out.shape[1]]
            column += out.shape[1]

    return call(
        body,
        info,
        [],
        [Far(p) for p in pieces],
        [],
        [Near(like((rows, w), bf16)) for w in widths],
        [pltpu.VMEM((rows, wide), bf16), pltpu.SemaphoreType.DMA((1, len(pieces)))],
    )


def attention_scratch(width, size, pieces):
    return [
        *(pltpu.VMEM((width, k * size), bf16) for k in (3, 1, 4)),
        pltpu.SemaphoreType.DMA((1, len(pieces))),
    ]


def encoder_attention(info, normed, pieces):
    blocks, part, width = normed[0].shape
    slot = part * len(normed)
    size = pieces[0].shape[1] // 4
    count = size // HDIM

    def body(info, rows, pieces, outs, _, scratch):
        qkv, probs, context = outs[:3]
        w_in, w_out, together, signals = scratch
        b = pl.program_id(0)

        @pl.when(b == 0)
        def _():
            assemble(info, pieces, (together,), signals)
            w_in[...] = together[:, : 3 * size]
            w_out[...] = together[:, 3 * size :]

        qkv[0] = dot(token_rows(rows), w_in[...]).astype(bf16)
        allowed = slots_used(info, b, part, slot)
        query, keys, vals = head_parts(qkv[0], 3)
        found = []
        for k, scores in enumerate([dot_t(q * SCALE, t) for q, t in zip(query, keys, strict=True)]):
            scores = jnp.where(allowed, scores, masked_score)
            spread_out = jnp.exp(scores - jnp.max(scores, axis=-1, keepdims=True))
            inverse = 1.0 / jnp.sum(spread_out, axis=-1, keepdims=True)
            found.append((spread_out * inverse).astype(bf16))
            probs[0, k] = found[-1]
        found = [dot(w, v) for w, v in zip(found, vals, strict=True)]
        context[0] = jnp.concatenate(found, axis=1).astype(bf16)
        emit(dot_t(context[0], w_out[...]), outs[3:])

    return call(
        body,
        info,
        normed,
        [Far(p) for p in pieces],
        [
            like((blocks, slot, 3 * size), bf16),
            like((blocks, count, slot, slot), bf16),
            like((blocks, slot, size), bf16),
            *partial_rows(blocks, part, width),
        ],
        [],
        attention_scratch(width, size, pieces),
        flops=2 * blocks * slot * (width * size * 4 + 8 * slot * size),
        steps=blocks,
    )


def encoder_attention_back(info, grads, normed, qkv, probs, context, weights, gains):
    blocks, part, width = normed[0].shape
    slot = part * len(normed)
    size = context.shape[2]

    def body(info, stepped, fixed, outs, ends, scratch):
        grad_refs, normed_refs = stepped[:4], stepped[4:8]
        qkv, probs, context = stepped[8:]
        w_in, w_out, gains = fixed
        pieces, gain_out = ends[:-1], ends[-1]
        total_in, total_out, moved = scratch
        b = pl.program_id(0)

        @pl.when(b == 0)
        def _():
            total_in[...] = jnp.zeros_like(total_in)
            total_out[...] = jnp.zeros_like(total_out)
            gain_out[...] = jnp.zeros_like(gain_out)

        grad = token_rows(grad_refs)
        rows = token_rows(normed_refs)
        dcontext = dot(grad, w_out[...]).astype(bf16)
        query, keys, vals = head_parts(qkv[0], 3)
        cuts = head_parts(dcontext, 1)[0]
        backs = [dot_t(c, v) for c, v in zip(cuts, vals, strict=True)]
        dvals = [t_dot(probs[0, k], c) for k, c in enumerate(cuts)]
        lows = []
        for k, back in enumerate(backs):
            wide = probs[0, k].astype(f32)
            low = wide * (back - jnp.sum(wide * back, axis=-1, keepdims=True))
            lows.append(low.astype(bf16))
        dquery = [dot(d, t) * SCALE for d, t in zip(lows, keys, strict=True)]
        dkeys = [t_dot(d, q) * SCALE for d, q in zip(lows, query, strict=True)]
        moved[...] = jnp.concatenate([*dquery, *dkeys, *dvals], axis=1).astype(bf16)
        partial = dot_t(moved[...], w_in[...])
        emit(partial, outs)
        gain_out[...] += jnp.sum(partial * rows.astype(f32), axis=0, keepdims=True) / gains[0:1, :]
        total_in[...] += t_dot(rows, moved[...])
        total_out[...] += t_dot(grad, context[0])

        @pl.when(b == blocks - 1)
        def _():
            hand_out(info, (total_in, total_out), pieces)

    results = call(
        body,
        info,
        [*grads, *normed, qkv, probs, context],
        [*(Close(w) for w in weights), gains],
        partial_rows(blocks, part, width),
        [*piece_shapes(width // 8, 4 * size), like((1, width), f32)],
        [
            pltpu.VMEM((width, 3 * size), f32),
            pltpu.VMEM((width, size), f32),
            pltpu.VMEM((slot, 3 * size), bf16),
        ],
        flops=2 * blocks * slot * (width * size * 8 + 20 * slot * size),
        steps=blocks,
    )
    return results[:4], results[4:12], results[12]


def ffn_scratch(width, hidden, pieces):
    return [
        *[pltpu.VMEM((width, hidden), bf16)] * 2,
        pltpu.SemaphoreType.DMA((2, len(pieces))),
    ]


def encoder_ffn(info, normed, pieces, hidden):
    blocks, part, width = normed[0].shape
    slot = part * len(normed)

    def body(info, rows, pieces, outs, _, scratch):
        active, slope = outs[:2]
        w_inner, w_outer, signals = scratch

        @pl.when(pl.program_id(0) == 0)
        def _():
            assemble(info, pieces, (w_inner, w_outer), signals)

        value, bend = gelu_both(dot(token_rows(rows), w_inner[...]))
        low = value.astype(bf16)
        active[...] = low.reshape(active.shape)
        slope[...] = bend.astype(bf16).reshape(slope.shape)
        emit(dot_t(low, w_outer[...]), outs[2:])

    return call(
        body,
        info,
        normed,
        [Far(p) for p in pieces],
        [*[like((blocks, slot, hidden), bf16)] * 2, *partial_rows(blocks, part, width)],
        [],
        ffn_scratch(width, hidden, pieces),
        flops=4 * blocks * slot * width * hidden,
        steps=blocks // 2,
        each=2,
    )


def encoder_ffn_back(info, grads, slope, weights):
    blocks, (_, part, width) = slope.shape[0], grads[0].shape
    slot = part * len(grads)
    hidden = slope.shape[2]

    def body(info, stepped, weights, outs, ends, scratch):
        dinner = outs[0]
        w_inner, w_outer = weights
        back = dot(token_rows(stepped[:4]), w_outer[...])
        low = (back * stepped[4][...].reshape(back.shape).astype(f32)).astype(bf16)
        dinner[...] = low.reshape(dinner.shape)
        emit(dot_t(low, w_inner[...]), outs[1:])

    return call(
        body,
        info,
        [*grads, slope],
        [Close(w) for w in weights],
        [like((blocks, slot, hidden), bf16), *partial_rows(blocks, part, width)],
        [],
        flops=4 * blocks * slot * width * hidden,
        steps=blocks // 2,
        each=2,
    )


def weight_grads(info, pairs, more=(), cut=True):
    blocks, (_, part, width) = pairs[0][1].shape[0], pairs[0][0][0].shape
    widths = [right.shape[2] for _, right in pairs]

    def body(info, stepped, more, __, ends, totals):
        totals = totals if cut else ends
        for k, total in enumerate(totals):
            left, right = token_rows(stepped[5 * k : 5 * k + 4]), stepped[5 * k + 4]
            total[...] = t_dot(left, right[...].reshape(left.shape[0], total.shape[1]))
        if cut:
            hand_out(info, (*totals, *more), ends)

    return call(
        body,
        info,
        [a for left, right in pairs for a in (*left, right)],
        more,
        [],
        piece_shapes(width // 8, sum(widths) + sum(m.shape[1] for m in more))
        if cut
        else [like((width, w), f32) for w in widths],
        [pltpu.VMEM((width, w), f32) for w in widths] if cut else [],
        flops=2 * blocks * part * 4 * width * sum(widths),
        each=blocks,
    )


def finish(info, terms, widths, turned):
    terms = [part(t) for t in terms]
    rows = terms[0].array.shape[0]
    shapes = [(w, rows) if t else (rows, w) for w, t in zip(widths, turned, strict=True)]

    def body(info, _, ins, __, outs, ___):
        total = terms[0].read(ins[0])
        for term, ref in zip(terms[1:], ins[1:], strict=True):
            total = total + term.read(ref).astype(f32)
        column = 0
        for out, wide, turn in zip(outs, widths, turned, strict=True):
            found = total[:, column : column + wide]
            out[...] = found.T if turn else found
            column += wide

    return call(body, info, [], [t.array for t in terms], [], [like(s, f32) for s in shapes])


def cross_forward(info, states, weights, decoder, own_question, count_q, count_pass):
    rows_in, terms, gains = decoder
    blocks = count_q * count_pass
    _, part, width = states[0].shape
    slot = part * len(states)
    rows_dec = rows_in.shape[0]
    size = weights[1].shape[1]
    steps = 2

    def body(info, rows, fixed, outs, ends, scratch):
        weight, w_query, rows_in, *terms, gains, question = fixed
        after_self, normed, queries, stats = ends
        held = scratch[0]
        b = pl.program_id(0)

        @pl.when(b == 0)
        def _():
            after_self[...] = rows_in[...].astype(f32) + summed(terms)
            normed[...] = norm_rows(after_self[...], gains[1:2, :]).astype(bf16)
            queries[...] = dot(normed[...], w_query[...]).astype(bf16)

        made = dot(token_rows(rows), weight[...]).astype(bf16)
        outs[0][...] = made.reshape(outs[0].shape)
        each = made.shape[0]
        held[pl.ds(pl.multiple_of(b * each, each), each), :] = made

        @pl.when(b == steps - 1)
        def _():
            allowed = keys_used(info, question, range(blocks), part, slot, count_pass)
            lane = lax.broadcasted_iota(jnp.int32, (rows_dec, HDIM), 1)
            keys, vals = head_parts(held[...], 2)
            asking = head_parts(queries[...], 1)[0]
            scores = [dot_t(q * SCALE, t) for q, t in zip(asking, keys, strict=True)]
            for k, score in enumerate(scores):
                score = jnp.where(allowed, score, masked_score)
                top = jnp.max(score, axis=-1, keepdims=True)
                spread_out = jnp.exp(score - top)
                total = jnp.sum(spread_out, axis=-1, keepdims=True)
                at = k * LANES
                stats[:, at : at + HDIM] = dot(spread_out.astype(bf16), vals[k])
                stats[:, at + HDIM : at + LANES] = jnp.where(lane == 0, top, total)

    return call(
        body,
        info,
        states,
        [*(Close(w) for w in weights), rows_in, *terms, gains, own_question],
        [like((blocks, slot, 2 * size), bf16)],
        [
            Later(like((rows_dec, width), f32)),
            Later(like((rows_dec, width), bf16)),
            like((rows_dec, size), bf16),
            like((rows_dec, size // HDIM * LANES), f32),
        ],
        [pltpu.VMEM((blocks * slot, 2 * size), bf16)],
        flops=4 * blocks * slot * width * size,
        steps=steps,
        each=blocks // steps,
    )


def merged(first, second):
    lane = lax.broadcasted_iota(jnp.int32, (first.shape[0], HDIM), 1)
    found = []
    for at in range(0, first.shape[1], LANES):
        tops = [v[:, at + HDIM : at + HDIM + 1] for v in (first, second)]
        totals = [v[:, at + HDIM + 1 : at + HDIM + 2] for v in (first, second)]
        top = jnp.maximum(*tops)
        scales = [jnp.exp(t - top) for t in tops]
        total = totals[0] * scales[0] + totals[1] * scales[1]
        found.append(first[:, at : at + HDIM] * scales[0] + second[:, at : at + HDIM] * scales[1])
        found.append(jnp.where(lane == 0, top, total))
    return jnp.concatenate(found, axis=1)


def in_order(info, bits, own, other):
    later = (info[BLK] & bits) != 0
    return jnp.where(later, other, own), jnp.where(later, own, other)


def merge(info, own, other, bits):
    def body(info, _, ins, __, outs, ___):
        outs[0][...] = merged(*in_order(info, bits, ins[0][...], ins[1][...]))

    return call(body, info, [], [own, other], [], [like(own.shape, f32)])[0]


def cross_out(info, stats, bits, w_output):
    rows, columns = stats[0].shape
    size = columns // LANES * HDIM
    width = w_output.shape[0]

    def body(info, _, ins, __, outs, scratch):
        w_output = ins[-1]
        out, log_total, context, own, sent = outs
        values = [r[...] for r in ins[:-1]]
        near = merged(*in_order(info, bits[0], *values[:2]))
        far = merged(*in_order(info, bits[0], *values[2:]))
        stats = merged(*in_order(info, bits[1], near, far))
        log_total[...] = jnp.zeros_like(log_total)
        for k, at in enumerate(heads_in(size)):
            base = k * LANES
            top = stats[:, base + HDIM : base + HDIM + 1]
            total = stats[:, base + HDIM + 1 : base + HDIM + 2]
            out[:, at] = stats[:, base : base + HDIM] / total
            log_total[:, k : k + 1] = top + jnp.log(total)
        context[...] = out[...].astype(bf16)
        own[...] = dot_t(context[...], w_output[...])
        sent[...] = own[...].astype(bf16)

    return call(
        body,
        info,
        [],
        [*stats, w_output],
        [],
        [
            like((rows, size), f32),
            like((rows, LANES), f32),
            Later(like((rows, size), bf16)),
            like((rows, width), f32),
            like((rows, width), bf16),
        ],
        flops=2 * rows * size * width,
    )


def cross_back(info, key_vals, inputs, own_question, count_pass, slot, part):
    cotangent, after_cross, terms, gains, w_output, out, log_total, queries, weight = inputs
    blocks = key_vals.shape[0]
    rows_dec, width = after_cross.shape
    size = queries.shape[1]

    def body(info, stepped, fixed, outs, ends, scratch):
        cotangent, after_cross, own, r1, r2, r3, gains, w_output, out, log_total, queries, weight, question = fixed
        key_vals = stepped[0]
        dkey_vals = outs[0]
        dcross, dcross_low, gain_out, dqueries = ends
        total = summed((own, r1, r2, r3))
        back, gain_out[...] = norm_back(after_cross[...], gains[2:3, :], total)
        dcross[...] = cotangent[...].astype(f32) + back
        dcross_low[...] = dcross[...].astype(bf16)
        dcontext = dot(dcross_low[...], w_output[...]).astype(bf16)
        allowed = keys_used(info, question, range(blocks), part, slot, count_pass)
        keys, vals = head_parts(key_vals[...].reshape(blocks * slot, 2 * size), 2)
        asking = head_parts(queries[...], 1)[0]
        cuts = head_parts(dcontext, 1)[0]
        outs_of = head_parts(out[...], 1)[0]
        scores = [dot_t(q * SCALE, t) for q, t in zip(asking, keys, strict=True)]
        backs = [dot_t(c, v) for c, v in zip(cuts, vals, strict=True)]
        probs, lows = [], []
        for k, score in enumerate(scores):
            row_term = jnp.sum(cuts[k].astype(f32) * outs_of[k], axis=-1, keepdims=True)
            score = jnp.where(allowed, score, masked_score)
            probs.append(jnp.exp(score - log_total[:, k : k + 1]))
            lows.append((probs[k] * (backs[k] - row_term)).astype(bf16))
        dvals = [t_dot(p.astype(bf16), c) for p, c in zip(probs, cuts, strict=True)]
        dkeys = [t_dot(d, q) * SCALE for d, q in zip(lows, asking, strict=True)]
        found = [dot(d, t) * SCALE for d, t in zip(lows, keys, strict=True)]
        dqueries[...] = jnp.concatenate(found, axis=1)
        made = jnp.concatenate([*dkeys, *dvals], axis=1).astype(bf16)
        dkey_vals[...] = made.reshape(dkey_vals.shape)
        emit(dot_t(made, weight[...]), outs[1:])

    return call(
        body,
        info,
        [key_vals],
        [
            cotangent,
            after_cross,
            *terms,
            gains,
            w_output,
            out,
            log_total,
            queries,
            Close(weight),
            own_question,
        ],
        [like(key_vals.shape, bf16), *partial_rows(blocks, part, width)],
        [
            Later(like((rows_dec, width), f32)),
            Later(like((rows_dec, width), bf16)),
            Later(like((rows_dec, width), f32)),
            like((rows_dec, size), f32),
        ],
        flops=4 * blocks * slot * width * size,
        each=blocks,
    )


def summed(refs):
    count = refs[0].shape[0]

    def rows(ref):
        return ref[...] if len(ref.shape) == 2 else ref[0, :count, :]

    terms = [rows(ref).astype(f32) for ref in refs[1:]]
    total = refs[0][...]
    for term in terms:
        total = total + term
    return total


def decoder_self(info, rows, gains, pieces, column_from, size, order):
    count, width = rows.shape

    def body(info, _, ins, __, outs, scratch):
        rows, gains, order_q, order_k = ins[:4]
        normed, qkv, probs, context, own, sent, weight = outs
        assemble(info, ins[4:], (weight,), scratch[0], column_from)
        normed[...] = norm_rows(rows[...].astype(f32), gains[0:1, :]).astype(bf16)
        qkv[...] = dot(normed[...], weight[:, : 3 * size]).astype(bf16)
        query_at, key_at = order_q[...], order_k[...]
        same = lax.div(query_at, 1000) == lax.div(key_at, 1000)
        allowed = same & (key_at <= query_at) & (key_at >= 0) & (query_at >= 0)
        for k, at in enumerate(heads_in(size)):
            query, keys, vals = (qkv[:, j * size + at.start : j * size + at.stop] for j in range(3))
            scores = jnp.where(allowed, dot_t(query, keys) * SCALE, masked_score)
            spread_out = jnp.exp(scores - jnp.max(scores, axis=-1, keepdims=True))
            share_out = spread_out / jnp.sum(spread_out, axis=-1, keepdims=True)
            share_out = jnp.where(allowed, share_out, 0.0)
            probs[k] = share_out
            context[:, at] = dot(share_out.astype(bf16), vals).astype(bf16)
        own[...] = dot_t(context[...], weight[:, 3 * size :])
        sent[...] = own[...].astype(bf16)

    return call(
        body,
        info,
        [],
        [rows, gains, *order, *(Far(p) for p in pieces)],
        [],
        [
            Later(like((count, width), bf16)),
            Later(like((count, 3 * size), bf16)),
            Later(like((size // HDIM, count, count), f32)),
            Later(like((count, size), bf16)),
            like((count, width), f32),
            like((count, width), bf16),
            Later(like((width, 4 * size), bf16)),
        ],
        [pltpu.SemaphoreType.DMA((1, len(pieces)))],
        flops=2 * count * width * size * 4,
    )


def decoder_back(info, cotangent, pieces):
    count, width = cotangent.shape
    hidden = pieces[0].shape[1] // 2

    def body(info, _, ins, __, outs, scratch):
        w_inner, w_outer, back = outs
        assemble(info, ins[1:], (w_inner, w_outer), scratch[0])
        back[...] = dot(ins[0][...], w_outer[...])

    return call(
        body,
        info,
        [],
        [cotangent, *(Far(p) for p in pieces)],
        [],
        [Near(like((width, hidden), bf16)), like((width, hidden), bf16), like((count, hidden), f32)],
        [pltpu.SemaphoreType.DMA((2, len(pieces)))],
        flops=2 * count * width * hidden,
    )


def decoder_ffn(info, after_self, terms, back, gains, w_inner):
    count, width = after_self.shape
    hidden = w_inner.shape[1]

    def body(info, _, ins, __, outs, scratch):
        after_self, own, r1, r2, r3, back, gains, w_inner = ins
        after_cross, normed, active, dinner, own_back, sent_back = outs
        after_cross[...] = after_self[...] + summed((own, r1, r2, r3))
        normed[...] = norm_rows(after_cross[...], gains[2:3, :]).astype(bf16)
        value, slope = gelu_both(dot(normed[...], w_inner[...]))
        active[...] = value.astype(bf16)
        dinner[...] = (slope * back[...]).astype(bf16)
        own_back[...] = dot_t(dinner[...], w_inner[...])
        sent_back[...] = own_back[...].astype(bf16)

    return call(
        body,
        info,
        [],
        [after_self, *terms, back, gains, Close(w_inner)],
        [],
        [
            like((count, width), f32),
            Later(like((count, width), bf16)),
            Later(like((count, hidden), bf16)),
            Later(like((count, hidden), bf16)),
            like((count, width), f32),
            like((count, width), bf16),
        ],
        flops=4 * count * width * hidden,
    )


def rows_back(info, terms, weight):
    (count, size), width = terms[0].shape, weight.shape[0]

    def body(info, _, ins, __, outs, scratch):
        low, own, sent = outs
        total = ins[0][...]
        for term in ins[1:-1]:
            total = total + term[...]
        low[...] = total.astype(bf16)
        own[...] = dot_t(low[...], ins[-1][...])
        sent[...] = own[...].astype(bf16)

    return call(
        body,
        info,
        [],
        [*terms, weight],
        [],
        [
            Later(like((count, size), bf16)),
            like((count, width), f32),
            like((count, width), bf16),
        ],
        flops=2 * count * width * size,
    )


def decoder_self_back(
    info, dcross, after_self, terms, gains, weight, qkv, probs
):
    count, width = after_self.shape
    size = weight.shape[1] // 4

    def body(info, _, ins, __, outs, scratch):
        dcross, after_self, *terms, gains, weight, qkv, probs = ins
        dself, dself_low, gain_rows, moved, own_back, sent_back = outs
        back, gain_rows[...] = norm_back(after_self[...], gains[1:2, :], summed(terms))
        dself[...] = dcross[...] + back
        dself_low[...] = dself[...].astype(bf16)
        dcontext = dot(dself_low[...], weight[:, 3 * size :]).astype(bf16)
        for k, at in enumerate(heads_in(size)):
            query, keys, vals = (qkv[:, j * size + at.start : j * size + at.stop] for j in range(3))
            share_out = probs[k]
            dprobs = dot_t(dcontext[:, at], vals)
            dscores = share_out * (dprobs - jnp.sum(share_out * dprobs, axis=-1, keepdims=True))
            dscores = dscores.astype(bf16)
            found = (
                dot(dscores, keys) * SCALE,
                t_dot(dscores, query) * SCALE,
                t_dot(share_out.astype(bf16), dcontext[:, at]),
            )
            for j, term in enumerate(found):
                moved[:, j * size + at.start : j * size + at.stop] = term.astype(bf16)
        own_back[...] = dot_t(moved[...], weight[:, : 3 * size])
        sent_back[...] = own_back[...].astype(bf16)

    return call(
        body,
        info,
        [],
        [dcross, after_self, *terms, gains, weight, qkv, probs],
        [],
        [
            like((count, width), f32),
            Later(like((count, width), bf16)),
            like((count, width), f32),
            Later(like((count, 3 * size), bf16)),
            like((count, width), f32),
            like((count, width), bf16),
        ],
        flops=2 * count * width * size * 8,
    )


def own_rows(info, values, dec_own):
    found = values[:dec_own]
    for k in range(1, values.shape[0] // dec_own):
        found = jnp.where(info[HEAD] == k, values[k * dec_own : (k + 1) * dec_own], found)
    return found


def decoder_ends(
    info, rows, dself, terms, gains, after_cross, out_terms, gain_rows, gain_sums, dec_own
):
    count, width = dself.shape

    def body(info, _, ins, __, outs, scratch):
        rows, dself, after_cross, gains = ins[:4]
        three, four, zero, one = ins[-4:]
        grad, states, found = outs
        total, out_total = summed(ins[4:8]), summed(ins[8:12])
        back, two = norm_back(rows[...].astype(f32), gains[0:1, :], total)
        grad[...] = own_rows(info, dself[...] + back, dec_own)
        states[...] = own_rows(info, after_cross[...] + out_total, dec_own).astype(bf16)
        row = lax.div(lax.broadcasted_iota(jnp.int32, (count, 1), 0), dec_own)
        mine = (row == info[HEAD]) & (info[BLK] == 0)
        found[0:1, :] = zero[...]
        found[1:2, :] = one[...]
        for k, values in enumerate((two, three[...], four[...])):
            found[2 + k : 3 + k, :] = jnp.sum(jnp.where(mine, values, 0.0), axis=0, keepdims=True)

    return call(
        body,
        info,
        [],
        [rows, dself, after_cross, gains, *terms, *out_terms, *gain_rows, *gain_sums],
        [],
        [like((dec_own, width), f32), like((dec_own, width), bf16), like((5, width), f32)],
    )


def decoder_weight_grads(info, own, pairs_in, pairs_out):
    count, width = pairs_in[0][0].shape

    def body(info, _, ins, __, outs, scratch):
        row = lax.broadcasted_iota(jnp.int32, (own, width), 0) + info[BLK] * own
        column = lax.broadcasted_iota(jnp.int32, (own, width), 1)
        pick = jnp.where(row == column, 1.0, 0.0).astype(bf16)
        outs, ins = iter(outs), iter(ins)
        for _, _, arrays in pairs_in:
            left, right = next(ins)[...], next(ins)[...]
            found = t_dot(dot_t(left, pick).astype(bf16), right)
            wide = found.shape[1] // arrays
            for k in range(arrays):
                next(outs)[...] = found[:, k * wide : (k + 1) * wide]
        for _ in pairs_out:
            left, right = next(ins)[...], next(ins)[...]
            next(outs)[...] = t_dot(left, dot_t(right, pick).astype(bf16))

    outs = [like((own, r.shape[1] // n), f32) for _, r, n in pairs_in for _ in range(n)]
    outs += [like((l.shape[1], own), f32) for l, _ in pairs_out]
    flat = [a for pair in pairs_in for a in pair[:2]] + [a for pair in pairs_out for a in pair]
    return call(body, info, [], flat, [], outs, flops=2 * count * own * width * 10, least=0)


def shards(
    encoder_input,
    passage_lengths,
    decoder_input,
    encoder_query,
    encoder_key,
    encoder_value,
    encoder_output,
    encoder_inner,
    encoder_outer,
    decoder_query,
    decoder_key,
    decoder_value,
    decoder_output,
    cross_query,
    cross_key,
    cross_value,
    cross_output,
    decoder_inner,
    decoder_outer,
    encoder_gains,
    decoder_gains,
    encoder_cotangent,
    decoder_cotangent,
):
    head, blk = lax.axis_index("head"), lax.axis_index("blk")
    blk_count, head_count = lax.axis_size("blk"), lax.axis_size("head")
    count_q, count_pass, part, width = encoder_input.shape
    blocks = count_q * count_pass
    slot = part * head_count
    own = width // blk_count
    if blk_count == 8:
        places = jnp.asarray(place_table(8))[blk]
    else:
        places = jnp.arange(8, dtype=jnp.int32)
    info = jnp.concatenate(
        [places, jnp.stack([head, blk]).astype(jnp.int32), passage_lengths.reshape(blocks)]
    )

    size, units = encoder_query.shape[1], encoder_inner.shape[1]
    inputs = encoder_input.reshape(blocks, part, width)
    dec_part = decoder_input.shape[1]
    dec_own = count_q * dec_part
    dec_rows = dec_own * head_count
    filled = -(-dec_rows // 16) * 16

    attention = jnp.concatenate(
        [encoder_query, encoder_key, encoder_value, encoder_output.T], axis=1
    )
    attention, inputs = sync(attention, inputs)
    attention = fetch_step(fetch_start(attention), -1, 1)
    first = by_rows(
        lambda x, g: (norm_rows(x, g[0:1]),), info, [inputs], [encoder_gains], [bf16]
    )[0]
    attention, first = sync(attention, first)

    attention = fetch_step(attention, -2, 2)
    first_all = [first, swap(first, "head", 1), swap(first, "head", 2)]
    ffn = jnp.concatenate(
        [
            encoder_inner,
            encoder_outer.T,
            decoder_query,
            decoder_key,
            decoder_value,
            decoder_output.T,
            cross_key,
            cross_value,
            cross_query,
            cross_output.T,
        ],
        axis=1,
    )
    at_self, at_cross = 2 * units, 2 * units + 4 * size
    attention, ffn = sync(attention, ffn)

    attention = fetch_step(attention, -3, 3)
    pair = jnp.stack([decoder_input, decoder_cotangent]).reshape(2, dec_own, width)
    both = lax.all_gather(pair, "head", axis=1, tiled=True)
    both = jnp.pad(both, ((0, 0), (0, filled - dec_rows), (0, 0)))
    attention, first_all, ffn, both = sync(attention, first_all, ffn, both)

    attention, ffn = fetch_step(attention, -4), fetch_step(fetch_start(ffn), 1)
    first_all.append(swap(first_all[2], "head", 1))
    dec_ffn = jnp.concatenate([decoder_inner, decoder_outer.T], axis=1)
    attention, ffn, first_all, dec_ffn = sync(attention, ffn, first_all, dec_ffn)

    ffn = fetch_step(ffn, -1, 2)
    qkv, probs, context, *partial = encoder_attention(
        info, first_all, in_turn(attention)
    )
    partial, ffn = sync(partial, ffn)

    def to_core(partial):
        return swap(partial[3], "head", 1)

    def to_chip(partial, corner):
        far = (partial[2] + corner.astype(f32)).astype(bf16)
        return [swap(far, "head", 2), swap(partial[1], "head", 1)]

    ffn = fetch_step(ffn, -2, 3)
    partial, corner = sync(partial, to_core(partial))
    partial, arrived, ffn = sync(partial, to_chip(partial, corner), ffn)

    def enter_ffn(x, a, b, c, g):
        hidden = x + a + b + c
        return hidden, norm_rows(hidden, g[1:2])

    hidden, second = by_rows(
        enter_ffn, info, [inputs, partial[0], *arrived], [encoder_gains], [f32, bf16]
    )
    ffn = fetch_step(ffn, -3, 4)
    def spread(rows):
        return [rows, swap(rows, "head", 1), swap(rows, "head", 2)]

    def riders(all_rows):
        return [Rider(rows, blocks) for rows in all_rows[1:]]

    second, dec_ffn = sync(second, dec_ffn)
    second_all = spread(second)
    second_all, ffn, dec_ffn = sync(second_all, ffn, dec_ffn)
    dec_ffn = fetch_step(fetch_start(dec_ffn), -1, 1)
    second_all.append(swap(second_all[2], "head", 1))
    second_all, ffn = sync(second_all, ffn)
    ffn = in_turn(ffn)

    active, slope, *partial = encoder_ffn(info, second_all, ffn, units)
    partial, dec_ffn = sync(partial, dec_ffn)
    partial, corner, both, dec_ffn = sync(partial, to_core(partial), both, dec_ffn)
    dec_in, cotangent = both[0], both[1]

    index = np.arange(filled)
    question = (index % dec_own) // dec_part
    position = index // dec_own * dec_part + index % dec_part
    order = np.where(index < dec_rows, question * 1000 + position, -1).astype(np.int32)
    order = (jnp.asarray(order[:, None]), jnp.asarray(order[None, :]))
    question = jnp.asarray(question[:, None].astype(np.int32))

    arrived = to_chip(partial, corner)
    dec_ffn = fetch_step(dec_ffn, -2, 2)
    third, dec_qkv, dec_probs, dec_context, mine, sent, w_self = decoder_self(
        info, dec_in, decoder_gains, ffn, at_self, size, order
    )
    partial, arrived, mine, sent, dec_ffn = sync(partial, arrived, mine, sent, dec_ffn)
    states, states_sent = by_rows(
        lambda h, a, b, c: (h + a + b + c,),
        info,
        [hidden, partial[0], *arrived],
        [],
        [bf16],
        riders=sent,
    )
    states_sent, dec_ffn = sync(states_sent, dec_ffn)
    states_all = spread(states_sent)
    dec_ffn = fetch_step(dec_ffn, -3, 3)
    w_cross, w_cross_query, w_cross_output = gathered(
        info, ffn, (2 * size, size, size), at_cross
    )
    states_all, dec_ffn, w_cross = sync(states_all, dec_ffn, w_cross)
    dec_ffn = fetch_step(dec_ffn, -4)
    states_all = sync(*states_all, swap(states_all[2], "head", 1))

    key_vals, after_self, fourth, queries, stats = cross_forward(
        info,
        states_all,
        (w_cross, w_cross_query),
        (dec_in, [mine, *riders(states_all)], decoder_gains),
        question,
        count_q,
        count_pass,
    )
    bits = [1 << k for k in range((blk_count - 1).bit_length())]
    last_two = (bits[-2], bits[-1], bits[-2] + bits[-1])
    for k in bits[:-2]:
        stats = merge(info, stats, swap(stats, "blk", k), k)
    stats, dec_ffn = sync(stats, dec_ffn)
    stats_all = [stats, *(swap(stats, "blk", k) for k in last_two)]
    w_dec_inner, w_dec_outer, outer_back = decoder_back(info, cotangent, in_turn(dec_ffn))
    stats_all, outer_back = sync(stats_all, outer_back)
    out, log_total, cross_context, mine, sent = cross_out(
        info, stats_all, bits[-2:], w_cross_output
    )
    after_cross, fifth, dec_active, dec_dinner, mine, sent = decoder_ffn(
        info, after_self, [mine, *share(sent)], outer_back, decoder_gains, w_dec_inner
    )
    dkey_vals, *rest = cross_back(
        info,
        key_vals,
        (
            cotangent,
            after_cross,
            [mine, *share(sent)],
            decoder_gains,
            w_cross_output,
            out,
            log_total,
            queries,
            w_cross,
        ),
        question,
        count_pass,
        slot,
        part,
    )
    partial, (dcross, dcross_low, gain_four, dqueries) = rest[:4], rest[4:]

    def some(value, which):
        for k in which:
            value = value + swap(value, "blk", k)
        return value

    partial, dqueries, dkey_vals = sync(partial, dqueries, dkey_vals)
    partial, corner, dkey_vals, dqueries = sync(partial, to_core(partial), dkey_vals, dqueries)
    arrived = to_chip(partial, corner)
    dqueries = some(dqueries, bits[:-1])
    cross_sum = weight_grads(info, [(states_all, dkey_vals)], cut=False)[0]
    _, out_mine, out_sent = rows_back(info, [dec_active], w_dec_outer)
    partial, arrived, cross_sum, dqueries, out_sent = sync(
        partial, arrived, cross_sum, dqueries, out_sent
    )

    def enter_back(cot, a, b, c):
        grad = cot + a + b + c
        return grad, grad

    dstates, dstates_low = by_rows(
        enter_back,
        info,
        [encoder_cotangent.reshape(blocks, part, width), partial[0], *arrived],
        [],
        [f32, bf16],
        riders=out_sent,
        kept=False,
    )
    dstates_low, cross_sum, dqueries = sync(dstates_low, cross_sum, dqueries)
    dstates_all = spread(dstates_low)
    terms = [dqueries, swap(dqueries, "blk", bits[-1])]
    dqueries, mine, sent = rows_back(info, terms, w_cross_query)
    w_ffn = gathered(info, ffn, (units, units))
    dstates_all, sent, w_ffn = sync(dstates_all, sent, w_ffn)
    terms = [mine, *share(sent)]
    dstates_all = sync(*dstates_all, swap(dstates_all[2], "head", 1))
    out_terms = [out_mine, *riders(dstates_all)]
    dinner, *partial = encoder_ffn_back(info, dstates_all, slope, w_ffn)
    partial, dinner, terms = sync(partial, dinner, terms)
    partial, corner, dinner, dstates_all = sync(partial, to_core(partial), dinner, dstates_all)
    arrived = to_chip(partial, corner)
    dself, dself_low, gain_three, dself_qkv, own_back, sent_back = decoder_self_back(
        info,
        dcross,
        after_self,
        terms,
        decoder_gains,
        w_self,
        dec_qkv,
        dec_probs,
    )
    ffn_sums = weight_grads(
        info, [(second_all, dinner), (dstates_all, active)], [cross_sum]
    )
    partial, arrived, ffn_sums, sent_back = sync(partial, arrived, ffn_sums, sent_back)

    def middle_back(dy, h, a, b, c, g):
        back, gain_rows = norm_back(h, g[1:2], a + b + c)
        grad = dy + back
        return grad, grad, gain_rows

    dhidden, dhidden_low, gain_one = by_rows(
        middle_back,
        info,
        [dstates, hidden, partial[0], *arrived],
        [encoder_gains],
        [f32, bf16],
        gain=True,
        riders=sent_back,
        kept=False,
    )
    dhidden_low, ffn_sums = sync(dhidden_low, ffn_sums)
    dhidden_all = spread(dhidden_low)
    ffn_moving = reduce_step(info, (ffn_sums, None, 1))[0]
    w_attention = gathered(info, in_turn(attention), (3 * size, size))
    dhidden_all, ffn_moving, w_attention = sync(dhidden_all, ffn_moving, w_attention)
    ffn_moving = reduce_step(info, (ffn_sums, ffn_moving, 2))[0]
    dhidden_all = sync(*dhidden_all, swap(dhidden_all[2], "head", 1))
    terms = [own_back, *riders(dhidden_all)]

    partial, sums, gain_zero = encoder_attention_back(
        info, dhidden_all, first_all, qkv, probs, context, w_attention, encoder_gains
    )
    partial, sums, ffn_moving, gain_zero = sync(partial, sums, ffn_moving, gain_zero)
    ffn_moving, moving = reduce_step(info, (ffn_sums, ffn_moving, 3), (sums, None, 1))[:2]
    corner = to_core(partial)
    dec_grad, dec_states, gains = decoder_ends(
        info,
        dec_in,
        dself,
        terms,
        decoder_gains,
        after_cross,
        out_terms,
        [gain_three, gain_four],
        [gain_zero, gain_one],
        dec_own,
    )
    for k in (1, 2):
        gains = gains + swap(gains, "head", k)
    (
        grad_dec_query,
        grad_dec_key,
        grad_dec_value,
        grad_cross_query,
        grad_dec_inner,
        grad_dec_outer,
        grad_dec_output,
        grad_cross_output,
    ) = decoder_weight_grads(
        info,
        own,
        [
            (third, dself_qkv, 3),
            (fourth, dqueries, 1),
            (fifth, dec_dinner, 1),
            (cotangent, dec_active, 1),
        ],
        [(dec_context, dself_low), (cross_context, dcross_low)],
    )
    partial, corner, moving, gains, ffn_moving, grad_dec_query = sync(
        partial, corner, moving, gains, ffn_moving, grad_dec_query
    )

    def dec_shape(values):
        return values.reshape(count_q, dec_part, width)

    ffn_moving, moving = reduce_step(info, (ffn_sums, ffn_moving, 4), (sums, moving, 2))[:2]
    arrived = to_chip(partial, corner)
    gains = some(gains, bits[:1])
    partial, arrived, moving, gains, ffn_moving = sync(
        partial, arrived, moving, gains, ffn_moving
    )

    def last_back(dh, x, a, b, c, g):
        return (dh + norm_back(x, g[0:1], a + b + c)[0],)

    moving = reduce_step(info, (sums, moving, 3))[0]
    gains = some(gains, bits[1:-1])
    input_grad = by_rows(
        last_back,
        info,
        [dhidden, inputs, partial[0], *arrived],
        [encoder_gains],
        [f32],
    )[0]
    moving, gains, input_grad, ffn_moving = sync(moving, gains, input_grad, ffn_moving)
    moving, (gains, ffn_moving) = reduce_step(info, (sums, moving, 4), hold=(gains, ffn_moving))
    last = swap(gains, "blk", bits[-1])
    grad_inner, grad_outer, grad_cross_key, grad_cross_value = finish(
        info,
        reduce_terms(ffn_sums, ffn_moving),
        (units, units, size, size),
        (False,) * 4,
    )
    enc_gain_grads, dec_gain_grads = gains[:2] + last[:2], gains[2:] + last[2:]
    grad_query, grad_key, grad_value, grad_output = finish(
        info, reduce_terms(sums, moving), (size,) * 4, (False, False, False, True)
    )

    return (
        states.reshape(encoder_input.shape),
        dec_shape(dec_states),
        input_grad.reshape(encoder_input.shape),
        dec_shape(dec_grad),
        grad_query,
        grad_key,
        grad_value,
        grad_output,
        grad_inner,
        grad_outer.T,
        grad_dec_query,
        grad_dec_key,
        grad_dec_value,
        grad_dec_output,
        grad_cross_query,
        grad_cross_key,
        grad_cross_value,
        grad_cross_output,
        grad_dec_inner,
        grad_dec_outer.T,
        enc_gain_grads,
        dec_gain_grads,
    )


def solution(mesh):
    placed = (
        P(None, "blk", "head", None),
        P(None, "blk"),
        P(None, "head", None),
        P("blk", "head"),
        P("blk", "head"),
        P("blk", "head"),
        P("head", "blk"),
        P("blk", "head"),
        P("head", "blk"),
        P("blk", "head"),
        P("blk", "head"),
        P("blk", "head"),
        P("head", "blk"),
        P("blk", "head"),
        P("blk", "head"),
        P("blk", "head"),
        P("head", "blk"),
        P("blk", "head"),
        P("head", "blk"),
        P(),
        P(),
        P(None, "blk", "head", None),
        P(None, "head", None),
    )
    return jax.shard_map(
        shards,
        mesh=mesh,
        in_specs=placed,
        out_specs=(placed[0], placed[2], placed[0], placed[2], *placed[3:19], P(), P()),
        check_vma=False,
    )
```

```python
import math

import jax
import jax.numpy as jnp
import numpy as np
from jax import lax
from jax.experimental import pallas as pl
from jax.experimental.pallas import tpu as pltpu
from jax.sharding import PartitionSpec as P

HDIM = 64
SCALE = HDIM ** (-0.5)
LANES = 128
EPS = 1e-06
VMEM_LIMIT = 24 * 1024 * 1024
LARGE = 1 << 19
masked_score = -1000000000.0
f32 = jnp.float32
bf16 = jnp.bfloat16

PLACES, HEAD, BLK, LENGTHS = 0, 8, 9, 10


def swap(value, axis, bits):
    size = lax.axis_size(axis)
    return lax.ppermute(value, axis, [(i, i ^ bits) for i in range(size)])


def sync(*values):
    return lax.optimization_barrier(values)


def share(value):
    return [swap(value, "head", k) for k in (1, 2, 3)]


def ring_order(count):
    return [*range(0, count, 2), *range(count - 1, 0, -2)]


OFFSETS = (0, -1, 1, -2, 2, -3, 3, -4)


def ring_steps(count):
    order = ring_order(count)
    forth = [(order[i], order[(i + 1) % count]) for i in range(count)]
    return forth, [(b, a) for a, b in forth]


def place_table(count):
    order = ring_order(count)
    at = {b: i for i, b in enumerate(order)}
    return np.array(
        [[order[(at[b] + o) % count] for o in OFFSETS] for b in range(count)], np.int32
    )


def gather_rows(own):
    return lax.all_gather(own, "blk", axis=0, tiled=True)


def fetch_start(own):
    if lax.axis_size("blk") == 8:
        return {0: own}
    return dict(zip(OFFSETS, jnp.split(gather_rows(own), 8, axis=0), strict=True))


def fetch_step(pieces, *offsets):
    count = lax.axis_size("blk")
    if count != 8:
        return pieces
    forth, back = ring_steps(count)
    more = {
        k: lax.ppermute(pieces[k + 1 if k < 0 else k - 1], "blk", forth if k < 0 else back)
        for k in offsets
    }
    return {**pieces, **more}


def in_turn(pieces):
    return [pieces[k] if k in pieces else pieces[-k] for k in OFFSETS]


@jax.tree_util.register_pytree_node_class
class Part:
    def __init__(self, array, start, width):
        self.array, self.start, self.width = array, start, width

    def tree_flatten(self):
        return (self.array,), (self.start, self.width)

    @classmethod
    def tree_unflatten(cls, places, arrays):
        return cls(*arrays, *places)

    def read(self, ref):
        return ref[:, self.start : self.start + self.width]


def part(value):
    return value if isinstance(value, Part) else Part(value, 0, value.shape[1])


def reduce_step(info, *rings, hold=None):
    count = lax.axis_size("blk")
    if count != 8:
        return [[] for _ in rings] + [hold]
    forth, back = ring_steps(count)
    plan = [[], []]
    for pieces, moving, step in rings:
        by = dict(zip(OFFSETS, pieces, strict=True))
        plan[0].append([*([] if step == 1 else [moving[0]]), by[(-4, 3, 2, 1)[step - 1]]])
        if step < 4:
            plan[1].append([*([] if step == 1 else [moving[1]]), by[(-3, -2, -1)[step - 1]]])
    plan = [p for p in plan if p]
    if len(rings) == 1 and rings[0][2] == 1:
        sent = [p[0][0] for p in plan]
    else:
        parts = [part(v) for p in plan for terms in p for v in terms]

        def body(info, _, ins, __, outs, ___):
            found = iter(zip(parts, ins, strict=True))
            for out, p in zip(outs, plan, strict=True):
                column = 0
                for terms in p:
                    values = [piece.read(ref) for piece, ref in (next(found) for _ in terms)]
                    total = values[0]
                    if len(values) == 2:
                        total = (total.astype(f32) + values[1].astype(f32)).astype(bf16)
                    out[:, column : column + total.shape[1]] = total
                    column += total.shape[1]

        rows = rings[0][0][0].shape[0]
        wide = [sum(part(terms[0]).width for terms in p) for p in plan]
        shapes = [like((rows, w), bf16) for w in wide]
        came_in = {id(m.array) for _, moving, _ in rings for m in moving or ()}
        given = [Close(p.array) if id(p.array) in came_in else p.array for p in parts]
        sent = call(body, info, [], given, [], [Near(v) for v in shapes], least=0)
    if hold is not None:
        sent, hold = sync(sent, hold)
    came = [lax.ppermute(v, "blk", way) for v, way in zip(sent, (forth, back), strict=False)]
    results, column = [], 0
    for k, (pieces, moving, step) in enumerate(rings):
        wide = pieces[0].shape[1]
        found = [Part(came[0], column, wide)]
        if step == 4:
            found.append(moving[1])
        else:
            before = sum(r[0][0].shape[1] for r in rings[:k] if r[2] < 4)
            found.append(Part(came[1], before, wide))
        results.append(found)
        column += wide
    return [*results, hold]


def reduce_terms(pieces, moving):
    if lax.axis_size("blk") != 8:
        everything = jnp.concatenate([p.astype(f32) for p in pieces], axis=0)
        return [lax.psum_scatter(everything, "blk", scatter_dimension=0, tiled=True)]
    return [pieces[0], *moving]


def dot(left, right, over=(1, 0)):
    return lax.dot_general(
        left, right, (((over[0],), (over[1],)), ((), ())), preferred_element_type=f32
    )


def dot_t(left, right):
    return dot(left, right, (1, 1))


def t_dot(left, right):
    return dot(left, right, (0, 0))


def norm_rows(values, gain):
    return values * lax.rsqrt(jnp.mean(values * values, axis=-1, keepdims=True) + EPS) * gain


def norm_back(values, gain, grad):
    inverse = lax.rsqrt(jnp.mean(values * values, axis=-1, keepdims=True) + EPS)
    unit = values * inverse
    weighted = grad * gain
    along = jnp.mean(weighted * unit, axis=-1, keepdims=True)
    return inverse * (weighted - unit * along), grad * unit


def gelu_both(values):
    root = math.sqrt(2.0 / math.pi)
    square = values * values
    bent = jnp.tanh(root * values * (1.0 + 0.044715 * square))
    half = 0.5 * (1.0 + bent)
    slope = half + 0.5 * values * (1.0 - bent * bent) * root * (1.0 + 3 * 0.044715 * square)
    return values * half, slope


def heads_in(width):
    return [slice(at, at + HDIM) for at in range(0, width, HDIM)]


def head_parts(values, count):
    size = values.shape[1] // count
    return [[values[:, j * size :][:, at] for at in heads_in(size)] for j in range(count)]


def by_passage(found, count):
    rows = [
        jnp.concatenate(found[at : at + count], axis=1) for at in range(0, len(found), count)
    ]
    return jnp.concatenate(rows, axis=0)


def assemble(info, pieces, targets, signals, column_from=0):
    rows = pieces[0].shape[0]
    copies = []
    for t, piece in enumerate(pieces):
        at = pl.ds(pl.multiple_of(info[PLACES + t] * rows, 16), rows)
        column = column_from
        for k, target in enumerate(targets):
            wide = target.shape[1]
            copies.append(
                pltpu.make_async_copy(
                    piece.at[:, column : column + wide], target.at[at, :], signals.at[k, t]
                )
            )
            column += wide
    for copy in copies:
        copy.start()
    for copy in copies:
        copy.wait()


def hand_out(info, sources, pieces):
    rows = pieces[0].shape[0]
    for t, piece in enumerate(pieces):
        at = pl.ds(pl.multiple_of(info[PLACES + t] * rows, 16), rows)
        column = 0
        for source in sources:
            piece[:, column : column + source.shape[1]] = source[at, :].astype(piece.dtype)
            column += source.shape[1]


def token_rows(refs):
    return jnp.concatenate([r[k] for k in range(refs[0].shape[0]) for r in refs], axis=0)


def emit(partial, outs):
    each, part, _ = outs[0].shape
    for k in range(each):
        for r, out in enumerate(outs):
            at = (k * len(outs) + r) * part
            out[k] = partial[at : at + part].astype(out.dtype)


def slots_used(info, b, part, slot):
    column = lax.broadcasted_iota(jnp.int32, (1, slot), 1)
    position = (lax.div(column, part) ^ info[HEAD]) * part + lax.rem(column, part)
    return position < info[LENGTHS + b]


def keys_used(info, question, passages, part, slot, count_pass):
    return jnp.concatenate(
        [
            slots_used(info, k, part, slot) & (question[...] == k // count_pass)
            for k in passages
        ],
        axis=1,
    )


def call(
    body, info, stepped, fixed, out_stepped, out_fixed, scratch=(), flops=0, steps=1, near=False, least=LARGE, each=1
):
    def by_step(shape):
        last = shape[0] // each - 1
        return pl.BlockSpec((each, *shape[1:]), lambda b: (jnp.minimum(b, last),) + (0,) * (len(shape) - 1))

    def whole(a):
        if type(a) is Far:
            return pl.BlockSpec(memory_space=pltpu.HBM)
        if isinstance(a, Rider):
            return pl.BlockSpec(a.shape, lambda b: (a.index, 0, 0))
        index = (0, a.index) if type(a) is Columns else (0,) * len(a.shape)
        return pl.BlockSpec(a.shape, lambda b: index)

    counts = [len(stepped), len(fixed), len(out_stepped), len(out_fixed), len(scratch)]
    stops = np.cumsum(counts)

    def split(info_ref, *refs):
        body(info_ref, *(refs[e - c : e] for c, e in zip(counts, stops, strict=True)))

    def large(a):
        return not near and math.prod(a.shape) * a.dtype.itemsize >= least

    def given(a):
        array = a.array if isinstance(a, (Columns, Far, Rider)) else a
        far = (large(a) and not isinstance(a, Close)) or (isinstance(a, Rider) and a.far)
        return pltpu.with_memory_space_constraint(array, pltpu.HBM) if far else array

    def made(a):
        if isinstance(a, Later) or (large(a) and not isinstance(a, Near)):
            return pltpu.HBM(a.shape, a.dtype)
        return a.array if isinstance(a, Near) else a

    arrays = [*stepped, *fixed, *out_stepped, *out_fixed]
    moved = sum(math.prod(a.shape) * a.dtype.itemsize for a in arrays)
    return pl.pallas_call(
        split,
        grid=(steps,),
        in_specs=[
            pl.BlockSpec(memory_space=pltpu.SMEM),
            *(by_step(a.shape) for a in stepped),
            *(whole(a) for a in fixed),
        ],
        out_specs=[
            *(by_step(a.shape) for a in out_stepped),
            *(whole(a) for a in out_fixed),
        ],
        out_shape=[made(a) for a in (*out_stepped, *out_fixed)],
        scratch_shapes=list(scratch),
        compiler_params=pltpu.CompilerParams(
            dimension_semantics=("arbitrary",), vmem_limit_bytes=VMEM_LIMIT
        ),
        cost_estimate=pl.CostEstimate(
            flops=int(flops), bytes_accessed=int(moved), transcendentals=0
        ),
    )(info, *(given(a) for a in (*stepped, *fixed)))


class Columns:
    def __init__(self, array, width, index):
        self.array, self.index, self.dtype = array, index, array.dtype
        self.shape = (array.shape[0], width)


class Near(Columns):
    def __init__(self, array):
        self.array, self.shape, self.dtype = array, array.shape, array.dtype


class Later(Near):
    pass


class Rider:
    def __init__(self, array, index, far):
        self.array, self.index, self.dtype, self.far = array, index, array.dtype, far
        self.shape = (1, *array.shape[1:])


class Far:
    def __init__(self, array):
        self.array, self.shape, self.dtype = array, array.shape, array.dtype


class Close(Far):
    pass


def like(shape, dtype):
    return jax.ShapeDtypeStruct(tuple(shape), dtype)


def by_rows(fn, info, stepped, fixed, dtypes, gain=False, riders=None, kept=True):
    steps, _, width = stepped[0].shape
    count = 0 if riders is None else 1
    alone = [like(stepped[0].shape, d) for d in dtypes]
    outs = alone if riders is None or kept else alone[:-1]
    more = 0 if riders is None else riders.shape[0]
    together = [like((steps + count, *stepped[0].shape[1:]), dtypes[-1])] if more else []

    def body(info_ref, ins, whole, outs, sums, _):
        b = pl.program_id(0)
        if more:
            whole, rows = whole[:-1], whole[-1]

        @pl.when(b < steps)
        def _():
            results = fn(*(r[0].astype(f32) for r in ins), *(r[...] for r in whole))
            for out, value in zip(outs, results, strict=False):
                out[0] = value.astype(out.dtype)
            if more:
                outs[-1][0] = results[len(dtypes) - 1].astype(outs[-1].dtype)
            for total in sums:
                found = jnp.sum(results[-1], axis=0, keepdims=True)

                @pl.when(b == 0)
                def _():
                    total[...] = found

                @pl.when(b > 0)
                def _():
                    total[...] += found

        if more:

            @pl.when(b == steps)
            def _():
                outs[-1][0, :more, :] = rows[...]

    return call(
        body,
        info,
        stepped,
        [*fixed, riders] if more else fixed,
        [*outs, *together],
        [like((1, width), f32)] * gain,
        flops=10 * math.prod(stepped[0].shape),
        steps=steps + count,
        near=True,
    )


def partial_rows(blocks, part, width):
    return [Near(like((blocks, part, width), d)) for d in (f32, bf16, f32, bf16)]


def piece_shapes(rows, columns):
    return [Later(like((rows, columns), d)) for d in (f32, *[bf16] * 7)]


def gathered(info, pieces, widths, column_from=0):
    rows, wide = pieces[0].shape[0] * len(pieces), sum(widths)

    def body(info, _, ins, __, outs, scratch):
        together, signals = scratch
        assemble(info, ins, (together,), signals, column_from)
        column = 0
        for out in outs:
            out[...] = together[:, column : column + out.shape[1]]
            column += out.shape[1]

    return call(
        body,
        info,
        [],
        [Far(p) for p in pieces],
        [],
        [Near(like((rows, w), bf16)) for w in widths],
        [pltpu.VMEM((rows, wide), bf16), pltpu.SemaphoreType.DMA((1, len(pieces)))],
    )


def attention_scratch(width, size, pieces):
    return [
        *(pltpu.VMEM((width, k * size), bf16) for k in (3, 1, 4)),
        pltpu.SemaphoreType.DMA((1, len(pieces))),
    ]


def encoder_attention(info, normed, pieces):
    blocks, part, width = normed[0].shape
    slot = part * len(normed)
    size = pieces[0].shape[1] // 4
    count = size // HDIM
    each = 2

    def body(info, rows, pieces, outs, _, scratch):
        qkv, probs, context = outs[:3]
        w_in, w_out, together, signals = scratch
        b = pl.program_id(0)

        @pl.when(b == 0)
        def _():
            assemble(info, pieces, (together,), signals)
            w_in[...] = together[:, : 3 * size]
            w_out[...] = together[:, 3 * size :]

        made = dot(token_rows(rows), w_in[...]).astype(bf16)
        qkv[...] = made.reshape(qkv.shape)
        parts = [head_parts(made[p * slot : (p + 1) * slot], 3) for p in range(each)]
        pairs = [(p, k) for p in range(each) for k in range(count)]
        scores = [dot_t(parts[p][0][k] * SCALE, parts[p][1][k]) for p, k in pairs]
        allowed = [slots_used(info, b * each + p, part, slot) for p in range(each)]
        found = []
        for (p, k), score in zip(pairs, scores, strict=True):
            score = jnp.where(allowed[p], score, masked_score)
            spread_out = jnp.exp(score - jnp.max(score, axis=-1, keepdims=True))
            inverse = 1.0 / jnp.sum(spread_out, axis=-1, keepdims=True)
            found.append((spread_out * inverse).astype(bf16))
            probs[p, k] = found[-1]
        found = [dot(w, parts[p][2][k]) for (p, k), w in zip(pairs, found, strict=True)]
        joined = by_passage(found, count).astype(bf16)
        context[...] = joined.reshape(context.shape)
        emit(dot_t(joined, w_out[...]), outs[3:])

    return call(
        body,
        info,
        normed,
        [Far(p) for p in pieces],
        [
            like((blocks, slot, 3 * size), bf16),
            like((blocks, count, slot, slot), bf16),
            like((blocks, slot, size), bf16),
            *partial_rows(blocks, part, width),
        ],
        [],
        attention_scratch(width, size, pieces),
        flops=2 * blocks * slot * (width * size * 4 + 8 * slot * size),
        steps=blocks // each,
        each=each,
    )


def encoder_attention_back(info, grads, normed, qkv, probs, context, weights, gains):
    blocks, part, width = normed[0].shape
    slot = part * len(normed)
    size = context.shape[2]
    each = 2

    def body(info, stepped, fixed, outs, ends, scratch):
        grad_refs, normed_refs = stepped[:4], stepped[4:8]
        qkv, probs, context = stepped[8:]
        w_in, w_out, gains = fixed
        pieces, gain_out = ends[:-1], ends[-1]
        total_in, total_out = scratch
        b = pl.program_id(0)

        @pl.when(b == 0)
        def _():
            total_in[...] = jnp.zeros_like(total_in)
            total_out[...] = jnp.zeros_like(total_out)
            gain_out[...] = jnp.zeros_like(gain_out)

        grad = token_rows(grad_refs)
        rows = token_rows(normed_refs)
        dcontext = dot(grad, w_out[...]).astype(bf16)
        parts = [head_parts(qkv[p], 3) for p in range(each)]
        cuts = [c for p in range(each) for c in head_parts(dcontext[p * slot : (p + 1) * slot], 1)[0]]
        pairs = [(p, k) for p in range(each) for k in range(size // HDIM)]
        backs = [dot_t(c, parts[p][2][k]) for (p, k), c in zip(pairs, cuts, strict=True)]
        dvals = [t_dot(probs[p, k], c) for (p, k), c in zip(pairs, cuts, strict=True)]
        lows = []
        for (p, k), back in zip(pairs, backs, strict=True):
            wide = probs[p, k].astype(f32)
            low = wide * (back - jnp.sum(wide * back, axis=-1, keepdims=True))
            lows.append(low.astype(bf16))
        dquery = [dot(d, parts[p][1][k]) * SCALE for (p, k), d in zip(pairs, lows, strict=True)]
        dkeys = [t_dot(d, parts[p][0][k]) * SCALE for (p, k), d in zip(pairs, lows, strict=True)]
        count = size // HDIM
        moved = jnp.concatenate(
            [by_passage(found, count) for found in (dquery, dkeys, dvals)], axis=1
        ).astype(bf16)
        partial = dot_t(moved, w_in[...])
        emit(partial, outs)
        gain_out[...] += jnp.sum(partial * rows.astype(f32), axis=0, keepdims=True) / gains[0:1, :]
        total_in[...] += t_dot(rows, moved)
        total_out[...] += t_dot(grad, context[...].reshape(grad.shape[0], size))

        @pl.when(b == blocks // each - 1)
        def _():
            hand_out(info, (total_in, total_out), pieces)

    results = call(
        body,
        info,
        [*grads, *normed, qkv, probs, context],
        [*(Close(w) for w in weights), gains],
        partial_rows(blocks, part, width),
        [*piece_shapes(width // 8, 4 * size), like((1, width), f32)],
        [
            pltpu.VMEM((width, 3 * size), f32),
            pltpu.VMEM((width, size), f32),
        ],
        flops=2 * blocks * slot * (width * size * 8 + 20 * slot * size),
        steps=blocks // each,
        each=each,
    )
    return results[:4], results[4:12], results[12]


def ffn_scratch(width, hidden, pieces):
    return [
        *[pltpu.VMEM((width, hidden), bf16)] * 2,
        pltpu.SemaphoreType.DMA((2, len(pieces))),
    ]


def encoder_ffn(info, normed, pieces, hidden):
    blocks, part, width = normed[0].shape
    slot = part * len(normed)

    def body(info, rows, pieces, outs, _, scratch):
        active, slope = outs[:2]
        w_inner, w_outer, signals = scratch

        @pl.when(pl.program_id(0) == 0)
        def _():
            assemble(info, pieces, (w_inner, w_outer), signals)

        value, bend = gelu_both(dot(token_rows(rows), w_inner[...]))
        low = value.astype(bf16)
        active[...] = low.reshape(active.shape)
        slope[...] = bend.astype(bf16).reshape(slope.shape)
        emit(dot_t(low, w_outer[...]), outs[2:])

    return call(
        body,
        info,
        normed,
        [Far(p) for p in pieces],
        [*[like((blocks, slot, hidden), bf16)] * 2, *partial_rows(blocks, part, width)],
        [],
        ffn_scratch(width, hidden, pieces),
        flops=4 * blocks * slot * width * hidden,
        steps=blocks // 2,
        each=2,
    )


def encoder_ffn_back(info, grads, slope, weights):
    blocks, (_, part, width) = slope.shape[0], grads[0].shape
    slot = part * len(grads)
    hidden = slope.shape[2]

    def body(info, stepped, weights, outs, ends, scratch):
        dinner = outs[0]
        w_inner, w_outer = weights
        back = dot(token_rows(stepped[:4]), w_outer[...])
        low = (back * stepped[4][...].reshape(back.shape).astype(f32)).astype(bf16)
        dinner[...] = low.reshape(dinner.shape)
        emit(dot_t(low, w_inner[...]), outs[1:])

    return call(
        body,
        info,
        [*grads, slope],
        [Close(w) for w in weights],
        [like((blocks, slot, hidden), bf16), *partial_rows(blocks, part, width)],
        [],
        flops=4 * blocks * slot * width * hidden,
        steps=blocks // 2,
        each=2,
    )


def weight_grads(info, pairs, more=(), cut=True):
    blocks, (_, part, width) = pairs[0][1].shape[0], pairs[0][0][0].shape
    widths = [right.shape[2] for _, right in pairs]

    def body(info, stepped, more, __, ends, totals):
        totals = totals if cut else ends
        for k, total in enumerate(totals):
            left, right = token_rows(stepped[5 * k : 5 * k + 4]), stepped[5 * k + 4]
            total[...] = t_dot(left, right[...].reshape(left.shape[0], total.shape[1]))
        if cut:
            hand_out(info, (*totals, *more), ends)

    return call(
        body,
        info,
        [a for left, right in pairs for a in (*left, right)],
        more,
        [],
        piece_shapes(width // 8, sum(widths) + sum(m.shape[1] for m in more))
        if cut
        else [like((width, w), f32) for w in widths],
        [pltpu.VMEM((width, w), f32) for w in widths] if cut else [],
        flops=2 * blocks * part * 4 * width * sum(widths),
        each=blocks,
    )


def finish(info, terms, widths, turned):
    terms = [part(t) for t in terms]
    rows = terms[0].array.shape[0]
    shapes = [(w, rows) if t else (rows, w) for w, t in zip(widths, turned, strict=True)]

    def body(info, _, ins, __, outs, ___):
        total = terms[0].read(ins[0])
        for term, ref in zip(terms[1:], ins[1:], strict=True):
            total = total + term.read(ref).astype(f32)
        column = 0
        for out, wide, turn in zip(outs, widths, turned, strict=True):
            found = total[:, column : column + wide]
            out[...] = found.T if turn else found
            column += wide

    return call(body, info, [], [t.array for t in terms], [], [like(s, f32) for s in shapes])


def cross_forward(info, states, weights, decoder, own_question, count_q, count_pass):
    rows_in, terms, gains = decoder
    blocks = count_q * count_pass
    _, part, width = states[0].shape
    slot = part * len(states)
    rows_dec = rows_in.shape[0]
    size = weights[1].shape[1]
    steps = 2

    def body(info, rows, fixed, outs, ends, scratch):
        weight, w_query, rows_in, *terms, gains, question = fixed
        after_self, normed, queries, stats = ends
        held = scratch[0]
        b = pl.program_id(0)

        @pl.when(b == 0)
        def _():
            after_self[...] = rows_in[...].astype(f32) + summed(terms)
            normed[...] = norm_rows(after_self[...], gains[1:2, :]).astype(bf16)
            queries[...] = dot(normed[...], w_query[...]).astype(bf16)

        made = dot(token_rows(rows), weight[...]).astype(bf16)
        outs[0][...] = made.reshape(outs[0].shape)
        each = made.shape[0]
        held[pl.ds(pl.multiple_of(b * each, each), each), :] = made

        @pl.when(b == steps - 1)
        def _():
            allowed = keys_used(info, question, range(blocks), part, slot, count_pass)
            lane = lax.broadcasted_iota(jnp.int32, (rows_dec, HDIM), 1)
            keys, vals = head_parts(held[...], 2)
            asking = head_parts(queries[...], 1)[0]
            scores = [dot_t(q * SCALE, t) for q, t in zip(asking, keys, strict=True)]
            for k, score in enumerate(scores):
                score = jnp.where(allowed, score, masked_score)
                top = jnp.max(score, axis=-1, keepdims=True)
                spread_out = jnp.exp(score - top)
                total = jnp.sum(spread_out, axis=-1, keepdims=True)
                at = k * LANES
                stats[:, at : at + HDIM] = dot(spread_out.astype(bf16), vals[k])
                stats[:, at + HDIM : at + LANES] = jnp.where(lane == 0, top, total)

    return call(
        body,
        info,
        states,
        [*(Close(w) for w in weights), rows_in, *terms, gains, own_question],
        [like((blocks, slot, 2 * size), bf16)],
        [
            Later(like((rows_dec, width), f32)),
            Later(like((rows_dec, width), bf16)),
            like((rows_dec, size), bf16),
            like((rows_dec, size // HDIM * LANES), f32),
        ],
        [pltpu.VMEM((blocks * slot, 2 * size), bf16)],
        flops=4 * blocks * slot * width * size,
        steps=steps,
        each=blocks // steps,
    )


def merged(first, second):
    lane = lax.broadcasted_iota(jnp.int32, (first.shape[0], HDIM), 1)
    found = []
    for at in range(0, first.shape[1], LANES):
        tops = [v[:, at + HDIM : at + HDIM + 1] for v in (first, second)]
        totals = [v[:, at + HDIM + 1 : at + HDIM + 2] for v in (first, second)]
        top = jnp.maximum(*tops)
        scales = [jnp.exp(t - top) for t in tops]
        total = totals[0] * scales[0] + totals[1] * scales[1]
        found.append(first[:, at : at + HDIM] * scales[0] + second[:, at : at + HDIM] * scales[1])
        found.append(jnp.where(lane == 0, top, total))
    return jnp.concatenate(found, axis=1)


def in_order(info, bits, own, other):
    later = (info[BLK] & bits) != 0
    return jnp.where(later, other, own), jnp.where(later, own, other)


def merge(info, own, other, bits):
    def body(info, _, ins, __, outs, ___):
        outs[0][...] = merged(*in_order(info, bits, ins[0][...], ins[1][...]))

    return call(body, info, [], [own, other], [], [like(own.shape, f32)])[0]


def cross_out(info, stats, bits, w_output):
    rows, columns = stats[0].shape
    size = columns // LANES * HDIM
    width = w_output.shape[0]

    def body(info, _, ins, __, outs, scratch):
        w_output = ins[-1]
        out, log_total, context, own, sent = outs
        values = [r[...] for r in ins[:-1]]
        near = merged(*in_order(info, bits[0], *values[:2]))
        far = merged(*in_order(info, bits[0], *values[2:]))
        stats = merged(*in_order(info, bits[1], near, far))
        log_total[...] = jnp.zeros_like(log_total)
        for k, at in enumerate(heads_in(size)):
            base = k * LANES
            top = stats[:, base + HDIM : base + HDIM + 1]
            total = stats[:, base + HDIM + 1 : base + HDIM + 2]
            out[:, at] = stats[:, base : base + HDIM] / total
            log_total[:, k : k + 1] = top + jnp.log(total)
        context[...] = out[...].astype(bf16)
        own[...] = dot_t(context[...], w_output[...])
        sent[...] = own[...].astype(bf16)

    return call(
        body,
        info,
        [],
        [*stats, w_output],
        [],
        [
            like((rows, size), f32),
            like((rows, LANES), f32),
            Later(like((rows, size), bf16)),
            like((rows, width), f32),
            like((rows, width), bf16),
        ],
        flops=2 * rows * size * width,
    )


def cross_back(info, key_vals, inputs, own_question, count_pass, slot, part):
    cotangent, after_cross, terms, gains, w_output, out, log_total, queries, weight = inputs
    blocks = key_vals.shape[0]
    rows_dec, width = after_cross.shape
    size = queries.shape[1]

    def body(info, stepped, fixed, outs, ends, scratch):
        cotangent, after_cross, own, r1, r2, r3, gains, w_output, out, log_total, queries, weight, question = fixed
        key_vals = stepped[0]
        dkey_vals = outs[0]
        dcross, dcross_low, gain_out, dqueries = ends
        total = summed((own, r1, r2, r3))
        back, gain_out[...] = norm_back(after_cross[...], gains[2:3, :], total)
        dcross[...] = cotangent[...].astype(f32) + back
        dcross_low[...] = dcross[...].astype(bf16)
        dcontext = dot(dcross_low[...], w_output[...]).astype(bf16)
        allowed = keys_used(info, question, range(blocks), part, slot, count_pass)
        keys, vals = head_parts(key_vals[...].reshape(blocks * slot, 2 * size), 2)
        asking = head_parts(queries[...], 1)[0]
        cuts = head_parts(dcontext, 1)[0]
        outs_of = head_parts(out[...], 1)[0]
        scores = [dot_t(q * SCALE, t) for q, t in zip(asking, keys, strict=True)]
        backs = [dot_t(c, v) for c, v in zip(cuts, vals, strict=True)]
        probs, lows = [], []
        for k, score in enumerate(scores):
            row_term = jnp.sum(cuts[k].astype(f32) * outs_of[k], axis=-1, keepdims=True)
            score = jnp.where(allowed, score, masked_score)
            probs.append(jnp.exp(score - log_total[:, k : k + 1]))
            lows.append((probs[k] * (backs[k] - row_term)).astype(bf16))
        dvals = [t_dot(p.astype(bf16), c) for p, c in zip(probs, cuts, strict=True)]
        dkeys = [t_dot(d, q) * SCALE for d, q in zip(lows, asking, strict=True)]
        found = [dot(d, t) * SCALE for d, t in zip(lows, keys, strict=True)]
        dqueries[...] = jnp.concatenate(found, axis=1)
        made = jnp.concatenate([*dkeys, *dvals], axis=1).astype(bf16)
        dkey_vals[...] = made.reshape(dkey_vals.shape)
        emit(dot_t(made, weight[...]), outs[1:])

    return call(
        body,
        info,
        [key_vals],
        [
            cotangent,
            after_cross,
            *terms,
            gains,
            w_output,
            out,
            log_total,
            queries,
            Close(weight),
            own_question,
        ],
        [like(key_vals.shape, bf16), *partial_rows(blocks, part, width)],
        [
            Later(like((rows_dec, width), f32)),
            Later(like((rows_dec, width), bf16)),
            Later(like((rows_dec, width), f32)),
            like((rows_dec, size), f32),
        ],
        flops=4 * blocks * slot * width * size,
        each=blocks,
    )


def summed(refs):
    count = refs[0].shape[0]

    def rows(ref):
        return ref[...] if len(ref.shape) == 2 else ref[0, :count, :]

    terms = [rows(ref).astype(f32) for ref in refs[1:]]
    total = refs[0][...]
    for term in terms:
        total = total + term
    return total


def decoder_self(info, rows, gains, pieces, column_from, size, order):
    count, width = rows.shape

    def body(info, _, ins, __, outs, scratch):
        rows, gains, order_q, order_k = ins[:4]
        normed, qkv, probs, context, own, sent, weight = outs
        assemble(info, ins[4:], (weight,), scratch[0], column_from)
        normed[...] = norm_rows(rows[...].astype(f32), gains[0:1, :]).astype(bf16)
        qkv[...] = dot(normed[...], weight[:, : 3 * size]).astype(bf16)
        query_at, key_at = order_q[...], order_k[...]
        same = lax.div(query_at, 1000) == lax.div(key_at, 1000)
        allowed = same & (key_at <= query_at) & (key_at >= 0) & (query_at >= 0)
        for k, at in enumerate(heads_in(size)):
            query, keys, vals = (qkv[:, j * size + at.start : j * size + at.stop] for j in range(3))
            scores = jnp.where(allowed, dot_t(query, keys) * SCALE, masked_score)
            spread_out = jnp.exp(scores - jnp.max(scores, axis=-1, keepdims=True))
            share_out = spread_out / jnp.sum(spread_out, axis=-1, keepdims=True)
            share_out = jnp.where(allowed, share_out, 0.0)
            probs[k] = share_out
            context[:, at] = dot(share_out.astype(bf16), vals).astype(bf16)
        own[...] = dot_t(context[...], weight[:, 3 * size :])
        sent[...] = own[...].astype(bf16)

    return call(
        body,
        info,
        [],
        [rows, gains, *order, *(Far(p) for p in pieces)],
        [],
        [
            Later(like((count, width), bf16)),
            Later(like((count, 3 * size), bf16)),
            Later(like((size // HDIM, count, count), f32)),
            Later(like((count, size), bf16)),
            like((count, width), f32),
            like((count, width), bf16),
            Later(like((width, 4 * size), bf16)),
        ],
        [pltpu.SemaphoreType.DMA((1, len(pieces)))],
        flops=2 * count * width * size * 4,
    )


def decoder_back(info, cotangent, pieces):
    count, width = cotangent.shape
    hidden = pieces[0].shape[1] // 2

    def body(info, _, ins, __, outs, scratch):
        w_inner, w_outer, back = outs
        assemble(info, ins[1:], (w_inner, w_outer), scratch[0])
        back[...] = dot(ins[0][...], w_outer[...])

    return call(
        body,
        info,
        [],
        [cotangent, *(Far(p) for p in pieces)],
        [],
        [Near(like((width, hidden), bf16)), like((width, hidden), bf16), like((count, hidden), f32)],
        [pltpu.SemaphoreType.DMA((2, len(pieces)))],
        flops=2 * count * width * hidden,
    )


def decoder_ffn(info, after_self, terms, back, gains, w_inner):
    count, width = after_self.shape
    hidden = w_inner.shape[1]

    def body(info, _, ins, __, outs, scratch):
        after_self, own, r1, r2, r3, back, gains, w_inner = ins
        after_cross, normed, active, dinner, own_back, sent_back = outs
        after_cross[...] = after_self[...] + summed((own, r1, r2, r3))
        normed[...] = norm_rows(after_cross[...], gains[2:3, :]).astype(bf16)
        value, slope = gelu_both(dot(normed[...], w_inner[...]))
        active[...] = value.astype(bf16)
        dinner[...] = (slope * back[...]).astype(bf16)
        own_back[...] = dot_t(dinner[...], w_inner[...])
        sent_back[...] = own_back[...].astype(bf16)

    return call(
        body,
        info,
        [],
        [after_self, *terms, back, gains, Close(w_inner)],
        [],
        [
            like((count, width), f32),
            Later(like((count, width), bf16)),
            Later(like((count, hidden), bf16)),
            Later(like((count, hidden), bf16)),
            like((count, width), f32),
            like((count, width), bf16),
        ],
        flops=4 * count * width * hidden,
    )


def rows_back(info, terms, weight):
    (count, size), width = terms[0].shape, weight.shape[0]

    def body(info, _, ins, __, outs, scratch):
        low, own, sent = outs
        total = ins[0][...]
        for term in ins[1:-1]:
            total = total + term[...]
        low[...] = total.astype(bf16)
        own[...] = dot_t(low[...], ins[-1][...])
        sent[...] = own[...].astype(bf16)

    return call(
        body,
        info,
        [],
        [*terms, weight],
        [],
        [
            Later(like((count, size), bf16)),
            like((count, width), f32),
            like((count, width), bf16),
        ],
        flops=2 * count * width * size,
    )


def decoder_self_back(
    info, dcross, after_self, terms, gains, weight, qkv, probs
):
    count, width = after_self.shape
    size = weight.shape[1] // 4

    def body(info, _, ins, __, outs, scratch):
        dcross, after_self, *terms, gains, weight, qkv, probs = ins
        dself, dself_low, gain_rows, moved, own_back, sent_back = outs
        back, gain_rows[...] = norm_back(after_self[...], gains[1:2, :], summed(terms))
        dself[...] = dcross[...] + back
        dself_low[...] = dself[...].astype(bf16)
        dcontext = dot(dself_low[...], weight[:, 3 * size :]).astype(bf16)
        for k, at in enumerate(heads_in(size)):
            query, keys, vals = (qkv[:, j * size + at.start : j * size + at.stop] for j in range(3))
            share_out = probs[k]
            dprobs = dot_t(dcontext[:, at], vals)
            dscores = share_out * (dprobs - jnp.sum(share_out * dprobs, axis=-1, keepdims=True))
            dscores = dscores.astype(bf16)
            found = (
                dot(dscores, keys) * SCALE,
                t_dot(dscores, query) * SCALE,
                t_dot(share_out.astype(bf16), dcontext[:, at]),
            )
            for j, term in enumerate(found):
                moved[:, j * size + at.start : j * size + at.stop] = term.astype(bf16)
        own_back[...] = dot_t(moved[...], weight[:, : 3 * size])
        sent_back[...] = own_back[...].astype(bf16)

    return call(
        body,
        info,
        [],
        [dcross, after_self, *terms, gains, weight, qkv, probs],
        [],
        [
            like((count, width), f32),
            Later(like((count, width), bf16)),
            like((count, width), f32),
            Later(like((count, 3 * size), bf16)),
            like((count, width), f32),
            like((count, width), bf16),
        ],
        flops=2 * count * width * size * 8,
    )


def own_rows(info, values, dec_own):
    found = values[:dec_own]
    for k in range(1, values.shape[0] // dec_own):
        found = jnp.where(info[HEAD] == k, values[k * dec_own : (k + 1) * dec_own], found)
    return found


def decoder_ends(
    info, rows, dself, terms, gains, after_cross, out_terms, gain_rows, gain_sums, dec_own
):
    count, width = dself.shape

    def body(info, _, ins, __, outs, scratch):
        rows, dself, after_cross, gains = ins[:4]
        three, four, zero, one = ins[-4:]
        grad, states, found = outs
        total, out_total = summed(ins[4:8]), summed(ins[8:12])
        back, two = norm_back(rows[...].astype(f32), gains[0:1, :], total)
        grad[...] = own_rows(info, dself[...] + back, dec_own)
        states[...] = own_rows(info, after_cross[...] + out_total, dec_own).astype(bf16)
        row = lax.div(lax.broadcasted_iota(jnp.int32, (count, 1), 0), dec_own)
        mine = (row == info[HEAD]) & (info[BLK] == 0)
        found[0:1, :] = zero[...]
        found[1:2, :] = one[...]
        for k, values in enumerate((two, three[...], four[...])):
            found[2 + k : 3 + k, :] = jnp.sum(jnp.where(mine, values, 0.0), axis=0, keepdims=True)

    return call(
        body,
        info,
        [],
        [rows, dself, after_cross, gains, *terms, *out_terms, *gain_rows, *gain_sums],
        [],
        [like((dec_own, width), f32), like((dec_own, width), bf16), like((5, width), f32)],
    )


def decoder_weight_grads(info, own, pairs_in, pairs_out):
    count, width = pairs_in[0][0].shape

    def body(info, _, ins, __, outs, scratch):
        row = lax.broadcasted_iota(jnp.int32, (own, width), 0) + info[BLK] * own
        column = lax.broadcasted_iota(jnp.int32, (own, width), 1)
        pick = jnp.where(row == column, 1.0, 0.0).astype(bf16)
        outs, ins = iter(outs), iter(ins)
        for _, _, arrays in pairs_in:
            left, right = next(ins)[...], next(ins)[...]
            found = t_dot(dot_t(left, pick).astype(bf16), right)
            wide = found.shape[1] // arrays
            for k in range(arrays):
                next(outs)[...] = found[:, k * wide : (k + 1) * wide]
        for _ in pairs_out:
            left, right = next(ins)[...], next(ins)[...]
            next(outs)[...] = t_dot(left, dot_t(right, pick).astype(bf16))

    outs = [like((own, r.shape[1] // n), f32) for _, r, n in pairs_in for _ in range(n)]
    outs += [like((l.shape[1], own), f32) for l, _ in pairs_out]
    flat = [a for pair in pairs_in for a in pair[:2]] + [a for pair in pairs_out for a in pair]
    return call(body, info, [], flat, [], outs, flops=2 * count * own * width * 10, least=0)


def shards(
    encoder_input,
    passage_lengths,
    decoder_input,
    encoder_query,
    encoder_key,
    encoder_value,
    encoder_output,
    encoder_inner,
    encoder_outer,
    decoder_query,
    decoder_key,
    decoder_value,
    decoder_output,
    cross_query,
    cross_key,
    cross_value,
    cross_output,
    decoder_inner,
    decoder_outer,
    encoder_gains,
    decoder_gains,
    encoder_cotangent,
    decoder_cotangent,
):
    head, blk = lax.axis_index("head"), lax.axis_index("blk")
    blk_count, head_count = lax.axis_size("blk"), lax.axis_size("head")
    count_q, count_pass, part, width = encoder_input.shape
    blocks = count_q * count_pass
    slot = part * head_count
    own = width // blk_count
    if blk_count == 8:
        places = jnp.asarray(place_table(8))[blk]
    else:
        places = jnp.arange(8, dtype=jnp.int32)
    info = jnp.concatenate(
        [places, jnp.stack([head, blk]).astype(jnp.int32), passage_lengths.reshape(blocks)]
    )

    size, units = encoder_query.shape[1], encoder_inner.shape[1]
    inputs = encoder_input.reshape(blocks, part, width)
    dec_part = decoder_input.shape[1]
    dec_own = count_q * dec_part
    dec_rows = dec_own * head_count
    filled = -(-dec_rows // 16) * 16

    attention = jnp.concatenate(
        [encoder_query, encoder_key, encoder_value, encoder_output.T], axis=1
    )
    attention, inputs = sync(attention, inputs)
    attention = fetch_step(fetch_start(attention), -1, 1)
    first = by_rows(
        lambda x, g: (norm_rows(x, g[0:1]),), info, [inputs], [encoder_gains], [bf16]
    )[0]
    attention, first = sync(attention, first)

    attention = fetch_step(attention, -2, 2)
    first_all = [first, swap(first, "head", 1), swap(first, "head", 2)]
    ffn = jnp.concatenate(
        [
            encoder_inner,
            encoder_outer.T,
            decoder_query,
            decoder_key,
            decoder_value,
            decoder_output.T,
            cross_key,
            cross_value,
            cross_query,
            cross_output.T,
        ],
        axis=1,
    )
    at_self, at_cross = 2 * units, 2 * units + 4 * size
    attention, ffn = sync(attention, ffn)

    attention = fetch_step(attention, -3, 3)
    pair = jnp.stack([decoder_input, decoder_cotangent]).reshape(2, dec_own, width)
    both = lax.all_gather(pair, "head", axis=1, tiled=True)
    both = jnp.pad(both, ((0, 0), (0, filled - dec_rows), (0, 0)))
    attention, first_all, ffn, both = sync(attention, first_all, ffn, both)

    attention, ffn = fetch_step(attention, -4), fetch_step(fetch_start(ffn), 1)
    first_all.append(swap(first_all[2], "head", 1))
    dec_ffn = jnp.concatenate([decoder_inner, decoder_outer.T], axis=1)
    attention, ffn, first_all, dec_ffn = sync(attention, ffn, first_all, dec_ffn)

    ffn = fetch_step(ffn, -1, 2)
    qkv, probs, context, *partial = encoder_attention(
        info, first_all, in_turn(attention)
    )
    partial, ffn = sync(partial, ffn)

    def to_core(partial):
        return swap(partial[3], "head", 1)

    def to_chip(partial, corner):
        far = (partial[2] + corner.astype(f32)).astype(bf16)
        return [swap(far, "head", 2), swap(partial[1], "head", 1)]

    ffn = fetch_step(ffn, -2, 3)
    partial, corner = sync(partial, to_core(partial))
    partial, arrived, ffn = sync(partial, to_chip(partial, corner), ffn)

    def enter_ffn(x, a, b, c, g):
        hidden = x + a + b + c
        return hidden, norm_rows(hidden, g[1:2])

    hidden, second = by_rows(
        enter_ffn, info, [inputs, partial[0], *arrived], [encoder_gains], [f32, bf16]
    )
    ffn = fetch_step(ffn, -3, 4)
    def spread(rows):
        return [rows, swap(rows, "head", 1), swap(rows, "head", 2)]

    def riders(all_rows, far=True):
        return [Rider(rows, blocks, far) for rows in all_rows[1:]]

    second, dec_ffn = sync(second, dec_ffn)
    second_all = spread(second)
    second_all, ffn, dec_ffn = sync(second_all, ffn, dec_ffn)
    dec_ffn = fetch_step(fetch_start(dec_ffn), -1, 1)
    second_all.append(swap(second_all[2], "head", 1))
    second_all, ffn = sync(second_all, ffn)
    ffn = in_turn(ffn)

    active, slope, *partial = encoder_ffn(info, second_all, ffn, units)
    partial, dec_ffn = sync(partial, dec_ffn)
    partial, corner, both, dec_ffn = sync(partial, to_core(partial), both, dec_ffn)
    dec_in, cotangent = both[0], both[1]

    index = np.arange(filled)
    question = (index % dec_own) // dec_part
    position = index // dec_own * dec_part + index % dec_part
    order = np.where(index < dec_rows, question * 1000 + position, -1).astype(np.int32)
    order = (jnp.asarray(order[:, None]), jnp.asarray(order[None, :]))
    question = jnp.asarray(question[:, None].astype(np.int32))

    arrived = to_chip(partial, corner)
    dec_ffn = fetch_step(dec_ffn, -2, 2)
    third, dec_qkv, dec_probs, dec_context, mine, sent, w_self = decoder_self(
        info, dec_in, decoder_gains, ffn, at_self, size, order
    )
    partial, arrived, mine, sent, dec_ffn = sync(partial, arrived, mine, sent, dec_ffn)
    (states_sent,) = by_rows(
        lambda h, a, b, c: (h + a + b + c,),
        info,
        [hidden, partial[0], *arrived],
        [],
        [bf16],
        riders=sent,
        kept=False,
    )
    states_sent, dec_ffn = sync(states_sent, dec_ffn)
    states = states_sent[:blocks]
    states_all = spread(states_sent)
    dec_ffn = fetch_step(dec_ffn, -3, 3)
    w_cross, w_cross_query, w_cross_output = gathered(
        info, ffn, (2 * size, size, size), at_cross
    )
    states_all, dec_ffn, w_cross, states = sync(states_all, dec_ffn, w_cross, states)
    dec_ffn = fetch_step(dec_ffn, -4)
    states_all = sync(*states_all, swap(states_all[2], "head", 1))

    key_vals, after_self, fourth, queries, stats = cross_forward(
        info,
        states_all,
        (w_cross, w_cross_query),
        (dec_in, [mine, *riders(states_all, False)], decoder_gains),
        question,
        count_q,
        count_pass,
    )
    bits = [1 << k for k in range((blk_count - 1).bit_length())]
    last_two = (bits[-2], bits[-1], bits[-2] + bits[-1])
    for k in bits[:-2]:
        stats = merge(info, stats, swap(stats, "blk", k), k)
    stats, dec_ffn = sync(stats, dec_ffn)
    stats_all = [stats, *(swap(stats, "blk", k) for k in last_two)]
    w_dec_inner, w_dec_outer, outer_back = decoder_back(info, cotangent, in_turn(dec_ffn))
    stats_all, outer_back = sync(stats_all, outer_back)
    out, log_total, cross_context, mine, sent = cross_out(
        info, stats_all, bits[-2:], w_cross_output
    )
    after_cross, fifth, dec_active, dec_dinner, mine, sent = decoder_ffn(
        info, after_self, [mine, *share(sent)], outer_back, decoder_gains, w_dec_inner
    )
    dkey_vals, *rest = cross_back(
        info,
        key_vals,
        (
            cotangent,
            after_cross,
            [mine, *share(sent)],
            decoder_gains,
            w_cross_output,
            out,
            log_total,
            queries,
            w_cross,
        ),
        question,
        count_pass,
        slot,
        part,
    )
    partial, (dcross, dcross_low, gain_four, dqueries) = rest[:4], rest[4:]

    def some(value, which):
        for k in which:
            value = value + swap(value, "blk", k)
        return value

    partial, dqueries, dkey_vals = sync(partial, dqueries, dkey_vals)
    partial, corner, dkey_vals, dqueries = sync(partial, to_core(partial), dkey_vals, dqueries)
    arrived = to_chip(partial, corner)
    dqueries = some(dqueries, bits[:-1])
    cross_sum = weight_grads(info, [(states_all, dkey_vals)], cut=False)[0]
    _, out_mine, out_sent = rows_back(info, [dec_active], w_dec_outer)
    partial, arrived, cross_sum, dqueries, out_sent = sync(
        partial, arrived, cross_sum, dqueries, out_sent
    )

    def enter_back(cot, a, b, c):
        grad = cot + a + b + c
        return grad, grad

    dstates, dstates_low = by_rows(
        enter_back,
        info,
        [encoder_cotangent.reshape(blocks, part, width), partial[0], *arrived],
        [],
        [f32, bf16],
        riders=out_sent,
        kept=False,
    )
    dstates_low, cross_sum, dqueries = sync(dstates_low, cross_sum, dqueries)
    dstates_all = spread(dstates_low)
    terms = [dqueries, swap(dqueries, "blk", bits[-1])]
    dqueries, mine, sent = rows_back(info, terms, w_cross_query)
    w_ffn = gathered(info, ffn, (units, units))
    dstates_all, sent, w_ffn = sync(dstates_all, sent, w_ffn)
    terms = [mine, *share(sent)]
    dstates_all = sync(*dstates_all, swap(dstates_all[2], "head", 1))
    out_terms = [out_mine, *riders(dstates_all)]
    dinner, *partial = encoder_ffn_back(info, dstates_all, slope, w_ffn)
    partial, dinner, terms = sync(partial, dinner, terms)
    partial, corner, dinner, dstates_all = sync(partial, to_core(partial), dinner, dstates_all)
    arrived = to_chip(partial, corner)
    dself, dself_low, gain_three, dself_qkv, own_back, sent_back = decoder_self_back(
        info,
        dcross,
        after_self,
        terms,
        decoder_gains,
        w_self,
        dec_qkv,
        dec_probs,
    )
    ffn_sums = weight_grads(
        info, [(second_all, dinner), (dstates_all, active)], [cross_sum]
    )
    partial, arrived, ffn_sums, sent_back = sync(partial, arrived, ffn_sums, sent_back)

    def middle_back(dy, h, a, b, c, g):
        back, gain_rows = norm_back(h, g[1:2], a + b + c)
        grad = dy + back
        return grad, grad, gain_rows

    dhidden, dhidden_low, gain_one = by_rows(
        middle_back,
        info,
        [dstates, hidden, partial[0], *arrived],
        [encoder_gains],
        [f32, bf16],
        gain=True,
        riders=sent_back,
        kept=False,
    )
    dhidden_low, ffn_sums = sync(dhidden_low, ffn_sums)
    dhidden_all = spread(dhidden_low)
    ffn_moving = reduce_step(info, (ffn_sums, None, 1))[0]
    w_attention = gathered(info, in_turn(attention), (3 * size, size))
    dhidden_all, ffn_moving, w_attention = sync(dhidden_all, ffn_moving, w_attention)
    ffn_moving = reduce_step(info, (ffn_sums, ffn_moving, 2))[0]
    dhidden_all = sync(*dhidden_all, swap(dhidden_all[2], "head", 1))
    terms = [own_back, *riders(dhidden_all)]

    partial, sums, gain_zero = encoder_attention_back(
        info, dhidden_all, first_all, qkv, probs, context, w_attention, encoder_gains
    )
    partial, sums, ffn_moving, gain_zero = sync(partial, sums, ffn_moving, gain_zero)
    ffn_moving, moving = reduce_step(info, (ffn_sums, ffn_moving, 3), (sums, None, 1))[:2]
    corner = to_core(partial)
    dec_grad, dec_states, gains = decoder_ends(
        info,
        dec_in,
        dself,
        terms,
        decoder_gains,
        after_cross,
        out_terms,
        [gain_three, gain_four],
        [gain_zero, gain_one],
        dec_own,
    )
    for k in (1, 2):
        gains = gains + swap(gains, "head", k)
    (
        grad_dec_query,
        grad_dec_key,
        grad_dec_value,
        grad_cross_query,
        grad_dec_inner,
        grad_dec_outer,
        grad_dec_output,
        grad_cross_output,
    ) = decoder_weight_grads(
        info,
        own,
        [
            (third, dself_qkv, 3),
            (fourth, dqueries, 1),
            (fifth, dec_dinner, 1),
            (cotangent, dec_active, 1),
        ],
        [(dec_context, dself_low), (cross_context, dcross_low)],
    )
    partial, corner, moving, gains, ffn_moving, grad_dec_query = sync(
        partial, corner, moving, gains, ffn_moving, grad_dec_query
    )

    def dec_shape(values):
        return values.reshape(count_q, dec_part, width)

    ffn_moving, moving = reduce_step(info, (ffn_sums, ffn_moving, 4), (sums, moving, 2))[:2]
    arrived = to_chip(partial, corner)
    gains = some(gains, bits[:1])
    partial, arrived, moving, gains, ffn_moving = sync(
        partial, arrived, moving, gains, ffn_moving
    )

    def last_back(dh, x, a, b, c, g):
        return (dh + norm_back(x, g[0:1], a + b + c)[0],)

    moving = reduce_step(info, (sums, moving, 3))[0]
    gains = some(gains, bits[1:-1])
    input_grad = by_rows(
        last_back,
        info,
        [dhidden, inputs, partial[0], *arrived],
        [encoder_gains],
        [f32],
    )[0]
    moving, gains, input_grad, ffn_moving = sync(moving, gains, input_grad, ffn_moving)
    moving, (gains, ffn_moving) = reduce_step(info, (sums, moving, 4), hold=(gains, ffn_moving))
    last = swap(gains, "blk", bits[-1])
    grad_inner, grad_outer, grad_cross_key, grad_cross_value = finish(
        info,
        reduce_terms(ffn_sums, ffn_moving),
        (units, units, size, size),
        (False,) * 4,
    )
    enc_gain_grads, dec_gain_grads = gains[:2] + last[:2], gains[2:] + last[2:]
    grad_query, grad_key, grad_value, grad_output = finish(
        info, reduce_terms(sums, moving), (size,) * 4, (False, False, False, True)
    )

    return (
        states.reshape(encoder_input.shape),
        dec_shape(dec_states),
        input_grad.reshape(encoder_input.shape),
        dec_shape(dec_grad),
        grad_query,
        grad_key,
        grad_value,
        grad_output,
        grad_inner,
        grad_outer.T,
        grad_dec_query,
        grad_dec_key,
        grad_dec_value,
        grad_dec_output,
        grad_cross_query,
        grad_cross_key,
        grad_cross_value,
        grad_cross_output,
        grad_dec_inner,
        grad_dec_outer.T,
        enc_gain_grads,
        dec_gain_grads,
    )


def solution(mesh):
    placed = (
        P(None, "blk", "head", None),
        P(None, "blk"),
        P(None, "head", None),
        P("blk", "head"),
        P("blk", "head"),
        P("blk", "head"),
        P("head", "blk"),
        P("blk", "head"),
        P("head", "blk"),
        P("blk", "head"),
        P("blk", "head"),
        P("blk", "head"),
        P("head", "blk"),
        P("blk", "head"),
        P("blk", "head"),
        P("blk", "head"),
        P("head", "blk"),
        P("blk", "head"),
        P("head", "blk"),
        P(),
        P(),
        P(None, "blk", "head", None),
        P(None, "head", None),
    )
    return jax.shard_map(
        shards,
        mesh=mesh,
        in_specs=placed,
        out_specs=(placed[0], placed[2], placed[0], placed[2], *placed[3:19], P(), P()),
        check_vma=False,
    )
```

```python
import math

import jax
import jax.numpy as jnp
import numpy as np
from jax import lax
from jax.experimental import pallas as pl
from jax.experimental.pallas import tpu as pltpu
from jax.sharding import PartitionSpec as P

HDIM = 64
SCALE = HDIM ** (-0.5)
LANES = 128
EPS = 1e-06
VMEM_LIMIT = 24 * 1024 * 1024
LARGE = 1 << 20
masked_score = -1000000000.0
f32 = jnp.float32
bf16 = jnp.bfloat16

PLACES, HEAD, BLK, LENGTHS = 0, 8, 9, 10


def swap(value, axis, bits):
    size = lax.axis_size(axis)
    return lax.ppermute(value, axis, [(i, i ^ bits) for i in range(size)])


def sync(*values):
    return lax.optimization_barrier(values)


def share(value):
    return [swap(value, "head", k) for k in (1, 2, 3)]


def ring_order(count):
    return [*range(0, count, 2), *range(count - 1, 0, -2)]


OFFSETS = (0, -1, 1, -2, 2, -3, 3, -4)


def ring_steps(count):
    order = ring_order(count)
    forth = [(order[i], order[(i + 1) % count]) for i in range(count)]
    return forth, [(b, a) for a, b in forth]


def place_table(count):
    order = ring_order(count)
    at = {b: i for i, b in enumerate(order)}
    return np.array(
        [[order[(at[b] + o) % count] for o in OFFSETS] for b in range(count)], np.int32
    )


def gather_rows(own):
    return lax.all_gather(own, "blk", axis=0, tiled=True)


def fetch_start(own):
    if lax.axis_size("blk") == 8:
        return {0: own}
    return dict(zip(OFFSETS, jnp.split(gather_rows(own), 8, axis=0), strict=True))


def fetch_step(pieces, *offsets):
    count = lax.axis_size("blk")
    if count != 8:
        return pieces
    forth, back = ring_steps(count)
    more = {
        k: lax.ppermute(pieces[k + 1 if k < 0 else k - 1], "blk", forth if k < 0 else back)
        for k in offsets
    }
    return {**pieces, **more}


def in_turn(pieces):
    return [pieces[k] if k in pieces else pieces[-k] for k in OFFSETS]


@jax.tree_util.register_pytree_node_class
class Part:
    def __init__(self, array, start, width):
        self.array, self.start, self.width = array, start, width

    def tree_flatten(self):
        return (self.array,), (self.start, self.width)

    @classmethod
    def tree_unflatten(cls, places, arrays):
        return cls(*arrays, *places)

    def read(self, ref):
        return ref[:, self.start : self.start + self.width]


def part(value):
    return value if isinstance(value, Part) else Part(value, 0, value.shape[1])


def reduce_step(info, *rings, hold=None):
    count = lax.axis_size("blk")
    if count != 8:
        return [[] for _ in rings] + [hold]
    forth, back = ring_steps(count)
    plan = [[], []]
    for pieces, moving, step in rings:
        by = dict(zip(OFFSETS, pieces, strict=True))
        plan[0].append([*([] if step == 1 else [moving[0]]), by[(-4, 3, 2, 1)[step - 1]]])
        if step < 4:
            plan[1].append([*([] if step == 1 else [moving[1]]), by[(-3, -2, -1)[step - 1]]])
    plan = [p for p in plan if p]
    if len(rings) == 1 and rings[0][2] == 1:
        sent = [p[0][0] for p in plan]
    else:
        parts = [part(v) for p in plan for terms in p for v in terms]

        def body(info, _, ins, __, outs, ___):
            found = iter(zip(parts, ins, strict=True))
            for out, p in zip(outs, plan, strict=True):
                column = 0
                for terms in p:
                    values = [piece.read(ref) for piece, ref in (next(found) for _ in terms)]
                    total = values[0]
                    if len(values) == 2:
                        total = (total.astype(f32) + values[1].astype(f32)).astype(bf16)
                    out[:, column : column + total.shape[1]] = total
                    column += total.shape[1]

        rows = rings[0][0][0].shape[0]
        wide = [sum(part(terms[0]).width for terms in p) for p in plan]
        shapes = [like((rows, w), bf16) for w in wide]
        came_in = {id(m.array) for _, moving, _ in rings for m in moving or ()}
        given = [Close(p.array) if id(p.array) in came_in else p.array for p in parts]
        sent = call(body, info, [], given, [], [Near(v) for v in shapes], least=0)
    if hold is not None:
        sent, hold = sync(sent, hold)
    came = [lax.ppermute(v, "blk", way) for v, way in zip(sent, (forth, back), strict=False)]
    results, column = [], 0
    for k, (pieces, moving, step) in enumerate(rings):
        wide = pieces[0].shape[1]
        found = [Part(came[0], column, wide)]
        if step == 4:
            found.append(moving[1])
        else:
            before = sum(r[0][0].shape[1] for r in rings[:k] if r[2] < 4)
            found.append(Part(came[1], before, wide))
        results.append(found)
        column += wide
    return [*results, hold]


def reduce_terms(pieces, moving):
    if lax.axis_size("blk") != 8:
        everything = jnp.concatenate([p.astype(f32) for p in pieces], axis=0)
        return [lax.psum_scatter(everything, "blk", scatter_dimension=0, tiled=True)]
    return [pieces[0], *moving]


def dot(left, right, over=(1, 0)):
    return lax.dot_general(
        left, right, (((over[0],), (over[1],)), ((), ())), preferred_element_type=f32
    )


def dot_t(left, right):
    return dot(left, right, (1, 1))


def t_dot(left, right):
    return dot(left, right, (0, 0))


def norm_rows(values, gain):
    return values * lax.rsqrt(jnp.mean(values * values, axis=-1, keepdims=True) + EPS) * gain


def norm_back(values, gain, grad):
    inverse = lax.rsqrt(jnp.mean(values * values, axis=-1, keepdims=True) + EPS)
    unit = values * inverse
    weighted = grad * gain
    along = jnp.mean(weighted * unit, axis=-1, keepdims=True)
    return inverse * (weighted - unit * along), grad * unit


def gelu_both(values):
    root = math.sqrt(2.0 / math.pi)
    square = values * values
    bent = jnp.tanh(root * values * (1.0 + 0.044715 * square))
    half = 0.5 * (1.0 + bent)
    slope = half + 0.5 * values * (1.0 - bent * bent) * root * (1.0 + 3 * 0.044715 * square)
    return values * half, slope


def heads_in(width):
    return [slice(at, at + HDIM) for at in range(0, width, HDIM)]


def head_parts(values, count):
    size = values.shape[1] // count
    return [[values[:, j * size :][:, at] for at in heads_in(size)] for j in range(count)]


def by_passage(found, count):
    rows = [
        jnp.concatenate(found[at : at + count], axis=1) for at in range(0, len(found), count)
    ]
    return jnp.concatenate(rows, axis=0)


def assemble(info, pieces, targets, signals, column_from=0):
    rows = pieces[0].shape[0]
    copies = []
    for t, piece in enumerate(pieces):
        at = pl.ds(pl.multiple_of(info[PLACES + t] * rows, 16), rows)
        column = column_from
        for k, target in enumerate(targets):
            wide = target.shape[1]
            copies.append(
                pltpu.make_async_copy(
                    piece.at[:, column : column + wide], target.at[at, :], signals.at[k, t]
                )
            )
            column += wide
    for copy in copies:
        copy.start()
    for copy in copies:
        copy.wait()


def hand_out(info, sources, pieces):
    rows = pieces[0].shape[0]
    for t, piece in enumerate(pieces):
        at = pl.ds(pl.multiple_of(info[PLACES + t] * rows, 16), rows)
        column = 0
        for source in sources:
            piece[:, column : column + source.shape[1]] = source[at, :].astype(piece.dtype)
            column += source.shape[1]


def token_rows(refs):
    return jnp.concatenate([r[k] for k in range(refs[0].shape[0]) for r in refs], axis=0)


def emit(partial, outs):
    each, part, _ = outs[0].shape
    for k in range(each):
        for r, out in enumerate(outs):
            at = (k * len(outs) + r) * part
            out[k] = partial[at : at + part].astype(out.dtype)


def slots_used(info, b, part, slot):
    column = lax.broadcasted_iota(jnp.int32, (1, slot), 1)
    position = (lax.div(column, part) ^ info[HEAD]) * part + lax.rem(column, part)
    return position < info[LENGTHS + b]


def keys_used(info, question, passages, part, slot, count_pass):
    return jnp.concatenate(
        [
            slots_used(info, k, part, slot) & (question[...] == k // count_pass)
            for k in passages
        ],
        axis=1,
    )


def call(
    body, info, stepped, fixed, out_stepped, out_fixed, scratch=(), flops=0, steps=1, near=False, least=LARGE, each=1
):
    def by_step(shape):
        last = shape[0] // each - 1
        return pl.BlockSpec((each, *shape[1:]), lambda b: (jnp.minimum(b, last),) + (0,) * (len(shape) - 1))

    def whole(a):
        if type(a) is Far:
            return pl.BlockSpec(memory_space=pltpu.HBM)
        if isinstance(a, Rider):
            return pl.BlockSpec(a.shape, lambda b: (a.index, 0, 0))
        index = (0, a.index) if type(a) is Columns else (0,) * len(a.shape)
        return pl.BlockSpec(a.shape, lambda b: index)

    counts = [len(stepped), len(fixed), len(out_stepped), len(out_fixed), len(scratch)]
    stops = np.cumsum(counts)

    def split(info_ref, *refs):
        body(info_ref, *(refs[e - c : e] for c, e in zip(counts, stops, strict=True)))

    def large(a):
        return not near and math.prod(a.shape) * a.dtype.itemsize >= least

    def given(a):
        array = a.array if isinstance(a, (Columns, Far, Rider)) else a
        far = (large(a) and not isinstance(a, Close)) or (isinstance(a, Rider) and a.far)
        return pltpu.with_memory_space_constraint(array, pltpu.HBM) if far else array

    def made(a):
        if isinstance(a, Later) or (large(a) and not isinstance(a, Near)):
            return pltpu.HBM(a.shape, a.dtype)
        return a.array if isinstance(a, Near) else a

    arrays = [*stepped, *fixed, *out_stepped, *out_fixed]
    moved = sum(math.prod(a.shape) * a.dtype.itemsize for a in arrays)
    return pl.pallas_call(
        split,
        grid=(steps,),
        in_specs=[
            pl.BlockSpec(memory_space=pltpu.SMEM),
            *(by_step(a.shape) for a in stepped),
            *(whole(a) for a in fixed),
        ],
        out_specs=[
            *(by_step(a.shape) for a in out_stepped),
            *(whole(a) for a in out_fixed),
        ],
        out_shape=[made(a) for a in (*out_stepped, *out_fixed)],
        scratch_shapes=list(scratch),
        compiler_params=pltpu.CompilerParams(
            dimension_semantics=("arbitrary",), vmem_limit_bytes=VMEM_LIMIT
        ),
        cost_estimate=pl.CostEstimate(
            flops=int(flops), bytes_accessed=int(moved), transcendentals=0
        ),
    )(info, *(given(a) for a in (*stepped, *fixed)))


class Columns:
    def __init__(self, array, width, index):
        self.array, self.index, self.dtype = array, index, array.dtype
        self.shape = (array.shape[0], width)


class Near(Columns):
    def __init__(self, array):
        self.array, self.shape, self.dtype = array, array.shape, array.dtype


class Later(Near):
    pass


class Rider:
    def __init__(self, array, index, far):
        self.array, self.index, self.dtype, self.far = array, index, array.dtype, far
        self.shape = (1, *array.shape[1:])


class Far:
    def __init__(self, array):
        self.array, self.shape, self.dtype = array, array.shape, array.dtype


class Close(Far):
    pass


def like(shape, dtype):
    return jax.ShapeDtypeStruct(tuple(shape), dtype)


def by_rows(fn, info, stepped, fixed, dtypes, gain=False, riders=None, kept=True):
    steps, _, width = stepped[0].shape
    count = 0 if riders is None else 1
    alone = [like(stepped[0].shape, d) for d in dtypes]
    outs = alone if riders is None or kept else alone[:-1]
    more = 0 if riders is None else riders.shape[0]
    together = [like((steps + count, *stepped[0].shape[1:]), dtypes[-1])] if more else []

    def body(info_ref, ins, whole, outs, sums, _):
        b = pl.program_id(0)
        if more:
            whole, rows = whole[:-1], whole[-1]

        @pl.when(b < steps)
        def _():
            results = fn(*(r[0].astype(f32) for r in ins), *(r[...] for r in whole))
            for out, value in zip(outs, results, strict=False):
                out[0] = value.astype(out.dtype)
            if more:
                outs[-1][0] = results[len(dtypes) - 1].astype(outs[-1].dtype)
            for total in sums:
                found = jnp.sum(results[-1], axis=0, keepdims=True)

                @pl.when(b == 0)
                def _():
                    total[...] = found

                @pl.when(b > 0)
                def _():
                    total[...] += found

        if more:

            @pl.when(b == steps)
            def _():
                outs[-1][0, :more, :] = rows[...]

    return call(
        body,
        info,
        stepped,
        [*fixed, riders] if more else fixed,
        [*outs, *together],
        [like((1, width), f32)] * gain,
        flops=10 * math.prod(stepped[0].shape),
        steps=steps + count,
        near=True,
    )


def partial_rows(blocks, part, width):
    return [Near(like((blocks, part, width), d)) for d in (f32, bf16, f32, bf16)]


def piece_shapes(rows, columns):
    return [Later(like((rows, columns), d)) for d in (f32, *[bf16] * 7)]


def gathered(info, pieces, widths, column_from=0):
    rows, wide = pieces[0].shape[0] * len(pieces), sum(widths)

    def body(info, _, ins, __, outs, scratch):
        together, signals = scratch
        assemble(info, ins, (together,), signals, column_from)
        column = 0
        for out in outs:
            out[...] = together[:, column : column + out.shape[1]]
            column += out.shape[1]

    return call(
        body,
        info,
        [],
        [Far(p) for p in pieces],
        [],
        [Near(like((rows, w), bf16)) for w in widths],
        [pltpu.VMEM((rows, wide), bf16), pltpu.SemaphoreType.DMA((1, len(pieces)))],
    )


def attention_scratch(width, size, pieces):
    return [
        *(pltpu.VMEM((width, k * size), bf16) for k in (3, 1, 4)),
        pltpu.SemaphoreType.DMA((1, len(pieces))),
    ]


def encoder_attention(info, normed, pieces):
    blocks, part, width = normed[0].shape
    slot = part * len(normed)
    size = pieces[0].shape[1] // 4
    count = size // HDIM
    each = 2

    def body(info, rows, pieces, outs, _, scratch):
        qkv, probs, context = outs[:3]
        w_in, w_out, together, signals = scratch
        b = pl.program_id(0)

        @pl.when(b == 0)
        def _():
            assemble(info, pieces, (together,), signals)
            w_in[...] = together[:, : 3 * size]
            w_out[...] = together[:, 3 * size :]

        made = dot(token_rows(rows), w_in[...]).astype(bf16)
        qkv[...] = made.reshape(qkv.shape)
        parts = [head_parts(made[p * slot : (p + 1) * slot], 3) for p in range(each)]
        pairs = [(p, k) for p in range(each) for k in range(count)]
        scores = [dot_t(parts[p][0][k] * SCALE, parts[p][1][k]) for p, k in pairs]
        allowed = [slots_used(info, b * each + p, part, slot) for p in range(each)]
        found = []
        for (p, k), score in zip(pairs, scores, strict=True):
            score = jnp.where(allowed[p], score, masked_score)
            spread_out = jnp.exp(score - jnp.max(score, axis=-1, keepdims=True))
            inverse = 1.0 / jnp.sum(spread_out, axis=-1, keepdims=True)
            found.append((spread_out * inverse).astype(bf16))
            probs[p, k] = found[-1]
        found = [dot(w, parts[p][2][k]) for (p, k), w in zip(pairs, found, strict=True)]
        joined = by_passage(found, count).astype(bf16)
        context[...] = joined.reshape(context.shape)
        emit(dot_t(joined, w_out[...]), outs[3:])

    return call(
        body,
        info,
        normed,
        [Far(p) for p in pieces],
        [
            like((blocks, slot, 3 * size), bf16),
            like((blocks, count, slot, slot), bf16),
            like((blocks, slot, size), bf16),
            *partial_rows(blocks, part, width),
        ],
        [],
        attention_scratch(width, size, pieces),
        flops=2 * blocks * slot * (width * size * 4 + 8 * slot * size),
        steps=blocks // each,
        each=each,
    )


def encoder_attention_back(info, grads, normed, qkv, probs, context, weights, gains):
    blocks, part, width = normed[0].shape
    slot = part * len(normed)
    size = context.shape[2]
    each = 2

    def body(info, stepped, fixed, outs, ends, scratch):
        grad_refs, normed_refs = stepped[:4], stepped[4:8]
        qkv, probs, context = stepped[8:]
        w_in, w_out, gains = fixed
        pieces, gain_out = ends[:-1], ends[-1]
        total_in, total_out = scratch
        b = pl.program_id(0)

        @pl.when(b == 0)
        def _():
            total_in[...] = jnp.zeros_like(total_in)
            total_out[...] = jnp.zeros_like(total_out)
            gain_out[...] = jnp.zeros_like(gain_out)

        grad = token_rows(grad_refs)
        rows = token_rows(normed_refs)
        dcontext = dot(grad, w_out[...]).astype(bf16)
        parts = [head_parts(qkv[p], 3) for p in range(each)]
        cuts = [c for p in range(each) for c in head_parts(dcontext[p * slot : (p + 1) * slot], 1)[0]]
        pairs = [(p, k) for p in range(each) for k in range(size // HDIM)]
        backs = [dot_t(c, parts[p][2][k]) for (p, k), c in zip(pairs, cuts, strict=True)]
        dvals = [t_dot(probs[p, k], c) for (p, k), c in zip(pairs, cuts, strict=True)]
        lows = []
        for (p, k), back in zip(pairs, backs, strict=True):
            wide = probs[p, k].astype(f32)
            low = wide * (back - jnp.sum(wide * back, axis=-1, keepdims=True))
            lows.append(low.astype(bf16))
        dquery = [dot(d, parts[p][1][k]) * SCALE for (p, k), d in zip(pairs, lows, strict=True)]
        dkeys = [t_dot(d, parts[p][0][k]) * SCALE for (p, k), d in zip(pairs, lows, strict=True)]
        count = size // HDIM
        moved = jnp.concatenate(
            [by_passage(found, count) for found in (dquery, dkeys, dvals)], axis=1
        ).astype(bf16)
        partial = dot_t(moved, w_in[...])
        emit(partial, outs)
        gain_out[...] += jnp.sum(partial * rows.astype(f32), axis=0, keepdims=True) / gains[0:1, :]
        total_in[...] += t_dot(rows, moved)
        total_out[...] += t_dot(grad, context[...].reshape(grad.shape[0], size))

        @pl.when(b == blocks // each - 1)
        def _():
            hand_out(info, (total_in, total_out), pieces)

    results = call(
        body,
        info,
        [*grads, *normed, qkv, probs, context],
        [*(Close(w) for w in weights), gains],
        partial_rows(blocks, part, width),
        [*piece_shapes(width // 8, 4 * size), like((1, width), f32)],
        [
            pltpu.VMEM((width, 3 * size), f32),
            pltpu.VMEM((width, size), f32),
        ],
        flops=2 * blocks * slot * (width * size * 8 + 20 * slot * size),
        steps=blocks // each,
        each=each,
    )
    return results[:4], results[4:12], results[12]


def ffn_scratch(width, hidden, pieces):
    return [
        *[pltpu.VMEM((width, hidden), bf16)] * 2,
        pltpu.SemaphoreType.DMA((2, len(pieces))),
    ]


def encoder_ffn(info, normed, pieces, hidden):
    blocks, part, width = normed[0].shape
    slot = part * len(normed)

    def body(info, rows, pieces, outs, _, scratch):
        active, slope = outs[:2]
        w_inner, w_outer, signals = scratch

        @pl.when(pl.program_id(0) == 0)
        def _():
            assemble(info, pieces, (w_inner, w_outer), signals)

        value, bend = gelu_both(dot(token_rows(rows), w_inner[...]))
        low = value.astype(bf16)
        active[...] = low.reshape(active.shape)
        slope[...] = bend.astype(bf16).reshape(slope.shape)
        emit(dot_t(low, w_outer[...]), outs[2:])

    return call(
        body,
        info,
        normed,
        [Far(p) for p in pieces],
        [*[like((blocks, slot, hidden), bf16)] * 2, *partial_rows(blocks, part, width)],
        [],
        ffn_scratch(width, hidden, pieces),
        flops=4 * blocks * slot * width * hidden,
        steps=blocks // 2,
        each=2,
    )


def encoder_ffn_back(info, grads, slope, weights):
    blocks, (_, part, width) = slope.shape[0], grads[0].shape
    slot = part * len(grads)
    hidden = slope.shape[2]

    def body(info, stepped, weights, outs, ends, scratch):
        dinner = outs[0]
        w_inner, w_outer = weights
        back = dot(token_rows(stepped[:4]), w_outer[...])
        low = (back * stepped[4][...].reshape(back.shape).astype(f32)).astype(bf16)
        dinner[...] = low.reshape(dinner.shape)
        emit(dot_t(low, w_inner[...]), outs[1:])

    return call(
        body,
        info,
        [*grads, slope],
        [Close(w) for w in weights],
        [like((blocks, slot, hidden), bf16), *partial_rows(blocks, part, width)],
        [],
        flops=4 * blocks * slot * width * hidden,
        steps=blocks // 2,
        each=2,
    )


def weight_grads(info, pairs, more=(), cut=True):
    blocks, (_, part, width) = pairs[0][1].shape[0], pairs[0][0][0].shape
    widths = [right.shape[2] for _, right in pairs]

    def body(info, stepped, more, __, ends, totals):
        totals = totals if cut else ends
        for k, total in enumerate(totals):
            left, right = token_rows(stepped[5 * k : 5 * k + 4]), stepped[5 * k + 4]
            total[...] = t_dot(left, right[...].reshape(left.shape[0], total.shape[1]))
        if cut:
            hand_out(info, (*totals, *more), ends)

    return call(
        body,
        info,
        [a for left, right in pairs for a in (*left, right)],
        more,
        [],
        piece_shapes(width // 8, sum(widths) + sum(m.shape[1] for m in more))
        if cut
        else [like((width, w), f32) for w in widths],
        [pltpu.VMEM((width, w), f32) for w in widths] if cut else [],
        flops=2 * blocks * part * 4 * width * sum(widths),
        each=blocks,
    )


def finish(info, terms, widths, turned):
    terms = [part(t) for t in terms]
    rows = terms[0].array.shape[0]
    shapes = [(w, rows) if t else (rows, w) for w, t in zip(widths, turned, strict=True)]

    def body(info, _, ins, __, outs, ___):
        total = terms[0].read(ins[0])
        for term, ref in zip(terms[1:], ins[1:], strict=True):
            total = total + term.read(ref).astype(f32)
        column = 0
        for out, wide, turn in zip(outs, widths, turned, strict=True):
            found = total[:, column : column + wide]
            out[...] = found.T if turn else found
            column += wide

    return call(body, info, [], [t.array for t in terms], [], [like(s, f32) for s in shapes])


def cross_forward(info, states, weights, decoder, own_question, count_q, count_pass):
    rows_in, terms, gains = decoder
    blocks = count_q * count_pass
    _, part, width = states[0].shape
    slot = part * len(states)
    rows_dec = rows_in.shape[0]
    size = weights[1].shape[1]
    steps = 2

    def body(info, rows, fixed, outs, ends, scratch):
        weight, w_query, rows_in, *terms, gains, question = fixed
        after_self, normed, queries, stats = ends
        held = scratch[0]
        b = pl.program_id(0)

        @pl.when(b == 0)
        def _():
            after_self[...] = rows_in[...].astype(f32) + summed(terms)
            normed[...] = norm_rows(after_self[...], gains[1:2, :]).astype(bf16)
            queries[...] = dot(normed[...], w_query[...]).astype(bf16)

        made = dot(token_rows(rows), weight[...]).astype(bf16)
        outs[0][...] = made.reshape(outs[0].shape)
        each = made.shape[0]
        held[pl.ds(pl.multiple_of(b * each, each), each), :] = made

        @pl.when(b == steps - 1)
        def _():
            allowed = keys_used(info, question, range(blocks), part, slot, count_pass)
            lane = lax.broadcasted_iota(jnp.int32, (rows_dec, HDIM), 1)
            keys, vals = head_parts(held[...], 2)
            asking = head_parts(queries[...], 1)[0]
            scores = [dot_t(q * SCALE, t) for q, t in zip(asking, keys, strict=True)]
            for k, score in enumerate(scores):
                score = jnp.where(allowed, score, masked_score)
                top = jnp.max(score, axis=-1, keepdims=True)
                spread_out = jnp.exp(score - top)
                total = jnp.sum(spread_out, axis=-1, keepdims=True)
                at = k * LANES
                stats[:, at : at + HDIM] = dot(spread_out.astype(bf16), vals[k])
                stats[:, at + HDIM : at + LANES] = jnp.where(lane == 0, top, total)

    return call(
        body,
        info,
        states,
        [*(Close(w) for w in weights), rows_in, *terms, gains, own_question],
        [like((blocks, slot, 2 * size), bf16)],
        [
            Later(like((rows_dec, width), f32)),
            Later(like((rows_dec, width), bf16)),
            like((rows_dec, size), bf16),
            like((rows_dec, size // HDIM * LANES), f32),
        ],
        [pltpu.VMEM((blocks * slot, 2 * size), bf16)],
        flops=4 * blocks * slot * width * size,
        steps=steps,
        each=blocks // steps,
    )


def merged(first, second):
    lane = lax.broadcasted_iota(jnp.int32, (first.shape[0], HDIM), 1)
    found = []
    for at in range(0, first.shape[1], LANES):
        tops = [v[:, at + HDIM : at + HDIM + 1] for v in (first, second)]
        totals = [v[:, at + HDIM + 1 : at + HDIM + 2] for v in (first, second)]
        top = jnp.maximum(*tops)
        scales = [jnp.exp(t - top) for t in tops]
        total = totals[0] * scales[0] + totals[1] * scales[1]
        found.append(first[:, at : at + HDIM] * scales[0] + second[:, at : at + HDIM] * scales[1])
        found.append(jnp.where(lane == 0, top, total))
    return jnp.concatenate(found, axis=1)


def in_order(info, bits, own, other):
    later = (info[BLK] & bits) != 0
    return jnp.where(later, other, own), jnp.where(later, own, other)


def merge(info, own, other, bits):
    def body(info, _, ins, __, outs, ___):
        outs[0][...] = merged(*in_order(info, bits, ins[0][...], ins[1][...]))

    return call(body, info, [], [own, other], [], [like(own.shape, f32)])[0]


def cross_out(info, stats, bits, w_output):
    rows, columns = stats[0].shape
    size = columns // LANES * HDIM
    width = w_output.shape[0]

    def body(info, _, ins, __, outs, scratch):
        w_output = ins[-1]
        out, log_total, context, own, sent = outs
        values = [r[...] for r in ins[:-1]]
        near = merged(*in_order(info, bits[0], *values[:2]))
        far = merged(*in_order(info, bits[0], *values[2:]))
        stats = merged(*in_order(info, bits[1], near, far))
        log_total[...] = jnp.zeros_like(log_total)
        for k, at in enumerate(heads_in(size)):
            base = k * LANES
            top = stats[:, base + HDIM : base + HDIM + 1]
            total = stats[:, base + HDIM + 1 : base + HDIM + 2]
            out[:, at] = stats[:, base : base + HDIM] / total
            log_total[:, k : k + 1] = top + jnp.log(total)
        context[...] = out[...].astype(bf16)
        own[...] = dot_t(context[...], w_output[...])
        sent[...] = own[...].astype(bf16)

    return call(
        body,
        info,
        [],
        [*stats, w_output],
        [],
        [
            like((rows, size), f32),
            like((rows, LANES), f32),
            Later(like((rows, size), bf16)),
            like((rows, width), f32),
            like((rows, width), bf16),
        ],
        flops=2 * rows * size * width,
    )


def cross_back(info, key_vals, inputs, own_question, count_pass, slot, part):
    cotangent, after_cross, terms, gains, w_output, out, log_total, queries, weight = inputs
    blocks = key_vals.shape[0]
    rows_dec, width = after_cross.shape
    size = queries.shape[1]

    def body(info, stepped, fixed, outs, ends, scratch):
        cotangent, after_cross, own, r1, r2, r3, gains, w_output, out, log_total, queries, weight, question = fixed
        key_vals = stepped[0]
        dkey_vals = outs[0]
        dcross, dcross_low, gain_out, dqueries = ends
        total = summed((own, r1, r2, r3))
        back, gain_out[...] = norm_back(after_cross[...], gains[2:3, :], total)
        dcross[...] = cotangent[...].astype(f32) + back
        dcross_low[...] = dcross[...].astype(bf16)
        dcontext = dot(dcross_low[...], w_output[...]).astype(bf16)
        allowed = keys_used(info, question, range(blocks), part, slot, count_pass)
        keys, vals = head_parts(key_vals[...].reshape(blocks * slot, 2 * size), 2)
        asking = head_parts(queries[...], 1)[0]
        cuts = head_parts(dcontext, 1)[0]
        outs_of = head_parts(out[...], 1)[0]
        scores = [dot_t(q * SCALE, t) for q, t in zip(asking, keys, strict=True)]
        backs = [dot_t(c, v) for c, v in zip(cuts, vals, strict=True)]
        probs, lows = [], []
        for k, score in enumerate(scores):
            row_term = jnp.sum(cuts[k].astype(f32) * outs_of[k], axis=-1, keepdims=True)
            score = jnp.where(allowed, score, masked_score)
            probs.append(jnp.exp(score - log_total[:, k : k + 1]))
            lows.append((probs[k] * (backs[k] - row_term)).astype(bf16))
        dvals = [t_dot(p.astype(bf16), c) for p, c in zip(probs, cuts, strict=True)]
        dkeys = [t_dot(d, q) * SCALE for d, q in zip(lows, asking, strict=True)]
        found = [dot(d, t) * SCALE for d, t in zip(lows, keys, strict=True)]
        dqueries[...] = jnp.concatenate(found, axis=1)
        made = jnp.concatenate([*dkeys, *dvals], axis=1).astype(bf16)
        dkey_vals[...] = made.reshape(dkey_vals.shape)
        emit(dot_t(made, weight[...]), outs[1:])

    return call(
        body,
        info,
        [key_vals],
        [
            cotangent,
            after_cross,
            *terms,
            gains,
            w_output,
            out,
            log_total,
            queries,
            Close(weight),
            own_question,
        ],
        [like(key_vals.shape, bf16), *partial_rows(blocks, part, width)],
        [
            Later(like((rows_dec, width), f32)),
            Later(like((rows_dec, width), bf16)),
            Later(like((rows_dec, width), f32)),
            like((rows_dec, size), f32),
        ],
        flops=4 * blocks * slot * width * size,
        each=blocks,
    )


def summed(refs):
    count = refs[0].shape[0]

    def rows(ref):
        return ref[...] if len(ref.shape) == 2 else ref[0, :count, :]

    terms = [rows(ref).astype(f32) for ref in refs[1:]]
    total = refs[0][...]
    for term in terms:
        total = total + term
    return total


def decoder_self(info, rows, gains, pieces, column_from, size, order):
    count, width = rows.shape

    def body(info, _, ins, __, outs, scratch):
        rows, gains, order_q, order_k = ins[:4]
        normed, qkv, probs, context, own, sent, weight = outs
        assemble(info, ins[4:], (weight,), scratch[0], column_from)
        normed[...] = norm_rows(rows[...].astype(f32), gains[0:1, :]).astype(bf16)
        qkv[...] = dot(normed[...], weight[:, : 3 * size]).astype(bf16)
        query_at, key_at = order_q[...], order_k[...]
        same = lax.div(query_at, 1000) == lax.div(key_at, 1000)
        allowed = same & (key_at <= query_at) & (key_at >= 0) & (query_at >= 0)
        for k, at in enumerate(heads_in(size)):
            query, keys, vals = (qkv[:, j * size + at.start : j * size + at.stop] for j in range(3))
            scores = jnp.where(allowed, dot_t(query, keys) * SCALE, masked_score)
            spread_out = jnp.exp(scores - jnp.max(scores, axis=-1, keepdims=True))
            share_out = spread_out / jnp.sum(spread_out, axis=-1, keepdims=True)
            share_out = jnp.where(allowed, share_out, 0.0)
            probs[k] = share_out
            context[:, at] = dot(share_out.astype(bf16), vals).astype(bf16)
        own[...] = dot_t(context[...], weight[:, 3 * size :])
        sent[...] = own[...].astype(bf16)

    return call(
        body,
        info,
        [],
        [rows, gains, *order, *(Far(p) for p in pieces)],
        [],
        [
            Later(like((count, width), bf16)),
            Later(like((count, 3 * size), bf16)),
            Later(like((size // HDIM, count, count), f32)),
            Later(like((count, size), bf16)),
            like((count, width), f32),
            like((count, width), bf16),
            Later(like((width, 4 * size), bf16)),
        ],
        [pltpu.SemaphoreType.DMA((1, len(pieces)))],
        flops=2 * count * width * size * 4,
    )


def decoder_back(info, cotangent, pieces):
    count, width = cotangent.shape
    hidden = pieces[0].shape[1] // 2

    def body(info, _, ins, __, outs, scratch):
        w_inner, w_outer, back = outs
        assemble(info, ins[1:], (w_inner, w_outer), scratch[0])
        back[...] = dot(ins[0][...], w_outer[...])

    return call(
        body,
        info,
        [],
        [cotangent, *(Far(p) for p in pieces)],
        [],
        [Near(like((width, hidden), bf16)), like((width, hidden), bf16), like((count, hidden), f32)],
        [pltpu.SemaphoreType.DMA((2, len(pieces)))],
        flops=2 * count * width * hidden,
    )


def decoder_ffn(info, after_self, terms, back, gains, w_inner):
    count, width = after_self.shape
    hidden = w_inner.shape[1]

    def body(info, _, ins, __, outs, scratch):
        after_self, own, r1, r2, r3, back, gains, w_inner = ins
        after_cross, normed, active, dinner, own_back, sent_back = outs
        after_cross[...] = after_self[...] + summed((own, r1, r2, r3))
        normed[...] = norm_rows(after_cross[...], gains[2:3, :]).astype(bf16)
        value, slope = gelu_both(dot(normed[...], w_inner[...]))
        active[...] = value.astype(bf16)
        dinner[...] = (slope * back[...]).astype(bf16)
        own_back[...] = dot_t(dinner[...], w_inner[...])
        sent_back[...] = own_back[...].astype(bf16)

    return call(
        body,
        info,
        [],
        [after_self, *terms, back, gains, Close(w_inner)],
        [],
        [
            like((count, width), f32),
            Later(like((count, width), bf16)),
            Later(like((count, hidden), bf16)),
            Later(like((count, hidden), bf16)),
            like((count, width), f32),
            like((count, width), bf16),
        ],
        flops=4 * count * width * hidden,
    )


def rows_back(info, terms, weight):
    (count, size), width = terms[0].shape, weight.shape[0]

    def body(info, _, ins, __, outs, scratch):
        low, own, sent = outs
        total = ins[0][...]
        for term in ins[1:-1]:
            total = total + term[...]
        low[...] = total.astype(bf16)
        own[...] = dot_t(low[...], ins[-1][...])
        sent[...] = own[...].astype(bf16)

    return call(
        body,
        info,
        [],
        [*terms, weight],
        [],
        [
            Later(like((count, size), bf16)),
            like((count, width), f32),
            like((count, width), bf16),
        ],
        flops=2 * count * width * size,
    )


def decoder_self_back(
    info, dcross, after_self, terms, gains, weight, qkv, probs
):
    count, width = after_self.shape
    size = weight.shape[1] // 4

    def body(info, _, ins, __, outs, scratch):
        dcross, after_self, *terms, gains, weight, qkv, probs = ins
        dself, dself_low, gain_rows, moved, own_back, sent_back = outs
        back, gain_rows[...] = norm_back(after_self[...], gains[1:2, :], summed(terms))
        dself[...] = dcross[...] + back
        dself_low[...] = dself[...].astype(bf16)
        dcontext = dot(dself_low[...], weight[:, 3 * size :]).astype(bf16)
        for k, at in enumerate(heads_in(size)):
            query, keys, vals = (qkv[:, j * size + at.start : j * size + at.stop] for j in range(3))
            share_out = probs[k]
            dprobs = dot_t(dcontext[:, at], vals)
            dscores = share_out * (dprobs - jnp.sum(share_out * dprobs, axis=-1, keepdims=True))
            dscores = dscores.astype(bf16)
            found = (
                dot(dscores, keys) * SCALE,
                t_dot(dscores, query) * SCALE,
                t_dot(share_out.astype(bf16), dcontext[:, at]),
            )
            for j, term in enumerate(found):
                moved[:, j * size + at.start : j * size + at.stop] = term.astype(bf16)
        own_back[...] = dot_t(moved[...], weight[:, : 3 * size])
        sent_back[...] = own_back[...].astype(bf16)

    return call(
        body,
        info,
        [],
        [dcross, after_self, *terms, gains, weight, qkv, probs],
        [],
        [
            like((count, width), f32),
            Later(like((count, width), bf16)),
            like((count, width), f32),
            Later(like((count, 3 * size), bf16)),
            like((count, width), f32),
            like((count, width), bf16),
        ],
        flops=2 * count * width * size * 8,
    )


def own_rows(info, values, dec_own):
    found = values[:dec_own]
    for k in range(1, values.shape[0] // dec_own):
        found = jnp.where(info[HEAD] == k, values[k * dec_own : (k + 1) * dec_own], found)
    return found


def decoder_ends(
    info, rows, dself, terms, gains, after_cross, out_terms, gain_rows, gain_sums, dec_own
):
    count, width = dself.shape

    def body(info, _, ins, __, outs, scratch):
        rows, dself, after_cross, gains = ins[:4]
        three, four, zero, one = ins[-4:]
        grad, states, found = outs
        total, out_total = summed(ins[4:8]), summed(ins[8:12])
        back, two = norm_back(rows[...].astype(f32), gains[0:1, :], total)
        grad[...] = own_rows(info, dself[...] + back, dec_own)
        states[...] = own_rows(info, after_cross[...] + out_total, dec_own).astype(bf16)
        row = lax.div(lax.broadcasted_iota(jnp.int32, (count, 1), 0), dec_own)
        mine = (row == info[HEAD]) & (info[BLK] == 0)
        found[0:1, :] = zero[...]
        found[1:2, :] = one[...]
        for k, values in enumerate((two, three[...], four[...])):
            found[2 + k : 3 + k, :] = jnp.sum(jnp.where(mine, values, 0.0), axis=0, keepdims=True)

    return call(
        body,
        info,
        [],
        [rows, dself, after_cross, gains, *terms, *out_terms, *gain_rows, *gain_sums],
        [],
        [like((dec_own, width), f32), like((dec_own, width), bf16), like((5, width), f32)],
    )


def decoder_weight_grads(info, own, pairs_in, pairs_out):
    count, width = pairs_in[0][0].shape

    def body(info, _, ins, __, outs, scratch):
        row = lax.broadcasted_iota(jnp.int32, (own, width), 0) + info[BLK] * own
        column = lax.broadcasted_iota(jnp.int32, (own, width), 1)
        pick = jnp.where(row == column, 1.0, 0.0).astype(bf16)
        outs, ins = iter(outs), iter(ins)
        for _, _, arrays in pairs_in:
            left, right = next(ins)[...], next(ins)[...]
            found = t_dot(dot_t(left, pick).astype(bf16), right)
            wide = found.shape[1] // arrays
            for k in range(arrays):
                next(outs)[...] = found[:, k * wide : (k + 1) * wide]
        for _ in pairs_out:
            left, right = next(ins)[...], next(ins)[...]
            next(outs)[...] = t_dot(left, dot_t(right, pick).astype(bf16))

    outs = [like((own, r.shape[1] // n), f32) for _, r, n in pairs_in for _ in range(n)]
    outs += [like((l.shape[1], own), f32) for l, _ in pairs_out]
    flat = [a for pair in pairs_in for a in pair[:2]] + [a for pair in pairs_out for a in pair]
    return call(body, info, [], flat, [], outs, flops=2 * count * own * width * 10, least=0)


def shards(
    encoder_input,
    passage_lengths,
    decoder_input,
    encoder_query,
    encoder_key,
    encoder_value,
    encoder_output,
    encoder_inner,
    encoder_outer,
    decoder_query,
    decoder_key,
    decoder_value,
    decoder_output,
    cross_query,
    cross_key,
    cross_value,
    cross_output,
    decoder_inner,
    decoder_outer,
    encoder_gains,
    decoder_gains,
    encoder_cotangent,
    decoder_cotangent,
):
    head, blk = lax.axis_index("head"), lax.axis_index("blk")
    blk_count, head_count = lax.axis_size("blk"), lax.axis_size("head")
    count_q, count_pass, part, width = encoder_input.shape
    blocks = count_q * count_pass
    slot = part * head_count
    own = width // blk_count
    if blk_count == 8:
        places = jnp.asarray(place_table(8))[blk]
    else:
        places = jnp.arange(8, dtype=jnp.int32)
    info = jnp.concatenate(
        [places, jnp.stack([head, blk]).astype(jnp.int32), passage_lengths.reshape(blocks)]
    )

    size, units = encoder_query.shape[1], encoder_inner.shape[1]
    inputs = encoder_input.reshape(blocks, part, width)
    dec_part = decoder_input.shape[1]
    dec_own = count_q * dec_part
    dec_rows = dec_own * head_count
    filled = -(-dec_rows // 16) * 16

    attention = jnp.concatenate(
        [encoder_query, encoder_key, encoder_value, encoder_output.T], axis=1
    )
    attention, inputs = sync(attention, inputs)
    attention = fetch_step(fetch_start(attention), -1, 1)
    first = by_rows(
        lambda x, g: (norm_rows(x, g[0:1]),), info, [inputs], [encoder_gains], [bf16]
    )[0]
    attention, first = sync(attention, first)

    attention = fetch_step(attention, -2, 2)
    first_all = [first, swap(first, "head", 1), swap(first, "head", 2)]
    ffn = jnp.concatenate(
        [
            encoder_inner,
            encoder_outer.T,
            decoder_query,
            decoder_key,
            decoder_value,
            decoder_output.T,
            cross_key,
            cross_value,
            cross_query,
            cross_output.T,
        ],
        axis=1,
    )
    at_self, at_cross = 2 * units, 2 * units + 4 * size
    attention, ffn = sync(attention, ffn)

    attention = fetch_step(attention, -3, 3)
    pair = jnp.stack([decoder_input, decoder_cotangent]).reshape(2, dec_own, width)
    both = lax.all_gather(pair, "head", axis=1, tiled=True)
    both = jnp.pad(both, ((0, 0), (0, filled - dec_rows), (0, 0)))
    attention, first_all, ffn, both = sync(attention, first_all, ffn, both)

    attention, ffn = fetch_step(attention, -4), fetch_step(fetch_start(ffn), 1)
    first_all.append(swap(first_all[2], "head", 1))
    dec_ffn = jnp.concatenate([decoder_inner, decoder_outer.T], axis=1)
    attention, ffn, first_all, dec_ffn = sync(attention, ffn, first_all, dec_ffn)

    ffn = fetch_step(ffn, -1, 2)
    qkv, probs, context, *partial = encoder_attention(
        info, first_all, in_turn(attention)
    )
    partial, ffn = sync(partial, ffn)

    def to_core(partial):
        return swap(partial[3], "head", 1)

    def to_chip(partial, corner):
        far = (partial[2] + corner.astype(f32)).astype(bf16)
        return [swap(far, "head", 2), swap(partial[1], "head", 1)]

    ffn = fetch_step(ffn, -2, 3)
    partial, corner = sync(partial, to_core(partial))
    partial, arrived, ffn = sync(partial, to_chip(partial, corner), ffn)

    def enter_ffn(x, a, b, c, g):
        hidden = x + a + b + c
        return hidden, norm_rows(hidden, g[1:2])

    hidden, second = by_rows(
        enter_ffn, info, [inputs, partial[0], *arrived], [encoder_gains], [f32, bf16]
    )
    ffn = fetch_step(ffn, -3, 4)
    def spread(rows):
        return [rows, swap(rows, "head", 1), swap(rows, "head", 2)]

    def riders(all_rows, far=True):
        return [Rider(rows, blocks, far) for rows in all_rows[1:]]

    second, dec_ffn = sync(second, dec_ffn)
    second_all = spread(second)
    second_all, ffn, dec_ffn = sync(second_all, ffn, dec_ffn)
    dec_ffn = fetch_step(fetch_start(dec_ffn), -1, 1)
    second_all.append(swap(second_all[2], "head", 1))
    second_all, ffn = sync(second_all, ffn)
    ffn = in_turn(ffn)

    active, slope, *partial = encoder_ffn(info, second_all, ffn, units)
    partial, dec_ffn = sync(partial, dec_ffn)
    partial, corner, both, dec_ffn = sync(partial, to_core(partial), both, dec_ffn)
    dec_in, cotangent = both[0], both[1]

    index = np.arange(filled)
    question = (index % dec_own) // dec_part
    position = index // dec_own * dec_part + index % dec_part
    order = np.where(index < dec_rows, question * 1000 + position, -1).astype(np.int32)
    order = (jnp.asarray(order[:, None]), jnp.asarray(order[None, :]))
    question = jnp.asarray(question[:, None].astype(np.int32))

    arrived = to_chip(partial, corner)
    dec_ffn = fetch_step(dec_ffn, -2, 2)
    third, dec_qkv, dec_probs, dec_context, mine, sent, w_self = decoder_self(
        info, dec_in, decoder_gains, ffn, at_self, size, order
    )
    partial, arrived, mine, sent, dec_ffn = sync(partial, arrived, mine, sent, dec_ffn)
    (states_sent,) = by_rows(
        lambda h, a, b, c: (h + a + b + c,),
        info,
        [hidden, partial[0], *arrived],
        [],
        [bf16],
        riders=sent,
        kept=False,
    )
    states_sent, dec_ffn = sync(states_sent, dec_ffn)
    states = states_sent[:blocks]
    states_all = spread(states_sent)
    dec_ffn = fetch_step(dec_ffn, -3, 3)
    w_cross, w_cross_query, w_cross_output = gathered(
        info, ffn, (2 * size, size, size), at_cross
    )
    states_all, dec_ffn, w_cross, states = sync(states_all, dec_ffn, w_cross, states)
    dec_ffn = fetch_step(dec_ffn, -4)
    states_all = sync(*states_all, swap(states_all[2], "head", 1))

    key_vals, after_self, fourth, queries, stats = cross_forward(
        info,
        states_all,
        (w_cross, w_cross_query),
        (dec_in, [mine, *riders(states_all, False)], decoder_gains),
        question,
        count_q,
        count_pass,
    )
    bits = [1 << k for k in range((blk_count - 1).bit_length())]
    last_two = (bits[-2], bits[-1], bits[-2] + bits[-1])
    for k in bits[:-2]:
        stats = merge(info, stats, swap(stats, "blk", k), k)
    stats, dec_ffn = sync(stats, dec_ffn)
    stats_all = [stats, *(swap(stats, "blk", k) for k in last_two)]
    w_dec_inner, w_dec_outer, outer_back = decoder_back(info, cotangent, in_turn(dec_ffn))
    stats_all, outer_back = sync(stats_all, outer_back)
    out, log_total, cross_context, mine, sent = cross_out(
        info, stats_all, bits[-2:], w_cross_output
    )
    after_cross, fifth, dec_active, dec_dinner, mine, sent = decoder_ffn(
        info, after_self, [mine, *share(sent)], outer_back, decoder_gains, w_dec_inner
    )
    dkey_vals, *rest = cross_back(
        info,
        key_vals,
        (
            cotangent,
            after_cross,
            [mine, *share(sent)],
            decoder_gains,
            w_cross_output,
            out,
            log_total,
            queries,
            w_cross,
        ),
        question,
        count_pass,
        slot,
        part,
    )
    partial, (dcross, dcross_low, gain_four, dqueries) = rest[:4], rest[4:]

    def some(value, which):
        for k in which:
            value = value + swap(value, "blk", k)
        return value

    partial, dqueries, dkey_vals = sync(partial, dqueries, dkey_vals)
    partial, corner, dkey_vals, dqueries = sync(partial, to_core(partial), dkey_vals, dqueries)
    arrived = to_chip(partial, corner)
    dqueries = some(dqueries, bits[:-1])
    cross_sum = weight_grads(info, [(states_all, dkey_vals)], cut=False)[0]
    _, out_mine, out_sent = rows_back(info, [dec_active], w_dec_outer)
    partial, arrived, cross_sum, dqueries, out_sent = sync(
        partial, arrived, cross_sum, dqueries, out_sent
    )

    def enter_back(cot, a, b, c):
        grad = cot + a + b + c
        return grad, grad

    dstates, dstates_low = by_rows(
        enter_back,
        info,
        [encoder_cotangent.reshape(blocks, part, width), partial[0], *arrived],
        [],
        [f32, bf16],
        riders=out_sent,
        kept=False,
    )
    dstates_low, cross_sum, dqueries = sync(dstates_low, cross_sum, dqueries)
    dstates_all = spread(dstates_low)
    terms = [dqueries, swap(dqueries, "blk", bits[-1])]
    dqueries, mine, sent = rows_back(info, terms, w_cross_query)
    w_ffn = gathered(info, ffn, (units, units))
    dstates_all, sent, w_ffn = sync(dstates_all, sent, w_ffn)
    terms = [mine, *share(sent)]
    dstates_all = sync(*dstates_all, swap(dstates_all[2], "head", 1))
    out_terms = [out_mine, *riders(dstates_all)]
    dinner, *partial = encoder_ffn_back(info, dstates_all, slope, w_ffn)
    partial, dinner, terms = sync(partial, dinner, terms)
    partial, corner, dinner, dstates_all = sync(partial, to_core(partial), dinner, dstates_all)
    arrived = to_chip(partial, corner)
    dself, dself_low, gain_three, dself_qkv, own_back, sent_back = decoder_self_back(
        info,
        dcross,
        after_self,
        terms,
        decoder_gains,
        w_self,
        dec_qkv,
        dec_probs,
    )
    ffn_sums = weight_grads(
        info, [(second_all, dinner), (dstates_all, active)], [cross_sum]
    )
    partial, arrived, ffn_sums, sent_back = sync(partial, arrived, ffn_sums, sent_back)

    def middle_back(dy, h, a, b, c, g):
        back, gain_rows = norm_back(h, g[1:2], a + b + c)
        grad = dy + back
        return grad, grad, gain_rows

    dhidden, dhidden_low, gain_one = by_rows(
        middle_back,
        info,
        [dstates, hidden, partial[0], *arrived],
        [encoder_gains],
        [f32, bf16],
        gain=True,
        riders=sent_back,
        kept=False,
    )
    dhidden_low, ffn_sums = sync(dhidden_low, ffn_sums)
    dhidden_all = spread(dhidden_low)
    ffn_moving = reduce_step(info, (ffn_sums, None, 1))[0]
    w_attention = gathered(info, in_turn(attention), (3 * size, size))
    dhidden_all, ffn_moving, w_attention = sync(dhidden_all, ffn_moving, w_attention)
    ffn_moving = reduce_step(info, (ffn_sums, ffn_moving, 2))[0]
    dhidden_all = sync(*dhidden_all, swap(dhidden_all[2], "head", 1))
    terms = [own_back, *riders(dhidden_all)]

    partial, sums, gain_zero = encoder_attention_back(
        info, dhidden_all, first_all, qkv, probs, context, w_attention, encoder_gains
    )
    partial, sums, ffn_moving, gain_zero = sync(partial, sums, ffn_moving, gain_zero)
    ffn_moving, moving = reduce_step(info, (ffn_sums, ffn_moving, 3), (sums, None, 1))[:2]
    corner = to_core(partial)
    dec_grad, dec_states, gains = decoder_ends(
        info,
        dec_in,
        dself,
        terms,
        decoder_gains,
        after_cross,
        out_terms,
        [gain_three, gain_four],
        [gain_zero, gain_one],
        dec_own,
    )
    for k in (1, 2):
        gains = gains + swap(gains, "head", k)
    (
        grad_dec_query,
        grad_dec_key,
        grad_dec_value,
        grad_cross_query,
        grad_dec_inner,
        grad_dec_outer,
        grad_dec_output,
        grad_cross_output,
    ) = decoder_weight_grads(
        info,
        own,
        [
            (third, dself_qkv, 3),
            (fourth, dqueries, 1),
            (fifth, dec_dinner, 1),
            (cotangent, dec_active, 1),
        ],
        [(dec_context, dself_low), (cross_context, dcross_low)],
    )
    partial, corner, moving, gains, ffn_moving, grad_dec_query = sync(
        partial, corner, moving, gains, ffn_moving, grad_dec_query
    )

    def dec_shape(values):
        return values.reshape(count_q, dec_part, width)

    ffn_moving, moving = reduce_step(info, (ffn_sums, ffn_moving, 4), (sums, moving, 2))[:2]
    arrived = to_chip(partial, corner)
    gains = some(gains, bits[:1])
    partial, arrived, moving, gains, ffn_moving = sync(
        partial, arrived, moving, gains, ffn_moving
    )

    def last_back(dh, x, a, b, c, g):
        return (dh + norm_back(x, g[0:1], a + b + c)[0],)

    moving = reduce_step(info, (sums, moving, 3))[0]
    gains = some(gains, bits[1:-1])
    input_grad = by_rows(
        last_back,
        info,
        [dhidden, inputs, partial[0], *arrived],
        [encoder_gains],
        [f32],
    )[0]
    moving, gains, input_grad, ffn_moving = sync(moving, gains, input_grad, ffn_moving)
    moving, (gains, ffn_moving) = reduce_step(info, (sums, moving, 4), hold=(gains, ffn_moving))
    last = swap(gains, "blk", bits[-1])
    grad_inner, grad_outer, grad_cross_key, grad_cross_value = finish(
        info,
        reduce_terms(ffn_sums, ffn_moving),
        (units, units, size, size),
        (False,) * 4,
    )
    enc_gain_grads, dec_gain_grads = gains[:2] + last[:2], gains[2:] + last[2:]
    grad_query, grad_key, grad_value, grad_output = finish(
        info, reduce_terms(sums, moving), (size,) * 4, (False, False, False, True)
    )

    return (
        states.reshape(encoder_input.shape),
        dec_shape(dec_states),
        input_grad.reshape(encoder_input.shape),
        dec_shape(dec_grad),
        grad_query,
        grad_key,
        grad_value,
        grad_output,
        grad_inner,
        grad_outer.T,
        grad_dec_query,
        grad_dec_key,
        grad_dec_value,
        grad_dec_output,
        grad_cross_query,
        grad_cross_key,
        grad_cross_value,
        grad_cross_output,
        grad_dec_inner,
        grad_dec_outer.T,
        enc_gain_grads,
        dec_gain_grads,
    )


def solution(mesh):
    placed = (
        P(None, "blk", "head", None),
        P(None, "blk"),
        P(None, "head", None),
        P("blk", "head"),
        P("blk", "head"),
        P("blk", "head"),
        P("head", "blk"),
        P("blk", "head"),
        P("head", "blk"),
        P("blk", "head"),
        P("blk", "head"),
        P("blk", "head"),
        P("head", "blk"),
        P("blk", "head"),
        P("blk", "head"),
        P("blk", "head"),
        P("head", "blk"),
        P("blk", "head"),
        P("head", "blk"),
        P(),
        P(),
        P(None, "blk", "head", None),
        P(None, "head", None),
    )
    return jax.shard_map(
        shards,
        mesh=mesh,
        in_specs=placed,
        out_specs=(placed[0], placed[2], placed[0], placed[2], *placed[3:19], P(), P()),
        check_vma=False,
    )
```

```python
import math

import jax
import jax.numpy as jnp
import numpy as np
from jax import lax
from jax.experimental import pallas as pl
from jax.experimental.pallas import tpu as pltpu
from jax.sharding import PartitionSpec as P

HDIM = 64
SCALE = HDIM ** (-0.5)
LANES = 128
EPS = 1e-06
VMEM_LIMIT = 24 * 1024 * 1024
LARGE = 1 << 21
masked_score = -1000000000.0
f32 = jnp.float32
bf16 = jnp.bfloat16

PLACES, HEAD, BLK, LENGTHS = 0, 8, 9, 10


def swap(value, axis, bits):
    size = lax.axis_size(axis)
    return lax.ppermute(value, axis, [(i, i ^ bits) for i in range(size)])


def sync(*values):
    return lax.optimization_barrier(values)


def share(value):
    return [swap(value, "head", k) for k in (1, 2, 3)]


def ring_order(count):
    return [*range(0, count, 2), *range(count - 1, 0, -2)]


OFFSETS = (0, -1, 1, -2, 2, -3, 3, -4)


def ring_steps(count):
    order = ring_order(count)
    forth = [(order[i], order[(i + 1) % count]) for i in range(count)]
    return forth, [(b, a) for a, b in forth]


def place_table(count):
    order = ring_order(count)
    at = {b: i for i, b in enumerate(order)}
    return np.array(
        [[order[(at[b] + o) % count] for o in OFFSETS] for b in range(count)], np.int32
    )


def gather_rows(own):
    return lax.all_gather(own, "blk", axis=0, tiled=True)


def fetch_start(own):
    if lax.axis_size("blk") == 8:
        return {0: own}
    return dict(zip(OFFSETS, jnp.split(gather_rows(own), 8, axis=0), strict=True))


def fetch_step(pieces, *offsets):
    count = lax.axis_size("blk")
    if count != 8:
        return pieces
    forth, back = ring_steps(count)
    more = {
        k: lax.ppermute(pieces[k + 1 if k < 0 else k - 1], "blk", forth if k < 0 else back)
        for k in offsets
    }
    return {**pieces, **more}


def in_turn(pieces):
    return [pieces[k] if k in pieces else pieces[-k] for k in OFFSETS]


@jax.tree_util.register_pytree_node_class
class Part:
    def __init__(self, array, start, width):
        self.array, self.start, self.width = array, start, width

    def tree_flatten(self):
        return (self.array,), (self.start, self.width)

    @classmethod
    def tree_unflatten(cls, places, arrays):
        return cls(*arrays, *places)

    def read(self, ref):
        return ref[:, self.start : self.start + self.width]


def part(value):
    return value if isinstance(value, Part) else Part(value, 0, value.shape[1])


def reduce_step(info, *rings, hold=None):
    count = lax.axis_size("blk")
    if count != 8:
        return [[] for _ in rings] + [hold]
    forth, back = ring_steps(count)
    plan = [[], []]
    for pieces, moving, step in rings:
        by = dict(zip(OFFSETS, pieces, strict=True))
        plan[0].append([*([] if step == 1 else [moving[0]]), by[(-4, 3, 2, 1)[step - 1]]])
        if step < 4:
            plan[1].append([*([] if step == 1 else [moving[1]]), by[(-3, -2, -1)[step - 1]]])
    plan = [p for p in plan if p]
    if len(rings) == 1 and rings[0][2] == 1:
        sent = [p[0][0] for p in plan]
    else:
        parts = [part(v) for p in plan for terms in p for v in terms]

        def body(info, _, ins, __, outs, ___):
            found = iter(zip(parts, ins, strict=True))
            for out, p in zip(outs, plan, strict=True):
                column = 0
                for terms in p:
                    values = [piece.read(ref) for piece, ref in (next(found) for _ in terms)]
                    total = values[0]
                    if len(values) == 2:
                        total = (total.astype(f32) + values[1].astype(f32)).astype(bf16)
                    out[:, column : column + total.shape[1]] = total
                    column += total.shape[1]

        rows = rings[0][0][0].shape[0]
        wide = [sum(part(terms[0]).width for terms in p) for p in plan]
        shapes = [like((rows, w), bf16) for w in wide]
        came_in = {id(m.array) for _, moving, _ in rings for m in moving or ()}
        given = [Close(p.array) if id(p.array) in came_in else p.array for p in parts]
        sent = call(body, info, [], given, [], [Near(v) for v in shapes], least=0)
    if hold is not None:
        sent, hold = sync(sent, hold)
    came = [lax.ppermute(v, "blk", way) for v, way in zip(sent, (forth, back), strict=False)]
    results, column = [], 0
    for k, (pieces, moving, step) in enumerate(rings):
        wide = pieces[0].shape[1]
        found = [Part(came[0], column, wide)]
        if step == 4:
            found.append(moving[1])
        else:
            before = sum(r[0][0].shape[1] for r in rings[:k] if r[2] < 4)
            found.append(Part(came[1], before, wide))
        results.append(found)
        column += wide
    return [*results, hold]


def reduce_terms(pieces, moving):
    if lax.axis_size("blk") != 8:
        everything = jnp.concatenate([p.astype(f32) for p in pieces], axis=0)
        return [lax.psum_scatter(everything, "blk", scatter_dimension=0, tiled=True)]
    return [pieces[0], *moving]


def dot(left, right, over=(1, 0)):
    return lax.dot_general(
        left, right, (((over[0],), (over[1],)), ((), ())), preferred_element_type=f32
    )


def dot_t(left, right):
    return dot(left, right, (1, 1))


def t_dot(left, right):
    return dot(left, right, (0, 0))


def norm_rows(values, gain):
    return values * lax.rsqrt(jnp.mean(values * values, axis=-1, keepdims=True) + EPS) * gain


def norm_back(values, gain, grad):
    inverse = lax.rsqrt(jnp.mean(values * values, axis=-1, keepdims=True) + EPS)
    unit = values * inverse
    weighted = grad * gain
    along = jnp.mean(weighted * unit, axis=-1, keepdims=True)
    return inverse * (weighted - unit * along), grad * unit


def gelu_both(values):
    root = math.sqrt(2.0 / math.pi)
    square = values * values
    bent = jnp.tanh(root * values * (1.0 + 0.044715 * square))
    half = 0.5 * (1.0 + bent)
    slope = half + 0.5 * values * (1.0 - bent * bent) * root * (1.0 + 3 * 0.044715 * square)
    return values * half, slope


def heads_in(width):
    return [slice(at, at + HDIM) for at in range(0, width, HDIM)]


def head_parts(values, count):
    size = values.shape[1] // count
    return [[values[:, j * size :][:, at] for at in heads_in(size)] for j in range(count)]


def by_passage(found, count):
    rows = [
        jnp.concatenate(found[at : at + count], axis=1) for at in range(0, len(found), count)
    ]
    return jnp.concatenate(rows, axis=0)


def assemble(info, pieces, targets, signals, column_from=0):
    rows = pieces[0].shape[0]
    copies = []
    for t, piece in enumerate(pieces):
        at = pl.ds(pl.multiple_of(info[PLACES + t] * rows, 16), rows)
        column = column_from
        for k, target in enumerate(targets):
            wide = target.shape[1]
            copies.append(
                pltpu.make_async_copy(
                    piece.at[:, column : column + wide], target.at[at, :], signals.at[k, t]
                )
            )
            column += wide
    for copy in copies:
        copy.start()
    for copy in copies:
        copy.wait()


def hand_out(info, sources, pieces):
    rows = pieces[0].shape[0]
    for t, piece in enumerate(pieces):
        at = pl.ds(pl.multiple_of(info[PLACES + t] * rows, 16), rows)
        column = 0
        for source in sources:
            piece[:, column : column + source.shape[1]] = source[at, :].astype(piece.dtype)
            column += source.shape[1]


def token_rows(refs):
    return jnp.concatenate([r[k] for k in range(refs[0].shape[0]) for r in refs], axis=0)


def emit(partial, outs):
    each, part, _ = outs[0].shape
    for k in range(each):
        for r, out in enumerate(outs):
            at = (k * len(outs) + r) * part
            out[k] = partial[at : at + part].astype(out.dtype)


def slots_used(info, b, part, slot):
    column = lax.broadcasted_iota(jnp.int32, (1, slot), 1)
    position = (lax.div(column, part) ^ info[HEAD]) * part + lax.rem(column, part)
    return position < info[LENGTHS + b]


def keys_used(info, question, passages, part, slot, count_pass):
    return jnp.concatenate(
        [
            slots_used(info, k, part, slot) & (question[...] == k // count_pass)
            for k in passages
        ],
        axis=1,
    )


def call(
    body, info, stepped, fixed, out_stepped, out_fixed, scratch=(), flops=0, steps=1, near=False, least=LARGE, each=1
):
    def by_step(shape):
        last = shape[0] // each - 1
        return pl.BlockSpec((each, *shape[1:]), lambda b: (jnp.minimum(b, last),) + (0,) * (len(shape) - 1))

    def whole(a):
        if type(a) is Far:
            return pl.BlockSpec(memory_space=pltpu.HBM)
        if isinstance(a, Rider):
            return pl.BlockSpec(a.shape, lambda b: (a.index, 0, 0))
        index = (0, a.index) if type(a) is Columns else (0,) * len(a.shape)
        return pl.BlockSpec(a.shape, lambda b: index)

    counts = [len(stepped), len(fixed), len(out_stepped), len(out_fixed), len(scratch)]
    stops = np.cumsum(counts)

    def split(info_ref, *refs):
        body(info_ref, *(refs[e - c : e] for c, e in zip(counts, stops, strict=True)))

    def large(a):
        return not near and math.prod(a.shape) * a.dtype.itemsize >= least

    def given(a):
        array = a.array if isinstance(a, (Columns, Far, Rider)) else a
        far = (large(a) and not isinstance(a, Close)) or (isinstance(a, Rider) and a.far)
        return pltpu.with_memory_space_constraint(array, pltpu.HBM) if far else array

    def made(a):
        if isinstance(a, Later) or (large(a) and not isinstance(a, Near)):
            return pltpu.HBM(a.shape, a.dtype)
        return a.array if isinstance(a, Near) else a

    arrays = [*stepped, *fixed, *out_stepped, *out_fixed]
    moved = sum(math.prod(a.shape) * a.dtype.itemsize for a in arrays)
    return pl.pallas_call(
        split,
        grid=(steps,),
        in_specs=[
            pl.BlockSpec(memory_space=pltpu.SMEM),
            *(by_step(a.shape) for a in stepped),
            *(whole(a) for a in fixed),
        ],
        out_specs=[
            *(by_step(a.shape) for a in out_stepped),
            *(whole(a) for a in out_fixed),
        ],
        out_shape=[made(a) for a in (*out_stepped, *out_fixed)],
        scratch_shapes=list(scratch),
        compiler_params=pltpu.CompilerParams(
            dimension_semantics=("arbitrary",), vmem_limit_bytes=VMEM_LIMIT
        ),
        cost_estimate=pl.CostEstimate(
            flops=int(flops), bytes_accessed=int(moved), transcendentals=0
        ),
    )(info, *(given(a) for a in (*stepped, *fixed)))


class Columns:
    def __init__(self, array, width, index):
        self.array, self.index, self.dtype = array, index, array.dtype
        self.shape = (array.shape[0], width)


class Near(Columns):
    def __init__(self, array):
        self.array, self.shape, self.dtype = array, array.shape, array.dtype


class Later(Near):
    pass


class Rider:
    def __init__(self, array, index, far):
        self.array, self.index, self.dtype, self.far = array, index, array.dtype, far
        self.shape = (1, *array.shape[1:])


class Far:
    def __init__(self, array):
        self.array, self.shape, self.dtype = array, array.shape, array.dtype


class Close(Far):
    pass


def like(shape, dtype):
    return jax.ShapeDtypeStruct(tuple(shape), dtype)


def by_rows(fn, info, stepped, fixed, dtypes, gain=False, riders=None, kept=True):
    steps, _, width = stepped[0].shape
    count = 0 if riders is None else 1
    alone = [like(stepped[0].shape, d) for d in dtypes]
    outs = alone if riders is None or kept else alone[:-1]
    more = 0 if riders is None else riders.shape[0]
    together = [like((steps + count, *stepped[0].shape[1:]), dtypes[-1])] if more else []

    def body(info_ref, ins, whole, outs, sums, _):
        b = pl.program_id(0)
        if more:
            whole, rows = whole[:-1], whole[-1]

        @pl.when(b < steps)
        def _():
            results = fn(*(r[0].astype(f32) for r in ins), *(r[...] for r in whole))
            for out, value in zip(outs, results, strict=False):
                out[0] = value.astype(out.dtype)
            if more:
                outs[-1][0] = results[len(dtypes) - 1].astype(outs[-1].dtype)
            for total in sums:
                found = jnp.sum(results[-1], axis=0, keepdims=True)

                @pl.when(b == 0)
                def _():
                    total[...] = found

                @pl.when(b > 0)
                def _():
                    total[...] += found

        if more:

            @pl.when(b == steps)
            def _():
                outs[-1][0, :more, :] = rows[...]

    return call(
        body,
        info,
        stepped,
        [*fixed, riders] if more else fixed,
        [*outs, *together],
        [like((1, width), f32)] * gain,
        flops=10 * math.prod(stepped[0].shape),
        steps=steps + count,
        near=True,
    )


def partial_rows(blocks, part, width):
    return [Near(like((blocks, part, width), d)) for d in (f32, bf16, f32, bf16)]


def piece_shapes(rows, columns):
    return [Later(like((rows, columns), d)) for d in (f32, *[bf16] * 7)]


def gathered(info, pieces, widths, column_from=0):
    rows, wide = pieces[0].shape[0] * len(pieces), sum(widths)

    def body(info, _, ins, __, outs, scratch):
        together, signals = scratch
        assemble(info, ins, (together,), signals, column_from)
        column = 0
        for out in outs:
            out[...] = together[:, column : column + out.shape[1]]
            column += out.shape[1]

    return call(
        body,
        info,
        [],
        [Far(p) for p in pieces],
        [],
        [Near(like((rows, w), bf16)) for w in widths],
        [pltpu.VMEM((rows, wide), bf16), pltpu.SemaphoreType.DMA((1, len(pieces)))],
    )


def attention_scratch(width, size, pieces):
    return [
        *(pltpu.VMEM((width, k * size), bf16) for k in (3, 1, 4)),
        pltpu.SemaphoreType.DMA((1, len(pieces))),
    ]


def encoder_attention(info, normed, pieces):
    blocks, part, width = normed[0].shape
    slot = part * len(normed)
    size = pieces[0].shape[1] // 4
    count = size // HDIM
    each = 2

    def body(info, rows, pieces, outs, _, scratch):
        qkv, probs, context = outs[:3]
        w_in, w_out, together, signals = scratch
        b = pl.program_id(0)

        @pl.when(b == 0)
        def _():
            assemble(info, pieces, (together,), signals)
            w_in[...] = together[:, : 3 * size]
            w_out[...] = together[:, 3 * size :]

        made = dot(token_rows(rows), w_in[...]).astype(bf16)
        qkv[...] = made.reshape(qkv.shape)
        parts = [head_parts(made[p * slot : (p + 1) * slot], 3) for p in range(each)]
        pairs = [(p, k) for p in range(each) for k in range(count)]
        scores = [dot_t(parts[p][0][k] * SCALE, parts[p][1][k]) for p, k in pairs]
        allowed = [slots_used(info, b * each + p, part, slot) for p in range(each)]
        found = []
        for (p, k), score in zip(pairs, scores, strict=True):
            score = jnp.where(allowed[p], score, masked_score)
            spread_out = jnp.exp(score - jnp.max(score, axis=-1, keepdims=True))
            inverse = 1.0 / jnp.sum(spread_out, axis=-1, keepdims=True)
            found.append((spread_out * inverse).astype(bf16))
            probs[p, k] = found[-1]
        found = [dot(w, parts[p][2][k]) for (p, k), w in zip(pairs, found, strict=True)]
        joined = by_passage(found, count).astype(bf16)
        context[...] = joined.reshape(context.shape)
        emit(dot_t(joined, w_out[...]), outs[3:])

    return call(
        body,
        info,
        normed,
        [Far(p) for p in pieces],
        [
            like((blocks, slot, 3 * size), bf16),
            like((blocks, count, slot, slot), bf16),
            like((blocks, slot, size), bf16),
            *partial_rows(blocks, part, width),
        ],
        [],
        attention_scratch(width, size, pieces),
        flops=2 * blocks * slot * (width * size * 4 + 8 * slot * size),
        steps=blocks // each,
        each=each,
    )


def encoder_attention_back(info, grads, normed, qkv, probs, context, weights, gains):
    blocks, part, width = normed[0].shape
    slot = part * len(normed)
    size = context.shape[2]
    each = 2

    def body(info, stepped, fixed, outs, ends, scratch):
        grad_refs, normed_refs = stepped[:4], stepped[4:8]
        qkv, probs, context = stepped[8:]
        w_in, w_out, gains = fixed
        pieces, gain_out = ends[:-1], ends[-1]
        total_in, total_out = scratch
        b = pl.program_id(0)

        @pl.when(b == 0)
        def _():
            total_in[...] = jnp.zeros_like(total_in)
            total_out[...] = jnp.zeros_like(total_out)
            gain_out[...] = jnp.zeros_like(gain_out)

        grad = token_rows(grad_refs)
        rows = token_rows(normed_refs)
        dcontext = dot(grad, w_out[...]).astype(bf16)
        parts = [head_parts(qkv[p], 3) for p in range(each)]
        cuts = [c for p in range(each) for c in head_parts(dcontext[p * slot : (p + 1) * slot], 1)[0]]
        pairs = [(p, k) for p in range(each) for k in range(size // HDIM)]
        backs = [dot_t(c, parts[p][2][k]) for (p, k), c in zip(pairs, cuts, strict=True)]
        dvals = [t_dot(probs[p, k], c) for (p, k), c in zip(pairs, cuts, strict=True)]
        lows = []
        for (p, k), back in zip(pairs, backs, strict=True):
            wide = probs[p, k].astype(f32)
            low = wide * (back - jnp.sum(wide * back, axis=-1, keepdims=True))
            lows.append(low.astype(bf16))
        dquery = [dot(d, parts[p][1][k]) * SCALE for (p, k), d in zip(pairs, lows, strict=True)]
        dkeys = [t_dot(d, parts[p][0][k]) * SCALE for (p, k), d in zip(pairs, lows, strict=True)]
        count = size // HDIM
        moved = jnp.concatenate(
            [by_passage(found, count) for found in (dquery, dkeys, dvals)], axis=1
        ).astype(bf16)
        partial = dot_t(moved, w_in[...])
        emit(partial, outs)
        gain_out[...] += jnp.sum(partial * rows.astype(f32), axis=0, keepdims=True) / gains[0:1, :]
        total_in[...] += t_dot(rows, moved)
        total_out[...] += t_dot(grad, context[...].reshape(grad.shape[0], size))

        @pl.when(b == blocks // each - 1)
        def _():
            hand_out(info, (total_in, total_out), pieces)

    results = call(
        body,
        info,
        [*grads, *normed, qkv, probs, context],
        [*(Close(w) for w in weights), gains],
        partial_rows(blocks, part, width),
        [*piece_shapes(width // 8, 4 * size), like((1, width), f32)],
        [
            pltpu.VMEM((width, 3 * size), f32),
            pltpu.VMEM((width, size), f32),
        ],
        flops=2 * blocks * slot * (width * size * 8 + 20 * slot * size),
        steps=blocks // each,
        each=each,
    )
    return results[:4], results[4:12], results[12]


def ffn_scratch(width, hidden, pieces):
    return [
        *[pltpu.VMEM((width, hidden), bf16)] * 2,
        pltpu.SemaphoreType.DMA((2, len(pieces))),
    ]


def encoder_ffn(info, normed, pieces, hidden):
    blocks, part, width = normed[0].shape
    slot = part * len(normed)

    def body(info, rows, pieces, outs, _, scratch):
        active, slope = outs[:2]
        w_inner, w_outer, signals = scratch

        @pl.when(pl.program_id(0) == 0)
        def _():
            assemble(info, pieces, (w_inner, w_outer), signals)

        value, bend = gelu_both(dot(token_rows(rows), w_inner[...]))
        low = value.astype(bf16)
        active[...] = low.reshape(active.shape)
        slope[...] = bend.astype(bf16).reshape(slope.shape)
        emit(dot_t(low, w_outer[...]), outs[2:])

    return call(
        body,
        info,
        normed,
        [Far(p) for p in pieces],
        [*[like((blocks, slot, hidden), bf16)] * 2, *partial_rows(blocks, part, width)],
        [],
        ffn_scratch(width, hidden, pieces),
        flops=4 * blocks * slot * width * hidden,
        steps=blocks // 2,
        each=2,
    )


def encoder_ffn_back(info, grads, slope, weights):
    blocks, (_, part, width) = slope.shape[0], grads[0].shape
    slot = part * len(grads)
    hidden = slope.shape[2]

    def body(info, stepped, weights, outs, ends, scratch):
        dinner = outs[0]
        w_inner, w_outer = weights
        back = dot(token_rows(stepped[:4]), w_outer[...])
        low = (back * stepped[4][...].reshape(back.shape).astype(f32)).astype(bf16)
        dinner[...] = low.reshape(dinner.shape)
        emit(dot_t(low, w_inner[...]), outs[1:])

    return call(
        body,
        info,
        [*grads, slope],
        [Close(w) for w in weights],
        [like((blocks, slot, hidden), bf16), *partial_rows(blocks, part, width)],
        [],
        flops=4 * blocks * slot * width * hidden,
        steps=blocks // 2,
        each=2,
    )


def weight_grads(info, pairs, more=(), cut=True):
    blocks, (_, part, width) = pairs[0][1].shape[0], pairs[0][0][0].shape
    widths = [right.shape[2] for _, right in pairs]

    def body(info, stepped, more, __, ends, totals):
        totals = totals if cut else ends
        for k, total in enumerate(totals):
            left, right = token_rows(stepped[5 * k : 5 * k + 4]), stepped[5 * k + 4]
            total[...] = t_dot(left, right[...].reshape(left.shape[0], total.shape[1]))
        if cut:
            hand_out(info, (*totals, *more), ends)

    return call(
        body,
        info,
        [a for left, right in pairs for a in (*left, right)],
        more,
        [],
        piece_shapes(width // 8, sum(widths) + sum(m.shape[1] for m in more))
        if cut
        else [like((width, w), f32) for w in widths],
        [pltpu.VMEM((width, w), f32) for w in widths] if cut else [],
        flops=2 * blocks * part * 4 * width * sum(widths),
        each=blocks,
    )


def finish(info, terms, widths, turned):
    terms = [part(t) for t in terms]
    rows = terms[0].array.shape[0]
    shapes = [(w, rows) if t else (rows, w) for w, t in zip(widths, turned, strict=True)]

    def body(info, _, ins, __, outs, ___):
        total = terms[0].read(ins[0])
        for term, ref in zip(terms[1:], ins[1:], strict=True):
            total = total + term.read(ref).astype(f32)
        column = 0
        for out, wide, turn in zip(outs, widths, turned, strict=True):
            found = total[:, column : column + wide]
            out[...] = found.T if turn else found
            column += wide

    return call(body, info, [], [t.array for t in terms], [], [like(s, f32) for s in shapes])


def cross_forward(info, states, weights, decoder, own_question, count_q, count_pass):
    rows_in, terms, gains = decoder
    blocks = count_q * count_pass
    _, part, width = states[0].shape
    slot = part * len(states)
    rows_dec = rows_in.shape[0]
    size = weights[1].shape[1]
    steps = 2

    def body(info, rows, fixed, outs, ends, scratch):
        weight, w_query, rows_in, *terms, gains, question = fixed
        after_self, normed, queries, stats = ends
        held = scratch[0]
        b = pl.program_id(0)

        @pl.when(b == 0)
        def _():
            after_self[...] = rows_in[...].astype(f32) + summed(terms)
            normed[...] = norm_rows(after_self[...], gains[1:2, :]).astype(bf16)
            queries[...] = dot(normed[...], w_query[...]).astype(bf16)

        made = dot(token_rows(rows), weight[...]).astype(bf16)
        outs[0][...] = made.reshape(outs[0].shape)
        each = made.shape[0]
        held[pl.ds(pl.multiple_of(b * each, each), each), :] = made

        @pl.when(b == steps - 1)
        def _():
            allowed = keys_used(info, question, range(blocks), part, slot, count_pass)
            lane = lax.broadcasted_iota(jnp.int32, (rows_dec, HDIM), 1)
            keys, vals = head_parts(held[...], 2)
            asking = head_parts(queries[...], 1)[0]
            scores = [dot_t(q * SCALE, t) for q, t in zip(asking, keys, strict=True)]
            for k, score in enumerate(scores):
                score = jnp.where(allowed, score, masked_score)
                top = jnp.max(score, axis=-1, keepdims=True)
                spread_out = jnp.exp(score - top)
                total = jnp.sum(spread_out, axis=-1, keepdims=True)
                at = k * LANES
                stats[:, at : at + HDIM] = dot(spread_out.astype(bf16), vals[k])
                stats[:, at + HDIM : at + LANES] = jnp.where(lane == 0, top, total)

    return call(
        body,
        info,
        states,
        [*(Close(w) for w in weights), rows_in, *terms, gains, own_question],
        [like((blocks, slot, 2 * size), bf16)],
        [
            Later(like((rows_dec, width), f32)),
            Later(like((rows_dec, width), bf16)),
            like((rows_dec, size), bf16),
            like((rows_dec, size // HDIM * LANES), f32),
        ],
        [pltpu.VMEM((blocks * slot, 2 * size), bf16)],
        flops=4 * blocks * slot * width * size,
        steps=steps,
        each=blocks // steps,
    )


def merged(first, second):
    lane = lax.broadcasted_iota(jnp.int32, (first.shape[0], HDIM), 1)
    found = []
    for at in range(0, first.shape[1], LANES):
        tops = [v[:, at + HDIM : at + HDIM + 1] for v in (first, second)]
        totals = [v[:, at + HDIM + 1 : at + HDIM + 2] for v in (first, second)]
        top = jnp.maximum(*tops)
        scales = [jnp.exp(t - top) for t in tops]
        total = totals[0] * scales[0] + totals[1] * scales[1]
        found.append(first[:, at : at + HDIM] * scales[0] + second[:, at : at + HDIM] * scales[1])
        found.append(jnp.where(lane == 0, top, total))
    return jnp.concatenate(found, axis=1)


def in_order(info, bits, own, other):
    later = (info[BLK] & bits) != 0
    return jnp.where(later, other, own), jnp.where(later, own, other)


def merge(info, own, other, bits):
    def body(info, _, ins, __, outs, ___):
        outs[0][...] = merged(*in_order(info, bits, ins[0][...], ins[1][...]))

    return call(body, info, [], [own, other], [], [like(own.shape, f32)])[0]


def cross_out(info, stats, bits, w_output):
    rows, columns = stats[0].shape
    size = columns // LANES * HDIM
    width = w_output.shape[0]

    def body(info, _, ins, __, outs, scratch):
        w_output = ins[-1]
        out, log_total, context, own, sent = outs
        values = [r[...] for r in ins[:-1]]
        near = merged(*in_order(info, bits[0], *values[:2]))
        far = merged(*in_order(info, bits[0], *values[2:]))
        stats = merged(*in_order(info, bits[1], near, far))
        log_total[...] = jnp.zeros_like(log_total)
        for k, at in enumerate(heads_in(size)):
            base = k * LANES
            top = stats[:, base + HDIM : base + HDIM + 1]
            total = stats[:, base + HDIM + 1 : base + HDIM + 2]
            out[:, at] = stats[:, base : base + HDIM] / total
            log_total[:, k : k + 1] = top + jnp.log(total)
        context[...] = out[...].astype(bf16)
        own[...] = dot_t(context[...], w_output[...])
        sent[...] = own[...].astype(bf16)

    return call(
        body,
        info,
        [],
        [*stats, w_output],
        [],
        [
            like((rows, size), f32),
            like((rows, LANES), f32),
            Later(like((rows, size), bf16)),
            like((rows, width), f32),
            like((rows, width), bf16),
        ],
        flops=2 * rows * size * width,
    )


def cross_back(info, key_vals, inputs, own_question, count_pass, slot, part):
    cotangent, after_cross, terms, gains, w_output, out, log_total, queries, weight = inputs
    blocks = key_vals.shape[0]
    rows_dec, width = after_cross.shape
    size = queries.shape[1]

    def body(info, stepped, fixed, outs, ends, scratch):
        cotangent, after_cross, own, r1, r2, r3, gains, w_output, out, log_total, queries, weight, question = fixed
        key_vals = stepped[0]
        dkey_vals = outs[0]
        dcross, dcross_low, gain_out, dqueries = ends
        total = summed((own, r1, r2, r3))
        back, gain_out[...] = norm_back(after_cross[...], gains[2:3, :], total)
        dcross[...] = cotangent[...].astype(f32) + back
        dcross_low[...] = dcross[...].astype(bf16)
        dcontext = dot(dcross_low[...], w_output[...]).astype(bf16)
        allowed = keys_used(info, question, range(blocks), part, slot, count_pass)
        keys, vals = head_parts(key_vals[...].reshape(blocks * slot, 2 * size), 2)
        asking = head_parts(queries[...], 1)[0]
        cuts = head_parts(dcontext, 1)[0]
        outs_of = head_parts(out[...], 1)[0]
        scores = [dot_t(q * SCALE, t) for q, t in zip(asking, keys, strict=True)]
        backs = [dot_t(c, v) for c, v in zip(cuts, vals, strict=True)]
        probs, lows = [], []
        for k, score in enumerate(scores):
            row_term = jnp.sum(cuts[k].astype(f32) * outs_of[k], axis=-1, keepdims=True)
            score = jnp.where(allowed, score, masked_score)
            probs.append(jnp.exp(score - log_total[:, k : k + 1]))
            lows.append((probs[k] * (backs[k] - row_term)).astype(bf16))
        dvals = [t_dot(p.astype(bf16), c) for p, c in zip(probs, cuts, strict=True)]
        dkeys = [t_dot(d, q) * SCALE for d, q in zip(lows, asking, strict=True)]
        found = [dot(d, t) * SCALE for d, t in zip(lows, keys, strict=True)]
        dqueries[...] = jnp.concatenate(found, axis=1)
        made = jnp.concatenate([*dkeys, *dvals], axis=1).astype(bf16)
        dkey_vals[...] = made.reshape(dkey_vals.shape)
        emit(dot_t(made, weight[...]), outs[1:])

    return call(
        body,
        info,
        [key_vals],
        [
            cotangent,
            after_cross,
            *terms,
            gains,
            w_output,
            out,
            log_total,
            queries,
            Close(weight),
            own_question,
        ],
        [like(key_vals.shape, bf16), *partial_rows(blocks, part, width)],
        [
            Later(like((rows_dec, width), f32)),
            Later(like((rows_dec, width), bf16)),
            Later(like((rows_dec, width), f32)),
            like((rows_dec, size), f32),
        ],
        flops=4 * blocks * slot * width * size,
        each=blocks,
    )


def summed(refs):
    count = refs[0].shape[0]

    def rows(ref):
        return ref[...] if len(ref.shape) == 2 else ref[0, :count, :]

    terms = [rows(ref).astype(f32) for ref in refs[1:]]
    total = refs[0][...]
    for term in terms:
        total = total + term
    return total


def decoder_self(info, rows, gains, pieces, column_from, size, order):
    count, width = rows.shape

    def body(info, _, ins, __, outs, scratch):
        rows, gains, order_q, order_k = ins[:4]
        normed, qkv, probs, context, own, sent, weight = outs
        assemble(info, ins[4:], (weight,), scratch[0], column_from)
        normed[...] = norm_rows(rows[...].astype(f32), gains[0:1, :]).astype(bf16)
        qkv[...] = dot(normed[...], weight[:, : 3 * size]).astype(bf16)
        query_at, key_at = order_q[...], order_k[...]
        same = lax.div(query_at, 1000) == lax.div(key_at, 1000)
        allowed = same & (key_at <= query_at) & (key_at >= 0) & (query_at >= 0)
        for k, at in enumerate(heads_in(size)):
            query, keys, vals = (qkv[:, j * size + at.start : j * size + at.stop] for j in range(3))
            scores = jnp.where(allowed, dot_t(query, keys) * SCALE, masked_score)
            spread_out = jnp.exp(scores - jnp.max(scores, axis=-1, keepdims=True))
            share_out = spread_out / jnp.sum(spread_out, axis=-1, keepdims=True)
            share_out = jnp.where(allowed, share_out, 0.0)
            probs[k] = share_out
            context[:, at] = dot(share_out.astype(bf16), vals).astype(bf16)
        own[...] = dot_t(context[...], weight[:, 3 * size :])
        sent[...] = own[...].astype(bf16)

    return call(
        body,
        info,
        [],
        [rows, gains, *order, *(Far(p) for p in pieces)],
        [],
        [
            Later(like((count, width), bf16)),
            Later(like((count, 3 * size), bf16)),
            Later(like((size // HDIM, count, count), f32)),
            Later(like((count, size), bf16)),
            like((count, width), f32),
            like((count, width), bf16),
            Later(like((width, 4 * size), bf16)),
        ],
        [pltpu.SemaphoreType.DMA((1, len(pieces)))],
        flops=2 * count * width * size * 4,
    )


def decoder_back(info, cotangent, pieces):
    count, width = cotangent.shape
    hidden = pieces[0].shape[1] // 2

    def body(info, _, ins, __, outs, scratch):
        w_inner, w_outer, back = outs
        assemble(info, ins[1:], (w_inner, w_outer), scratch[0])
        back[...] = dot(ins[0][...], w_outer[...])

    return call(
        body,
        info,
        [],
        [cotangent, *(Far(p) for p in pieces)],
        [],
        [Near(like((width, hidden), bf16)), like((width, hidden), bf16), like((count, hidden), f32)],
        [pltpu.SemaphoreType.DMA((2, len(pieces)))],
        flops=2 * count * width * hidden,
    )


def decoder_ffn(info, after_self, terms, back, gains, w_inner):
    count, width = after_self.shape
    hidden = w_inner.shape[1]

    def body(info, _, ins, __, outs, scratch):
        after_self, own, r1, r2, r3, back, gains, w_inner = ins
        after_cross, normed, active, dinner, own_back, sent_back = outs
        after_cross[...] = after_self[...] + summed((own, r1, r2, r3))
        normed[...] = norm_rows(after_cross[...], gains[2:3, :]).astype(bf16)
        value, slope = gelu_both(dot(normed[...], w_inner[...]))
        active[...] = value.astype(bf16)
        dinner[...] = (slope * back[...]).astype(bf16)
        own_back[...] = dot_t(dinner[...], w_inner[...])
        sent_back[...] = own_back[...].astype(bf16)

    return call(
        body,
        info,
        [],
        [after_self, *terms, back, gains, Close(w_inner)],
        [],
        [
            like((count, width), f32),
            Later(like((count, width), bf16)),
            Later(like((count, hidden), bf16)),
            Later(like((count, hidden), bf16)),
            like((count, width), f32),
            like((count, width), bf16),
        ],
        flops=4 * count * width * hidden,
    )


def rows_back(info, terms, weight):
    (count, size), width = terms[0].shape, weight.shape[0]

    def body(info, _, ins, __, outs, scratch):
        low, own, sent = outs
        total = ins[0][...]
        for term in ins[1:-1]:
            total = total + term[...]
        low[...] = total.astype(bf16)
        own[...] = dot_t(low[...], ins[-1][...])
        sent[...] = own[...].astype(bf16)

    return call(
        body,
        info,
        [],
        [*terms, weight],
        [],
        [
            Later(like((count, size), bf16)),
            like((count, width), f32),
            like((count, width), bf16),
        ],
        flops=2 * count * width * size,
    )


def decoder_self_back(
    info, dcross, after_self, terms, gains, weight, qkv, probs
):
    count, width = after_self.shape
    size = weight.shape[1] // 4

    def body(info, _, ins, __, outs, scratch):
        dcross, after_self, *terms, gains, weight, qkv, probs = ins
        dself, dself_low, gain_rows, moved, own_back, sent_back = outs
        back, gain_rows[...] = norm_back(after_self[...], gains[1:2, :], summed(terms))
        dself[...] = dcross[...] + back
        dself_low[...] = dself[...].astype(bf16)
        dcontext = dot(dself_low[...], weight[:, 3 * size :]).astype(bf16)
        for k, at in enumerate(heads_in(size)):
            query, keys, vals = (qkv[:, j * size + at.start : j * size + at.stop] for j in range(3))
            share_out = probs[k]
            dprobs = dot_t(dcontext[:, at], vals)
            dscores = share_out * (dprobs - jnp.sum(share_out * dprobs, axis=-1, keepdims=True))
            dscores = dscores.astype(bf16)
            found = (
                dot(dscores, keys) * SCALE,
                t_dot(dscores, query) * SCALE,
                t_dot(share_out.astype(bf16), dcontext[:, at]),
            )
            for j, term in enumerate(found):
                moved[:, j * size + at.start : j * size + at.stop] = term.astype(bf16)
        own_back[...] = dot_t(moved[...], weight[:, : 3 * size])
        sent_back[...] = own_back[...].astype(bf16)

    return call(
        body,
        info,
        [],
        [dcross, after_self, *terms, gains, weight, qkv, probs],
        [],
        [
            like((count, width), f32),
            Later(like((count, width), bf16)),
            like((count, width), f32),
            Later(like((count, 3 * size), bf16)),
            like((count, width), f32),
            like((count, width), bf16),
        ],
        flops=2 * count * width * size * 8,
    )


def own_rows(info, values, dec_own):
    found = values[:dec_own]
    for k in range(1, values.shape[0] // dec_own):
        found = jnp.where(info[HEAD] == k, values[k * dec_own : (k + 1) * dec_own], found)
    return found


def decoder_ends(
    info, rows, dself, terms, gains, after_cross, out_terms, gain_rows, gain_sums, dec_own
):
    count, width = dself.shape

    def body(info, _, ins, __, outs, scratch):
        rows, dself, after_cross, gains = ins[:4]
        three, four, zero, one = ins[-4:]
        grad, states, found = outs
        total, out_total = summed(ins[4:8]), summed(ins[8:12])
        back, two = norm_back(rows[...].astype(f32), gains[0:1, :], total)
        grad[...] = own_rows(info, dself[...] + back, dec_own)
        states[...] = own_rows(info, after_cross[...] + out_total, dec_own).astype(bf16)
        row = lax.div(lax.broadcasted_iota(jnp.int32, (count, 1), 0), dec_own)
        mine = (row == info[HEAD]) & (info[BLK] == 0)
        found[0:1, :] = zero[...]
        found[1:2, :] = one[...]
        for k, values in enumerate((two, three[...], four[...])):
            found[2 + k : 3 + k, :] = jnp.sum(jnp.where(mine, values, 0.0), axis=0, keepdims=True)

    return call(
        body,
        info,
        [],
        [rows, dself, after_cross, gains, *terms, *out_terms, *gain_rows, *gain_sums],
        [],
        [like((dec_own, width), f32), like((dec_own, width), bf16), like((5, width), f32)],
    )


def decoder_weight_grads(info, own, pairs_in, pairs_out):
    count, width = pairs_in[0][0].shape

    def body(info, _, ins, __, outs, scratch):
        row = lax.broadcasted_iota(jnp.int32, (own, width), 0) + info[BLK] * own
        column = lax.broadcasted_iota(jnp.int32, (own, width), 1)
        pick = jnp.where(row == column, 1.0, 0.0).astype(bf16)
        outs, ins = iter(outs), iter(ins)
        for _, _, arrays in pairs_in:
            left, right = next(ins)[...], next(ins)[...]
            found = t_dot(dot_t(left, pick).astype(bf16), right)
            wide = found.shape[1] // arrays
            for k in range(arrays):
                next(outs)[...] = found[:, k * wide : (k + 1) * wide]
        for _ in pairs_out:
            left, right = next(ins)[...], next(ins)[...]
            next(outs)[...] = t_dot(left, dot_t(right, pick).astype(bf16))

    outs = [like((own, r.shape[1] // n), f32) for _, r, n in pairs_in for _ in range(n)]
    outs += [like((l.shape[1], own), f32) for l, _ in pairs_out]
    flat = [a for pair in pairs_in for a in pair[:2]] + [a for pair in pairs_out for a in pair]
    return call(body, info, [], flat, [], outs, flops=2 * count * own * width * 10, least=0)


def shards(
    encoder_input,
    passage_lengths,
    decoder_input,
    encoder_query,
    encoder_key,
    encoder_value,
    encoder_output,
    encoder_inner,
    encoder_outer,
    decoder_query,
    decoder_key,
    decoder_value,
    decoder_output,
    cross_query,
    cross_key,
    cross_value,
    cross_output,
    decoder_inner,
    decoder_outer,
    encoder_gains,
    decoder_gains,
    encoder_cotangent,
    decoder_cotangent,
):
    head, blk = lax.axis_index("head"), lax.axis_index("blk")
    blk_count, head_count = lax.axis_size("blk"), lax.axis_size("head")
    count_q, count_pass, part, width = encoder_input.shape
    blocks = count_q * count_pass
    slot = part * head_count
    own = width // blk_count
    if blk_count == 8:
        places = jnp.asarray(place_table(8))[blk]
    else:
        places = jnp.arange(8, dtype=jnp.int32)
    info = jnp.concatenate(
        [places, jnp.stack([head, blk]).astype(jnp.int32), passage_lengths.reshape(blocks)]
    )

    size, units = encoder_query.shape[1], encoder_inner.shape[1]
    inputs = encoder_input.reshape(blocks, part, width)
    dec_part = decoder_input.shape[1]
    dec_own = count_q * dec_part
    dec_rows = dec_own * head_count
    filled = -(-dec_rows // 16) * 16

    attention = jnp.concatenate(
        [encoder_query, encoder_key, encoder_value, encoder_output.T], axis=1
    )
    attention, inputs = sync(attention, inputs)
    attention = fetch_step(fetch_start(attention), -1, 1)
    first = by_rows(
        lambda x, g: (norm_rows(x, g[0:1]),), info, [inputs], [encoder_gains], [bf16]
    )[0]
    attention, first = sync(attention, first)

    attention = fetch_step(attention, -2, 2)
    first_all = [first, swap(first, "head", 1), swap(first, "head", 2)]
    ffn = jnp.concatenate(
        [
            encoder_inner,
            encoder_outer.T,
            decoder_query,
            decoder_key,
            decoder_value,
            decoder_output.T,
            cross_key,
            cross_value,
            cross_query,
            cross_output.T,
        ],
        axis=1,
    )
    at_self, at_cross = 2 * units, 2 * units + 4 * size
    attention, ffn = sync(attention, ffn)

    attention = fetch_step(attention, -3, 3)
    pair = jnp.stack([decoder_input, decoder_cotangent]).reshape(2, dec_own, width)
    both = lax.all_gather(pair, "head", axis=1, tiled=True)
    both = jnp.pad(both, ((0, 0), (0, filled - dec_rows), (0, 0)))
    attention, first_all, ffn, both = sync(attention, first_all, ffn, both)

    attention, ffn = fetch_step(attention, -4), fetch_step(fetch_start(ffn), 1)
    first_all.append(swap(first_all[2], "head", 1))
    dec_ffn = jnp.concatenate([decoder_inner, decoder_outer.T], axis=1)
    attention, ffn, first_all, dec_ffn = sync(attention, ffn, first_all, dec_ffn)

    ffn = fetch_step(ffn, -1, 2)
    qkv, probs, context, *partial = encoder_attention(
        info, first_all, in_turn(attention)
    )
    partial, ffn = sync(partial, ffn)

    def to_core(partial):
        return swap(partial[3], "head", 1)

    def to_chip(partial, corner):
        far = (partial[2] + corner.astype(f32)).astype(bf16)
        return [swap(far, "head", 2), swap(partial[1], "head", 1)]

    ffn = fetch_step(ffn, -2, 3)
    partial, corner = sync(partial, to_core(partial))
    partial, arrived, ffn = sync(partial, to_chip(partial, corner), ffn)

    def enter_ffn(x, a, b, c, g):
        hidden = x + a + b + c
        return hidden, norm_rows(hidden, g[1:2])

    hidden, second = by_rows(
        enter_ffn, info, [inputs, partial[0], *arrived], [encoder_gains], [f32, bf16]
    )
    ffn = fetch_step(ffn, -3, 4)
    def spread(rows):
        return [rows, swap(rows, "head", 1), swap(rows, "head", 2)]

    def riders(all_rows, far=True):
        return [Rider(rows, blocks, far) for rows in all_rows[1:]]

    second, dec_ffn = sync(second, dec_ffn)
    second_all = spread(second)
    second_all, ffn, dec_ffn = sync(second_all, ffn, dec_ffn)
    dec_ffn = fetch_step(fetch_start(dec_ffn), -1, 1)
    second_all.append(swap(second_all[2], "head", 1))
    second_all, ffn = sync(second_all, ffn)
    ffn = in_turn(ffn)

    active, slope, *partial = encoder_ffn(info, second_all, ffn, units)
    partial, dec_ffn = sync(partial, dec_ffn)
    partial, corner, both, dec_ffn = sync(partial, to_core(partial), both, dec_ffn)
    dec_in, cotangent = both[0], both[1]

    index = np.arange(filled)
    question = (index % dec_own) // dec_part
    position = index // dec_own * dec_part + index % dec_part
    order = np.where(index < dec_rows, question * 1000 + position, -1).astype(np.int32)
    order = (jnp.asarray(order[:, None]), jnp.asarray(order[None, :]))
    question = jnp.asarray(question[:, None].astype(np.int32))

    arrived = to_chip(partial, corner)
    dec_ffn = fetch_step(dec_ffn, -2, 2)
    third, dec_qkv, dec_probs, dec_context, mine, sent, w_self = decoder_self(
        info, dec_in, decoder_gains, ffn, at_self, size, order
    )
    partial, arrived, mine, sent, dec_ffn = sync(partial, arrived, mine, sent, dec_ffn)
    (states_sent,) = by_rows(
        lambda h, a, b, c: (h + a + b + c,),
        info,
        [hidden, partial[0], *arrived],
        [],
        [bf16],
        riders=sent,
        kept=False,
    )
    states_sent, dec_ffn = sync(states_sent, dec_ffn)
    states = states_sent[:blocks]
    states_all = spread(states_sent)
    dec_ffn = fetch_step(dec_ffn, -3, 3)
    w_cross, w_cross_query, w_cross_output = gathered(
        info, ffn, (2 * size, size, size), at_cross
    )
    states_all, dec_ffn, w_cross, states = sync(states_all, dec_ffn, w_cross, states)
    dec_ffn = fetch_step(dec_ffn, -4)
    states_all = sync(*states_all, swap(states_all[2], "head", 1))

    key_vals, after_self, fourth, queries, stats = cross_forward(
        info,
        states_all,
        (w_cross, w_cross_query),
        (dec_in, [mine, *riders(states_all, False)], decoder_gains),
        question,
        count_q,
        count_pass,
    )
    bits = [1 << k for k in range((blk_count - 1).bit_length())]
    last_two = (bits[-2], bits[-1], bits[-2] + bits[-1])
    for k in bits[:-2]:
        stats = merge(info, stats, swap(stats, "blk", k), k)
    stats, dec_ffn = sync(stats, dec_ffn)
    stats_all = [stats, *(swap(stats, "blk", k) for k in last_two)]
    w_dec_inner, w_dec_outer, outer_back = decoder_back(info, cotangent, in_turn(dec_ffn))
    stats_all, outer_back = sync(stats_all, outer_back)
    out, log_total, cross_context, mine, sent = cross_out(
        info, stats_all, bits[-2:], w_cross_output
    )
    after_cross, fifth, dec_active, dec_dinner, mine, sent = decoder_ffn(
        info, after_self, [mine, *share(sent)], outer_back, decoder_gains, w_dec_inner
    )
    dkey_vals, *rest = cross_back(
        info,
        key_vals,
        (
            cotangent,
            after_cross,
            [mine, *share(sent)],
            decoder_gains,
            w_cross_output,
            out,
            log_total,
            queries,
            w_cross,
        ),
        question,
        count_pass,
        slot,
        part,
    )
    partial, (dcross, dcross_low, gain_four, dqueries) = rest[:4], rest[4:]

    def some(value, which):
        for k in which:
            value = value + swap(value, "blk", k)
        return value

    partial, dqueries, dkey_vals = sync(partial, dqueries, dkey_vals)
    partial, corner, dkey_vals, dqueries = sync(partial, to_core(partial), dkey_vals, dqueries)
    arrived = to_chip(partial, corner)
    dqueries = some(dqueries, bits[:-1])
    cross_sum = weight_grads(info, [(states_all, dkey_vals)], cut=False)[0]
    _, out_mine, out_sent = rows_back(info, [dec_active], w_dec_outer)
    partial, arrived, cross_sum, dqueries, out_sent = sync(
        partial, arrived, cross_sum, dqueries, out_sent
    )

    def enter_back(cot, a, b, c):
        grad = cot + a + b + c
        return grad, grad

    dstates, dstates_low = by_rows(
        enter_back,
        info,
        [encoder_cotangent.reshape(blocks, part, width), partial[0], *arrived],
        [],
        [f32, bf16],
        riders=out_sent,
        kept=False,
    )
    dstates_low, cross_sum, dqueries = sync(dstates_low, cross_sum, dqueries)
    dstates_all = spread(dstates_low)
    terms = [dqueries, swap(dqueries, "blk", bits[-1])]
    dqueries, mine, sent = rows_back(info, terms, w_cross_query)
    w_ffn = gathered(info, ffn, (units, units))
    dstates_all, sent, w_ffn = sync(dstates_all, sent, w_ffn)
    terms = [mine, *share(sent)]
    dstates_all = sync(*dstates_all, swap(dstates_all[2], "head", 1))
    out_terms = [out_mine, *riders(dstates_all)]
    dinner, *partial = encoder_ffn_back(info, dstates_all, slope, w_ffn)
    partial, dinner, terms = sync(partial, dinner, terms)
    partial, corner, dinner, dstates_all = sync(partial, to_core(partial), dinner, dstates_all)
    arrived = to_chip(partial, corner)
    dself, dself_low, gain_three, dself_qkv, own_back, sent_back = decoder_self_back(
        info,
        dcross,
        after_self,
        terms,
        decoder_gains,
        w_self,
        dec_qkv,
        dec_probs,
    )
    ffn_sums = weight_grads(
        info, [(second_all, dinner), (dstates_all, active)], [cross_sum]
    )
    partial, arrived, ffn_sums, sent_back = sync(partial, arrived, ffn_sums, sent_back)

    def middle_back(dy, h, a, b, c, g):
        back, gain_rows = norm_back(h, g[1:2], a + b + c)
        grad = dy + back
        return grad, grad, gain_rows

    dhidden, dhidden_low, gain_one = by_rows(
        middle_back,
        info,
        [dstates, hidden, partial[0], *arrived],
        [encoder_gains],
        [f32, bf16],
        gain=True,
        riders=sent_back,
        kept=False,
    )
    dhidden_low, ffn_sums = sync(dhidden_low, ffn_sums)
    dhidden_all = spread(dhidden_low)
    ffn_moving = reduce_step(info, (ffn_sums, None, 1))[0]
    w_attention = gathered(info, in_turn(attention), (3 * size, size))
    dhidden_all, ffn_moving, w_attention = sync(dhidden_all, ffn_moving, w_attention)
    ffn_moving = reduce_step(info, (ffn_sums, ffn_moving, 2))[0]
    dhidden_all = sync(*dhidden_all, swap(dhidden_all[2], "head", 1))
    terms = [own_back, *riders(dhidden_all)]

    partial, sums, gain_zero = encoder_attention_back(
        info, dhidden_all, first_all, qkv, probs, context, w_attention, encoder_gains
    )
    partial, sums, ffn_moving, gain_zero = sync(partial, sums, ffn_moving, gain_zero)
    ffn_moving, moving = reduce_step(info, (ffn_sums, ffn_moving, 3), (sums, None, 1))[:2]
    corner = to_core(partial)
    dec_grad, dec_states, gains = decoder_ends(
        info,
        dec_in,
        dself,
        terms,
        decoder_gains,
        after_cross,
        out_terms,
        [gain_three, gain_four],
        [gain_zero, gain_one],
        dec_own,
    )
    for k in (1, 2):
        gains = gains + swap(gains, "head", k)
    (
        grad_dec_query,
        grad_dec_key,
        grad_dec_value,
        grad_cross_query,
        grad_dec_inner,
        grad_dec_outer,
        grad_dec_output,
        grad_cross_output,
    ) = decoder_weight_grads(
        info,
        own,
        [
            (third, dself_qkv, 3),
            (fourth, dqueries, 1),
            (fifth, dec_dinner, 1),
            (cotangent, dec_active, 1),
        ],
        [(dec_context, dself_low), (cross_context, dcross_low)],
    )
    partial, corner, moving, gains, ffn_moving, grad_dec_query = sync(
        partial, corner, moving, gains, ffn_moving, grad_dec_query
    )

    def dec_shape(values):
        return values.reshape(count_q, dec_part, width)

    ffn_moving, moving = reduce_step(info, (ffn_sums, ffn_moving, 4), (sums, moving, 2))[:2]
    arrived = to_chip(partial, corner)
    gains = some(gains, bits[:1])
    partial, arrived, moving, gains, ffn_moving = sync(
        partial, arrived, moving, gains, ffn_moving
    )

    def last_back(dh, x, a, b, c, g):
        return (dh + norm_back(x, g[0:1], a + b + c)[0],)

    moving = reduce_step(info, (sums, moving, 3))[0]
    gains = some(gains, bits[1:-1])
    input_grad = by_rows(
        last_back,
        info,
        [dhidden, inputs, partial[0], *arrived],
        [encoder_gains],
        [f32],
    )[0]
    moving, gains, input_grad, ffn_moving = sync(moving, gains, input_grad, ffn_moving)
    moving, (gains, ffn_moving) = reduce_step(info, (sums, moving, 4), hold=(gains, ffn_moving))
    last = swap(gains, "blk", bits[-1])
    grad_inner, grad_outer, grad_cross_key, grad_cross_value = finish(
        info,
        reduce_terms(ffn_sums, ffn_moving),
        (units, units, size, size),
        (False,) * 4,
    )
    enc_gain_grads, dec_gain_grads = gains[:2] + last[:2], gains[2:] + last[2:]
    grad_query, grad_key, grad_value, grad_output = finish(
        info, reduce_terms(sums, moving), (size,) * 4, (False, False, False, True)
    )

    return (
        states.reshape(encoder_input.shape),
        dec_shape(dec_states),
        input_grad.reshape(encoder_input.shape),
        dec_shape(dec_grad),
        grad_query,
        grad_key,
        grad_value,
        grad_output,
        grad_inner,
        grad_outer.T,
        grad_dec_query,
        grad_dec_key,
        grad_dec_value,
        grad_dec_output,
        grad_cross_query,
        grad_cross_key,
        grad_cross_value,
        grad_cross_output,
        grad_dec_inner,
        grad_dec_outer.T,
        enc_gain_grads,
        dec_gain_grads,
    )


def solution(mesh):
    placed = (
        P(None, "blk", "head", None),
        P(None, "blk"),
        P(None, "head", None),
        P("blk", "head"),
        P("blk", "head"),
        P("blk", "head"),
        P("head", "blk"),
        P("blk", "head"),
        P("head", "blk"),
        P("blk", "head"),
        P("blk", "head"),
        P("blk", "head"),
        P("head", "blk"),
        P("blk", "head"),
        P("blk", "head"),
        P("blk", "head"),
        P("head", "blk"),
        P("blk", "head"),
        P("head", "blk"),
        P(),
        P(),
        P(None, "blk", "head", None),
        P(None, "head", None),
    )
    return jax.shard_map(
        shards,
        mesh=mesh,
        in_specs=placed,
        out_specs=(placed[0], placed[2], placed[0], placed[2], *placed[3:19], P(), P()),
        check_vma=False,
    )
```
